32 devices in a mesh: rep: 4 (over x, core), tm: 8 (over z, y).
Axes of the slice: x: 2, y: 2, z: 4, core: 2. Of those that a mesh axis runs over, the one named last changes fastest.
Arguments:
- frames: bfloat16 [4, 32768, 512], P('rep', 'tm'), may hold values from -20 to 20
- first_weight: bfloat16 [2, 512, 512], replicated, may hold values from -0.1875 to 0.1875
- first_bias: float32 [512], replicated, may hold values from -4 to 4
- second_weight: bfloat16 [2, 512, 256], replicated, may hold values from -0.1875 to 0.1875
Outputs:
- propagated: float32 [4, 32768, 256], P('rep', 'tm')
- residual: float32 [4, 32768, 256], P('rep', 'tm')
The draws below stay inside these ranges and needn't reach their ends.
All inputs are finite; a program needn't handle non-finite values.
Results may differ from the reference program's by a relative error of at most 0.008.
Values may be sent and summed in bfloat16 or wider, within the bound.
No kernel may reach another device: no remote copies, remote signals or barrier semaphores. Data moves between devices by JAX's collectives and lax.ppermute only.
A program may use at most 64 MiB of HBM per device.

```python
import math
from functools import partial
import jax
import jax.numpy as jnp
from jax import lax

CH = 512
HID = 512
FEAT = 256
D1 = 32
D2 = 256
LAG = 1024
NF = 32768
REPS = 4


def draw_frames(key, part):
    wave_count = 32
    keys = jax.random.split(key, 4)
    times = jnp.arange(NF, dtype=jnp.float32) / NF
    replica = jnp.arange(REPS, dtype=jnp.float32) / REPS
    scales = jnp.exp(math.log(3.0) * (times[None, :] + replica[:, None])) / 3.0
    frequency = jax.random.uniform(keys[0], (wave_count,), jnp.float32, 2.0, 40.0)
    phase_shift = jax.random.uniform(keys[1], (REPS, wave_count), jnp.float32, 0.0, 2.0 * math.pi)
    mixing = jax.random.normal(keys[2], (wave_count, CH), jnp.float32) * (1.5 / math.sqrt(wave_count))
    waves = jnp.sin(2.0 * math.pi * frequency[None, None, :] * times[None, :, None] + phase_shift[:, None, :])
    slow_part = jnp.einsum('rtk,kc->rtc', waves, mixing)
    rough_part = jax.random.normal(keys[3], (REPS, NF, CH), jnp.float32)
    values = (slow_part + rough_part) * scales[:, :, None]
    return jnp.clip(values, -20.0, 20.0).astype(jnp.bfloat16)


def gaussian(key, shape, scale, bound, kind=jnp.bfloat16):
    return jnp.clip(scale * jax.random.normal(key, shape, jnp.float32), -bound, bound).astype(kind)


def setup_inputs(seed: int = 0) -> dict:
    key_of = jax.random.split(jax.random.key(seed), 5)
    frames = draw_frames(jax.random.fold_in(key_of[4], 71), 0)
    first_weight = gaussian(key_of[1], (2, CH, HID), (2 * CH) ** -0.5, 0.1875)
    first_bias = gaussian(key_of[2], (HID,), 1.0, 4.0, jnp.float32)
    second_weight = gaussian(key_of[3], (2, HID, FEAT), (2 * HID) ** -0.5, 0.1875)
    return dict(frames=frames, first_weight=first_weight, first_bias=first_bias, second_weight=second_weight)


ridge_level = 0.001

def layer_pair(current, previous, weights):
    return jnp.dot(current.astype(jnp.float32), weights[0].astype(jnp.float32), preferred_element_type=jnp.float32) + jnp.dot(previous.astype(jnp.float32), weights[1].astype(jnp.float32), preferred_element_type=jnp.float32)

def features_of(frame_block, first_weight, first_bias, second_weight):
    earlier_frames = jnp.concatenate([jnp.zeros((D1, CH), jnp.bfloat16), frame_block[:NF - D1]], 0)
    hidden = jax.nn.silu(layer_pair(frame_block, earlier_frames, first_weight) + first_bias).astype(jnp.bfloat16)
    earlier_hidden = jnp.concatenate([jnp.zeros((D2, HID), jnp.bfloat16), hidden[:NF - D2]], 0)
    return layer_pair(hidden, earlier_hidden, second_weight).astype(jnp.bfloat16)

def pair_stats(feature):
    paired = jnp.concatenate([feature[:NF - LAG], feature[LAG:]], 1)
    gram_full = jnp.dot(paired.T.astype(jnp.float32), paired.astype(jnp.float32), preferred_element_type=jnp.float32)
    return (gram_full, jnp.sum(paired.astype(jnp.float32), axis=0))

def reference(frames, first_weight, first_bias, second_weight):
    feature = lax.map(partial(features_of, first_weight=first_weight, first_bias=first_bias, second_weight=second_weight), frames)
    grams, column_sums = lax.map(pair_stats, feature)
    gram_total = jnp.sum(grams, axis=0)
    sum_total = jnp.sum(column_sums, axis=0)
    pair_count = jnp.asarray(REPS * (NF - LAG), jnp.float32)
    mean_vec = (sum_total[:FEAT] + sum_total[FEAT:]) / (2.0 * pair_count)
    centre = 2.0 * pair_count * (mean_vec[:, None] * mean_vec[None, :])
    inst_moment = gram_total[:FEAT, :FEAT] + gram_total[FEAT:, FEAT:] - centre
    lag_moment = gram_total[:FEAT, FEAT:] + gram_total[FEAT:, :FEAT] - centre
    identity = jnp.eye(FEAT, dtype=jnp.float32)
    factor = jnp.linalg.cholesky(inst_moment / (2.0 * pair_count) + ridge_level * identity)
    inverse = lax.linalg.triangular_solve(factor, identity, left_side=True, lower=True)
    half_step = jnp.dot(inverse, lag_moment / (2.0 * pair_count), precision=lax.Precision.HIGHEST)
    koopman = jnp.dot(half_step, inverse.T, precision=lax.Precision.HIGHEST)

    def project(block):
        whitened = jnp.dot(block.astype(jnp.float32) - mean_vec, inverse.T, precision=lax.Precision.HIGHEST)
        propagated = jnp.dot(whitened, koopman.T, precision=lax.Precision.HIGHEST)
        residual = jnp.concatenate([whitened[LAG:] - propagated[:NF - LAG], jnp.zeros((LAG, FEAT), jnp.float32)], 0)
        return (propagated, residual)
    propagated, residual = lax.map(project, feature)
    return (propagated, residual)
```

```python
from functools import partial

import jax
import jax.numpy as jnp
from jax import lax
from jax.experimental import pallas as pl
from jax.experimental.pallas import tpu as pltpu
from jax.sharding import PartitionSpec as P

D1 = 32
D2 = 256
LAG = 1024
RIDGE = 0.001
CHUNK = 512
PANEL = 16
VMEM_LIMIT = 56 * 1024 * 1024

F32 = jnp.float32
BF16 = jnp.bfloat16
HIGHEST = lax.Precision.HIGHEST


def passed_along(value, axis, steps):
    count = lax.axis_size(axis)
    first, last = (max(0, -steps), min(count, count - steps))
    return lax.ppermute(value, axis, [(source, source + steps) for source in range(first, last)])


def across(a, b, precision=None):
    return lax.dot_general(a, b, (((1,), (1,)), ((), ())), precision=precision, preferred_element_type=F32)


def gram(a, b):
    return lax.dot_general(a, b, (((0,), (0,)), ((), ())), preferred_element_type=F32)


def silu(x):
    half = 0.5 * x
    return half + half * jnp.tanh(half)


def feature_kernel(live_ref, x_ref, halo_ref, w1_ref, b1_ref, w2_ref, out_ref, last_x, last_h):
    bias = b1_ref[...]

    def hidden_of(current, previous):
        both = jnp.concatenate([current, previous], 1)
        return silu(jnp.dot(both, w1_ref[...], preferred_element_type=F32) + bias).astype(BF16)

    @pl.when(pl.program_id(0) == 0)
    def _():
        rows = halo_ref.shape[0]
        live = live_ref[0] > 0
        previous_x = halo_ref[rows - D1 :, :]
        before = hidden_of(halo_ref[rows - D2 :, :], halo_ref[rows - D2 - D1 : rows - D1, :])
        last_x[...] = jnp.where(live, previous_x, jnp.zeros_like(previous_x))
        last_h[...] = jnp.where(live, before, jnp.zeros_like(before))

    rows = x_ref.shape[0]
    x = x_ref[...]
    hidden = hidden_of(x, jnp.concatenate([last_x[...], x[: rows - D1]], 0))
    earlier = jnp.concatenate([last_h[...], hidden[: rows - D2]], 0)
    both = jnp.concatenate([hidden, earlier], 1)
    out_ref[...] = jnp.dot(both, w2_ref[...], preferred_element_type=F32).astype(BF16)
    last_x[...] = x[rows - D1 :]
    last_h[...] = hidden[rows - D2 :]


def features(live, frames, first_block, block_count, halo, halo_block, w1, b1, w2):
    channels, hid, feat = frames.shape[1], w1.shape[1], w2.shape[1]
    whole = lambda i: (0, 0)
    return pl.pallas_call(
        feature_kernel,
        grid=(block_count,),
        in_specs=[
            pl.BlockSpec(memory_space=pltpu.SMEM),
            pl.BlockSpec((CHUNK, channels), lambda i: (i + first_block, 0)),
            pl.BlockSpec((halo_block, channels), whole),
            pl.BlockSpec(w1.shape, whole),
            pl.BlockSpec(b1.shape, whole),
            pl.BlockSpec(w2.shape, whole),
        ],
        out_specs=pl.BlockSpec((CHUNK, feat), lambda i: (i, 0)),
        out_shape=jax.ShapeDtypeStruct((block_count * CHUNK, feat), BF16),
        scratch_shapes=[pltpu.VMEM((D1, channels), BF16), pltpu.VMEM((D2, hid), BF16)],
        compiler_params=pltpu.CompilerParams(vmem_limit_bytes=VMEM_LIMIT),
    )(live, frames, halo, w1, b1, w2)


def column_sum(rows):
    ones = jnp.ones((8, rows.shape[0]), BF16)
    return jnp.dot(ones, rows, preferred_element_type=F32)[0:1]


def moment_kernel(edge_ref, head_ref, body_ref, ahead_ref, out_ref, inst, lag, total):
    feat = head_ref.shape[1]
    lag_chunks = LAG // CHUNK
    chunks = 1 + body_ref.shape[0] // CHUNK

    def chunk(index):
        if index == 0:
            return head_ref[...]
        if index < chunks:
            return body_ref[(index - 1) * CHUNK : index * CHUNK, :]
        return ahead_ref[(index - chunks) * CHUNK : (index - chunks + 1) * CHUNK, :]

    weights = [2.0 - edge_ref[0].astype(F32), 2.0, 2.0 - edge_ref[1].astype(F32)]
    inst[...] = jnp.zeros_like(inst)
    lag[...] = jnp.zeros_like(lag)
    total[...] = jnp.zeros_like(total)
    for index in range(chunks):
        weight = weights[(index >= lag_chunks) + (index >= chunks - lag_chunks)]
        now = chunk(index)
        inst[...] += weight * gram(now, now)
        lag[...] += gram(now, chunk(index + lag_chunks))
        total[...] += weight * column_sum(now)

    both = lag[...] + lag[...].T
    row = lax.broadcasted_iota(jnp.int32, (feat, feat), 0)
    column = lax.broadcasted_iota(jnp.int32, (feat, feat), 1)
    out_ref[:, :feat] = jnp.where(column >= row, inst[...], both)
    out_ref[:, feat:] = jnp.zeros((feat, out_ref.shape[1] - feat), F32)
    diagonal = jnp.sum(jnp.where(column == row, both, 0.0), 0, keepdims=True)
    for half in range(feat // 128):
        part = slice(half * 128, half * 128 + 128)
        out_ref[half : half + 1, feat:] = total[:, part]
        out_ref[half + 2 : half + 3, feat:] = diagonal[:, part]


def moments(edge, head, body, ahead):
    feat = body.shape[1]
    vmem = pl.BlockSpec(memory_space=pltpu.VMEM)
    return pl.pallas_call(
        moment_kernel,
        in_specs=[pl.BlockSpec(memory_space=pltpu.SMEM), vmem, vmem, vmem],
        out_specs=vmem,
        out_shape=jax.ShapeDtypeStruct((feat, feat + 128), F32),
        scratch_shapes=[pltpu.VMEM((feat, feat), F32), pltpu.VMEM((feat, feat), F32), pltpu.VMEM((1, feat), F32)],
        compiler_params=pltpu.CompilerParams(vmem_limit_bytes=VMEM_LIMIT),
    )(edge, head, body, ahead)


def three_parts(x):
    high = x.astype(BF16)
    rest = x - high.astype(F32)
    middle = rest.astype(BF16)
    low = (rest - middle.astype(F32)).astype(BF16)
    return high, middle, low


def inverse_factor(work):
    size = work.shape[0]
    lane = lax.broadcasted_iota(jnp.int32, (PANEL, size), 1)
    sub = lax.broadcasted_iota(jnp.int32, (PANEL, size), 0)
    sub_narrow = lax.broadcasted_iota(jnp.int32, (PANEL, 128), 0)
    for start in range(0, size, PANEL):
        stop = start + PANEL
        panel = work[start:stop, :]
        columns = [
            jnp.broadcast_to(panel[:, start + k : start + k + 1], (PANEL, 128)) for k in range(PANEL)
        ]
        panel = jnp.where(
            (lane >= start) & (lane < stop), jnp.where(lane - start == sub, 1.0, 0.0), panel
        )
        pivots = jnp.ones((PANEL, 128), F32)
        for j in range(PANEL):
            pivot = columns[j][j : j + 1, :]
            factor = columns[j] * (1.0 / pivot)
            pivots = jnp.where(sub_narrow == j, pivot, pivots)
            for k in range(j + 1, PANEL):
                columns[k] = columns[k] - factor * columns[k][j : j + 1, :]
            if j + 1 < PANEL:
                below = jnp.where(sub_narrow > j, factor, 0.0)
                wide = jnp.concatenate([below] * (size // 128), 1)
                panel = panel - wide * panel[j : j + 1, :]
        scale = lax.rsqrt(pivots)
        panel = panel * jnp.concatenate([scale] * (size // 128), 1)
        work[start:stop, :] = panel
        if stop < size:
            high, middle, low = three_parts(panel)
            left = jnp.concatenate([high, high, middle, high, low, middle], 0)
            right = jnp.concatenate([high, middle, high, low, high, middle], 0)
            first = stop // 128 * 128
            update = gram(left[:, first:], right)
            kept = lax.broadcasted_iota(jnp.int32, (size - stop, size), 1)
            kept = (kept < start) | (kept >= stop)
            work[stop:, :] = jnp.where(kept, work[stop:, :], 0.0) - update[stop - first :]
    row = lax.broadcasted_iota(jnp.int32, (size, size), 0)
    column = lax.broadcasted_iota(jnp.int32, (size, size), 1)
    return jnp.where(column <= row, work[...], 0.0)


def koopman_kernel(scale_ref, packed_ref, split_ref, shift_ref, work):
    feat = packed_ref.shape[0]
    scale = scale_ref[0]
    packed = packed_ref[:, :feat]
    extra = packed_ref[0:8, feat:]
    halves = feat // 128
    mean = jnp.concatenate([extra[h : h + 1] for h in range(halves)], 1) * scale
    diagonal = jnp.concatenate([extra[2 + h : 3 + h] for h in range(halves)], 1)
    row = lax.broadcasted_iota(jnp.int32, (feat, feat), 0)
    column = lax.broadcasted_iota(jnp.int32, (feat, feat), 1)
    turned = packed.T
    centre = jnp.broadcast_to(mean, (feat, feat))
    centre = centre * centre.T
    inst = jnp.where(column >= row, packed, turned)
    lag = jnp.where(column < row, packed, turned)
    lag = jnp.where(column == row, jnp.broadcast_to(diagonal, (feat, feat)), lag)
    work[...] = inst * scale - centre + jnp.where(column == row, RIDGE, 0.0)
    lag = lag * scale - centre
    inverse = inverse_factor(work)
    half_step = jnp.dot(inverse, lag, precision=HIGHEST, preferred_element_type=F32)
    koopman = across(half_step, inverse, HIGHEST)
    moved = jnp.dot(koopman, inverse, precision=HIGHEST, preferred_element_type=F32)
    for index, matrix in enumerate((inverse, moved)):
        high = matrix.astype(BF16)
        split_ref[2 * index] = high
        split_ref[2 * index + 1] = (matrix - high.astype(F32)).astype(BF16)
        rows = jnp.broadcast_to(mean, (8, feat))
        shift_ref[index] = across(rows, matrix, HIGHEST)


def koopman_parts(scale, packed):
    feat = packed.shape[0]
    vmem = pl.BlockSpec(memory_space=pltpu.VMEM)
    return pl.pallas_call(
        koopman_kernel,
        in_specs=[pl.BlockSpec(memory_space=pltpu.SMEM), vmem],
        out_specs=(vmem, vmem),
        out_shape=(
            jax.ShapeDtypeStruct((4, feat, feat), BF16),
            jax.ShapeDtypeStruct((2, 8, feat), F32),
        ),
        scratch_shapes=[pltpu.VMEM((feat, feat), F32)],
        compiler_params=pltpu.CompilerParams(vmem_limit_bytes=VMEM_LIMIT),
    )(scale, packed)


def project_kernel(
    edge_ref, head_ref, body_ref, later_ref, ahead_ref, split_ref, shift_ref, moved_ref, residual_ref
):
    step = pl.program_id(0)
    steps = pl.num_programs(0)
    lag_steps = LAG // CHUNK

    def product(block, index):
        return across(block, split_ref[2 * index]) + across(block, split_ref[2 * index + 1]) - shift_ref[index][0:1]

    current = jnp.where(step == 0, head_ref[...], body_ref[...])
    inside = step < steps - lag_steps
    later = jnp.where(inside, later_ref[...], ahead_ref[...])
    moved = product(current, 1)
    moved_ref[...] = moved
    live = inside | (edge_ref[1] == 0)
    residual_ref[...] = jnp.where(live, product(later, 0) - moved, 0.0)


def project(edge, head, body, ahead, split, shift):
    feat = body.shape[1]
    body_blocks = body.shape[0] // CHUNK
    steps = body_blocks + 1
    lag_steps = LAG // CHUNK
    block = (CHUNK, feat)
    out = jax.ShapeDtypeStruct((steps * CHUNK, feat), F32)
    return pl.pallas_call(
        project_kernel,
        grid=(steps,),
        in_specs=[
            pl.BlockSpec(memory_space=pltpu.SMEM),
            pl.BlockSpec(block, lambda i: (0, 0)),
            pl.BlockSpec(block, lambda i: (jnp.maximum(i - 1, 0), 0)),
            pl.BlockSpec(block, lambda i: (jnp.minimum(i - 1 + lag_steps, body_blocks - 1), 0)),
            pl.BlockSpec(block, lambda i: (jnp.maximum(i - (steps - lag_steps), 0), 0)),
            pl.BlockSpec(split.shape, lambda i: (0, 0, 0)),
            pl.BlockSpec(shift.shape, lambda i: (0, 0, 0)),
        ],
        out_specs=(pl.BlockSpec(block, lambda i: (i, 0)), pl.BlockSpec(block, lambda i: (i, 0))),
        out_shape=(out, out),
        compiler_params=pltpu.CompilerParams(vmem_limit_bytes=VMEM_LIMIT),
    )(edge, head, body, body, ahead, split, shift)


def summed(packed, axes, count):
    feat, width = packed.shape
    parts = packed.reshape(count, feat // count, width)
    parts = lax.all_to_all(parts, axes, 0, 0, tiled=True)
    mine = jnp.sum(parts, 0)
    return lax.all_gather(mine, axes, axis=0, tiled=True)


def on_device(device_count, frames, first_weight, first_bias, second_weight):
    frame_block = frames[0]
    row_count, channels = frame_block.shape
    hid, feat = second_weight.shape[1:]
    tm_index = lax.axis_index("tm")
    tm_count = lax.axis_size("tm")
    w1 = first_weight.reshape(2 * channels, hid)
    w2 = second_weight.reshape(2 * hid, feat)
    b1 = first_bias.reshape(1, hid)

    halo = passed_along(frame_block[row_count - D1 - D2 :], "tm", 1)
    yes = jnp.ones((1,), jnp.int32)
    body = features(yes, frame_block, 1, row_count // CHUNK - 1, frame_block, CHUNK, w1, b1, w2)
    live = (tm_index > 0).astype(jnp.int32).reshape(1)
    head = features(live, frame_block, 0, 1, halo, D1 + D2, w1, b1, w2)

    ahead = passed_along(jnp.concatenate([head, body[: LAG - CHUNK]], 0), "tm", -1)
    edge = jnp.stack([tm_index == 0, tm_index == tm_count - 1]).astype(jnp.int32)
    packed = moments(edge, head, body, ahead)
    packed = summed(packed, ("rep", "tm"), device_count)
    pair_count = lax.axis_size("rep") * (row_count * tm_count - LAG)
    scale = jnp.full((1,), 1.0 / (2.0 * pair_count), F32)
    split, shift = koopman_parts(scale, packed)
    propagated, residual = project(edge, head, body, ahead, split, shift)
    return (propagated[None], residual[None])


def solution(mesh):
    placed = (P("rep", "tm", None), P(), P(), P())
    return jax.shard_map(
        partial(on_device, mesh.size),
        mesh=mesh,
        in_specs=placed,
        out_specs=(P("rep", "tm", None), P("rep", "tm", None)),
        check_vma=False,
    )
```

```python
import jax
import jax.numpy as jnp
from jax import lax
from jax.experimental import pallas as pl
from jax.experimental.pallas import tpu as pltpu
from jax.sharding import PartitionSpec as P

D1 = 32
D2 = 256
LAG = 1024
RIDGE = 0.001
CHUNK = 512
BLOCK = 256
PANEL = 16
VMEM_LIMIT = 56 * 1024 * 1024

F32 = jnp.float32
BF16 = jnp.bfloat16
HIGHEST = lax.Precision.HIGHEST


def passed_along(value, axis, steps):
    count = lax.axis_size(axis)
    first, last = (max(0, -steps), min(count, count - steps))
    return lax.ppermute(value, axis, [(source, source + steps) for source in range(first, last)])


def across(a, b, precision=None):
    return lax.dot_general(a, b, (((1,), (1,)), ((), ())), precision=precision, preferred_element_type=F32)


def gram(a, b):
    return lax.dot_general(a, b, (((0,), (0,)), ((), ())), preferred_element_type=F32)


def silu(x):
    half = 0.5 * x
    return half + half * jnp.tanh(half)


def feature_steps(xs, hs, out_ref, out_start, count, w1_ref, b1_ref, w2_ref, begin, finish):
    channels = xs.shape[1]
    hid = hs.shape[1]
    bias = b1_ref[...]

    def hidden(step):
        at = pl.ds(step * BLOCK, BLOCK)
        after = pl.ds(step * BLOCK + D1, BLOCK)
        z = jnp.dot(xs[after, :], w1_ref[:channels, :], preferred_element_type=F32)
        z += jnp.dot(xs[at, :], w1_ref[channels:, :], preferred_element_type=F32)
        return silu(z + bias).astype(BF16)

    def feature(step):
        now = hs[pl.ds(step * BLOCK + D2, BLOCK), :]
        then = hs[pl.ds(step * BLOCK, BLOCK), :]
        value = jnp.dot(now, w2_ref[:hid, :], preferred_element_type=F32)
        value += jnp.dot(then, w2_ref[hid:, :], preferred_element_type=F32)
        value = value.astype(BF16)
        out_ref[pl.ds(out_start + step * BLOCK, BLOCK), :] = value
        return value

    for step in range(count + 1):
        begin(step)
        fresh = hidden(step)
        if step >= 2:
            finish(step - 2, feature(step - 2))
        hs[step * BLOCK : (step + 1) * BLOCK, :] = fresh
        if step == 0:
            yield
    finish(count - 1, feature(count - 1))


def run_steps(steps, after_first=None):
    for _ in steps:
        if after_first is not None:
            after_first()


def nothing(*_):
    return None


def early_kernel(frames_ref, w1_ref, b1_ref, w2_ref, out_ref, xs, hs, sem):
    copy = pltpu.make_async_copy(frames_ref.at[pl.ds(LAG // 2 - D1 - D2, xs.shape[0])], xs, sem)
    copy.start()
    copy.wait()
    run_steps(
        feature_steps(
            xs, hs, out_ref, 0, out_ref.shape[0] // BLOCK, w1_ref, b1_ref, w2_ref, nothing, nothing
        )
    )


def head_kernel(live_ref, frames_ref, halo_ref, w1_ref, b1_ref, w2_ref, out_ref, xs, hs, sem):
    halo_rows = halo_ref.shape[0]
    copy = pltpu.make_async_copy(
        frames_ref.at[pl.ds(0, out_ref.shape[0])], xs.at[pl.ds(halo_rows, out_ref.shape[0])], sem
    )
    copy.start()
    xs[:halo_rows, :] = halo_ref[...]
    copy.wait()

    def clear():
        before = hs[:D2, :]
        hs[:D2, :] = jnp.where(live_ref[0] > 0, before, jnp.zeros_like(before))

    run_steps(
        feature_steps(
            xs, hs, out_ref, 0, out_ref.shape[0] // BLOCK, w1_ref, b1_ref, w2_ref, nothing, nothing
        ),
        clear,
    )


def feature_scratch(rows, channels, hid):
    return [
        pltpu.VMEM((rows + D1 + D2, channels), BF16),
        pltpu.VMEM((rows + D2, hid), BF16),
    ]


def first_rows(kernel, operands, specs, w1, b1, w2):
    vmem = pl.BlockSpec(memory_space=pltpu.VMEM)
    rows = LAG // 2
    return pl.pallas_call(
        kernel,
        in_specs=specs + [vmem, vmem, vmem],
        out_specs=vmem,
        out_shape=jax.ShapeDtypeStruct((rows, w2.shape[1]), BF16),
        scratch_shapes=feature_scratch(rows, w1.shape[0] // 2, w1.shape[1]) + [pltpu.SemaphoreType.DMA],
        compiler_params=pltpu.CompilerParams(vmem_limit_bytes=VMEM_LIMIT),
    )(*operands, w1, b1, w2)


def column_sum(rows):
    ones = jnp.ones((8, rows.shape[0]), BF16)
    return jnp.dot(ones, rows, preferred_element_type=F32)


def body_kernel(
    edge_ref, frames_ref, head_ref, early_ref, w1_ref, b1_ref, w2_ref, out_ref, inst, lag, total, xs, hs, sems
):
    rows, feat = out_ref.shape
    first = LAG - D1 - D2
    count = (rows - LAG) // BLOCK
    pieces = [0] + [BLOCK * (2 * k + 1) + D1 for k in range(count // 2 + 1)]
    pieces = [p for p in pieces if p < rows - first] + [rows - first]
    copies = []
    for index, (lo, hi) in enumerate(zip(pieces[:-1], pieces[1:])):
        copy = pltpu.make_async_copy(
            frames_ref.at[pl.ds(first + lo, hi - lo)], xs.at[pl.ds(lo, hi - lo)], sems.at[index]
        )
        copy.start()
        copies.append((lo, copy))
    half = LAG // 2
    out_ref[:half, :] = head_ref[...]
    out_ref[half:LAG, :] = early_ref[...]
    weights = [2.0 - edge_ref[0].astype(F32), 2.0, 2.0 - edge_ref[1].astype(F32)]
    start = out_ref[:LAG, :]
    inst[...] = weights[0] * gram(start, start)
    total[...] = weights[0] * column_sum(start)
    lag[...] = jnp.zeros_like(lag)

    def begin(step):
        while copies and copies[0][0] < (step + 1) * BLOCK + D1:
            copies.pop(0)[1].wait()

    def finish(step, value):
        at = LAG + step * BLOCK
        weight = weights[2] if at >= rows - LAG else weights[1]
        both = gram(value, jnp.concatenate([value, out_ref[at - LAG : at - LAG + BLOCK, :]], 1))
        inst[...] += weight * both[:, :feat]
        lag[...] += both[:, feat:]
        total[...] += weight * column_sum(value)

    run_steps(feature_steps(xs, hs, out_ref, LAG, count, w1_ref, b1_ref, w2_ref, begin, finish))


def body(edge, frames, head, early, w1, b1, w2):
    rows, channels = frames.shape
    hid, feat = w1.shape[1], w2.shape[1]
    vmem = pl.BlockSpec(memory_space=pltpu.VMEM)
    square = jax.ShapeDtypeStruct((feat, feat), F32)
    return pl.pallas_call(
        body_kernel,
        in_specs=[pl.BlockSpec(memory_space=pltpu.SMEM), pl.BlockSpec(memory_space=pl.ANY)] + [vmem] * 5,
        out_specs=(vmem,) * 4,
        out_shape=(
            jax.ShapeDtypeStruct((rows, feat), BF16),
            square,
            square,
            jax.ShapeDtypeStruct((8, feat), F32),
        ),
        scratch_shapes=feature_scratch(rows - LAG, channels, hid)
        + [pltpu.SemaphoreType.DMA((rows // BLOCK,))],
        compiler_params=pltpu.CompilerParams(vmem_limit_bytes=VMEM_LIMIT),
    )(edge, frames, head, early, w1, b1, w2)


def pack_kernel(feature_ref, ahead_head_ref, ahead_early_ref, inst, lag, total, out_ref):
    feat = inst.shape[0]
    half = LAG // 2
    edge = feature_ref.shape[0] - LAG
    cross = lag[...] + gram(ahead_head_ref[...], feature_ref[edge : edge + half, :])
    cross += gram(ahead_early_ref[...], feature_ref[edge + half :, :])
    both = cross + cross.T
    row = lax.broadcasted_iota(jnp.int32, (feat, feat), 0)
    column = lax.broadcasted_iota(jnp.int32, (feat, feat), 1)
    out_ref[:feat, :] = jnp.where(column >= row, inst[...], both)
    out_ref[feat:, :] = jnp.zeros((out_ref.shape[0] - feat, feat), F32)
    out_ref[feat : feat + 1, :] = total[0:1, :]
    out_ref[feat + 1 : feat + 2, :] = jnp.sum(jnp.where(column == row, both, 0.0), 0, keepdims=True)


def pack(feature, ahead_head, ahead_early, inst, lag, total, packed_rows):
    vmem = pl.BlockSpec(memory_space=pltpu.VMEM)
    return pl.pallas_call(
        pack_kernel,
        in_specs=[vmem] * 6,
        out_specs=vmem,
        out_shape=jax.ShapeDtypeStruct((packed_rows, inst.shape[0]), F32),
        compiler_params=pltpu.CompilerParams(vmem_limit_bytes=VMEM_LIMIT),
    )(feature, ahead_head, ahead_early, inst, lag, total)


def three_parts(x):
    high = x.astype(BF16)
    rest = x - high.astype(F32)
    middle = rest.astype(BF16)
    low = (rest - middle.astype(F32)).astype(BF16)
    return high, middle, low


def inverse_factor(work):
    size = work.shape[0]
    lane = lax.broadcasted_iota(jnp.int32, (PANEL, size), 1)
    sub = lax.broadcasted_iota(jnp.int32, (PANEL, size), 0)
    sub_narrow = lax.broadcasted_iota(jnp.int32, (PANEL, 128), 0)
    for start in range(0, size, PANEL):
        stop = start + PANEL
        panel = work[start:stop, :]
        columns = [
            jnp.broadcast_to(panel[:, start + k : start + k + 1], (PANEL, 128)) for k in range(PANEL)
        ]
        panel = jnp.where(
            (lane >= start) & (lane < stop), jnp.where(lane - start == sub, 1.0, 0.0), panel
        )
        pivots = jnp.ones((PANEL, 128), F32)
        for j in range(PANEL):
            pivot = columns[j][j : j + 1, :]
            factor = columns[j] * (1.0 / pivot)
            pivots = jnp.where(sub_narrow == j, pivot, pivots)
            for k in range(j + 1, PANEL):
                columns[k] = columns[k] - factor * columns[k][j : j + 1, :]
            if j + 1 < PANEL:
                below = jnp.where(sub_narrow > j, factor, 0.0)
                wide = jnp.concatenate([below] * (size // 128), 1)
                panel = panel - wide * panel[j : j + 1, :]
        scale = lax.rsqrt(pivots)
        panel = panel * jnp.concatenate([scale] * (size // 128), 1)
        work[start:stop, :] = panel
        if stop < size:
            high, middle, low = three_parts(panel)
            left = jnp.concatenate([high, high, middle, high, low, middle], 0)
            right = jnp.concatenate([high, middle, high, low, high, middle], 0)
            first = stop // 128 * 128
            update = gram(left[:, first:], right)
            kept = lax.broadcasted_iota(jnp.int32, (size - stop, size), 1)
            kept = (kept < start) | (kept >= stop)
            work[stop:, :] = jnp.where(kept, work[stop:, :], 0.0) - update[stop - first :]
    row = lax.broadcasted_iota(jnp.int32, (size, size), 0)
    column = lax.broadcasted_iota(jnp.int32, (size, size), 1)
    return jnp.where(column <= row, work[...], 0.0)


def koopman_kernel(scale_ref, packed_ref, split_ref, shift_ref, work):
    feat = packed_ref.shape[1]
    scale = scale_ref[0]
    packed = packed_ref[:feat, :]
    mean = packed_ref[feat : feat + 1, :] * scale
    diagonal = packed_ref[feat + 1 : feat + 2, :]
    row = lax.broadcasted_iota(jnp.int32, (feat, feat), 0)
    column = lax.broadcasted_iota(jnp.int32, (feat, feat), 1)
    turned = packed.T
    centre = jnp.broadcast_to(mean, (feat, feat))
    centre = centre * centre.T
    inst = jnp.where(column >= row, packed, turned)
    lag = jnp.where(column < row, packed, turned)
    lag = jnp.where(column == row, jnp.broadcast_to(diagonal, (feat, feat)), lag)
    work[...] = inst * scale - centre + jnp.where(column == row, RIDGE, 0.0)
    lag = lag * scale - centre
    inverse = inverse_factor(work)
    half_step = jnp.dot(inverse, lag, precision=HIGHEST, preferred_element_type=F32)
    koopman = across(half_step, inverse, HIGHEST)
    moved = jnp.dot(koopman, inverse, precision=HIGHEST, preferred_element_type=F32)
    for index, matrix in enumerate((inverse, moved)):
        turned = matrix.T
        high = turned.astype(BF16)
        split_ref[2 * index] = high
        split_ref[2 * index + 1] = (turned - high.astype(F32)).astype(BF16)
        rows = jnp.broadcast_to(mean, (8, feat))
        shift_ref[index] = jnp.dot(rows, turned, precision=HIGHEST, preferred_element_type=F32)


def koopman_parts(scale, packed):
    feat = packed.shape[1]
    vmem = pl.BlockSpec(memory_space=pltpu.VMEM)
    return pl.pallas_call(
        koopman_kernel,
        in_specs=[pl.BlockSpec(memory_space=pltpu.SMEM), vmem],
        out_specs=(vmem, vmem),
        out_shape=(
            jax.ShapeDtypeStruct((4, feat, feat), BF16),
            jax.ShapeDtypeStruct((2, 8, feat), F32),
        ),
        scratch_shapes=[pltpu.VMEM((feat, feat), F32)],
        compiler_params=pltpu.CompilerParams(vmem_limit_bytes=VMEM_LIMIT),
    )(scale, packed)


def project_kernel(
    edge_ref, feature_ref, ahead_head_ref, ahead_early_ref, split_ref, shift_ref, moved_ref, residual_ref
):
    step = pl.program_id(0)
    inside = feature_ref.shape[0] // CHUNK - 2

    def product(block, index):
        value = jnp.dot(block, split_ref[2 * index], preferred_element_type=F32)
        value += jnp.dot(block, split_ref[2 * index + 1], preferred_element_type=F32)
        return value - shift_ref[index][0:1]

    def moved():
        value = product(feature_ref[pl.ds(pl.multiple_of(step * CHUNK, CHUNK), CHUNK), :], 1)
        moved_ref[...] = value
        return value

    @pl.when(step < inside)
    def _():
        later = feature_ref[pl.ds(pl.multiple_of(step * CHUNK + LAG, CHUNK), CHUNK), :]
        residual_ref[...] = product(later, 0) - moved()

    for index, ahead_ref in enumerate((ahead_head_ref, ahead_early_ref)):

        @pl.when(step == inside + index)
        def _():
            value = product(ahead_ref[...], 0) - moved()
            residual_ref[...] = jnp.where(edge_ref[1] > 0, 0.0, value)


def project(edge, feature, ahead_head, ahead_early, split, shift):
    rows, feat = feature.shape
    vmem = pl.BlockSpec(memory_space=pltpu.VMEM)
    out = jax.ShapeDtypeStruct((rows, feat), F32)
    block = pl.BlockSpec((CHUNK, feat), lambda i: (i, 0))
    return pl.pallas_call(
        project_kernel,
        grid=(rows // CHUNK,),
        in_specs=[pl.BlockSpec(memory_space=pltpu.SMEM)] + [vmem] * 5,
        out_specs=(block, block),
        out_shape=(out, out),
        compiler_params=pltpu.CompilerParams(vmem_limit_bytes=VMEM_LIMIT),
    )(edge, feature, ahead_head, ahead_early, split, shift)


def from_all(value, axis):
    copies = jnp.broadcast_to(value[None], (lax.axis_size(axis), *value.shape))
    return lax.all_to_all(copies, axis, 0, 0, tiled=True)


def summed(packed):
    rows, feat = packed.shape
    parts = packed.reshape(lax.axis_size("rep"), -1, feat)
    mine = jnp.sum(lax.all_to_all(parts, "rep", 0, 0, tiled=True), 0)
    mine = jnp.sum(from_all(mine, "tm"), 0)
    return from_all(mine, "rep").reshape(rows, feat)


def on_device(frames, first_weight, first_bias, second_weight):
    frame_block = frames[0]
    row_count, channels = frame_block.shape
    hid, feat = second_weight.shape[1:]
    tm_index = lax.axis_index("tm")
    tm_count = lax.axis_size("tm")
    rep_count = lax.axis_size("rep")
    weights = (
        first_weight.reshape(2 * channels, hid),
        first_bias.reshape(1, hid),
        second_weight.reshape(2 * hid, feat),
    )
    smem, anywhere, vmem = (pl.BlockSpec(memory_space=m) for m in (pltpu.SMEM, pl.ANY, pltpu.VMEM))

    halo = passed_along(frame_block[row_count - D1 - D2 :], "tm", 1)
    early = first_rows(early_kernel, (frame_block,), [anywhere], *weights)
    ahead_early = passed_along(early, "tm", -1)
    live = (tm_index > 0).astype(jnp.int32).reshape(1)
    head = first_rows(head_kernel, (live, frame_block, halo), [smem, anywhere, vmem], *weights)
    ahead_head = passed_along(head, "tm", -1)
    edge = jnp.stack([tm_index == 0, tm_index == tm_count - 1]).astype(jnp.int32)
    feature, inst, lag, total = body(edge, frame_block, head, early, *weights)
    unit = 8 * rep_count
    packed_rows = -(-(feat + 2) // unit) * unit
    packed = summed(pack(feature, ahead_head, ahead_early, inst, lag, total, packed_rows))
    pair_count = rep_count * (row_count * tm_count - LAG)
    scale = jnp.full((1,), 1.0 / (2.0 * pair_count), F32)
    split, shift = koopman_parts(scale, packed)
    propagated, residual = project(edge, feature, ahead_head, ahead_early, split, shift)
    return (propagated[None], residual[None])


def solution(mesh):
    placed = (P("rep", "tm", None), P(), P(), P())
    return jax.shard_map(
        on_device,
        mesh=mesh,
        in_specs=placed,
        out_specs=(P("rep", "tm", None), P("rep", "tm", None)),
        check_vma=False,
    )
```

```python
import jax
import jax.numpy as jnp
from jax import lax
from jax.experimental import pallas as pl
from jax.experimental.pallas import tpu as pltpu
from jax.sharding import Mesh, PartitionSpec as P

D1 = 32
D2 = 256
LAG = 1024
RIDGE = 0.001
CHUNK = 512
PANEL = 16
MIB = 1024 * 1024

F32 = jnp.float32
BF16 = jnp.bfloat16
HIGHEST = lax.Precision.HIGHEST


def passed_along(value, axis, steps):
    count = lax.axis_size(axis)
    first, last = (max(0, -steps), min(count, count - steps))
    return lax.ppermute(value, axis, [(source, source + steps) for source in range(first, last)])


def across(a, b, precision=None):
    return lax.dot_general(a, b, (((1,), (1,)), ((), ())), precision=precision, preferred_element_type=F32)


def gram(a, b):
    return lax.dot_general(a, b, (((0,), (0,)), ((), ())), preferred_element_type=F32)


def silu(x):
    half = 0.5 * x
    return half + half * jnp.tanh(half)


def hidden_rows(xs, hs, at, rows, w1_ref, b1_ref):
    channels = xs.shape[1]
    z = jnp.dot(xs[pl.ds(at + D1, rows), :], w1_ref[:channels, :], preferred_element_type=F32)
    z += jnp.dot(xs[pl.ds(at, rows), :], w1_ref[channels:, :], preferred_element_type=F32)
    return silu(z + b1_ref[...]).astype(BF16)


def feature_rows(hs, at, rows, w2_ref):
    hid = hs.shape[1]
    value = jnp.dot(hs[pl.ds(at + D2, rows), :], w2_ref[:hid, :], preferred_element_type=F32)
    value += jnp.dot(hs[pl.ds(at, rows), :], w2_ref[hid:, :], preferred_element_type=F32)
    return value.astype(BF16)


def early_kernel(frames_ref, w1_ref, b1_ref, w2_ref, out_ref, xs, hs, sem):
    copy = pltpu.make_async_copy(frames_ref.at[pl.ds(LAG // 2 - D1 - D2, xs.shape[0])], xs, sem)
    copy.start()
    copy.wait()
    for at in range(0, hs.shape[0], D2):
        hs[at : at + D2, :] = hidden_rows(xs, hs, at, D2, w1_ref, b1_ref)
    out_ref[...] = feature_rows(hs, 0, out_ref.shape[0], w2_ref)


def head_kernel(frames_ref, halo_ref, w1_ref, b1_ref, w2_ref, out_ref, xs, hs, sem):
    halo_rows = halo_ref.shape[0]
    copy = pltpu.make_async_copy(
        frames_ref.at[pl.ds(0, out_ref.shape[0])], xs.at[pl.ds(halo_rows, out_ref.shape[0])], sem
    )
    copy.start()
    xs[:halo_rows, :] = halo_ref[...]
    before = hidden_rows(xs, hs, 0, D2, w1_ref, b1_ref)
    hs[:D2, :] = jnp.where(lax.axis_index("tm") > 0, before, jnp.zeros_like(before))
    copy.wait()
    for at in range(D2, hs.shape[0], D2):
        hs[at : at + D2, :] = hidden_rows(xs, hs, at, D2, w1_ref, b1_ref)
    out_ref[...] = feature_rows(hs, 0, out_ref.shape[0], w2_ref)


def feature_scratch(rows, channels, hid):
    return [
        pltpu.VMEM((rows + D1 + D2, channels), BF16),
        pltpu.VMEM((rows + D2, hid), BF16),
    ]


def first_rows(kernel, operands, specs, w1, b1, w2):
    vmem = pl.BlockSpec(memory_space=pltpu.VMEM)
    rows = LAG // 2
    return pl.pallas_call(
        kernel,
        in_specs=specs + [vmem, vmem, vmem],
        out_specs=vmem,
        out_shape=jax.ShapeDtypeStruct((rows, w2.shape[1]), BF16),
        scratch_shapes=feature_scratch(rows, w1.shape[0] // 2, w1.shape[1]) + [pltpu.SemaphoreType.DMA],
        compiler_params=pltpu.CompilerParams(vmem_limit_bytes=8 * MIB),
    )(*operands, w1, b1, w2)


def column_sum(rows):
    ones = jnp.ones((8, rows.shape[0]), BF16)
    return jnp.dot(ones, rows, preferred_element_type=F32)


def body_kernel(frames_ref, head_ref, early_ref, w1_ref, b1_ref, w2_ref, out_ref, inst, lag, total, xs, hs, sems):
    rows, feat = out_ref.shape
    first = LAG - D1 - D2
    steps = (rows - LAG) // CHUNK

    def arriving(step):
        start = step * CHUNK + D1 + D2
        return pltpu.make_async_copy(
            frames_ref.at[pl.ds(first + start, CHUNK)], xs.at[pl.ds(start, CHUNK)], sems.at[step]
        )

    opening = pltpu.make_async_copy(
        frames_ref.at[pl.ds(first, D1 + D2)], xs.at[pl.ds(0, D1 + D2)], sems.at[steps]
    )
    opening.start()
    for step in range(steps):
        arriving(step).start()
    half = LAG // 2
    out_ref[:half, :] = head_ref[...]
    out_ref[half:LAG, :] = early_ref[...]
    tm_index, tm_last = lax.axis_index("tm"), lax.axis_size("tm") - 1
    first_weight = jnp.where(tm_index == 0, 1.0, 2.0)
    last_weight = jnp.where(tm_index == tm_last, 1.0, 2.0)
    start = out_ref[:LAG, :]
    inst[...] = first_weight * gram(start, start)
    total[...] = first_weight * column_sum(start)
    lag[...] = jnp.zeros_like(lag)
    opening.wait()
    hs[:D2, :] = hidden_rows(xs, hs, 0, D2, w1_ref, b1_ref)
    arriving(0).wait()
    hs[D2 : D2 + CHUNK, :] = hidden_rows(xs, hs, D2, CHUNK, w1_ref, b1_ref)

    def finish(step):
        value = feature_rows(hs, step * CHUNK, CHUNK, w2_ref)
        out_ref[pl.ds(LAG + step * CHUNK, CHUNK), :] = value
        weight = jnp.where(step >= steps - LAG // CHUNK, last_weight, 2.0)
        both = gram(value, jnp.concatenate([value, out_ref[pl.ds(step * CHUNK, CHUNK), :]], 1))
        inst[...] += weight * both[:, :feat]
        lag[...] += both[:, feat:]
        total[...] += weight * column_sum(value)

    def loop(step, carry):
        arriving(step + 1).wait()
        at = pl.multiple_of((step + 1) * CHUNK + D2, D2)
        fresh = hidden_rows(xs, hs, at, CHUNK, w1_ref, b1_ref)
        finish(step)
        hs[pl.ds(at, CHUNK), :] = fresh
        return carry

    lax.fori_loop(0, steps - 1, loop, 0)
    finish(steps - 1)


def body(frames, head, early, w1, b1, w2):
    rows, channels = frames.shape
    hid, feat = w1.shape[1], w2.shape[1]
    vmem = pl.BlockSpec(memory_space=pltpu.VMEM)
    square = jax.ShapeDtypeStruct((feat, feat), F32)
    return pl.pallas_call(
        body_kernel,
        in_specs=[pl.BlockSpec(memory_space=pl.ANY)] + [vmem] * 5,
        out_specs=(vmem,) * 4,
        out_shape=(
            jax.ShapeDtypeStruct((rows, feat), BF16),
            square,
            square,
            jax.ShapeDtypeStruct((8, feat), F32),
        ),
        scratch_shapes=feature_scratch(rows - LAG, channels, hid)
        + [pltpu.SemaphoreType.DMA((rows // CHUNK,))],
        compiler_params=pltpu.CompilerParams(vmem_limit_bytes=24 * MIB),
    )(frames, head, early, w1, b1, w2)


def pack_kernel(feature_ref, ahead_head_ref, ahead_early_ref, inst, lag, total, kept_ref, sent_ref, packed):
    feat = inst.shape[0]
    half = LAG // 2
    edge = feature_ref.shape[0] - LAG
    cross = lag[...] + gram(ahead_head_ref[...], feature_ref[edge : edge + half, :])
    cross += gram(ahead_early_ref[...], feature_ref[edge + half :, :])
    both = cross + cross.T
    row = lax.broadcasted_iota(jnp.int32, (feat, feat), 0)
    column = lax.broadcasted_iota(jnp.int32, (feat, feat), 1)
    packed[:, :feat] = jnp.where(column >= row, inst[...], both)
    packed[:, feat:] = jnp.zeros((feat, packed.shape[1] - feat), F32)
    diagonal = jnp.sum(jnp.where(column == row, both, 0.0), 0, keepdims=True)
    for index in range(feat // 128):
        part = slice(index * 128, index * 128 + 128)
        packed[index : index + 1, feat:] = total[0:1, part]
        packed[index + 2 : index + 3, feat:] = diagonal[:, part]
    share = kept_ref.shape[0]
    core = lax.axis_index("core")
    kept_ref[...] = packed[pl.ds(pl.multiple_of(core * share, share), share), :]
    sent_ref[...] = packed[pl.ds(pl.multiple_of((1 - core) * share, share), share), :]


def pack(feature, ahead_head, ahead_early, inst, lag, total):
    vmem = pl.BlockSpec(memory_space=pltpu.VMEM)
    feat = inst.shape[0]
    share = jax.ShapeDtypeStruct((feat // 2, feat + 128), F32)
    return pl.pallas_call(
        pack_kernel,
        in_specs=[vmem] * 6,
        out_specs=(vmem, vmem),
        out_shape=(share, share),
        scratch_shapes=[pltpu.VMEM((feat, feat + 128), F32)],
        compiler_params=pltpu.CompilerParams(vmem_limit_bytes=8 * MIB),
    )(feature, ahead_head, ahead_early, inst, lag, total)


def three_parts(x):
    high = x.astype(BF16)
    rest = x - high.astype(F32)
    middle = rest.astype(BF16)
    low = (rest - middle.astype(F32)).astype(BF16)
    return high, middle, low


def inverse_factor(work):
    size = work.shape[0]
    lane = lax.broadcasted_iota(jnp.int32, (PANEL, size), 1)
    sub = lax.broadcasted_iota(jnp.int32, (PANEL, size), 0)
    sub_narrow = lax.broadcasted_iota(jnp.int32, (PANEL, 128), 0)
    for start in range(0, size, PANEL):
        stop = start + PANEL
        panel = work[start:stop, :]
        columns = [
            jnp.broadcast_to(panel[:, start + k : start + k + 1], (PANEL, 128)) for k in range(PANEL)
        ]
        panel = jnp.where(
            (lane >= start) & (lane < stop), jnp.where(lane - start == sub, 1.0, 0.0), panel
        )
        pivots = jnp.ones((PANEL, 128), F32)
        for j in range(PANEL):
            pivot = columns[j][j : j + 1, :]
            factor = columns[j] * (1.0 / pivot)
            pivots = jnp.where(sub_narrow == j, pivot, pivots)
            for k in range(j + 1, PANEL):
                columns[k] = columns[k] - factor * columns[k][j : j + 1, :]
            if j + 1 < PANEL:
                below = jnp.where(sub_narrow > j, factor, 0.0)
                wide = jnp.concatenate([below] * (size // 128), 1)
                panel = panel - wide * panel[j : j + 1, :]
        scale = lax.rsqrt(pivots)
        panel = panel * jnp.concatenate([scale] * (size // 128), 1)
        work[start:stop, :] = panel
        if stop < size:
            high, middle, low = three_parts(panel)
            left = jnp.concatenate([high, high, middle, high, low, middle], 0)
            right = jnp.concatenate([high, middle, high, low, high, middle], 0)
            first = stop // 128 * 128
            update = gram(left[:, first:], right)
            kept = lax.broadcasted_iota(jnp.int32, (size - stop, size), 1)
            kept = (kept < start) | (kept >= stop)
            work[stop:, :] = jnp.where(kept, work[stop:, :], 0.0) - update[stop - first :]
    row = lax.broadcasted_iota(jnp.int32, (size, size), 0)
    column = lax.broadcasted_iota(jnp.int32, (size, size), 1)
    return jnp.where(column <= row, work[...], 0.0)


def koopman_kernel(scale_ref, mine_ref, other_ref, split_ref, shift_ref, work, packed_ref):
    share = mine_ref.shape[0]
    feat = 2 * share
    scale = scale_ref[0]
    core = lax.axis_index("core")
    packed_ref[pl.ds(pl.multiple_of(core * share, share), share), :] = mine_ref[...]
    packed_ref[pl.ds(pl.multiple_of((1 - core) * share, share), share), :] = other_ref[...]
    packed = packed_ref[:, :feat]
    halves = feat // 128
    mean = jnp.concatenate([packed_ref[h : h + 1, feat:] for h in range(halves)], 1) * scale
    diagonal = jnp.concatenate([packed_ref[2 + h : 3 + h, feat:] for h in range(halves)], 1)
    row = lax.broadcasted_iota(jnp.int32, (feat, feat), 0)
    column = lax.broadcasted_iota(jnp.int32, (feat, feat), 1)
    turned = packed.T
    centre = jnp.broadcast_to(mean, (feat, feat))
    centre = centre * centre.T
    inst = jnp.where(column >= row, packed, turned)
    lag = jnp.where(column < row, packed, turned)
    lag = jnp.where(column == row, jnp.broadcast_to(diagonal, (feat, feat)), lag)
    work[...] = inst * scale - centre + jnp.where(column == row, RIDGE, 0.0)
    lag = lag * scale - centre
    inverse = inverse_factor(work)
    half_step = jnp.dot(inverse, lag, precision=HIGHEST, preferred_element_type=F32)
    koopman = across(half_step, inverse, HIGHEST)
    moved = jnp.dot(koopman, inverse, precision=HIGHEST, preferred_element_type=F32)
    for index, matrix in enumerate((inverse, moved)):
        turned = matrix.T
        high = turned.astype(BF16)
        split_ref[2 * index] = high
        split_ref[2 * index + 1] = (turned - high.astype(F32)).astype(BF16)
        rows = jnp.broadcast_to(mean, (8, feat))
        shift_ref[index] = jnp.dot(rows, turned, precision=HIGHEST, preferred_element_type=F32)


def koopman_parts(scale, mine, other):
    feat = 2 * mine.shape[0]
    vmem = pl.BlockSpec(memory_space=pltpu.VMEM)
    return pl.pallas_call(
        koopman_kernel,
        in_specs=[pl.BlockSpec(memory_space=pltpu.SMEM), vmem, vmem],
        out_specs=(vmem, vmem),
        out_shape=(
            jax.ShapeDtypeStruct((4, feat, feat), BF16),
            jax.ShapeDtypeStruct((2, 8, feat), F32),
        ),
        scratch_shapes=[pltpu.VMEM((feat, feat), F32), pltpu.VMEM((feat, mine.shape[1]), F32)],
        compiler_params=pltpu.CompilerParams(vmem_limit_bytes=12 * MIB),
    )(scale, mine, other)


def project_kernel(
    feature_ref, ahead_head_ref, ahead_early_ref, split_ref, shift_ref, moved_ref, residual_ref
):
    step = pl.program_id(0)
    inside = feature_ref.shape[0] // CHUNK - 2

    def product(block, index):
        value = jnp.dot(block, split_ref[2 * index], preferred_element_type=F32)
        value += jnp.dot(block, split_ref[2 * index + 1], preferred_element_type=F32)
        return value - shift_ref[index][0:1]

    def moved():
        value = product(feature_ref[pl.ds(pl.multiple_of(step * CHUNK, CHUNK), CHUNK), :], 1)
        moved_ref[...] = value
        return value

    @pl.when(step < inside)
    def _():
        later = feature_ref[pl.ds(pl.multiple_of(step * CHUNK + LAG, CHUNK), CHUNK), :]
        residual_ref[...] = product(later, 0) - moved()

    for index, ahead_ref in enumerate((ahead_head_ref, ahead_early_ref)):

        @pl.when(step == inside + index)
        def _():
            value = product(ahead_ref[...], 0) - moved()
            at_end = lax.axis_index("tm") == lax.axis_size("tm") - 1
            residual_ref[...] = jnp.where(at_end, 0.0, value)


def project(feature, ahead_head, ahead_early, split, shift):
    rows, feat = feature.shape
    vmem = pl.BlockSpec(memory_space=pltpu.VMEM)
    out = jax.ShapeDtypeStruct((rows, feat), F32)
    block = pl.BlockSpec((CHUNK, feat), lambda i: (i, 0))
    return pl.pallas_call(
        project_kernel,
        grid=(rows // CHUNK,),
        in_specs=[vmem] * 5,
        out_specs=(block, block),
        out_shape=(out, out),
        compiler_params=pltpu.CompilerParams(vmem_limit_bytes=16 * MIB),
    )(feature, ahead_head, ahead_early, split, shift)


def summed(kept, sent):
    swap = [(0, 1), (1, 0)]
    chips = ("x", "tm")
    count = lax.axis_size("x") * lax.axis_size("tm")
    share, width = kept.shape
    parts = (kept + lax.ppermute(sent, "core", swap)).reshape(count, share // count, width)
    mine = jnp.sum(lax.all_to_all(parts, chips, 0, 0, tiled=True), 0)
    copies = jnp.broadcast_to(mine[None], parts.shape)
    mine = lax.all_to_all(copies, chips, 0, 0, tiled=True).reshape(share, width)
    return mine, lax.ppermute(mine, "core", swap)


def on_device(frames, first_weight, first_bias, second_weight):
    frame_block = frames[0]
    row_count, channels = frame_block.shape
    hid, feat = second_weight.shape[1:]
    weights = (
        first_weight.reshape(2 * channels, hid),
        first_bias.reshape(1, hid),
        second_weight.reshape(2 * hid, feat),
    )
    anywhere, vmem = (pl.BlockSpec(memory_space=m) for m in (pl.ANY, pltpu.VMEM))

    halo = passed_along(frame_block[row_count - D1 - D2 :], "tm", 1)
    early = first_rows(early_kernel, (frame_block,), [anywhere], *weights)
    ahead_early = passed_along(early, "tm", -1)
    head = first_rows(head_kernel, (frame_block, halo), [anywhere, vmem], *weights)
    ahead_head = passed_along(head, "tm", -1)
    feature, inst, lag, total = body(frame_block, head, early, *weights)
    mine, other = summed(*pack(feature, ahead_head, ahead_early, inst, lag, total))
    replicas = lax.axis_size("x") * lax.axis_size("core")
    pair_count = replicas * (row_count * lax.axis_size("tm") - LAG)
    scale = jnp.full((1,), 1.0 / (2.0 * pair_count), F32)
    split, shift = koopman_parts(scale, mine, other)
    propagated, residual = project(feature, ahead_head, ahead_early, split, shift)
    return (propagated[None], residual[None])


def solution(mesh):
    replicas, blocks = mesh.devices.shape
    chips = Mesh(mesh.devices.reshape(replicas // 2, 2, blocks), ("x", "core", "tm"))
    split = P(("x", "core"), "tm", None)
    return jax.shard_map(
        on_device,
        mesh=chips,
        in_specs=(split, P(), P(), P()),
        out_specs=(split, split),
        check_vma=False,
    )
```

```python
import jax
import jax.numpy as jnp
from jax import lax
from jax.experimental import pallas as pl
from jax.experimental.pallas import tpu as pltpu
from jax.sharding import Mesh, PartitionSpec as P

D1 = 32
D2 = 256
LAG = 1024
RIDGE = 0.001
CHUNK = 512
PANEL = 16
MIB = 1024 * 1024

F32 = jnp.float32
BF16 = jnp.bfloat16
HIGHEST = lax.Precision.HIGHEST


def passed_along(value, axis, steps):
    count = lax.axis_size(axis)
    first, last = (max(0, -steps), min(count, count - steps))
    return lax.ppermute(value, axis, [(source, source + steps) for source in range(first, last)])


def across(a, b, precision=None):
    return lax.dot_general(a, b, (((1,), (1,)), ((), ())), precision=precision, preferred_element_type=F32)


def gram(a, b):
    return lax.dot_general(a, b, (((0,), (0,)), ((), ())), preferred_element_type=F32)


def silu(x):
    half = 0.5 * x
    return half + half * jnp.tanh(half)


def hidden_rows(xs, at, rows, w1_ref, b1_ref):
    channels = xs.shape[1]
    z = jnp.dot(xs[pl.ds(at + D1, rows), :], w1_ref[:channels, :], preferred_element_type=F32)
    z += jnp.dot(xs[pl.ds(at, rows), :], w1_ref[channels:, :], preferred_element_type=F32)
    return silu(z + b1_ref[...]).astype(BF16)


def feature_rows(hs, at, rows, w2_ref):
    hid = hs.shape[1]
    value = jnp.dot(hs[pl.ds(at + D2, rows), :], w2_ref[:hid, :], preferred_element_type=F32)
    value += jnp.dot(hs[pl.ds(at, rows), :], w2_ref[hid:, :], preferred_element_type=F32)
    return value.astype(BF16)


def early_kernel(frames_ref, w1_in, b1_in, w2_in, out_ref, near_ref, w1_ref, b1_ref, w2_ref, hs, sems):
    half = LAG // 2
    first = half - D1 - D2
    rows = [(first, LAG - first), (0, first)]
    copies = [
        (frames_ref.at[pl.ds(at, count)], near_ref.at[pl.ds(at, count)]) for at, count in rows
    ] + [(w1_in, w1_ref), (b1_in, b1_ref), (w2_in, w2_ref)]
    copies = [pltpu.make_async_copy(*pair, sems.at[index]) for index, pair in enumerate(copies)]
    for index in (2, 0, 3, 4, 1):
        copies[index].start()
    for index in (2, 0, 3):
        copies[index].wait()
    for at in range(0, hs.shape[0], D2):
        hs[at : at + D2, :] = hidden_rows(near_ref, first + at, D2, w1_ref, b1_ref)
    copies[4].wait()
    out_ref[...] = feature_rows(hs, 0, half, w2_ref)
    copies[1].wait()


def head_kernel(near_ref, halo_ref, w1_ref, b1_ref, w2_ref, out_ref, xs, hs):
    halo_rows = halo_ref.shape[0]
    xs[:halo_rows, :] = halo_ref[...]
    xs[halo_rows:, :] = near_ref[: LAG // 2, :]
    before = hidden_rows(xs, 0, D2, w1_ref, b1_ref)
    hs[:D2, :] = jnp.where(lax.axis_index("tm") > 0, before, jnp.zeros_like(before))
    for at in range(D2, hs.shape[0], D2):
        hs[at : at + D2, :] = hidden_rows(xs, at, D2, w1_ref, b1_ref)
    out_ref[...] = feature_rows(hs, 0, out_ref.shape[0], w2_ref)


def feature_scratch(rows, channels, hid):
    return [
        pltpu.VMEM((rows + D1 + D2, channels), BF16),
        pltpu.VMEM((rows + D2, hid), BF16),
    ]


def early_rows(frames, w1, b1, w2):
    vmem = pl.BlockSpec(memory_space=pltpu.VMEM)
    hbm = pl.BlockSpec(memory_space=pltpu.HBM)
    half, channels, hid = LAG // 2, frames.shape[1], w1.shape[1]
    shapes = [((half, w2.shape[1]), BF16), ((LAG, channels), BF16), (w1.shape, BF16), (b1.shape, F32), (w2.shape, BF16)]
    return pl.pallas_call(
        early_kernel,
        in_specs=[hbm] * 4,
        out_specs=(vmem,) * 5,
        out_shape=tuple(jax.ShapeDtypeStruct(*shape) for shape in shapes),
        scratch_shapes=[pltpu.VMEM((half + D2, hid), BF16), pltpu.SemaphoreType.DMA((5,))],
        compiler_params=pltpu.CompilerParams(vmem_limit_bytes=12 * MIB),
    )(frames, w1, b1, w2)


def head_rows(near, halo, w1, b1, w2):
    vmem = pl.BlockSpec(memory_space=pltpu.VMEM)
    half = LAG // 2
    return pl.pallas_call(
        head_kernel,
        in_specs=[vmem] * 5,
        out_specs=vmem,
        out_shape=jax.ShapeDtypeStruct((half, w2.shape[1]), BF16),
        scratch_shapes=feature_scratch(half, near.shape[1], w1.shape[1]),
        compiler_params=pltpu.CompilerParams(vmem_limit_bytes=12 * MIB),
    )(near, halo, w1, b1, w2)


def column_sum(rows):
    ones = jnp.ones((8, rows.shape[0]), BF16)
    return jnp.dot(ones, rows, preferred_element_type=F32)


def body_kernel(frames_ref, near_ref, head_ref, early_ref, w1_ref, b1_ref, w2_ref, out_ref, inst, lag, total, xs, hs, sems):
    rows, feat = out_ref.shape
    first = LAG - D1 - D2
    steps = (rows - LAG) // CHUNK

    def arriving(step):
        start = step * CHUNK + D1 + D2
        return pltpu.make_async_copy(
            frames_ref.at[pl.ds(first + start, CHUNK)], xs.at[pl.ds(start, CHUNK)], sems.at[step]
        )

    for step in range(steps):
        arriving(step).start()
    xs[: D1 + D2, :] = near_ref[first:, :]
    half = LAG // 2
    out_ref[:half, :] = head_ref[...]
    out_ref[half:LAG, :] = early_ref[...]
    tm_index, tm_last = lax.axis_index("tm"), lax.axis_size("tm") - 1
    first_weight = jnp.where(tm_index == 0, 1.0, 2.0)
    last_weight = jnp.where(tm_index == tm_last, 1.0, 2.0)
    start = out_ref[:LAG, :]
    inst[...] = first_weight * gram(start, start)
    total[...] = first_weight * column_sum(start)
    lag[...] = jnp.zeros_like(lag)
    hs[:D2, :] = hidden_rows(xs, 0, D2, w1_ref, b1_ref)
    arriving(0).wait()
    hs[D2 : D2 + CHUNK, :] = hidden_rows(xs, D2, CHUNK, w1_ref, b1_ref)

    def finish(step):
        value = feature_rows(hs, step * CHUNK, CHUNK, w2_ref)
        out_ref[pl.ds(LAG + step * CHUNK, CHUNK), :] = value
        weight = jnp.where(step >= steps - LAG // CHUNK, last_weight, 2.0)
        both = gram(value, jnp.concatenate([value, out_ref[pl.ds(step * CHUNK, CHUNK), :]], 1))
        inst[...] += weight * both[:, :feat]
        lag[...] += both[:, feat:]
        total[...] += weight * column_sum(value)

    def loop(step, carry):
        arriving(step + 1).wait()
        at = pl.multiple_of((step + 1) * CHUNK + D2, D2)
        fresh = hidden_rows(xs, at, CHUNK, w1_ref, b1_ref)
        finish(step)
        hs[pl.ds(at, CHUNK), :] = fresh
        return carry

    lax.fori_loop(0, steps - 1, loop, 0)
    finish(steps - 1)


def body(frames, near, head, early, w1, b1, w2):
    rows, channels = frames.shape
    hid, feat = w1.shape[1], w2.shape[1]
    vmem = pl.BlockSpec(memory_space=pltpu.VMEM)
    square = jax.ShapeDtypeStruct((feat, feat), F32)
    return pl.pallas_call(
        body_kernel,
        in_specs=[pl.BlockSpec(memory_space=pltpu.HBM)] + [vmem] * 6,
        out_specs=(vmem,) * 4,
        out_shape=(
            jax.ShapeDtypeStruct((rows, feat), BF16),
            square,
            square,
            jax.ShapeDtypeStruct((8, feat), F32),
        ),
        scratch_shapes=feature_scratch(rows - LAG, channels, hid)
        + [pltpu.SemaphoreType.DMA((rows // CHUNK,))],
        compiler_params=pltpu.CompilerParams(vmem_limit_bytes=24 * MIB),
    )(frames, near, head, early, w1, b1, w2)


def pack_kernel(feature_ref, ahead_head_ref, ahead_early_ref, inst, lag, total, kept_ref, sent_ref, packed):
    feat = inst.shape[0]
    half = LAG // 2
    edge = feature_ref.shape[0] - LAG
    cross = lag[...] + gram(ahead_head_ref[...], feature_ref[edge : edge + half, :])
    cross += gram(ahead_early_ref[...], feature_ref[edge + half :, :])
    both = cross + cross.T
    row = lax.broadcasted_iota(jnp.int32, (feat, feat), 0)
    column = lax.broadcasted_iota(jnp.int32, (feat, feat), 1)
    packed[...] = jnp.where(column >= row, inst[...], both)
    sums = total[0:1, :]
    diagonal = jnp.sum(jnp.where(column == row, both, 0.0), 0, keepdims=True)
    core = lax.axis_index("core")
    for ref, owner in ((kept_ref, core), (sent_ref, 1 - core)):
        extra = jnp.where(owner == 0, sums, diagonal)
        for chunk, _, share_row, lanes in slots(ref.shape, feat):
            source = pl.ds(owner * (feat // 2) + share_row, 1)
            ref[chunk, 0:1, lanes] = packed[source, :]
        for chunk in range(ref.shape[0]):
            part = extra[:, chunk * 128 : chunk * 128 + 128] if chunk < feat // 128 else jnp.zeros((1, 128), F32)
            ref[chunk, 0:1, ref.shape[2] - 128 :] = part


def slots(shape, feat):
    rows = (shape[2] - 128) // feat
    for chunk in range(shape[0]):
        for row in range(rows):
            yield chunk, row, chunk * rows + row, slice(row * feat, (row + 1) * feat)


def pack(feature, ahead_head, ahead_early, inst, lag, total, chips):
    vmem = pl.BlockSpec(memory_space=pltpu.VMEM)
    feat = inst.shape[0]
    share = jax.ShapeDtypeStruct((chips, 1, feat // 2 // chips * feat + 128), F32)
    return pl.pallas_call(
        pack_kernel,
        in_specs=[vmem] * 6,
        out_specs=(vmem, vmem),
        out_shape=(share, share),
        scratch_shapes=[pltpu.VMEM((feat, feat), F32)],
        compiler_params=pltpu.CompilerParams(vmem_limit_bytes=8 * MIB),
    )(feature, ahead_head, ahead_early, inst, lag, total)


def three_parts(x):
    high = x.astype(BF16)
    rest = x - high.astype(F32)
    middle = rest.astype(BF16)
    low = (rest - middle.astype(F32)).astype(BF16)
    return high, middle, low


def repeated_parts(block, offset):
    lane = lax.broadcasted_iota(jnp.int32, block.shape, 1)
    base = jnp.where((lane >= offset) & (lane < offset + PANEL), block, 0.0)
    if offset:
        base = pltpu.roll(base, 128 - offset, 1)
    two = base + pltpu.roll(base, PANEL, 1)
    six = two + pltpu.roll(two, 2 * PANEL, 1) + pltpu.roll(two, 4 * PANEL, 1)
    high, middle, low = (part.astype(F32) for part in three_parts(six))
    place = lane // PANEL
    chosen = jnp.where((place == 2) | (place == 5), middle, jnp.where(place == 4, low, high))
    return chosen.astype(BF16)


def stacked_parts(rows):
    high, middle, low = three_parts(rows)
    rest = jnp.zeros((128 - 6 * PANEL, rows.shape[1]), BF16)
    return jnp.concatenate([high, middle, high, low, high, middle, rest], 0)


def inverse_factor(work):
    size = work.shape[0]
    lane = lax.broadcasted_iota(jnp.int32, (PANEL, size), 1)
    sub = lax.broadcasted_iota(jnp.int32, (PANEL, size), 0)
    sub_narrow = lax.broadcasted_iota(jnp.int32, (PANEL, 128), 0)

    def wide(x):
        return jnp.concatenate([x] * (size // 128), 1)

    for start in range(0, size, PANEL):
        stop = start + PANEL
        panel = work[start:stop, :]
        columns = [
            jnp.broadcast_to(panel[:, start + k : start + k + 1], (PANEL, 128)) for k in range(PANEL)
        ]
        panel = jnp.where(
            (lane >= start) & (lane < stop), jnp.where(lane - start == sub, 1.0, 0.0), panel
        )
        solved = panel
        slab = start // 128 * 128
        if stop < size:
            left = repeated_parts(work[stop:, slab : slab + 128], start - slab)
        pivots = jnp.ones((PANEL, 128), F32)
        pivot = columns[0][0:1, :]
        for j in range(PANEL):
            inverse = pl.reciprocal(pivot, approx=True)
            pivots = jnp.where(sub_narrow == j, pivot, pivots)
            factor = jnp.where(sub_narrow == j, 0.0, columns[j]) * inverse
            if j + 1 < PANEL:
                beside = columns[j + 1][j : j + 1, :]
                pivot = columns[j + 1][j + 1 : j + 2, :] - beside * beside * inverse
            for k in range(j + 1, PANEL):
                columns[k] = columns[k] - factor * columns[k][j : j + 1, :]
            if j + 1 < PANEL:
                below = jnp.where(sub_narrow > j, factor, 0.0)
                panel = panel - wide(below) * panel[j : j + 1, :]
            solved = solved - wide(factor) * solved[j : j + 1, :]
        if stop < size:
            right = stacked_parts(solved * wide(1.0 / pivots))
            update = jnp.dot(left, right, preferred_element_type=F32)
            kept = lax.broadcasted_iota(jnp.int32, (size - stop, size), 1)
            kept = (kept < start) | (kept >= stop)
            work[stop:, :] = jnp.where(kept, work[stop:, :], 0.0) - update
        work[start:stop, :] = panel * wide(lax.rsqrt(pivots))
    row = lax.broadcasted_iota(jnp.int32, (size, size), 0)
    column = lax.broadcasted_iota(jnp.int32, (size, size), 1)
    return jnp.where(column <= row, work[...], 0.0)


def koopman_kernel(scale_ref, mine_ref, other_ref, split_ref, shift_ref, work, packed_ref):
    feat = packed_ref.shape[1]
    scale = scale_ref[0]
    core = lax.axis_index("core")
    extras = []
    for ref, owner in ((mine_ref, core), (other_ref, 1 - core)):
        for chunk, _, share_row, lanes in slots(ref.shape, feat):
            packed_ref[pl.ds(owner * (feat // 2) + share_row, 1), :] = ref[chunk, 0:1, lanes]
        parts = [ref[chunk, 0:1, ref.shape[2] - 128 :] for chunk in range(feat // 128)]
        extras.append(jnp.concatenate(parts, 1))
    packed = packed_ref[...]
    mean = jnp.where(core == 0, extras[0], extras[1]) * scale
    diagonal = jnp.where(core == 0, extras[1], extras[0])
    row = lax.broadcasted_iota(jnp.int32, (feat, feat), 0)
    column = lax.broadcasted_iota(jnp.int32, (feat, feat), 1)
    turned = packed.T
    centre = jnp.broadcast_to(mean, (feat, feat))
    centre = centre * centre.T
    inst = jnp.where(column >= row, packed, turned)
    lag = jnp.where(column < row, packed, turned)
    lag = jnp.where(column == row, jnp.broadcast_to(diagonal, (feat, feat)), lag)
    work[...] = inst * scale - centre + jnp.where(column == row, RIDGE, 0.0)
    lag = lag * scale - centre
    inverse = inverse_factor(work)
    half_step = jnp.dot(inverse, lag, precision=HIGHEST, preferred_element_type=F32)
    koopman = across(half_step, inverse, HIGHEST)
    moved = jnp.dot(koopman, inverse, precision=HIGHEST, preferred_element_type=F32)
    for index, matrix in enumerate((inverse, moved)):
        turned = matrix.T
        high = turned.astype(BF16)
        split_ref[index, :feat, :] = high
        split_ref[index, feat:, :] = (turned - high.astype(F32)).astype(BF16)
        rows = jnp.broadcast_to(mean, (8, feat))
        shift_ref[index] = jnp.dot(rows, turned, precision=HIGHEST, preferred_element_type=F32)


def koopman_parts(scale, mine, other, feat):
    vmem = pl.BlockSpec(memory_space=pltpu.VMEM)
    return pl.pallas_call(
        koopman_kernel,
        in_specs=[pl.BlockSpec(memory_space=pltpu.SMEM), vmem, vmem],
        out_specs=(vmem, vmem),
        out_shape=(
            jax.ShapeDtypeStruct((2, 2 * feat, feat), BF16),
            jax.ShapeDtypeStruct((2, 8, feat), F32),
        ),
        scratch_shapes=[pltpu.VMEM((feat, feat), F32), pltpu.VMEM((feat, feat), F32)],
        compiler_params=pltpu.CompilerParams(vmem_limit_bytes=12 * MIB),
    )(scale, mine, other)


def project_kernel(
    feature_ref, ahead_head_ref, ahead_early_ref, split_ref, shift_ref, moved_ref, residual_ref
):
    step = pl.program_id(0)
    inside = feature_ref.shape[0] // CHUNK - 2

    def product(block, index):
        twice = jnp.concatenate([block, block], 1)
        return jnp.dot(twice, split_ref[index], preferred_element_type=F32) - shift_ref[index][0:1]

    def moved():
        value = product(feature_ref[pl.ds(pl.multiple_of(step * CHUNK, CHUNK), CHUNK), :], 1)
        moved_ref[...] = value
        return value

    @pl.when(step < inside)
    def _():
        later = feature_ref[pl.ds(pl.multiple_of(step * CHUNK + LAG, CHUNK), CHUNK), :]
        residual_ref[...] = product(later, 0) - moved()

    for index, ahead_ref in enumerate((ahead_head_ref, ahead_early_ref)):

        @pl.when(step == inside + index)
        def _():
            value = product(ahead_ref[...], 0) - moved()
            at_end = lax.axis_index("tm") == lax.axis_size("tm") - 1
            residual_ref[...] = jnp.where(at_end, 0.0, value)


def project(feature, ahead_head, ahead_early, split, shift):
    rows, feat = feature.shape
    vmem = pl.BlockSpec(memory_space=pltpu.VMEM)
    out = jax.ShapeDtypeStruct((rows, feat), F32)
    block = pl.BlockSpec((CHUNK, feat), lambda i: (i, 0))
    return pl.pallas_call(
        project_kernel,
        grid=(rows // CHUNK,),
        in_specs=[vmem] * 5,
        out_specs=(block, block),
        out_shape=(out, out),
        compiler_params=pltpu.CompilerParams(vmem_limit_bytes=16 * MIB),
    )(feature, ahead_head, ahead_early, split, shift)


def summed(kept, sent):
    swap = [(0, 1), (1, 0)]
    chips = ("x", "tm")
    parts = kept + lax.ppermute(sent, "core", swap)
    mine = jnp.sum(lax.all_to_all(parts, chips, 0, 0, tiled=True), 0, keepdims=True)
    mine = lax.all_to_all(jnp.broadcast_to(mine, parts.shape), chips, 0, 0, tiled=True)
    return mine, lax.ppermute(mine, "core", swap)


def on_device(frames, first_weight, first_bias, second_weight):
    frame_block = frames[0]
    row_count, channels = frame_block.shape
    hid, feat = second_weight.shape[1:]
    weights = (
        first_weight.reshape(2 * channels, hid),
        first_bias.reshape(1, hid),
        second_weight.reshape(2 * hid, feat),
    )
    halo = passed_along(frame_block[row_count - D1 - D2 :], "tm", 1)
    early, near, *weights = early_rows(frame_block, *weights)
    ahead_early = passed_along(early, "tm", -1)
    head = head_rows(near, halo, *weights)
    ahead_head = passed_along(head, "tm", -1)
    feature, inst, lag, total = body(frame_block, near, head, early, *weights)
    chips = lax.axis_size("x") * lax.axis_size("tm")
    mine, other = summed(*pack(feature, ahead_head, ahead_early, inst, lag, total, chips))
    replicas = lax.axis_size("x") * lax.axis_size("core")
    pair_count = replicas * (row_count * lax.axis_size("tm") - LAG)
    scale = jnp.full((1,), 1.0 / (2.0 * pair_count), F32)
    split, shift = koopman_parts(scale, mine, other, feat)
    propagated, residual = project(feature, ahead_head, ahead_early, split, shift)
    return (propagated[None], residual[None])


def solution(mesh):
    replicas, blocks = mesh.devices.shape
    chips = Mesh(mesh.devices.reshape(replicas // 2, 2, blocks), ("x", "core", "tm"))
    split = P(("x", "core"), "tm", None)
    return jax.shard_map(
        on_device,
        mesh=chips,
        in_specs=(split, P(), P(), P()),
        out_specs=(split, split),
        check_vma=False,
    )
```

```python
import jax
import jax.numpy as jnp
from jax import lax
from jax.experimental import pallas as pl
from jax.experimental.pallas import tpu as pltpu
from jax.sharding import Mesh, PartitionSpec as P

D1 = 32
D2 = 256
LAG = 1024
RIDGE = 0.001
CHUNK = 512
PANEL = 16
MIB = 1024 * 1024

F32 = jnp.float32
BF16 = jnp.bfloat16
HIGHEST = lax.Precision.HIGHEST


def passed_along(value, axis, steps):
    count = lax.axis_size(axis)
    first, last = (max(0, -steps), min(count, count - steps))
    return lax.ppermute(value, axis, [(source, source + steps) for source in range(first, last)])


def across(a, b, precision=None):
    return lax.dot_general(a, b, (((1,), (1,)), ((), ())), precision=precision, preferred_element_type=F32)


def gram(a, b):
    return lax.dot_general(a, b, (((0,), (0,)), ((), ())), preferred_element_type=F32)


def in_hbm(value):
    return pltpu.with_memory_space_constraint(value, pltpu.HBM)


def silu(x):
    half = 0.5 * x
    return half + half * jnp.tanh(half)


def hidden_rows(xs, at, rows, w1_ref, b1_ref):
    channels = xs.shape[1]
    z = jnp.dot(xs[pl.ds(at + D1, rows), :], w1_ref[:channels, :], preferred_element_type=F32)
    z += jnp.dot(xs[pl.ds(at, rows), :], w1_ref[channels:, :], preferred_element_type=F32)
    return silu(z + b1_ref[...]).astype(BF16)


def feature_rows(hs, at, rows, w2_ref):
    hid = hs.shape[1]
    value = jnp.dot(hs[pl.ds(at + D2, rows), :], w2_ref[:hid, :], preferred_element_type=F32)
    value += jnp.dot(hs[pl.ds(at, rows), :], w2_ref[hid:, :], preferred_element_type=F32)
    return value.astype(BF16)


def early_kernel(frames_ref, w1_in, b1_in, w2_in, out_ref, near_ref, w1_ref, b1_ref, w2_ref, hs, sems):
    half = LAG // 2
    first = half - D1 - D2
    rows = [(first, LAG - first), (0, first)]
    copies = [
        (frames_ref.at[pl.ds(at, count)], near_ref.at[pl.ds(at, count)]) for at, count in rows
    ] + [(w1_in, w1_ref), (b1_in, b1_ref), (w2_in, w2_ref)]
    copies = [pltpu.make_async_copy(*pair, sems.at[index]) for index, pair in enumerate(copies)]
    for index in (2, 0, 3, 4, 1):
        copies[index].start()
    for index in (2, 0, 3):
        copies[index].wait()
    for at in range(0, hs.shape[0], D2):
        hs[at : at + D2, :] = hidden_rows(near_ref, first + at, D2, w1_ref, b1_ref)
    copies[4].wait()
    out_ref[...] = feature_rows(hs, 0, half, w2_ref)
    copies[1].wait()


def head_kernel(near_ref, halo_ref, w1_ref, b1_ref, w2_ref, out_ref, xs, hs):
    halo_rows = halo_ref.shape[0]
    xs[:halo_rows, :] = halo_ref[...]
    xs[halo_rows:, :] = near_ref[: LAG // 2, :]
    before = hidden_rows(xs, 0, D2, w1_ref, b1_ref)
    hs[:D2, :] = jnp.where(lax.axis_index("tm") > 0, before, jnp.zeros_like(before))
    for at in range(D2, hs.shape[0], D2):
        hs[at : at + D2, :] = hidden_rows(xs, at, D2, w1_ref, b1_ref)
    out_ref[...] = feature_rows(hs, 0, out_ref.shape[0], w2_ref)


def feature_scratch(rows, channels, hid):
    return [
        pltpu.VMEM((rows + D1 + D2, channels), BF16),
        pltpu.VMEM((rows + D2, hid), BF16),
    ]


def early_rows(frames, w1, b1, w2):
    vmem = pl.BlockSpec(memory_space=pltpu.VMEM)
    hbm = pl.BlockSpec(memory_space=pltpu.HBM)
    half, channels, hid = LAG // 2, frames.shape[1], w1.shape[1]
    shapes = [((half, w2.shape[1]), BF16), ((LAG, channels), BF16), (w1.shape, BF16), (b1.shape, F32), (w2.shape, BF16)]
    return pl.pallas_call(
        early_kernel,
        in_specs=[hbm] * 4,
        out_specs=(vmem,) * 5,
        out_shape=tuple(jax.ShapeDtypeStruct(*shape) for shape in shapes),
        scratch_shapes=[pltpu.VMEM((half + D2, hid), BF16), pltpu.SemaphoreType.DMA((5,))],
        compiler_params=pltpu.CompilerParams(vmem_limit_bytes=12 * MIB),
    )(*(in_hbm(value) for value in (frames, w1, b1, w2)))


def head_rows(near, halo, w1, b1, w2):
    vmem = pl.BlockSpec(memory_space=pltpu.VMEM)
    half = LAG // 2
    return pl.pallas_call(
        head_kernel,
        in_specs=[vmem] * 5,
        out_specs=vmem,
        out_shape=jax.ShapeDtypeStruct((half, w2.shape[1]), BF16),
        scratch_shapes=feature_scratch(half, near.shape[1], w1.shape[1]),
        compiler_params=pltpu.CompilerParams(vmem_limit_bytes=12 * MIB),
    )(near, halo, w1, b1, w2)


def column_sum(rows):
    return jnp.sum(rows.astype(F32).reshape(-1, 8, rows.shape[1]), 0)


def body_kernel(frames_ref, near_ref, head_ref, early_ref, w1_ref, b1_ref, w2_ref, out_ref, inst, lag, total, xs, hs, sems):
    rows, feat = out_ref.shape
    first = LAG - D1 - D2
    steps = (rows - LAG) // CHUNK

    def arriving(step):
        start = step * CHUNK + D1 + D2
        return pltpu.make_async_copy(
            frames_ref.at[pl.ds(first + start, CHUNK)], xs.at[pl.ds(start, CHUNK)], sems.at[step]
        )

    for step in range(steps):
        arriving(step).start()
    xs[: D1 + D2, :] = near_ref[first:, :]
    half = LAG // 2
    out_ref[:half, :] = head_ref[...]
    out_ref[half:LAG, :] = early_ref[...]
    tm_index, tm_last = lax.axis_index("tm"), lax.axis_size("tm") - 1
    first_weight = jnp.where(tm_index == 0, 1.0, 2.0)
    last_weight = jnp.where(tm_index == tm_last, 1.0, 2.0)
    start = out_ref[:LAG, :]
    inst[...] = first_weight * gram(start, start)
    total[...] = first_weight * column_sum(start)
    lag[...] = jnp.zeros_like(lag)
    hs[:D2, :] = hidden_rows(xs, 0, D2, w1_ref, b1_ref)
    arriving(0).wait()
    hs[D2 : D2 + CHUNK, :] = hidden_rows(xs, D2, CHUNK, w1_ref, b1_ref)

    def finish(step):
        value = feature_rows(hs, step * CHUNK, CHUNK, w2_ref)
        at = step * CHUNK
        out_ref[LAG + at : LAG + at + CHUNK, :] = value
        weight = last_weight if step >= steps - LAG // CHUNK else 2.0
        both = gram(value, jnp.concatenate([value, out_ref[at : at + CHUNK, :]], 1))
        inst[...] += weight * both[:, :feat]
        lag[...] += both[:, feat:]
        total[...] += weight * column_sum(value)

    for step in range(steps - 1):
        arriving(step + 1).wait()
        at = (step + 1) * CHUNK + D2
        hs[at : at + CHUNK, :] = hidden_rows(xs, at, CHUNK, w1_ref, b1_ref)
        finish(step)
    finish(steps - 1)


def body(frames, near, head, early, w1, b1, w2):
    rows, channels = frames.shape
    hid, feat = w1.shape[1], w2.shape[1]
    vmem = pl.BlockSpec(memory_space=pltpu.VMEM)
    square = jax.ShapeDtypeStruct((feat, feat), F32)
    return pl.pallas_call(
        body_kernel,
        in_specs=[pl.BlockSpec(memory_space=pltpu.HBM)] + [vmem] * 6,
        out_specs=(vmem,) * 4,
        out_shape=(
            jax.ShapeDtypeStruct((rows, feat), BF16),
            square,
            square,
            jax.ShapeDtypeStruct((8, feat), F32),
        ),
        scratch_shapes=feature_scratch(rows - LAG, channels, hid)
        + [pltpu.SemaphoreType.DMA((rows // CHUNK,))],
        compiler_params=pltpu.CompilerParams(vmem_limit_bytes=24 * MIB),
    )(in_hbm(frames), near, head, early, w1, b1, w2)


def pack_kernel(feature_ref, ahead_head_ref, ahead_early_ref, inst, lag, total, kept_ref, sent_ref, packed):
    feat = inst.shape[0]
    half = LAG // 2
    edge = feature_ref.shape[0] - LAG
    cross = lag[...] + gram(ahead_head_ref[...], feature_ref[edge : edge + half, :])
    cross += gram(ahead_early_ref[...], feature_ref[edge + half :, :])
    both = cross + cross.T
    row = lax.broadcasted_iota(jnp.int32, (feat, feat), 0)
    column = lax.broadcasted_iota(jnp.int32, (feat, feat), 1)
    packed[...] = jnp.where(column >= row, inst[...], both)
    sums = jnp.sum(total[...], 0, keepdims=True)
    diagonal = jnp.sum(jnp.where(column == row, both, 0.0), 0, keepdims=True)
    core = lax.axis_index("core")
    for ref, owner in ((kept_ref, core), (sent_ref, 1 - core)):
        extra = jnp.where(owner == 0, sums, diagonal)
        for chunk, _, share_row, lanes in slots(ref.shape, feat):
            source = pl.ds(owner * (feat // 2) + share_row, 1)
            ref[chunk, 0:1, lanes] = packed[source, :]
        for chunk in range(ref.shape[0]):
            part = extra[:, chunk * 128 : chunk * 128 + 128] if chunk < feat // 128 else jnp.zeros((1, 128), F32)
            ref[chunk, 0:1, ref.shape[2] - 128 :] = part


def slots(shape, feat):
    rows = (shape[2] - 128) // feat
    for chunk in range(shape[0]):
        for row in range(rows):
            yield chunk, row, chunk * rows + row, slice(row * feat, (row + 1) * feat)


def pack(feature, ahead_head, ahead_early, inst, lag, total, chips):
    vmem = pl.BlockSpec(memory_space=pltpu.VMEM)
    feat = inst.shape[0]
    share = jax.ShapeDtypeStruct((chips, 1, feat // 2 // chips * feat + 128), F32)
    return pl.pallas_call(
        pack_kernel,
        in_specs=[vmem] * 6,
        out_specs=(vmem, vmem),
        out_shape=(share, share),
        scratch_shapes=[pltpu.VMEM((feat, feat), F32)],
        compiler_params=pltpu.CompilerParams(vmem_limit_bytes=8 * MIB),
    )(feature, ahead_head, ahead_early, inst, lag, total)


def three_parts(x):
    high = x.astype(BF16)
    rest = x - high.astype(F32)
    middle = rest.astype(BF16)
    low = (rest - middle.astype(F32)).astype(BF16)
    return high, middle, low


def repeated_parts(block, offset):
    lane = lax.broadcasted_iota(jnp.int32, block.shape, 1)
    base = jnp.where((lane >= offset) & (lane < offset + PANEL), block, 0.0)
    if offset:
        base = pltpu.roll(base, 128 - offset, 1)
    two = base + pltpu.roll(base, PANEL, 1)
    six = two + pltpu.roll(two, 2 * PANEL, 1) + pltpu.roll(two, 4 * PANEL, 1)
    high, middle, low = (part.astype(F32) for part in three_parts(six))
    place = lane // PANEL
    chosen = jnp.where((place == 2) | (place == 5), middle, jnp.where(place == 4, low, high))
    return chosen.astype(BF16)


def stacked_parts(rows):
    high, middle, low = three_parts(rows)
    rest = jnp.zeros((128 - 6 * PANEL, rows.shape[1]), BF16)
    return jnp.concatenate([high, middle, high, low, high, middle, rest], 0)


def inverse_factor(work):
    size = work.shape[0]
    lane = lax.broadcasted_iota(jnp.int32, (PANEL, size), 1)
    sub = lax.broadcasted_iota(jnp.int32, (PANEL, size), 0)
    sub_narrow = lax.broadcasted_iota(jnp.int32, (PANEL, 128), 0)

    def wide(x):
        return jnp.concatenate([x] * (size // 128), 1)

    def spread(x, j):
        return jnp.broadcast_to(x[j : j + 1, :], x.shape)

    for start in range(0, size, PANEL):
        stop = start + PANEL
        panel = work[start:stop, :]
        columns = [
            jnp.broadcast_to(panel[:, start + k : start + k + 1], (PANEL, 128)) for k in range(PANEL)
        ]
        panel = jnp.where(
            (lane >= start) & (lane < stop), jnp.where(lane - start == sub, 1.0, 0.0), panel
        )
        solved = panel
        slab = start // 128 * 128
        if stop < size:
            left = repeated_parts(work[stop:, slab : slab + 128], start - slab)
        pivots = jnp.ones((PANEL, 128), F32)
        pivot = spread(columns[0], 0)
        for j in range(PANEL):
            inverse = pl.reciprocal(pivot, approx=True)
            pivots = jnp.where(sub_narrow == j, pivot, pivots)
            factor = jnp.where(sub_narrow == j, 0.0, columns[j]) * inverse
            beside = [spread(columns[k], j) for k in range(j + 1, PANEL)]
            if j + 1 < PANEL:
                pivot = spread(columns[j + 1], j + 1) - beside[0] * beside[0] * inverse
            for k in range(j + 1, PANEL):
                columns[k] = columns[k] - factor * beside[k - j - 1]
            if j + 1 < PANEL:
                below = jnp.where(sub_narrow > j, factor, 0.0)
                panel = panel - wide(below) * spread(panel, j)
            solved = solved - wide(factor) * spread(solved, j)
        if stop < size:
            right = stacked_parts(solved * wide(1.0 / pivots))
            update = jnp.dot(left, right, preferred_element_type=F32)
            kept = lax.broadcasted_iota(jnp.int32, (size - stop, size), 1)
            kept = (kept < start) | (kept >= stop)
            work[stop:, :] = jnp.where(kept, work[stop:, :], 0.0) - update
        work[start:stop, :] = panel * wide(lax.rsqrt(pivots))
    row = lax.broadcasted_iota(jnp.int32, (size, size), 0)
    column = lax.broadcasted_iota(jnp.int32, (size, size), 1)
    return jnp.where(column <= row, work[...], 0.0)


def koopman_kernel(scale_ref, mine_ref, other_ref, split_ref, shift_ref, work, packed_ref):
    feat = packed_ref.shape[1]
    scale = scale_ref[0]
    core = lax.axis_index("core")
    extras = []
    for ref, owner in ((mine_ref, core), (other_ref, 1 - core)):
        for chunk, _, share_row, lanes in slots(ref.shape, feat):
            packed_ref[pl.ds(owner * (feat // 2) + share_row, 1), :] = ref[chunk, 0:1, lanes]
        parts = [ref[chunk, 0:1, ref.shape[2] - 128 :] for chunk in range(feat // 128)]
        extras.append(jnp.concatenate(parts, 1))
    packed = packed_ref[...]
    mean = jnp.where(core == 0, extras[0], extras[1]) * scale
    diagonal = jnp.where(core == 0, extras[1], extras[0])
    row = lax.broadcasted_iota(jnp.int32, (feat, feat), 0)
    column = lax.broadcasted_iota(jnp.int32, (feat, feat), 1)
    turned = packed.T
    centre = jnp.broadcast_to(mean, (feat, feat))
    centre = centre * centre.T
    inst = jnp.where(column >= row, packed, turned)
    lag = jnp.where(column < row, packed, turned)
    lag = jnp.where(column == row, jnp.broadcast_to(diagonal, (feat, feat)), lag)
    work[...] = inst * scale - centre + jnp.where(column == row, RIDGE, 0.0)
    lag = lag * scale - centre
    inverse = inverse_factor(work)
    half_step = jnp.dot(inverse, lag, precision=HIGHEST, preferred_element_type=F32)
    koopman = across(half_step, inverse, HIGHEST)
    moved = jnp.dot(koopman, inverse, precision=HIGHEST, preferred_element_type=F32)
    for index, matrix in enumerate((inverse, moved)):
        turned = matrix.T
        high = turned.astype(BF16)
        split_ref[index, :feat, :] = high
        split_ref[index, feat:, :] = (turned - high.astype(F32)).astype(BF16)
        rows = jnp.broadcast_to(mean, (8, feat))
        shift_ref[index] = jnp.dot(rows, turned, precision=HIGHEST, preferred_element_type=F32)


def koopman_parts(scale, mine, other, feat):
    vmem = pl.BlockSpec(memory_space=pltpu.VMEM)
    return pl.pallas_call(
        koopman_kernel,
        in_specs=[pl.BlockSpec(memory_space=pltpu.SMEM), vmem, vmem],
        out_specs=(vmem, vmem),
        out_shape=(
            jax.ShapeDtypeStruct((2, 2 * feat, feat), BF16),
            jax.ShapeDtypeStruct((2, 8, feat), F32),
        ),
        scratch_shapes=[pltpu.VMEM((feat, feat), F32), pltpu.VMEM((feat, feat), F32)],
        compiler_params=pltpu.CompilerParams(vmem_limit_bytes=12 * MIB),
    )(scale, mine, other)


def project_kernel(
    feature_ref, ahead_head_ref, ahead_early_ref, split_ref, shift_ref, moved_out, residual_out, moved, residual, sems
):
    rows = feature_ref.shape[0]
    half = LAG // 2
    at_end = lax.axis_index("tm") == lax.axis_size("tm") - 1

    def product(block, index):
        twice = jnp.concatenate([block, block], 1)
        return jnp.dot(twice, split_ref[index], preferred_element_type=F32) - shift_ref[index][0:1]

    copies = []
    for step in range(rows // CHUNK):
        here = slice(step * CHUNK, (step + 1) * CHUNK)
        start = step * CHUNK + LAG
        if start < rows:
            later = feature_ref[start : start + CHUNK, :]
        else:
            later = (ahead_head_ref if start == rows else ahead_early_ref)[...]
        now = product(feature_ref[here, :], 1)
        moved[here, :] = now
        gap = product(later, 0) - now
        residual[here, :] = gap if start < rows else jnp.where(at_end, 0.0, gap)
        for index, (source, target) in enumerate(((moved, moved_out), (residual, residual_out))):
            copy = pltpu.make_async_copy(source.at[here], target.at[here], sems.at[index, step])
            copy.start()
            copies.append(copy)
    for copy in copies:
        copy.wait()


def project(feature, ahead_head, ahead_early, split, shift):
    rows, feat = feature.shape
    vmem = pl.BlockSpec(memory_space=pltpu.VMEM)
    hbm = pl.BlockSpec(memory_space=pltpu.HBM)
    out = jax.ShapeDtypeStruct((rows, feat), F32)
    return pl.pallas_call(
        project_kernel,
        in_specs=[vmem] * 5,
        out_specs=(hbm, hbm),
        out_shape=(out, out),
        scratch_shapes=[
            pltpu.VMEM((rows, feat), F32),
            pltpu.VMEM((rows, feat), F32),
            pltpu.SemaphoreType.DMA((2, rows // CHUNK)),
        ],
        compiler_params=pltpu.CompilerParams(vmem_limit_bytes=24 * MIB),
    )(feature, ahead_head, ahead_early, split, shift)


def summed(kept, sent):
    swap = [(0, 1), (1, 0)]
    chips = ("x", "tm")
    parts = kept + lax.ppermute(sent, "core", swap)
    mine = jnp.sum(lax.all_to_all(parts, chips, 0, 0, tiled=True), 0, keepdims=True)
    mine = lax.all_to_all(jnp.broadcast_to(mine, parts.shape), chips, 0, 0, tiled=True)
    return mine, lax.ppermute(mine, "core", swap)


def on_device(frames, first_weight, first_bias, second_weight):
    frame_block = frames[0]
    row_count, channels = frame_block.shape
    hid, feat = second_weight.shape[1:]
    weights = (
        first_weight.reshape(2 * channels, hid),
        first_bias.reshape(1, hid),
        second_weight.reshape(2 * hid, feat),
    )
    halo = passed_along(frame_block[row_count - D1 - D2 :], "tm", 1)
    early, near, *weights = early_rows(frame_block, *weights)
    ahead_early = passed_along(early, "tm", -1)
    head = head_rows(near, halo, *weights)
    ahead_head = passed_along(head, "tm", -1)
    feature, inst, lag, total = body(frame_block, near, head, early, *weights)
    chips = lax.axis_size("x") * lax.axis_size("tm")
    mine, other = summed(*pack(feature, ahead_head, ahead_early, inst, lag, total, chips))
    replicas = lax.axis_size("x") * lax.axis_size("core")
    pair_count = replicas * (row_count * lax.axis_size("tm") - LAG)
    scale = jnp.full((1,), 1.0 / (2.0 * pair_count), F32)
    split, shift = koopman_parts(scale, mine, other, feat)
    propagated, residual = project(feature, ahead_head, ahead_early, split, shift)
    return (propagated[None], residual[None])


def solution(mesh):
    replicas, blocks = mesh.devices.shape
    chips = Mesh(mesh.devices.reshape(replicas // 2, 2, blocks), ("x", "core", "tm"))
    split = P(("x", "core"), "tm", None)
    return jax.shard_map(
        on_device,
        mesh=chips,
        in_specs=(split, P(), P(), P()),
        out_specs=(split, split),
        check_vma=False,
    )
```

```python
import jax
import jax.numpy as jnp
from jax import lax
from jax.experimental import pallas as pl
from jax.experimental.pallas import tpu as pltpu
from jax.sharding import Mesh, PartitionSpec as P

D1 = 32
D2 = 256
LAG = 1024
RIDGE = 0.001
CHUNK = 512
PANEL = 16
MIB = 1024 * 1024

F32 = jnp.float32
BF16 = jnp.bfloat16
HIGHEST = lax.Precision.HIGHEST


def passed_along(value, axis, steps):
    count = lax.axis_size(axis)
    first, last = (max(0, -steps), min(count, count - steps))
    return lax.ppermute(value, axis, [(source, source + steps) for source in range(first, last)])


def across(a, b, precision=None):
    return lax.dot_general(a, b, (((1,), (1,)), ((), ())), precision=precision, preferred_element_type=F32)


def gram(a, b):
    return lax.dot_general(a, b, (((0,), (0,)), ((), ())), preferred_element_type=F32)


def in_hbm(value):
    return pltpu.with_memory_space_constraint(value, pltpu.HBM)


def silu(x):
    half = 0.5 * x
    return half + half * jnp.tanh(half)


def hidden_rows(xs, at, rows, w1_ref, b1_ref):
    both = jnp.concatenate([xs[pl.ds(at + D1, rows), :], xs[pl.ds(at, rows), :]], 1)
    z = jnp.dot(both, w1_ref[...], preferred_element_type=F32)
    return silu(z + b1_ref[...]).astype(BF16)


def feature_rows(hs, at, rows, w2_ref):
    both = jnp.concatenate([hs[pl.ds(at + D2, rows), :], hs[pl.ds(at, rows), :]], 1)
    return jnp.dot(both, w2_ref[...], preferred_element_type=F32).astype(BF16)


def fetch_kernel(frames_ref, w1_in, b1_in, w2_in, last_ref, near_ref, w1_ref, b1_ref, w2_ref, sems):
    rows = frames_ref.shape[0]
    pairs = (
        (frames_ref.at[pl.ds(rows - D1 - D2, D1 + D2)], last_ref),
        (frames_ref.at[pl.ds(0, LAG)], near_ref),
        (w1_in, w1_ref),
        (b1_in, b1_ref),
        (w2_in, w2_ref),
    )
    copies = [pltpu.make_async_copy(*pair, sems.at[index]) for index, pair in enumerate(pairs)]
    for copy in copies:
        copy.start()
    for copy in copies:
        copy.wait()


def fetch(frames, w1, b1, w2):
    vmem = pl.BlockSpec(memory_space=pltpu.VMEM)
    hbm = pl.BlockSpec(memory_space=pltpu.HBM)
    channels = frames.shape[1]
    shapes = (((D1 + D2, channels), BF16), ((LAG, channels), BF16), (w1.shape, BF16), (b1.shape, F32), (w2.shape, BF16))
    return pl.pallas_call(
        fetch_kernel,
        in_specs=[hbm] * 4,
        out_specs=(vmem,) * 5,
        out_shape=tuple(jax.ShapeDtypeStruct(*shape) for shape in shapes),
        scratch_shapes=[pltpu.SemaphoreType.DMA((5,))],
        compiler_params=pltpu.CompilerParams(vmem_limit_bytes=8 * MIB),
    )(*(in_hbm(value) for value in (frames, w1, b1, w2)))


def early_kernel(near_ref, w1_ref, b1_ref, w2_ref, out_ref, hs):
    half = LAG // 2
    for at in range(0, hs.shape[0], D2):
        hs[at : at + D2, :] = hidden_rows(near_ref, half - D1 - D2 + at, D2, w1_ref, b1_ref)
    out_ref[...] = feature_rows(hs, 0, half, w2_ref)


def head_kernel(near_ref, halo_ref, w1_ref, b1_ref, w2_ref, out_ref, xs, hs):
    halo_rows = halo_ref.shape[0]
    xs[:halo_rows, :] = halo_ref[...]
    xs[halo_rows:, :] = near_ref[: LAG // 2, :]
    before = hidden_rows(xs, 0, D2, w1_ref, b1_ref)
    hs[:D2, :] = jnp.where(lax.axis_index("tm") > 0, before, jnp.zeros_like(before))
    for at in range(D2, hs.shape[0], D2):
        hs[at : at + D2, :] = hidden_rows(xs, at, D2, w1_ref, b1_ref)
    out_ref[...] = feature_rows(hs, 0, out_ref.shape[0], w2_ref)


def feature_scratch(rows, channels, hid):
    return [
        pltpu.VMEM((rows + D1 + D2, channels), BF16),
        pltpu.VMEM((rows + D2, hid), BF16),
    ]


def early_rows(near, w1, b1, w2):
    vmem = pl.BlockSpec(memory_space=pltpu.VMEM)
    half = LAG // 2
    return pl.pallas_call(
        early_kernel,
        in_specs=[vmem] * 4,
        out_specs=vmem,
        out_shape=jax.ShapeDtypeStruct((half, w2.shape[1]), BF16),
        scratch_shapes=[pltpu.VMEM((half + D2, w1.shape[1]), BF16)],
        compiler_params=pltpu.CompilerParams(vmem_limit_bytes=8 * MIB),
    )(near, w1, b1, w2)


def head_rows(near, halo, w1, b1, w2):
    vmem = pl.BlockSpec(memory_space=pltpu.VMEM)
    half = LAG // 2
    return pl.pallas_call(
        head_kernel,
        in_specs=[vmem] * 5,
        out_specs=vmem,
        out_shape=jax.ShapeDtypeStruct((half, w2.shape[1]), BF16),
        scratch_shapes=feature_scratch(half, near.shape[1], w1.shape[1]),
        compiler_params=pltpu.CompilerParams(vmem_limit_bytes=12 * MIB),
    )(near, halo, w1, b1, w2)


def column_sum(rows):
    return jnp.sum(rows.astype(F32).reshape(-1, 8, rows.shape[1]), 0)


def body_kernel(frames_ref, near_ref, head_ref, early_ref, w1_ref, b1_ref, w2_ref, out_ref, inst, lag, total, xs, hs, sems):
    rows, feat = out_ref.shape
    first = LAG - D1 - D2
    steps = (rows - LAG) // CHUNK

    def arriving(step):
        start = step * CHUNK + D1 + D2
        return pltpu.make_async_copy(
            frames_ref.at[pl.ds(first + start, CHUNK)], xs.at[pl.ds(start, CHUNK)], sems.at[step]
        )

    for step in range(steps):
        arriving(step).start()
    xs[: D1 + D2, :] = near_ref[first:, :]
    half = LAG // 2
    out_ref[:half, :] = head_ref[...]
    out_ref[half:LAG, :] = early_ref[...]
    tm_index, tm_last = lax.axis_index("tm"), lax.axis_size("tm") - 1
    first_weight = jnp.where(tm_index == 0, 1.0, 2.0)
    last_weight = jnp.where(tm_index == tm_last, 1.0, 2.0)
    start = out_ref[:LAG, :]
    inst[...] = first_weight * gram(start, start)
    total[...] = first_weight * column_sum(start)
    lag[...] = jnp.zeros_like(lag)
    hs[:D2, :] = hidden_rows(xs, 0, D2, w1_ref, b1_ref)
    arriving(0).wait()
    hs[D2 : D2 + CHUNK, :] = hidden_rows(xs, D2, CHUNK, w1_ref, b1_ref)

    def finish(step):
        value = feature_rows(hs, step * CHUNK, CHUNK, w2_ref)
        at = step * CHUNK
        out_ref[LAG + at : LAG + at + CHUNK, :] = value
        weight = last_weight if step >= steps - LAG // CHUNK else 2.0
        both = gram(value, jnp.concatenate([value, out_ref[at : at + CHUNK, :]], 1))
        inst[...] += weight * both[:, :feat]
        lag[...] += both[:, feat:]
        total[...] += weight * column_sum(value)

    for step in range(steps - 1):
        arriving(step + 1).wait()
        at = (step + 1) * CHUNK + D2
        hs[at : at + CHUNK, :] = hidden_rows(xs, at, CHUNK, w1_ref, b1_ref)
        finish(step)
    finish(steps - 1)


def body(frames, near, head, early, w1, b1, w2):
    rows, channels = frames.shape
    hid, feat = w1.shape[1], w2.shape[1]
    vmem = pl.BlockSpec(memory_space=pltpu.VMEM)
    square = jax.ShapeDtypeStruct((feat, feat), F32)
    return pl.pallas_call(
        body_kernel,
        in_specs=[pl.BlockSpec(memory_space=pltpu.HBM)] + [vmem] * 6,
        out_specs=(vmem,) * 4,
        out_shape=(
            jax.ShapeDtypeStruct((rows, feat), BF16),
            square,
            square,
            jax.ShapeDtypeStruct((8, feat), F32),
        ),
        scratch_shapes=feature_scratch(rows - LAG, channels, hid)
        + [pltpu.SemaphoreType.DMA((rows // CHUNK,))],
        compiler_params=pltpu.CompilerParams(vmem_limit_bytes=24 * MIB),
    )(in_hbm(frames), near, head, early, w1, b1, w2)


def pack_kernel(feature_ref, ahead_head_ref, ahead_early_ref, inst, lag, total, kept_ref, sent_ref, packed):
    feat = inst.shape[0]
    half = LAG // 2
    edge = feature_ref.shape[0] - LAG
    cross = lag[...] + gram(ahead_head_ref[...], feature_ref[edge : edge + half, :])
    cross += gram(ahead_early_ref[...], feature_ref[edge + half :, :])
    both = cross + cross.T
    row = lax.broadcasted_iota(jnp.int32, (feat, feat), 0)
    column = lax.broadcasted_iota(jnp.int32, (feat, feat), 1)
    packed[...] = jnp.where(column >= row, inst[...], both)
    sums = jnp.sum(total[...], 0, keepdims=True)
    diagonal = jnp.sum(jnp.where(column == row, both, 0.0), 0, keepdims=True)
    core = lax.axis_index("core")
    for ref, owner in ((kept_ref, core), (sent_ref, 1 - core)):
        extra = jnp.where(owner == 0, sums, diagonal)
        for chunk, _, share_row, lanes in slots(ref.shape, feat):
            source = pl.ds(owner * (feat // 2) + share_row, 1)
            ref[chunk, 0:1, lanes] = packed[source, :]
        for chunk in range(ref.shape[0]):
            part = extra[:, chunk * 128 : chunk * 128 + 128] if chunk < feat // 128 else jnp.zeros((1, 128), F32)
            ref[chunk, 0:1, ref.shape[2] - 128 :] = part


def slots(shape, feat):
    rows = (shape[2] - 128) // feat
    for chunk in range(shape[0]):
        for row in range(rows):
            yield chunk, row, chunk * rows + row, slice(row * feat, (row + 1) * feat)


def pack(feature, ahead_head, ahead_early, inst, lag, total, chips):
    vmem = pl.BlockSpec(memory_space=pltpu.VMEM)
    feat = inst.shape[0]
    share = jax.ShapeDtypeStruct((chips, 1, feat // 2 // chips * feat + 128), F32)
    return pl.pallas_call(
        pack_kernel,
        in_specs=[vmem] * 6,
        out_specs=(vmem, vmem),
        out_shape=(share, share),
        scratch_shapes=[pltpu.VMEM((feat, feat), F32)],
        compiler_params=pltpu.CompilerParams(vmem_limit_bytes=8 * MIB),
    )(feature, ahead_head, ahead_early, inst, lag, total)


def three_parts(x):
    high = x.astype(BF16)
    rest = x - high.astype(F32)
    middle = rest.astype(BF16)
    low = (rest - middle.astype(F32)).astype(BF16)
    return high, middle, low


def inverse_factor(work):
    size = work.shape[0]
    lane = lax.broadcasted_iota(jnp.int32, (PANEL, size), 1)
    sub = lax.broadcasted_iota(jnp.int32, (PANEL, size), 0)
    sub_narrow = lax.broadcasted_iota(jnp.int32, (PANEL, 128), 0)

    def wide(x):
        return jnp.concatenate([x] * (size // 128), 1)

    def spread(x, j):
        return jnp.broadcast_to(x[j : j + 1, :], x.shape)

    for start in range(0, size, PANEL):
        stop = start + PANEL
        panel = work[start:stop, :]
        columns = [
            jnp.broadcast_to(panel[:, start + k : start + k + 1], (PANEL, 128)) for k in range(PANEL)
        ]
        panel = jnp.where(
            (lane >= start) & (lane < stop), jnp.where(lane - start == sub, 1.0, 0.0), panel
        )
        pivots = jnp.ones((PANEL, 128), F32)
        pivot = spread(columns[0], 0)
        for j in range(PANEL):
            inverse = pl.reciprocal(pivot, approx=True)
            pivots = jnp.where(sub_narrow == j, pivot, pivots)
            if j + 1 == PANEL:
                break
            factor = jnp.where(sub_narrow > j, columns[j], 0.0) * inverse
            beside = [spread(columns[k], j) for k in range(j + 1, PANEL)]
            pivot = spread(columns[j + 1], j + 1) - beside[0] * beside[0] * inverse
            for k in range(j + 1, PANEL):
                columns[k] = columns[k] - factor * beside[k - j - 1]
            panel = panel - wide(factor) * spread(panel, j)
        panel = panel * wide(lax.rsqrt(pivots))
        work[start:stop, :] = panel
        if stop < size:
            high, middle, low = three_parts(panel)
            left = jnp.concatenate([high, high, middle, high, low, middle], 0)
            right = jnp.concatenate([high, middle, high, low, high, middle], 0)
            first = stop // 128 * 128
            update = gram(left[:, first:], right)
            kept = lax.broadcasted_iota(jnp.int32, (size - stop, size), 1)
            kept = (kept < start) | (kept >= stop)
            work[stop:, :] = jnp.where(kept, work[stop:, :], 0.0) - update[stop - first :]
    row = lax.broadcasted_iota(jnp.int32, (size, size), 0)
    column = lax.broadcasted_iota(jnp.int32, (size, size), 1)
    return jnp.where(column <= row, work[...], 0.0)


def koopman_kernel(scale_ref, mine_ref, other_ref, split_ref, shift_ref, work, packed_ref):
    feat = packed_ref.shape[1]
    scale = scale_ref[0]
    core = lax.axis_index("core")
    extras = []
    for ref, owner in ((mine_ref, core), (other_ref, 1 - core)):
        for chunk, _, share_row, lanes in slots(ref.shape, feat):
            packed_ref[pl.ds(owner * (feat // 2) + share_row, 1), :] = ref[chunk, 0:1, lanes]
        parts = [ref[chunk, 0:1, ref.shape[2] - 128 :] for chunk in range(feat // 128)]
        extras.append(jnp.concatenate(parts, 1))
    packed = packed_ref[...]
    mean = jnp.where(core == 0, extras[0], extras[1]) * scale
    diagonal = jnp.where(core == 0, extras[1], extras[0])
    row = lax.broadcasted_iota(jnp.int32, (feat, feat), 0)
    column = lax.broadcasted_iota(jnp.int32, (feat, feat), 1)
    turned = packed.T
    centre = jnp.broadcast_to(mean, (feat, feat))
    centre = centre * centre.T
    inst = jnp.where(column >= row, packed, turned)
    lag = jnp.where(column < row, packed, turned)
    lag = jnp.where(column == row, jnp.broadcast_to(diagonal, (feat, feat)), lag)
    work[...] = inst * scale - centre + jnp.where(column == row, RIDGE, 0.0)
    lag = lag * scale - centre
    inverse = inverse_factor(work)
    half_step = jnp.dot(inverse, lag, precision=HIGHEST, preferred_element_type=F32)
    koopman = across(half_step, inverse, HIGHEST)
    moved = jnp.dot(koopman, inverse, precision=HIGHEST, preferred_element_type=F32)
    for index, matrix in enumerate((inverse, moved)):
        turned = matrix.T
        high = turned.astype(BF16)
        split_ref[index, :feat, :] = high
        split_ref[index, feat:, :] = (turned - high.astype(F32)).astype(BF16)
        rows = jnp.broadcast_to(mean, (8, feat))
        shift_ref[index] = jnp.dot(rows, turned, precision=HIGHEST, preferred_element_type=F32)


def koopman_parts(scale, mine, other, feat):
    vmem = pl.BlockSpec(memory_space=pltpu.VMEM)
    return pl.pallas_call(
        koopman_kernel,
        in_specs=[pl.BlockSpec(memory_space=pltpu.SMEM), vmem, vmem],
        out_specs=(vmem, vmem),
        out_shape=(
            jax.ShapeDtypeStruct((2, 2 * feat, feat), BF16),
            jax.ShapeDtypeStruct((2, 8, feat), F32),
        ),
        scratch_shapes=[pltpu.VMEM((feat, feat), F32), pltpu.VMEM((feat, feat), F32)],
        compiler_params=pltpu.CompilerParams(vmem_limit_bytes=12 * MIB),
    )(scale, mine, other)


def project_kernel(
    feature_ref, ahead_head_ref, ahead_early_ref, split_ref, shift_ref, moved_out, residual_out, moved, residual, sems
):
    rows = feature_ref.shape[0]
    half = LAG // 2
    at_end = lax.axis_index("tm") == lax.axis_size("tm") - 1

    def product(block, index):
        twice = jnp.concatenate([block, block], 1)
        return jnp.dot(twice, split_ref[index], preferred_element_type=F32) - shift_ref[index][0:1]

    copies = []
    for step in range(rows // CHUNK):
        here = slice(step * CHUNK, (step + 1) * CHUNK)
        start = step * CHUNK + LAG
        if start < rows:
            later = feature_ref[start : start + CHUNK, :]
        else:
            later = (ahead_head_ref if start == rows else ahead_early_ref)[...]
        now = product(feature_ref[here, :], 1)
        moved[here, :] = now
        gap = product(later, 0) - now
        residual[here, :] = gap if start < rows else jnp.where(at_end, 0.0, gap)
        for index, (source, target) in enumerate(((moved, moved_out), (residual, residual_out))):
            copy = pltpu.make_async_copy(source.at[here], target.at[here], sems.at[index, step])
            copy.start()
            copies.append(copy)
    for copy in copies:
        copy.wait()


def project(feature, ahead_head, ahead_early, split, shift):
    rows, feat = feature.shape
    vmem = pl.BlockSpec(memory_space=pltpu.VMEM)
    hbm = pl.BlockSpec(memory_space=pltpu.HBM)
    out = jax.ShapeDtypeStruct((rows, feat), F32)
    return pl.pallas_call(
        project_kernel,
        in_specs=[vmem] * 5,
        out_specs=(hbm, hbm),
        out_shape=(out, out),
        scratch_shapes=[
            pltpu.VMEM((rows, feat), F32),
            pltpu.VMEM((rows, feat), F32),
            pltpu.SemaphoreType.DMA((2, rows // CHUNK)),
        ],
        compiler_params=pltpu.CompilerParams(vmem_limit_bytes=24 * MIB),
    )(feature, ahead_head, ahead_early, split, shift)


def swapped(value, axis, bit):
    return lax.ppermute(value, axis, [(i, i ^ bit) for i in range(lax.axis_size(axis))])


def upper(axis, bit):
    return lax.axis_index(axis) // bit % 2


def summed(kept, sent):
    bits = lambda axis: [1 << k for k in range(lax.axis_size(axis).bit_length() - 1)]
    halved = [("x", bit) for bit in bits("x")] + [("tm", bit) for bit in bits("tm")[:1]]
    mine = kept + swapped(sent, "core", 1)
    for axis, bit in halved:
        half = mine.shape[0] // 2
        up = upper(axis, bit)
        away = lax.dynamic_slice_in_dim(mine, (1 - up) * half, half)
        mine = lax.dynamic_slice_in_dim(mine, up * half, half) + swapped(away, axis, bit)
    for bit in bits("tm")[1:]:
        mine = mine + swapped(mine, "tm", bit)
    for axis, bit in reversed(halved):
        other = swapped(mine, axis, bit)
        in_upper = upper(axis, bit) == 1
        mine = jnp.concatenate([jnp.where(in_upper, other, mine), jnp.where(in_upper, mine, other)], 0)
    return mine, swapped(mine, "core", 1)


def on_device(frames, first_weight, first_bias, second_weight):
    frame_block = frames[0]
    row_count, channels = frame_block.shape
    hid, feat = second_weight.shape[1:]
    weights = (
        first_weight.reshape(2 * channels, hid),
        first_bias.reshape(1, hid),
        second_weight.reshape(2 * hid, feat),
    )
    last, near, *weights = fetch(frame_block, *weights)
    halo = passed_along(last, "tm", 1)
    early = early_rows(near, *weights)
    ahead_early = passed_along(early, "tm", -1)
    head = head_rows(near, halo, *weights)
    ahead_head = passed_along(head, "tm", -1)
    feature, inst, lag, total = body(frame_block, near, head, early, *weights)
    chips = lax.axis_size("x") * lax.axis_size("tm")
    mine, other = summed(*pack(feature, ahead_head, ahead_early, inst, lag, total, chips))
    replicas = lax.axis_size("x") * lax.axis_size("core")
    pair_count = replicas * (row_count * lax.axis_size("tm") - LAG)
    scale = jnp.full((1,), 1.0 / (2.0 * pair_count), F32)
    split, shift = koopman_parts(scale, mine, other, feat)
    propagated, residual = project(feature, ahead_head, ahead_early, split, shift)
    return (propagated[None], residual[None])


def solution(mesh):
    replicas, blocks = mesh.devices.shape
    chips = Mesh(mesh.devices.reshape(replicas // 2, 2, blocks), ("x", "core", "tm"))
    split = P(("x", "core"), "tm", None)
    return jax.shard_map(
        on_device,
        mesh=chips,
        in_specs=(split, P(), P(), P()),
        out_specs=(split, split),
        check_vma=False,
    )
```

```python
import jax
import jax.numpy as jnp
from jax import lax
from jax.experimental import pallas as pl
from jax.experimental.pallas import tpu as pltpu
from jax.sharding import Mesh, PartitionSpec as P

D1 = 32
D2 = 256
LAG = 1024
RIDGE = 0.001
CHUNK = 512
PANEL = 16
MIB = 1024 * 1024

F32 = jnp.float32
BF16 = jnp.bfloat16
HIGHEST = lax.Precision.HIGHEST


def passed_along(value, axis, steps):
    count = lax.axis_size(axis)
    first, last = (max(0, -steps), min(count, count - steps))
    return lax.ppermute(value, axis, [(source, source + steps) for source in range(first, last)])


def across(a, b, precision=None):
    return lax.dot_general(a, b, (((1,), (1,)), ((), ())), precision=precision, preferred_element_type=F32)


def gram(a, b):
    return lax.dot_general(a, b, (((0,), (0,)), ((), ())), preferred_element_type=F32)


def in_hbm(value):
    return pltpu.with_memory_space_constraint(value, pltpu.HBM)


def silu(x):
    half = 0.5 * x
    return half + half * jnp.tanh(half)


def hidden_rows(xs, at, rows, w1_ref, b1_ref):
    both = jnp.concatenate([xs[pl.ds(at + D1, rows), :], xs[pl.ds(at, rows), :]], 1)
    hid = w1_ref.shape[1]
    parts = []
    for lanes in (slice(0, hid // 2), slice(hid // 2, hid)):
        z = jnp.dot(both, w1_ref[:, lanes], preferred_element_type=F32)
        parts.append(silu(z + b1_ref[:, lanes]).astype(BF16))
    return jnp.concatenate(parts, 1)


def feature_rows(hs, at, rows, w2_ref):
    both = jnp.concatenate([hs[pl.ds(at + D2, rows), :], hs[pl.ds(at, rows), :]], 1)
    return jnp.dot(both, w2_ref[...], preferred_element_type=F32).astype(BF16)


def fetch_kernel(frames_ref, w1_in, b1_in, w2_in, last_ref, near_ref, w1_ref, b1_ref, w2_ref, sems):
    rows = frames_ref.shape[0]
    pairs = (
        (frames_ref.at[pl.ds(rows - D1 - D2, D1 + D2)], last_ref),
        (frames_ref.at[pl.ds(0, LAG)], near_ref),
        (w1_in, w1_ref),
        (b1_in, b1_ref),
        (w2_in, w2_ref),
    )
    copies = [pltpu.make_async_copy(*pair, sems.at[index]) for index, pair in enumerate(pairs)]
    for copy in copies:
        copy.start()
    for copy in copies:
        copy.wait()


def fetch(frames, w1, b1, w2):
    vmem = pl.BlockSpec(memory_space=pltpu.VMEM)
    hbm = pl.BlockSpec(memory_space=pltpu.HBM)
    channels = frames.shape[1]
    shapes = (((D1 + D2, channels), BF16), ((LAG, channels), BF16), (w1.shape, BF16), (b1.shape, F32), (w2.shape, BF16))
    return pl.pallas_call(
        fetch_kernel,
        in_specs=[hbm] * 4,
        out_specs=(vmem,) * 5,
        out_shape=tuple(jax.ShapeDtypeStruct(*shape) for shape in shapes),
        scratch_shapes=[pltpu.SemaphoreType.DMA((5,))],
        compiler_params=pltpu.CompilerParams(vmem_limit_bytes=8 * MIB),
    )(*(in_hbm(value) for value in (frames, w1, b1, w2)))


def first_weight():
    return jnp.where(lax.axis_index("tm") == 0, 1.0, 2.0)


def last_weight():
    return jnp.where(lax.axis_index("tm") == lax.axis_size("tm") - 1, 1.0, 2.0)


def early_kernel(
    frames_ref, near_ref, w1_ref, b1_ref, w2_ref, early_ref, middle_ref, hidden_ref, inst, total, xs, hs, sems
):
    half = LAG // 2
    first = half - D1 - D2

    def arriving(step):
        at = LAG + step * CHUNK
        return pltpu.make_async_copy(
            frames_ref.at[pl.ds(at, CHUNK)], xs.at[pl.ds(at - first, CHUNK)], sems.at[step]
        )

    steps = LAG // CHUNK
    for step in range(steps):
        arriving(step).start()
    xs[: LAG - first, :] = near_ref[first:, :]
    hs[: D2 + half, :] = hidden_rows(xs, 0, D2 + half, w1_ref, b1_ref)
    value = feature_rows(hs, 0, half, w2_ref)
    early_ref[...] = value
    inst[...] = first_weight() * gram(value, value)
    total[...] = first_weight() * column_sum(value)
    for step in range(steps):
        arriving(step).wait()
        at = half + step * CHUNK
        hs[at + D2 : at + D2 + CHUNK, :] = hidden_rows(xs, at + D2, CHUNK, w1_ref, b1_ref)
        value = feature_rows(hs, at, CHUNK, w2_ref)
        middle_ref[step * CHUNK : (step + 1) * CHUNK, :] = value
        inst[...] += 2.0 * gram(value, value)
        total[...] += 2.0 * column_sum(value)
    hidden_ref[...] = hs[hs.shape[0] - D2 :, :]


def head_kernel(near_ref, halo_ref, w1_ref, b1_ref, w2_ref, out_ref, xs, hs):
    halo_rows = halo_ref.shape[0]
    xs[:halo_rows, :] = halo_ref[...]
    xs[halo_rows:, :] = near_ref[: LAG // 2, :]
    before = hidden_rows(xs, 0, D2, w1_ref, b1_ref)
    hs[:D2, :] = jnp.where(lax.axis_index("tm") > 0, before, jnp.zeros_like(before))
    for at in range(D2, hs.shape[0], D2):
        hs[at : at + D2, :] = hidden_rows(xs, at, D2, w1_ref, b1_ref)
    out_ref[...] = feature_rows(hs, 0, out_ref.shape[0], w2_ref)


def feature_scratch(rows, channels, hid):
    return [
        pltpu.VMEM((rows + D1 + D2, channels), BF16),
        pltpu.VMEM((rows + D2, hid), BF16),
    ]


def early_rows(frames, near, w1, b1, w2):
    vmem = pl.BlockSpec(memory_space=pltpu.VMEM)
    hbm = pl.BlockSpec(memory_space=pltpu.HBM)
    half, hid, feat = LAG // 2, w1.shape[1], w2.shape[1]
    shapes = (((half, feat), BF16), ((LAG, feat), BF16), ((D2, hid), BF16), ((feat, feat), F32), ((8, feat), F32))
    return pl.pallas_call(
        early_kernel,
        in_specs=[hbm] + [vmem] * 4,
        out_specs=(vmem,) * 5,
        out_shape=tuple(jax.ShapeDtypeStruct(*shape) for shape in shapes),
        scratch_shapes=feature_scratch(half + LAG, near.shape[1], hid) + [pltpu.SemaphoreType.DMA((LAG // CHUNK,))],
        compiler_params=pltpu.CompilerParams(vmem_limit_bytes=16 * MIB),
    )(in_hbm(frames), near, w1, b1, w2)


def head_rows(near, halo, w1, b1, w2):
    vmem = pl.BlockSpec(memory_space=pltpu.VMEM)
    half = LAG // 2
    return pl.pallas_call(
        head_kernel,
        in_specs=[vmem] * 5,
        out_specs=vmem,
        out_shape=jax.ShapeDtypeStruct((half, w2.shape[1]), BF16),
        scratch_shapes=feature_scratch(half, near.shape[1], w1.shape[1]),
        compiler_params=pltpu.CompilerParams(vmem_limit_bytes=12 * MIB),
    )(near, halo, w1, b1, w2)


def column_sum(rows):
    return jnp.sum(rows.astype(F32).reshape(-1, 8, rows.shape[1]), 0)


def body_kernel(
    frames_ref, head_ref, early_ref, middle_ref, hidden_ref, inst_in, total_in, w1_ref, b1_ref, w2_ref,
    out_ref, inst, lag, total, xs, hs, sems
):
    rows, feat = out_ref.shape
    done = 2 * LAG
    steps = (rows - done) // CHUNK

    def arriving(step):
        more = D1 if step == 0 else 0
        at = step * CHUNK + D1 - more
        return pltpu.make_async_copy(
            frames_ref.at[pl.ds(done - D1 + at, CHUNK + more)], xs.at[pl.ds(at, CHUNK + more)], sems.at[step]
        )

    for step in range(steps):
        arriving(step).start()
    half = LAG // 2
    hs[:D2, :] = hidden_ref[...]
    out_ref[:half, :] = head_ref[...]
    out_ref[half:LAG, :] = early_ref[...]
    out_ref[LAG:done, :] = middle_ref[...]
    start = out_ref[:half, :]
    inst[...] = inst_in[...] + first_weight() * gram(start, start)
    total[...] = total_in[...] + first_weight() * column_sum(start)
    lag[...] = gram(out_ref[LAG : LAG + CHUNK, :], out_ref[:CHUNK, :])
    for at in range(CHUNK, LAG, CHUNK):
        lag[...] += gram(out_ref[LAG + at : LAG + at + CHUNK, :], out_ref[at : at + CHUNK, :])

    def hidden(step):
        arriving(step).wait()
        at = step * CHUNK
        hs[D2 + at : D2 + at + CHUNK, :] = hidden_rows(xs, at, CHUNK, w1_ref, b1_ref)

    def finish(step):
        value = feature_rows(hs, step * CHUNK, CHUNK, w2_ref)
        at = done + step * CHUNK
        out_ref[at : at + CHUNK, :] = value
        weight = last_weight() if at >= rows - LAG else 2.0
        both = gram(value, jnp.concatenate([value, out_ref[at - LAG : at - LAG + CHUNK, :]], 1))
        inst[...] += weight * both[:, :feat]
        lag[...] += both[:, feat:]
        total[...] += weight * column_sum(value)

    hidden(0)
    for step in range(steps - 1):
        hidden(step + 1)
        finish(step)
    finish(steps - 1)


def body(frames, head, early, middle, hidden, inst, total, w1, b1, w2):
    rows, channels = frames.shape
    hid, feat = w1.shape[1], w2.shape[1]
    vmem = pl.BlockSpec(memory_space=pltpu.VMEM)
    square = jax.ShapeDtypeStruct((feat, feat), F32)
    left = rows - 2 * LAG
    return pl.pallas_call(
        body_kernel,
        in_specs=[pl.BlockSpec(memory_space=pltpu.HBM)] + [vmem] * 9,
        out_specs=(vmem,) * 4,
        out_shape=(
            jax.ShapeDtypeStruct((rows, feat), BF16),
            square,
            square,
            jax.ShapeDtypeStruct((8, feat), F32),
        ),
        scratch_shapes=[
            pltpu.VMEM((left + D1, channels), BF16),
            pltpu.VMEM((left + D2, hid), BF16),
            pltpu.SemaphoreType.DMA((left // CHUNK,)),
        ],
        compiler_params=pltpu.CompilerParams(vmem_limit_bytes=24 * MIB),
    )(in_hbm(frames), head, early, middle, hidden, inst, total, w1, b1, w2)


def pack_kernel(feature_ref, ahead_head_ref, ahead_early_ref, inst, lag, total, kept_ref, sent_ref, packed):
    feat = inst.shape[0]
    half = LAG // 2
    edge = feature_ref.shape[0] - LAG
    cross = lag[...] + gram(ahead_head_ref[...], feature_ref[edge : edge + half, :])
    cross += gram(ahead_early_ref[...], feature_ref[edge + half :, :])
    both = cross + cross.T
    row = lax.broadcasted_iota(jnp.int32, (feat, feat), 0)
    column = lax.broadcasted_iota(jnp.int32, (feat, feat), 1)
    packed[...] = jnp.where(column >= row, inst[...], both)
    sums = jnp.sum(total[...], 0, keepdims=True)
    diagonal = jnp.sum(jnp.where(column == row, both, 0.0), 0, keepdims=True)
    core = lax.axis_index("core")
    for ref, owner in ((kept_ref, core), (sent_ref, 1 - core)):
        extra = jnp.where(owner == 0, sums, diagonal)
        for chunk, _, share_row, lanes in slots(ref.shape, feat):
            source = pl.ds(owner * (feat // 2) + share_row, 1)
            ref[chunk, 0:1, lanes] = packed[source, :]
        for chunk in range(ref.shape[0]):
            part = extra[:, chunk * 128 : chunk * 128 + 128] if chunk < feat // 128 else jnp.zeros((1, 128), F32)
            ref[chunk, 0:1, ref.shape[2] - 128 :] = part


def slots(shape, feat):
    rows = (shape[2] - 128) // feat
    for chunk in range(shape[0]):
        for row in range(rows):
            yield chunk, row, chunk * rows + row, slice(row * feat, (row + 1) * feat)


def pack(feature, ahead_head, ahead_early, inst, lag, total, chips):
    vmem = pl.BlockSpec(memory_space=pltpu.VMEM)
    feat = inst.shape[0]
    share = jax.ShapeDtypeStruct((chips, 1, feat // 2 // chips * feat + 128), F32)
    return pl.pallas_call(
        pack_kernel,
        in_specs=[vmem] * 6,
        out_specs=(vmem, vmem),
        out_shape=(share, share),
        scratch_shapes=[pltpu.VMEM((feat, feat), F32)],
        compiler_params=pltpu.CompilerParams(vmem_limit_bytes=8 * MIB),
    )(feature, ahead_head, ahead_early, inst, lag, total)


def three_parts(x):
    high = x.astype(BF16)
    rest = x - high.astype(F32)
    middle = rest.astype(BF16)
    low = (rest - middle.astype(F32)).astype(BF16)
    return high, middle, low


def inverse_factor(work):
    size = work.shape[0]
    lane = lax.broadcasted_iota(jnp.int32, (PANEL, size), 1)
    sub = lax.broadcasted_iota(jnp.int32, (PANEL, size), 0)
    sub_narrow = lax.broadcasted_iota(jnp.int32, (PANEL, 128), 0)

    def wide(x):
        return jnp.concatenate([x] * (size // 128), 1)

    def spread(x, j):
        return jnp.broadcast_to(x[j : j + 1, :], x.shape)

    for start in range(0, size, PANEL):
        stop = start + PANEL
        panel = work[start:stop, :]
        columns = [
            jnp.broadcast_to(panel[:, start + k : start + k + 1], (PANEL, 128)) for k in range(PANEL)
        ]
        panel = jnp.where(
            (lane >= start) & (lane < stop), jnp.where(lane - start == sub, 1.0, 0.0), panel
        )
        pivots = jnp.ones((PANEL, 128), F32)
        pivot = spread(columns[0], 0)
        for j in range(PANEL):
            inverse = pl.reciprocal(pivot, approx=True)
            pivots = jnp.where(sub_narrow == j, pivot, pivots)
            if j + 1 == PANEL:
                break
            factor = jnp.where(sub_narrow > j, columns[j], 0.0) * inverse
            beside = [spread(columns[k], j) for k in range(j + 1, PANEL)]
            pivot = spread(columns[j + 1], j + 1) - beside[0] * beside[0] * inverse
            for k in range(j + 1, PANEL):
                columns[k] = columns[k] - factor * beside[k - j - 1]
            panel = panel - wide(factor) * spread(panel, j)
        panel = panel * wide(lax.rsqrt(pivots))
        work[start:stop, :] = panel
        if stop < size:
            high, middle, low = three_parts(panel)
            left = jnp.concatenate([high, high, middle, high, low, middle], 0)
            right = jnp.concatenate([high, middle, high, low, high, middle], 0)
            first = stop // 128 * 128
            update = gram(left[:, first:], right)
            kept = lax.broadcasted_iota(jnp.int32, (size - stop, size), 1)
            kept = (kept < start) | (kept >= stop)
            work[stop:, :] = jnp.where(kept, work[stop:, :], 0.0) - update[stop - first :]
    row = lax.broadcasted_iota(jnp.int32, (size, size), 0)
    column = lax.broadcasted_iota(jnp.int32, (size, size), 1)
    return jnp.where(column <= row, work[...], 0.0)


def koopman_kernel(scale_ref, mine_ref, other_ref, split_ref, shift_ref, work, packed_ref):
    feat = packed_ref.shape[1]
    scale = scale_ref[0]
    core = lax.axis_index("core")
    extras = []
    for ref, owner in ((mine_ref, core), (other_ref, 1 - core)):
        for chunk, _, share_row, lanes in slots(ref.shape, feat):
            packed_ref[pl.ds(owner * (feat // 2) + share_row, 1), :] = ref[chunk, 0:1, lanes]
        parts = [ref[chunk, 0:1, ref.shape[2] - 128 :] for chunk in range(feat // 128)]
        extras.append(jnp.concatenate(parts, 1))
    packed = packed_ref[...]
    mean = jnp.where(core == 0, extras[0], extras[1]) * scale
    diagonal = jnp.where(core == 0, extras[1], extras[0])
    row = lax.broadcasted_iota(jnp.int32, (feat, feat), 0)
    column = lax.broadcasted_iota(jnp.int32, (feat, feat), 1)
    turned = packed.T
    centre = jnp.broadcast_to(mean, (feat, feat))
    centre = centre * centre.T
    inst = jnp.where(column >= row, packed, turned)
    lag = jnp.where(column < row, packed, turned)
    lag = jnp.where(column == row, jnp.broadcast_to(diagonal, (feat, feat)), lag)
    work[...] = inst * scale - centre + jnp.where(column == row, RIDGE, 0.0)
    lag = lag * scale - centre
    inverse = inverse_factor(work)
    half_step = jnp.dot(inverse, lag, precision=HIGHEST, preferred_element_type=F32)
    koopman = across(half_step, inverse, HIGHEST)
    moved = jnp.dot(koopman, inverse, precision=HIGHEST, preferred_element_type=F32)
    for index, matrix in enumerate((inverse, moved)):
        turned = matrix.T
        high = turned.astype(BF16)
        split_ref[index, :feat, :] = high
        split_ref[index, feat:, :] = (turned - high.astype(F32)).astype(BF16)
        rows = jnp.broadcast_to(mean, (8, feat))
        shift_ref[index] = jnp.dot(rows, turned, precision=HIGHEST, preferred_element_type=F32)


def koopman_parts(scale, mine, other, feat):
    vmem = pl.BlockSpec(memory_space=pltpu.VMEM)
    return pl.pallas_call(
        koopman_kernel,
        in_specs=[pl.BlockSpec(memory_space=pltpu.SMEM), vmem, vmem],
        out_specs=(vmem, vmem),
        out_shape=(
            jax.ShapeDtypeStruct((2, 2 * feat, feat), BF16),
            jax.ShapeDtypeStruct((2, 8, feat), F32),
        ),
        scratch_shapes=[pltpu.VMEM((feat, feat), F32), pltpu.VMEM((feat, feat), F32)],
        compiler_params=pltpu.CompilerParams(vmem_limit_bytes=12 * MIB),
    )(scale, mine, other)


def project_kernel(
    feature_ref, ahead_head_ref, ahead_early_ref, split_ref, shift_ref, moved_out, residual_out, moved, residual, sems
):
    rows = feature_ref.shape[0]
    half = LAG // 2
    at_end = lax.axis_index("tm") == lax.axis_size("tm") - 1

    def product(block, index):
        twice = jnp.concatenate([block, block], 1)
        return jnp.dot(twice, split_ref[index], preferred_element_type=F32) - shift_ref[index][0:1]

    copies = []
    for step in range(rows // CHUNK):
        here = slice(step * CHUNK, (step + 1) * CHUNK)
        start = step * CHUNK + LAG
        if start < rows:
            later = feature_ref[start : start + CHUNK, :]
        else:
            later = (ahead_head_ref if start == rows else ahead_early_ref)[...]
        now = product(feature_ref[here, :], 1)
        moved[here, :] = now
        gap = product(later, 0) - now
        residual[here, :] = gap if start < rows else jnp.where(at_end, 0.0, gap)
        for index, (source, target) in enumerate(((moved, moved_out), (residual, residual_out))):
            copy = pltpu.make_async_copy(source.at[here], target.at[here], sems.at[index, step])
            copy.start()
            copies.append(copy)
    for copy in copies:
        copy.wait()


def project(feature, ahead_head, ahead_early, split, shift):
    rows, feat = feature.shape
    vmem = pl.BlockSpec(memory_space=pltpu.VMEM)
    hbm = pl.BlockSpec(memory_space=pltpu.HBM)
    out = jax.ShapeDtypeStruct((rows, feat), F32)
    return pl.pallas_call(
        project_kernel,
        in_specs=[vmem] * 5,
        out_specs=(hbm, hbm),
        out_shape=(out, out),
        scratch_shapes=[
            pltpu.VMEM((rows, feat), F32),
            pltpu.VMEM((rows, feat), F32),
            pltpu.SemaphoreType.DMA((2, rows // CHUNK)),
        ],
        compiler_params=pltpu.CompilerParams(vmem_limit_bytes=24 * MIB),
    )(feature, ahead_head, ahead_early, split, shift)


def summed(kept, sent):
    swap = [(0, 1), (1, 0)]
    chips = ("x", "tm")
    parts = kept + lax.ppermute(sent, "core", swap)
    mine = jnp.sum(lax.all_to_all(parts, chips, 0, 0, tiled=True), 0, keepdims=True)
    mine = lax.all_to_all(jnp.broadcast_to(mine, parts.shape), chips, 0, 0, tiled=True)
    return mine, lax.ppermute(mine, "core", swap)


def on_device(frames, first_weight, first_bias, second_weight):
    frame_block = frames[0]
    row_count, channels = frame_block.shape
    hid, feat = second_weight.shape[1:]
    weights = (
        first_weight.reshape(2 * channels, hid),
        first_bias.reshape(1, hid),
        second_weight.reshape(2 * hid, feat),
    )
    last, near, *weights = fetch(frame_block, *weights)
    halo = passed_along(last, "tm", 1)
    early, middle, hidden, inst, total = early_rows(frame_block, near, *weights)
    ahead_early = passed_along(early, "tm", -1)
    head = head_rows(near, halo, *weights)
    ahead_head = passed_along(head, "tm", -1)
    feature, inst, lag, total = body(
        frame_block, head, early, middle, hidden, inst, total, *weights
    )
    chips = lax.axis_size("x") * lax.axis_size("tm")
    mine, other = summed(*pack(feature, ahead_head, ahead_early, inst, lag, total, chips))
    replicas = lax.axis_size("x") * lax.axis_size("core")
    pair_count = replicas * (row_count * lax.axis_size("tm") - LAG)
    scale = jnp.full((1,), 1.0 / (2.0 * pair_count), F32)
    split, shift = koopman_parts(scale, mine, other, feat)
    propagated, residual = project(feature, ahead_head, ahead_early, split, shift)
    return (propagated[None], residual[None])


def solution(mesh):
    replicas, blocks = mesh.devices.shape
    chips = Mesh(mesh.devices.reshape(replicas // 2, 2, blocks), ("x", "core", "tm"))
    split = P(("x", "core"), "tm", None)
    return jax.shard_map(
        on_device,
        mesh=chips,
        in_specs=(split, P(), P(), P()),
        out_specs=(split, split),
        check_vma=False,
    )
```

```python
import jax
import jax.numpy as jnp
from jax import lax
from jax.experimental import pallas as pl
from jax.experimental.pallas import tpu as pltpu
from jax.sharding import Mesh, PartitionSpec as P

D1 = 32
D2 = 256
LAG = 1024
RIDGE = 0.001
CHUNK = 512
PANEL = 16
MIB = 1024 * 1024

F32 = jnp.float32
BF16 = jnp.bfloat16
HIGHEST = lax.Precision.HIGHEST


def passed_along(value, axis, steps):
    count = lax.axis_size(axis)
    first, last = (max(0, -steps), min(count, count - steps))
    return lax.ppermute(value, axis, [(source, source + steps) for source in range(first, last)])


def across(a, b, precision=None):
    return lax.dot_general(a, b, (((1,), (1,)), ((), ())), precision=precision, preferred_element_type=F32)


def gram(a, b):
    return lax.dot_general(a, b, (((0,), (0,)), ((), ())), preferred_element_type=F32)


def feature_gram(a, b):
    size = a.shape[1]
    row = lax.broadcasted_iota(jnp.int32, (size, size), 0)
    column = lax.broadcasted_iota(jnp.int32, (size, size), 1)
    identity = jnp.where(row == column, 1.0, 0.0).astype(BF16)
    turned = across(identity, a).astype(BF16)
    return jnp.dot(turned, b, preferred_element_type=F32)


def in_hbm(value):
    return pltpu.with_memory_space_constraint(value, pltpu.HBM)


def silu(x):
    half = 0.5 * x
    return half + half * jnp.tanh(half)


def hidden_rows(xs, at, rows, w1_ref, b1_ref):
    both = jnp.concatenate([xs[pl.ds(at + D1, rows), :], xs[pl.ds(at, rows), :]], 1)
    hid = w1_ref.shape[1]
    parts = []
    for lanes in (slice(0, hid // 2), slice(hid // 2, hid)):
        z = jnp.dot(both, w1_ref[:, lanes], preferred_element_type=F32)
        parts.append(silu(z + b1_ref[:, lanes]).astype(BF16))
    return jnp.concatenate(parts, 1)


def feature_rows(hs, at, rows, w2_ref):
    both = jnp.concatenate([hs[pl.ds(at + D2, rows), :], hs[pl.ds(at, rows), :]], 1)
    return jnp.dot(both, w2_ref[...], preferred_element_type=F32).astype(BF16)


def fetch_kernel(frames_ref, w1_in, b1_in, w2_in, near_ref, w1_ref, b1_ref, w2_ref, sems):
    pairs = (
        (frames_ref.at[pl.ds(0, LAG)], near_ref),
        (w1_in, w1_ref),
        (b1_in, b1_ref),
        (w2_in, w2_ref),
    )
    copies = [pltpu.make_async_copy(*pair, sems.at[index]) for index, pair in enumerate(pairs)]
    for copy in copies:
        copy.start()
    for copy in copies:
        copy.wait()


def fetch(frames, w1, b1, w2):
    vmem = pl.BlockSpec(memory_space=pltpu.VMEM)
    hbm = pl.BlockSpec(memory_space=pltpu.HBM)
    channels = frames.shape[1]
    shapes = (((LAG, channels), BF16), (w1.shape, BF16), (b1.shape, F32), (w2.shape, BF16))
    return pl.pallas_call(
        fetch_kernel,
        in_specs=[hbm] * 4,
        out_specs=(vmem,) * 4,
        out_shape=tuple(jax.ShapeDtypeStruct(*shape) for shape in shapes),
        scratch_shapes=[pltpu.SemaphoreType.DMA((4,))],
        compiler_params=pltpu.CompilerParams(vmem_limit_bytes=8 * MIB),
    )(*(in_hbm(value) for value in (frames, w1, b1, w2)))


def first_weight():
    return jnp.where(lax.axis_index("tm") == 0, 1.0, 2.0)


def last_weight():
    return jnp.where(lax.axis_index("tm") == lax.axis_size("tm") - 1, 1.0, 2.0)


def early_kernel(
    frames_ref, near_ref, w1_ref, b1_ref, w2_ref, early_ref, middle_ref, hidden_ref, inst, total, xs, hs, sems
):
    half = LAG // 2
    first = half - D1 - D2

    def arriving(step):
        at = LAG + step * CHUNK
        return pltpu.make_async_copy(
            frames_ref.at[pl.ds(at, CHUNK)], xs.at[pl.ds(at - first, CHUNK)], sems.at[step]
        )

    steps = LAG // CHUNK
    for step in range(steps):
        arriving(step).start()
    xs[: LAG - first, :] = near_ref[first:, :]
    hs[: D2 + half, :] = hidden_rows(xs, 0, D2 + half, w1_ref, b1_ref)
    value = feature_rows(hs, 0, half, w2_ref)
    early_ref[...] = value
    inst[...] = first_weight() * feature_gram(value, value)
    total[...] = first_weight() * column_sum(value)
    for step in range(steps):
        arriving(step).wait()
        at = half + step * CHUNK
        hs[at + D2 : at + D2 + CHUNK, :] = hidden_rows(xs, at + D2, CHUNK, w1_ref, b1_ref)
        value = feature_rows(hs, at, CHUNK, w2_ref)
        middle_ref[step * CHUNK : (step + 1) * CHUNK, :] = value
        inst[...] += 2.0 * feature_gram(value, value)
        total[...] += 2.0 * column_sum(value)
    hidden_ref[...] = hs[hs.shape[0] - D2 :, :]


def head_kernel(near_ref, halo_ref, w1_ref, b1_ref, w2_ref, out_ref, xs, hs):
    halo_rows = halo_ref.shape[0]
    xs[:halo_rows, :] = halo_ref[...]
    xs[halo_rows:, :] = near_ref[: LAG // 2, :]
    before = hidden_rows(xs, 0, D2, w1_ref, b1_ref)
    hs[:D2, :] = jnp.where(lax.axis_index("tm") > 0, before, jnp.zeros_like(before))
    for at in range(D2, hs.shape[0], D2):
        hs[at : at + D2, :] = hidden_rows(xs, at, D2, w1_ref, b1_ref)
    out_ref[...] = feature_rows(hs, 0, out_ref.shape[0], w2_ref)


def feature_scratch(rows, channels, hid):
    return [
        pltpu.VMEM((rows + D1 + D2, channels), BF16),
        pltpu.VMEM((rows + D2, hid), BF16),
    ]


def early_rows(frames, near, w1, b1, w2):
    vmem = pl.BlockSpec(memory_space=pltpu.VMEM)
    hbm = pl.BlockSpec(memory_space=pltpu.HBM)
    half, hid, feat = LAG // 2, w1.shape[1], w2.shape[1]
    shapes = (((half, feat), BF16), ((LAG, feat), BF16), ((D2, hid), BF16), ((feat, feat), F32), ((8, feat), F32))
    return pl.pallas_call(
        early_kernel,
        in_specs=[hbm] + [vmem] * 4,
        out_specs=(vmem,) * 5,
        out_shape=tuple(jax.ShapeDtypeStruct(*shape) for shape in shapes),
        scratch_shapes=feature_scratch(half + LAG, near.shape[1], hid) + [pltpu.SemaphoreType.DMA((LAG // CHUNK,))],
        compiler_params=pltpu.CompilerParams(vmem_limit_bytes=16 * MIB),
    )(in_hbm(frames), near, w1, b1, w2)


def head_rows(near, halo, w1, b1, w2):
    vmem = pl.BlockSpec(memory_space=pltpu.VMEM)
    half = LAG // 2
    return pl.pallas_call(
        head_kernel,
        in_specs=[vmem] * 5,
        out_specs=vmem,
        out_shape=jax.ShapeDtypeStruct((half, w2.shape[1]), BF16),
        scratch_shapes=feature_scratch(half, near.shape[1], w1.shape[1]),
        compiler_params=pltpu.CompilerParams(vmem_limit_bytes=12 * MIB),
    )(near, halo, w1, b1, w2)


def column_sum(rows):
    return jnp.sum(rows.astype(F32).reshape(-1, 8, rows.shape[1]), 0)


def body_kernel(
    frames_ref, head_ref, early_ref, middle_ref, hidden_ref, inst_in, total_in, w1_ref, b1_ref, w2_ref,
    out_ref, inst, lag, total, xs, hs, sems
):
    rows, feat = out_ref.shape
    done = 2 * LAG
    steps = (rows - done) // CHUNK

    def arriving(step):
        more = D1 if step == 0 else 0
        at = step * CHUNK + D1 - more
        return pltpu.make_async_copy(
            frames_ref.at[pl.ds(done - D1 + at, CHUNK + more)], xs.at[pl.ds(at, CHUNK + more)], sems.at[step]
        )

    for step in range(steps):
        arriving(step).start()
    half = LAG // 2
    hs[:D2, :] = hidden_ref[...]
    out_ref[:half, :] = head_ref[...]
    out_ref[half:LAG, :] = early_ref[...]
    out_ref[LAG:done, :] = middle_ref[...]
    start = out_ref[:half, :]
    inst[...] = inst_in[...] + first_weight() * feature_gram(start, start)
    total[...] = total_in[...] + first_weight() * column_sum(start)
    lag[...] = feature_gram(out_ref[LAG : LAG + CHUNK, :], out_ref[:CHUNK, :])
    for at in range(CHUNK, LAG, CHUNK):
        lag[...] += feature_gram(out_ref[LAG + at : LAG + at + CHUNK, :], out_ref[at : at + CHUNK, :])

    def hidden(step):
        arriving(step).wait()
        at = step * CHUNK
        hs[D2 + at : D2 + at + CHUNK, :] = hidden_rows(xs, at, CHUNK, w1_ref, b1_ref)

    def finish(step):
        value = feature_rows(hs, step * CHUNK, CHUNK, w2_ref)
        at = done + step * CHUNK
        out_ref[at : at + CHUNK, :] = value
        weight = last_weight() if at >= rows - LAG else 2.0
        both = feature_gram(value, jnp.concatenate([value, out_ref[at - LAG : at - LAG + CHUNK, :]], 1))
        inst[...] += weight * both[:, :feat]
        lag[...] += both[:, feat:]
        total[...] += weight * column_sum(value)

    hidden(0)
    for step in range(steps - 1):
        hidden(step + 1)
        finish(step)
    finish(steps - 1)


def body(frames, head, early, middle, hidden, inst, total, w1, b1, w2):
    rows, channels = frames.shape
    hid, feat = w1.shape[1], w2.shape[1]
    vmem = pl.BlockSpec(memory_space=pltpu.VMEM)
    square = jax.ShapeDtypeStruct((feat, feat), F32)
    left = rows - 2 * LAG
    return pl.pallas_call(
        body_kernel,
        in_specs=[pl.BlockSpec(memory_space=pltpu.HBM)] + [vmem] * 9,
        out_specs=(vmem,) * 4,
        out_shape=(
            jax.ShapeDtypeStruct((rows, feat), BF16),
            square,
            square,
            jax.ShapeDtypeStruct((8, feat), F32),
        ),
        scratch_shapes=[
            pltpu.VMEM((left + D1, channels), BF16),
            pltpu.VMEM((left + D2, hid), BF16),
            pltpu.SemaphoreType.DMA((left // CHUNK,)),
        ],
        compiler_params=pltpu.CompilerParams(vmem_limit_bytes=24 * MIB),
    )(in_hbm(frames), head, early, middle, hidden, inst, total, w1, b1, w2)


def pack_kernel(feature_ref, ahead_head_ref, ahead_early_ref, inst, lag, total, kept_ref, sent_ref, packed):
    feat = inst.shape[0]
    half = LAG // 2
    edge = feature_ref.shape[0] - LAG
    cross = lag[...] + feature_gram(ahead_head_ref[...], feature_ref[edge : edge + half, :])
    cross += feature_gram(ahead_early_ref[...], feature_ref[edge + half :, :])
    both = cross + cross.T
    row = lax.broadcasted_iota(jnp.int32, (feat, feat), 0)
    column = lax.broadcasted_iota(jnp.int32, (feat, feat), 1)
    packed[...] = jnp.where(column >= row, inst[...], both)
    sums = jnp.sum(total[...], 0, keepdims=True)
    diagonal = jnp.sum(jnp.where(column == row, both, 0.0), 0, keepdims=True)
    core = lax.axis_index("core")
    for ref, owner in ((kept_ref, core), (sent_ref, 1 - core)):
        extra = jnp.where(owner == 0, sums, diagonal)
        for chunk, _, share_row, lanes in slots(ref.shape, feat):
            source = pl.ds(owner * (feat // 2) + share_row, 1)
            ref[chunk, 0:1, lanes] = packed[source, :]
        for chunk in range(ref.shape[0]):
            part = extra[:, chunk * 128 : chunk * 128 + 128] if chunk < feat // 128 else jnp.zeros((1, 128), F32)
            ref[chunk, 0:1, ref.shape[2] - 128 :] = part


def slots(shape, feat):
    rows = (shape[2] - 128) // feat
    for chunk in range(shape[0]):
        for row in range(rows):
            yield chunk, row, chunk * rows + row, slice(row * feat, (row + 1) * feat)


def pack(feature, ahead_head, ahead_early, inst, lag, total, chips):
    vmem = pl.BlockSpec(memory_space=pltpu.VMEM)
    feat = inst.shape[0]
    share = jax.ShapeDtypeStruct((chips, 1, feat // 2 // chips * feat + 128), F32)
    return pl.pallas_call(
        pack_kernel,
        in_specs=[vmem] * 6,
        out_specs=(vmem, vmem),
        out_shape=(share, share),
        scratch_shapes=[pltpu.VMEM((feat, feat), F32)],
        compiler_params=pltpu.CompilerParams(vmem_limit_bytes=8 * MIB),
    )(feature, ahead_head, ahead_early, inst, lag, total)


def three_parts(x):
    high = x.astype(BF16)
    rest = x - high.astype(F32)
    middle = rest.astype(BF16)
    low = (rest - middle.astype(F32)).astype(BF16)
    return high, middle, low


def inverse_factor(work):
    size = work.shape[0]
    lane = lax.broadcasted_iota(jnp.int32, (PANEL, size), 1)
    sub = lax.broadcasted_iota(jnp.int32, (PANEL, size), 0)
    sub_narrow = lax.broadcasted_iota(jnp.int32, (PANEL, 128), 0)

    def wide(x):
        return jnp.concatenate([x] * (size // 128), 1)

    def spread(x, j):
        return jnp.broadcast_to(x[j : j + 1, :], x.shape)

    for start in range(0, size, PANEL):
        stop = start + PANEL
        panel = work[start:stop, :]
        columns = [
            jnp.broadcast_to(panel[:, start + k : start + k + 1], (PANEL, 128)) for k in range(PANEL)
        ]
        panel = jnp.where(
            (lane >= start) & (lane < stop), jnp.where(lane - start == sub, 1.0, 0.0), panel
        )
        pivots = jnp.ones((PANEL, 128), F32)
        pivot = spread(columns[0], 0)
        for j in range(PANEL):
            inverse = pl.reciprocal(pivot, approx=True)
            pivots = jnp.where(sub_narrow == j, pivot, pivots)
            if j + 1 == PANEL:
                break
            factor = jnp.where(sub_narrow > j, columns[j], 0.0) * inverse
            beside = [spread(columns[k], j) for k in range(j + 1, PANEL)]
            pivot = spread(columns[j + 1], j + 1) - beside[0] * beside[0] * inverse
            for k in range(j + 1, PANEL):
                columns[k] = columns[k] - factor * beside[k - j - 1]
            panel = panel - wide(factor) * spread(panel, j)
        panel = panel * wide(lax.rsqrt(pivots))
        work[start:stop, :] = panel
        if stop < size:
            high, middle, low = three_parts(panel)
            left = jnp.concatenate([high, high, middle, high, low, middle], 0)
            right = jnp.concatenate([high, middle, high, low, high, middle], 0)
            first = stop // 128 * 128
            update = gram(left[:, first:], right)
            kept = lax.broadcasted_iota(jnp.int32, (size - stop, size), 1)
            kept = (kept < start) | (kept >= stop)
            work[stop:, :] = jnp.where(kept, work[stop:, :], 0.0) - update[stop - first :]
    row = lax.broadcasted_iota(jnp.int32, (size, size), 0)
    column = lax.broadcasted_iota(jnp.int32, (size, size), 1)
    return jnp.where(column <= row, work[...], 0.0)


def koopman_kernel(scale_ref, mine_ref, other_ref, split_ref, shift_ref, work, packed_ref):
    feat = packed_ref.shape[1]
    scale = scale_ref[0]
    core = lax.axis_index("core")
    extras = []
    for ref, owner in ((mine_ref, core), (other_ref, 1 - core)):
        for chunk, _, share_row, lanes in slots(ref.shape, feat):
            packed_ref[pl.ds(owner * (feat // 2) + share_row, 1), :] = ref[chunk, 0:1, lanes]
        parts = [ref[chunk, 0:1, ref.shape[2] - 128 :] for chunk in range(feat // 128)]
        extras.append(jnp.concatenate(parts, 1))
    packed = packed_ref[...]
    mean = jnp.where(core == 0, extras[0], extras[1]) * scale
    diagonal = jnp.where(core == 0, extras[1], extras[0])
    row = lax.broadcasted_iota(jnp.int32, (feat, feat), 0)
    column = lax.broadcasted_iota(jnp.int32, (feat, feat), 1)
    turned = packed.T
    centre = jnp.broadcast_to(mean, (feat, feat))
    centre = centre * centre.T
    inst = jnp.where(column >= row, packed, turned)
    lag = jnp.where(column < row, packed, turned)
    lag = jnp.where(column == row, jnp.broadcast_to(diagonal, (feat, feat)), lag)
    work[...] = inst * scale - centre + jnp.where(column == row, RIDGE, 0.0)
    lag = lag * scale - centre
    inverse = inverse_factor(work)
    half_step = jnp.dot(inverse, lag, precision=HIGHEST, preferred_element_type=F32)
    koopman = across(half_step, inverse, HIGHEST)
    moved = jnp.dot(koopman, inverse, precision=HIGHEST, preferred_element_type=F32)
    for index, matrix in enumerate((inverse, moved)):
        turned = matrix.T
        high = turned.astype(BF16)
        split_ref[index, :feat, :] = high
        split_ref[index, feat:, :] = (turned - high.astype(F32)).astype(BF16)
        rows = jnp.broadcast_to(mean, (8, feat))
        shift_ref[index] = jnp.dot(rows, turned, precision=HIGHEST, preferred_element_type=F32)


def koopman_parts(scale, mine, other, feat):
    vmem = pl.BlockSpec(memory_space=pltpu.VMEM)
    return pl.pallas_call(
        koopman_kernel,
        in_specs=[pl.BlockSpec(memory_space=pltpu.SMEM), vmem, vmem],
        out_specs=(vmem, vmem),
        out_shape=(
            jax.ShapeDtypeStruct((2, 2 * feat, feat), BF16),
            jax.ShapeDtypeStruct((2, 8, feat), F32),
        ),
        scratch_shapes=[pltpu.VMEM((feat, feat), F32), pltpu.VMEM((feat, feat), F32)],
        compiler_params=pltpu.CompilerParams(vmem_limit_bytes=12 * MIB),
    )(scale, mine, other)


def project_kernel(
    feature_ref, ahead_head_ref, ahead_early_ref, split_ref, shift_ref, moved_out, residual_out, moved, residual, sems
):
    rows = feature_ref.shape[0]
    half = LAG // 2
    at_end = lax.axis_index("tm") == lax.axis_size("tm") - 1

    def product(block, index):
        twice = jnp.concatenate([block, block], 1)
        return jnp.dot(twice, split_ref[index], preferred_element_type=F32) - shift_ref[index][0:1]

    copies = []
    for step in range(rows // CHUNK):
        here = slice(step * CHUNK, (step + 1) * CHUNK)
        start = step * CHUNK + LAG
        if start < rows:
            later = feature_ref[start : start + CHUNK, :]
        else:
            later = (ahead_head_ref if start == rows else ahead_early_ref)[...]
        now = product(feature_ref[here, :], 1)
        moved[here, :] = now
        gap = product(later, 0) - now
        residual[here, :] = gap if start < rows else jnp.where(at_end, 0.0, gap)
        for index, (source, target) in enumerate(((moved, moved_out), (residual, residual_out))):
            copy = pltpu.make_async_copy(source.at[here], target.at[here], sems.at[index, step])
            copy.start()
            copies.append(copy)
    for copy in copies:
        copy.wait()


def project(feature, ahead_head, ahead_early, split, shift):
    rows, feat = feature.shape
    vmem = pl.BlockSpec(memory_space=pltpu.VMEM)
    hbm = pl.BlockSpec(memory_space=pltpu.HBM)
    out = jax.ShapeDtypeStruct((rows, feat), F32)
    return pl.pallas_call(
        project_kernel,
        in_specs=[vmem] * 5,
        out_specs=(hbm, hbm),
        out_shape=(out, out),
        scratch_shapes=[
            pltpu.VMEM((rows, feat), F32),
            pltpu.VMEM((rows, feat), F32),
            pltpu.SemaphoreType.DMA((2, rows // CHUNK)),
        ],
        compiler_params=pltpu.CompilerParams(vmem_limit_bytes=24 * MIB),
    )(feature, ahead_head, ahead_early, split, shift)


def summed(kept, sent):
    swap = [(0, 1), (1, 0)]
    chips = ("x", "tm")
    parts = kept + lax.ppermute(sent, "core", swap)
    mine = jnp.sum(lax.all_to_all(parts, chips, 0, 0, tiled=True), 0, keepdims=True)
    mine = lax.all_to_all(jnp.broadcast_to(mine, parts.shape), chips, 0, 0, tiled=True)
    return mine, lax.ppermute(mine, "core", swap)


def on_device(frames, first_weight, first_bias, second_weight):
    frame_block = frames[0]
    row_count, channels = frame_block.shape
    hid, feat = second_weight.shape[1:]
    weights = (
        first_weight.reshape(2 * channels, hid),
        first_bias.reshape(1, hid),
        second_weight.reshape(2 * hid, feat),
    )
    halo = passed_along(frame_block[row_count - D1 - D2 :], "tm", 1)
    near, *weights = fetch(frame_block, *weights)
    early, middle, hidden, inst, total = early_rows(frame_block, near, *weights)
    ahead_early = passed_along(early, "tm", -1)
    head = head_rows(near, halo, *weights)
    ahead_head = passed_along(head, "tm", -1)
    feature, inst, lag, total = body(
        frame_block, head, early, middle, hidden, inst, total, *weights
    )
    chips = lax.axis_size("x") * lax.axis_size("tm")
    mine, other = summed(*pack(feature, ahead_head, ahead_early, inst, lag, total, chips))
    replicas = lax.axis_size("x") * lax.axis_size("core")
    pair_count = replicas * (row_count * lax.axis_size("tm") - LAG)
    scale = jnp.full((1,), 1.0 / (2.0 * pair_count), F32)
    split, shift = koopman_parts(scale, mine, other, feat)
    propagated, residual = project(feature, ahead_head, ahead_early, split, shift)
    return (propagated[None], residual[None])


def solution(mesh):
    replicas, blocks = mesh.devices.shape
    chips = Mesh(mesh.devices.reshape(replicas // 2, 2, blocks), ("x", "core", "tm"))
    split = P(("x", "core"), "tm", None)
    return jax.shard_map(
        on_device,
        mesh=chips,
        in_specs=(split, P(), P(), P()),
        out_specs=(split, split),
        check_vma=False,
    )
```

```python
import jax
import jax.numpy as jnp
from jax import lax
from jax.experimental import pallas as pl
from jax.experimental.pallas import tpu as pltpu
from jax.sharding import Mesh, PartitionSpec as P

D1 = 32
D2 = 256
LAG = 1024
RIDGE = 0.001
CHUNK = 512
PANEL = 16
MIB = 1024 * 1024

F32 = jnp.float32
BF16 = jnp.bfloat16


def passed_along(value, axis, steps):
    count = lax.axis_size(axis)
    first, last = (max(0, -steps), min(count, count - steps))
    return lax.ppermute(value, axis, [(source, source + steps) for source in range(first, last)])


def gram(a, b):
    return lax.dot_general(a, b, (((0,), (0,)), ((), ())), preferred_element_type=F32)


def in_hbm(value):
    return pltpu.with_memory_space_constraint(value, pltpu.HBM)


def silu(x):
    half = 0.5 * x
    return half + half * jnp.tanh(half)


def hidden_rows(xs, at, rows, w1_ref, b1_ref):
    both = jnp.concatenate([xs[pl.ds(at + D1, rows), :], xs[pl.ds(at, rows), :]], 1)
    hid = w1_ref.shape[1]
    parts = []
    for lanes in (slice(0, hid // 2), slice(hid // 2, hid)):
        z = jnp.dot(both, w1_ref[:, lanes], preferred_element_type=F32)
        parts.append(silu(z + b1_ref[:, lanes]).astype(BF16))
    return jnp.concatenate(parts, 1)


def feature_rows(hs, at, rows, w2_ref):
    both = jnp.concatenate([hs[pl.ds(at + D2, rows), :], hs[pl.ds(at, rows), :]], 1)
    return jnp.dot(both, w2_ref[...], preferred_element_type=F32).astype(BF16)


def fetch_kernel(frames_ref, w1_in, b1_in, w2_in, near_ref, w1_ref, b1_ref, w2_ref, sems):
    pairs = (
        (frames_ref.at[pl.ds(0, LAG)], near_ref),
        (w1_in, w1_ref),
        (b1_in, b1_ref),
        (w2_in, w2_ref),
    )
    copies = [pltpu.make_async_copy(*pair, sems.at[index]) for index, pair in enumerate(pairs)]
    for copy in copies:
        copy.start()
    for copy in copies:
        copy.wait()


def fetch(frames, w1, b1, w2):
    vmem = pl.BlockSpec(memory_space=pltpu.VMEM)
    hbm = pl.BlockSpec(memory_space=pltpu.HBM)
    channels = frames.shape[1]
    shapes = (((LAG, channels), BF16), (w1.shape, BF16), (b1.shape, F32), (w2.shape, BF16))
    return pl.pallas_call(
        fetch_kernel,
        in_specs=[hbm] * 4,
        out_specs=(vmem,) * 4,
        out_shape=tuple(jax.ShapeDtypeStruct(*shape) for shape in shapes),
        scratch_shapes=[pltpu.SemaphoreType.DMA((4,))],
        compiler_params=pltpu.CompilerParams(vmem_limit_bytes=8 * MIB),
    )(*(in_hbm(value) for value in (frames, w1, b1, w2)))


def early_kernel(frames_ref, near_ref, w1_ref, b1_ref, w2_ref, early_ref, middle_ref, hidden_ref, xs, hs, sems):
    half = LAG // 2
    first = half - D1 - D2

    def arriving(step):
        at = LAG + step * CHUNK
        return pltpu.make_async_copy(
            frames_ref.at[pl.ds(at, CHUNK)], xs.at[pl.ds(at - first, CHUNK)], sems.at[step]
        )

    steps = LAG // CHUNK
    for step in range(steps):
        arriving(step).start()
    xs[: LAG - first, :] = near_ref[first:, :]
    hs[: D2 + half, :] = hidden_rows(xs, 0, D2 + half, w1_ref, b1_ref)
    for step in range(steps):
        arriving(step).wait()
        at = half + step * CHUNK
        hs[at + D2 : at + D2 + CHUNK, :] = hidden_rows(xs, at + D2, CHUNK, w1_ref, b1_ref)
        if step == 0:
            early_ref[...] = feature_rows(hs, 0, half, w2_ref)
        else:
            middle_ref[(step - 1) * CHUNK : step * CHUNK, :] = feature_rows(hs, at - CHUNK, CHUNK, w2_ref)
    middle_ref[LAG - CHUNK :, :] = feature_rows(hs, half + LAG - CHUNK, CHUNK, w2_ref)
    hidden_ref[...] = hs[hs.shape[0] - D2 :, :]


def head_kernel(near_ref, halo_ref, w1_ref, b1_ref, w2_ref, out_ref, xs, hs):
    halo_rows = halo_ref.shape[0]
    xs[:halo_rows, :] = halo_ref[...]
    xs[halo_rows:, :] = near_ref[: LAG // 2, :]
    before = hidden_rows(xs, 0, D2, w1_ref, b1_ref)
    hs[:D2, :] = jnp.where(lax.axis_index("tm") > 0, before, jnp.zeros_like(before))
    for at in range(D2, hs.shape[0], D2):
        hs[at : at + D2, :] = hidden_rows(xs, at, D2, w1_ref, b1_ref)
    out_ref[...] = feature_rows(hs, 0, out_ref.shape[0], w2_ref)


def feature_scratch(rows, channels, hid):
    return [
        pltpu.VMEM((rows + D1 + D2, channels), BF16),
        pltpu.VMEM((rows + D2, hid), BF16),
    ]


def early_rows(frames, near, w1, b1, w2):
    vmem = pl.BlockSpec(memory_space=pltpu.VMEM)
    hbm = pl.BlockSpec(memory_space=pltpu.HBM)
    half, hid, feat = LAG // 2, w1.shape[1], w2.shape[1]
    shapes = (((half, feat), BF16), ((LAG, feat), BF16), ((D2, hid), BF16))
    return pl.pallas_call(
        early_kernel,
        in_specs=[hbm] + [vmem] * 4,
        out_specs=(vmem,) * 3,
        out_shape=tuple(jax.ShapeDtypeStruct(*shape) for shape in shapes),
        scratch_shapes=feature_scratch(half + LAG, near.shape[1], hid) + [pltpu.SemaphoreType.DMA((LAG // CHUNK,))],
        compiler_params=pltpu.CompilerParams(vmem_limit_bytes=16 * MIB),
    )(in_hbm(frames), near, w1, b1, w2)


def head_rows(near, halo, w1, b1, w2):
    vmem = pl.BlockSpec(memory_space=pltpu.VMEM)
    half = LAG // 2
    return pl.pallas_call(
        head_kernel,
        in_specs=[vmem] * 5,
        out_specs=vmem,
        out_shape=jax.ShapeDtypeStruct((half, w2.shape[1]), BF16),
        scratch_shapes=feature_scratch(half, near.shape[1], w1.shape[1]),
        compiler_params=pltpu.CompilerParams(vmem_limit_bytes=12 * MIB),
    )(near, halo, w1, b1, w2)


def body_kernel(
    frames_ref, head_ref, early_ref, middle_ref, hidden_ref, w1_ref, b1_ref, w2_ref, out_ref, xs, hs, sems
):
    rows = out_ref.shape[0]
    done = 2 * LAG
    steps = (rows - done) // CHUNK

    def arriving(step):
        more = D1 if step == 0 else 0
        at = step * CHUNK + D1 - more
        return pltpu.make_async_copy(
            frames_ref.at[pl.ds(done - D1 + at, CHUNK + more)], xs.at[pl.ds(at, CHUNK + more)], sems.at[step]
        )

    for step in range(steps):
        arriving(step).start()
    half = LAG // 2
    hs[:D2, :] = hidden_ref[...]
    out_ref[:half, :] = head_ref[...]
    out_ref[half:LAG, :] = early_ref[...]
    out_ref[LAG:done, :] = middle_ref[...]
    for step in range(steps + 1):
        at = step * CHUNK
        if step < steps:
            arriving(step).wait()
            hs[D2 + at : D2 + at + CHUNK, :] = hidden_rows(xs, at, CHUNK, w1_ref, b1_ref)
        if step:
            out_ref[done + at - CHUNK : done + at, :] = feature_rows(hs, at - CHUNK, CHUNK, w2_ref)


def body(frames, head, early, middle, hidden, w1, b1, w2):
    rows, channels = frames.shape
    hid, feat = w1.shape[1], w2.shape[1]
    vmem = pl.BlockSpec(memory_space=pltpu.VMEM)
    left = rows - 2 * LAG
    return pl.pallas_call(
        body_kernel,
        in_specs=[pl.BlockSpec(memory_space=pltpu.HBM)] + [vmem] * 7,
        out_specs=vmem,
        out_shape=jax.ShapeDtypeStruct((rows, feat), BF16),
        scratch_shapes=[
            pltpu.VMEM((left + D1, channels), BF16),
            pltpu.VMEM((left + D2, hid), BF16),
            pltpu.SemaphoreType.DMA((left // CHUNK,)),
        ],
        compiler_params=pltpu.CompilerParams(vmem_limit_bytes=16 * MIB),
    )(in_hbm(frames), head, early, middle, hidden, w1, b1, w2)


def column_sum(rows):
    parts = rows.astype(F32).reshape(4, -1, 8, rows.shape[1])
    return jnp.sum(jnp.sum(parts, 1), 0)


def moment_kernel(feature_ref, inst, lag, total):
    rows, feat = feature_ref.shape
    tm_index, tm_last = lax.axis_index("tm"), lax.axis_size("tm") - 1
    for at in range(0, rows, LAG):
        weight = 2.0
        if at == 0:
            weight = jnp.where(tm_index == 0, 1.0, 2.0)
        elif at == rows - LAG:
            weight = jnp.where(tm_index == tm_last, 1.0, 2.0)
        now = feature_ref[at : at + LAG, :]
        if at == 0:
            inst[...] = weight * gram(now, now)
            total[...] = weight * column_sum(now)
            continue
        both = gram(now, jnp.concatenate([now, feature_ref[at - LAG : at, :]], 1))
        inst[...] += weight * both[:, :feat]
        lag[...] = both[:, feat:] if at == LAG else lag[...] + both[:, feat:]
        total[...] += weight * column_sum(now)


def moments(feature):
    feat = feature.shape[1]
    vmem = pl.BlockSpec(memory_space=pltpu.VMEM)
    square = jax.ShapeDtypeStruct((feat, feat), F32)
    return pl.pallas_call(
        moment_kernel,
        in_specs=[vmem],
        out_specs=(vmem,) * 3,
        out_shape=(square, square, jax.ShapeDtypeStruct((8, feat), F32)),
        compiler_params=pltpu.CompilerParams(vmem_limit_bytes=12 * MIB),
    )(feature)


def pack_kernel(feature_ref, ahead_head_ref, ahead_early_ref, inst, lag, total, kept_ref, sent_ref, packed):
    feat = inst.shape[0]
    half = LAG // 2
    edge = feature_ref.shape[0] - LAG
    cross = lag[...] + gram(ahead_head_ref[...], feature_ref[edge : edge + half, :])
    cross += gram(ahead_early_ref[...], feature_ref[edge + half :, :])
    both = cross + cross.T
    row = lax.broadcasted_iota(jnp.int32, (feat, feat), 0)
    column = lax.broadcasted_iota(jnp.int32, (feat, feat), 1)
    packed[...] = jnp.where(column >= row, inst[...], both)
    sums = jnp.sum(total[...], 0, keepdims=True)
    diagonal = jnp.sum(jnp.where(column == row, both, 0.0), 0, keepdims=True)
    core = lax.axis_index("core")
    for ref, owner in ((kept_ref, core), (sent_ref, 1 - core)):
        extra = jnp.where(owner == 0, sums, diagonal)
        for chunk, _, share_row, lanes in slots(ref.shape, feat):
            source = pl.ds(owner * (feat // 2) + share_row, 1)
            ref[chunk, 0:1, lanes] = packed[source, :]
        for chunk in range(ref.shape[0]):
            part = extra[:, chunk * 128 : chunk * 128 + 128] if chunk < feat // 128 else jnp.zeros((1, 128), F32)
            ref[chunk, 0:1, ref.shape[2] - 128 :] = part


def slots(shape, feat):
    rows = (shape[2] - 128) // feat
    for chunk in range(shape[0]):
        for row in range(rows):
            yield chunk, row, chunk * rows + row, slice(row * feat, (row + 1) * feat)


def pack(feature, ahead_head, ahead_early, inst, lag, total, chips):
    vmem = pl.BlockSpec(memory_space=pltpu.VMEM)
    feat = inst.shape[0]
    share = jax.ShapeDtypeStruct((chips, 1, feat // 2 // chips * feat + 128), F32)
    return pl.pallas_call(
        pack_kernel,
        in_specs=[vmem] * 6,
        out_specs=(vmem, vmem),
        out_shape=(share, share),
        scratch_shapes=[pltpu.VMEM((feat, feat), F32)],
        compiler_params=pltpu.CompilerParams(vmem_limit_bytes=8 * MIB),
    )(feature, ahead_head, ahead_early, inst, lag, total)


def three_parts(x):
    high = x.astype(BF16)
    rest = x - high.astype(F32)
    middle = rest.astype(BF16)
    low = (rest - middle.astype(F32)).astype(BF16)
    return high, middle, low


def product(a, b):
    high, middle, low = three_parts(a)
    left = jnp.concatenate([high, high, middle, high, low, middle], 1)
    high, middle, low = three_parts(b)
    right = jnp.concatenate([high, middle, high, low, high, middle], 0)
    return jnp.dot(left, right, preferred_element_type=F32)


def inverse_factor(work):
    size = work.shape[0]
    lane = lax.broadcasted_iota(jnp.int32, (PANEL, size), 1)
    sub = lax.broadcasted_iota(jnp.int32, (PANEL, size), 0)
    sub_narrow = lax.broadcasted_iota(jnp.int32, (PANEL, 128), 0)

    def wide(x):
        return jnp.concatenate([x] * (size // 128), 1)

    def spread(x, j):
        return jnp.broadcast_to(x[j : j + 1, :], x.shape)

    for start in range(0, size, PANEL):
        stop = start + PANEL
        panel = work[start:stop, :]
        columns = [
            jnp.broadcast_to(panel[:, start + k : start + k + 1], (PANEL, 128)) for k in range(PANEL)
        ]
        panel = jnp.where(
            (lane >= start) & (lane < stop), jnp.where(lane - start == sub, 1.0, 0.0), panel
        )
        pivots = jnp.ones((PANEL, 128), F32)
        pivot = spread(columns[0], 0)
        for j in range(PANEL):
            inverse = pl.reciprocal(pivot, approx=True)
            pivots = jnp.where(sub_narrow == j, pivot, pivots)
            if j + 1 == PANEL:
                break
            factor = jnp.where(sub_narrow > j, columns[j], 0.0) * inverse
            beside = [spread(columns[k], j) for k in range(j + 1, PANEL)]
            pivot = spread(columns[j + 1], j + 1) - beside[0] * beside[0] * inverse
            for k in range(j + 1, PANEL):
                columns[k] = columns[k] - factor * beside[k - j - 1]
            panel = panel - wide(factor) * spread(panel, j)
        panel = panel * wide(lax.rsqrt(pivots))
        work[start:stop, :] = panel
        if stop < size:
            high, middle, low = three_parts(panel)
            left = jnp.concatenate([high, high, middle, high, low, middle], 0)
            right = jnp.concatenate([high, middle, high, low, high, middle], 0)
            first = stop // 128 * 128
            update = gram(left[:, first:], right)
            kept = lax.broadcasted_iota(jnp.int32, (size - stop, size), 1)
            kept = (kept < start) | (kept >= stop)
            work[stop:, :] = jnp.where(kept, work[stop:, :], 0.0) - update[stop - first :]
    row = lax.broadcasted_iota(jnp.int32, (size, size), 0)
    column = lax.broadcasted_iota(jnp.int32, (size, size), 1)
    return jnp.where(column <= row, work[...], 0.0)


def koopman_kernel(scale_ref, mine_ref, other_ref, split_ref, shift_ref, work, packed_ref):
    feat = packed_ref.shape[1]
    scale = scale_ref[0]
    core = lax.axis_index("core")
    extras = []
    for ref, owner in ((mine_ref, core), (other_ref, 1 - core)):
        for chunk, _, share_row, lanes in slots(ref.shape, feat):
            packed_ref[pl.ds(owner * (feat // 2) + share_row, 1), :] = ref[chunk, 0:1, lanes]
        parts = [ref[chunk, 0:1, ref.shape[2] - 128 :] for chunk in range(feat // 128)]
        extras.append(jnp.concatenate(parts, 1))
    packed = packed_ref[...]
    mean = jnp.where(core == 0, extras[0], extras[1]) * scale
    diagonal = jnp.where(core == 0, extras[1], extras[0])
    row = lax.broadcasted_iota(jnp.int32, (feat, feat), 0)
    column = lax.broadcasted_iota(jnp.int32, (feat, feat), 1)
    turned = packed.T
    mean_column = jnp.broadcast_to(mean, (feat, feat)).T
    centre = mean_column * mean
    inst = jnp.where(column >= row, packed, turned)
    lag = jnp.where(column < row, packed, turned)
    lag = jnp.where(column == row, jnp.broadcast_to(diagonal, (feat, feat)), lag)
    work[...] = inst * scale - centre + jnp.where(column == row, RIDGE, 0.0)
    lag = lag * scale - centre
    inverse = inverse_factor(work)
    inverse_turned = inverse.T
    koopman = product(product(inverse, lag), inverse_turned)
    moved_turned = product(inverse_turned, koopman)
    for index, matrix in enumerate((inverse_turned, moved_turned)):
        high = matrix.astype(BF16)
        split_ref[index, :feat, :] = high
        split_ref[index, feat:, :] = (matrix - high.astype(F32)).astype(BF16)
        shift = jnp.sum(mean_column * matrix, 0, keepdims=True)
        shift_ref[index] = jnp.broadcast_to(shift, (8, feat))


def koopman_parts(scale, mine, other, feat):
    vmem = pl.BlockSpec(memory_space=pltpu.VMEM)
    return pl.pallas_call(
        koopman_kernel,
        in_specs=[pl.BlockSpec(memory_space=pltpu.SMEM), vmem, vmem],
        out_specs=(vmem, vmem),
        out_shape=(
            jax.ShapeDtypeStruct((2, 2 * feat, feat), BF16),
            jax.ShapeDtypeStruct((2, 8, feat), F32),
        ),
        scratch_shapes=[pltpu.VMEM((feat, feat), F32), pltpu.VMEM((feat, feat), F32)],
        compiler_params=pltpu.CompilerParams(vmem_limit_bytes=12 * MIB),
    )(scale, mine, other)


def project_kernel(
    feature_ref, ahead_head_ref, ahead_early_ref, split_ref, shift_ref, moved_out, residual_out, moved, residual, sems
):
    rows = feature_ref.shape[0]
    half = LAG // 2
    at_end = lax.axis_index("tm") == lax.axis_size("tm") - 1

    def product(block, index):
        twice = jnp.concatenate([block, block], 1)
        return jnp.dot(twice, split_ref[index], preferred_element_type=F32) - shift_ref[index][0:1]

    copies = []
    for step in range(rows // CHUNK):
        here = slice(step * CHUNK, (step + 1) * CHUNK)
        start = step * CHUNK + LAG
        if start < rows:
            later = feature_ref[start : start + CHUNK, :]
        else:
            later = (ahead_head_ref if start == rows else ahead_early_ref)[...]
        now = product(feature_ref[here, :], 1)
        moved[here, :] = now
        gap = product(later, 0) - now
        residual[here, :] = gap if start < rows else jnp.where(at_end, 0.0, gap)
        for index, (source, target) in enumerate(((moved, moved_out), (residual, residual_out))):
            copy = pltpu.make_async_copy(source.at[here], target.at[here], sems.at[index, step])
            copy.start()
            copies.append(copy)
    for copy in copies:
        copy.wait()


def project(feature, ahead_head, ahead_early, split, shift):
    rows, feat = feature.shape
    vmem = pl.BlockSpec(memory_space=pltpu.VMEM)
    hbm = pl.BlockSpec(memory_space=pltpu.HBM)
    out = jax.ShapeDtypeStruct((rows, feat), F32)
    return pl.pallas_call(
        project_kernel,
        in_specs=[vmem] * 5,
        out_specs=(hbm, hbm),
        out_shape=(out, out),
        scratch_shapes=[
            pltpu.VMEM((rows, feat), F32),
            pltpu.VMEM((rows, feat), F32),
            pltpu.SemaphoreType.DMA((2, rows // CHUNK)),
        ],
        compiler_params=pltpu.CompilerParams(vmem_limit_bytes=24 * MIB),
    )(feature, ahead_head, ahead_early, split, shift)


def summed(kept, sent):
    swap = [(0, 1), (1, 0)]
    chips = ("x", "tm")
    parts = kept + lax.ppermute(sent, "core", swap)
    mine = jnp.sum(lax.all_to_all(parts, chips, 0, 0, tiled=True), 0, keepdims=True)
    mine = lax.all_to_all(jnp.broadcast_to(mine, parts.shape), chips, 0, 0, tiled=True)
    return mine, lax.ppermute(mine, "core", swap)


def on_device(frames, first_weight, first_bias, second_weight):
    frame_block = frames[0]
    row_count, channels = frame_block.shape
    hid, feat = second_weight.shape[1:]
    weights = (
        first_weight.reshape(2 * channels, hid),
        first_bias.reshape(1, hid),
        second_weight.reshape(2 * hid, feat),
    )
    halo = passed_along(frame_block[row_count - D1 - D2 :], "tm", 1)
    near, *weights = fetch(frame_block, *weights)
    early, middle, hidden = early_rows(frame_block, near, *weights)
    ahead_early = passed_along(early, "tm", -1)
    head = head_rows(near, halo, *weights)
    ahead_head = passed_along(head, "tm", -1)
    feature = body(frame_block, head, early, middle, hidden, *weights)
    inst, lag, total = moments(feature)
    chips = lax.axis_size("x") * lax.axis_size("tm")
    mine, other = summed(*pack(feature, ahead_head, ahead_early, inst, lag, total, chips))
    replicas = lax.axis_size("x") * lax.axis_size("core")
    pair_count = replicas * (row_count * lax.axis_size("tm") - LAG)
    scale = jnp.full((1,), 1.0 / (2.0 * pair_count), F32)
    split, shift = koopman_parts(scale, mine, other, feat)
    propagated, residual = project(feature, ahead_head, ahead_early, split, shift)
    return (propagated[None], residual[None])


def solution(mesh):
    replicas, blocks = mesh.devices.shape
    chips = Mesh(mesh.devices.reshape(replicas // 2, 2, blocks), ("x", "core", "tm"))
    split = P(("x", "core"), "tm", None)
    return jax.shard_map(
        on_device,
        mesh=chips,
        in_specs=(split, P(), P(), P()),
        out_specs=(split, split),
        check_vma=False,
    )
```

```python
import jax
import jax.numpy as jnp
from jax import lax
from jax.experimental import pallas as pl
from jax.experimental.pallas import tpu as pltpu
from jax.sharding import Mesh, PartitionSpec as P

D1 = 32
D2 = 256
LAG = 1024
RIDGE = 0.001
CHUNK = 512
EARLY = 1536
PANEL = 16
MIB = 1024 * 1024

F32 = jnp.float32
BF16 = jnp.bfloat16


def passed_along(value, axis, steps):
    count = lax.axis_size(axis)
    first, last = (max(0, -steps), min(count, count - steps))
    return lax.ppermute(value, axis, [(source, source + steps) for source in range(first, last)])


def gram(a, b):
    return lax.dot_general(a, b, (((0,), (0,)), ((), ())), preferred_element_type=F32)


def in_hbm(value):
    return pltpu.with_memory_space_constraint(value, pltpu.HBM)


def silu(x):
    half = 0.5 * x
    return half + half * jnp.tanh(half)


def hidden_rows(xs, at, rows, w1_ref, b1_ref):
    both = jnp.concatenate([xs[pl.ds(at + D1, rows), :], xs[pl.ds(at, rows), :]], 1)
    hid = w1_ref.shape[1]
    parts = []
    for lanes in (slice(0, hid // 2), slice(hid // 2, hid)):
        z = jnp.dot(both, w1_ref[:, lanes], preferred_element_type=F32)
        parts.append(silu(z + b1_ref[:, lanes]).astype(BF16))
    return jnp.concatenate(parts, 1)


def feature_rows(hs, at, rows, w2_ref):
    both = jnp.concatenate([hs[pl.ds(at + D2, rows), :], hs[pl.ds(at, rows), :]], 1)
    return jnp.dot(both, w2_ref[...], preferred_element_type=F32).astype(BF16)


def tail_kernel(frames_ref, w1_in, b1_in, w2_in, sent_ref, near_ref, w1_ref, b1_ref, w2_ref, xs, sems):
    rows = frames_ref.shape[0]
    pairs = (
        (frames_ref.at[pl.ds(rows - D1 - D2, D1 + D2)], xs),
        (w1_in, w1_ref),
        (b1_in, b1_ref),
        (w2_in, w2_ref),
        (frames_ref.at[pl.ds(0, LAG)], near_ref),
    )
    copies = [pltpu.make_async_copy(*pair, sems.at[index]) for index, pair in enumerate(pairs)]
    for copy in copies:
        copy.start()
    for copy in copies[:3]:
        copy.wait()
    hidden = hidden_rows(xs, 0, D2, w1_ref, b1_ref)
    copies[3].wait()
    hid, feat = hidden.shape[1], w2_ref.shape[1]
    sent_ref[:D2, :] = jnp.dot(hidden, w2_ref[hid:, :], preferred_element_type=F32).astype(BF16)
    for index in range(xs.shape[1] // feat):
        part = slice(D2 + index * D1, D2 + (index + 1) * D1)
        sent_ref[part, :] = xs[D2:, index * feat : (index + 1) * feat]
    copies[4].wait()


def tail_rows(frames, w1, b1, w2):
    vmem = pl.BlockSpec(memory_space=pltpu.VMEM)
    hbm = pl.BlockSpec(memory_space=pltpu.HBM)
    channels, feat = frames.shape[1], w2.shape[1]
    sent = (D2 + D1 * channels // feat, feat)
    shapes = ((sent, BF16), ((LAG, channels), BF16), (w1.shape, BF16), (b1.shape, F32), (w2.shape, BF16))
    return pl.pallas_call(
        tail_kernel,
        in_specs=[hbm] * 4,
        out_specs=(vmem,) * 5,
        out_shape=tuple(jax.ShapeDtypeStruct(*shape) for shape in shapes),
        scratch_shapes=[pltpu.VMEM((D1 + D2, channels), BF16), pltpu.SemaphoreType.DMA((5,))],
        compiler_params=pltpu.CompilerParams(vmem_limit_bytes=12 * MIB),
    )(*(in_hbm(value) for value in (frames, w1, b1, w2)))


def early_kernel(
    frames_ref, near_ref, w1_ref, b1_ref, w2_ref, early_ref, middle_ref, hidden_ref, far_ref, xs, hs, sems
):
    half = LAG // 2
    first = half - D1 - D2
    steps = (EARLY - LAG) // CHUNK

    def arriving(step):
        at = LAG + step * CHUNK
        return pltpu.make_async_copy(
            frames_ref.at[pl.ds(at, CHUNK)], xs.at[pl.ds(at - first, CHUNK)], sems.at[step]
        )

    for step in range(steps):
        arriving(step).start()
    later = pltpu.make_async_copy(
        frames_ref.at[pl.ds(EARLY - D1, far_ref.shape[0])], far_ref, sems.at[steps]
    )
    later.start()
    xs[: LAG - first, :] = near_ref[first:, :]
    hs[: D2 + half, :] = hidden_rows(xs, 0, D2 + half, w1_ref, b1_ref)
    for step in range(steps):
        arriving(step).wait()
        at = half + step * CHUNK
        hs[at + D2 : at + D2 + CHUNK, :] = hidden_rows(xs, at + D2, CHUNK, w1_ref, b1_ref)
        if step == 0:
            early_ref[...] = feature_rows(hs, 0, half, w2_ref)
        else:
            middle_ref[(step - 1) * CHUNK : step * CHUNK, :] = feature_rows(hs, at - CHUNK, CHUNK, w2_ref)
    middle_ref[(steps - 1) * CHUNK :, :] = feature_rows(hs, half + (steps - 1) * CHUNK, CHUNK, w2_ref)
    hidden_ref[...] = hs[hs.shape[0] - D2 :, :]
    later.wait()


def early_rows(frames, near, w1, b1, w2):
    vmem = pl.BlockSpec(memory_space=pltpu.VMEM)
    hbm = pl.BlockSpec(memory_space=pltpu.HBM)
    rows, channels = frames.shape
    half, hid, feat = LAG // 2, w1.shape[1], w2.shape[1]
    shapes = ((half, feat), (EARLY - LAG, feat), (D2, hid), (rows - EARLY + D1, channels))
    done = EARLY - half
    return pl.pallas_call(
        early_kernel,
        in_specs=[hbm] + [vmem] * 4,
        out_specs=(vmem,) * 4,
        out_shape=tuple(jax.ShapeDtypeStruct(shape, BF16) for shape in shapes),
        scratch_shapes=[
            pltpu.VMEM((done + D1 + D2, channels), BF16),
            pltpu.VMEM((done + D2, hid), BF16),
            pltpu.SemaphoreType.DMA(((EARLY - LAG) // CHUNK + 1,)),
        ],
        compiler_params=pltpu.CompilerParams(vmem_limit_bytes=16 * MIB),
    )(in_hbm(frames), near, w1, b1, w2)


def head_kernel(near_ref, halo_ref, w1_ref, b1_ref, w2_ref, out_ref, xs, hs):
    half = LAG // 2
    hid, feat = w1_ref.shape[1], w2_ref.shape[1]
    for index in range(xs.shape[1] // feat):
        part = slice(D2 + index * D1, D2 + (index + 1) * D1)
        xs[:D1, index * feat : (index + 1) * feat] = halo_ref[part, :]
    xs[D1:, :] = near_ref[:half, :]
    for at in range(0, half, D2):
        hs[at : at + D2, :] = hidden_rows(xs, at, D2, w1_ref, b1_ref)
    value = jnp.dot(hs[:D2, :], w2_ref[:hid, :], preferred_element_type=F32)
    out_ref[:D2, :] = (value + halo_ref[:D2, :].astype(F32)).astype(BF16)
    out_ref[D2:, :] = feature_rows(hs, 0, half - D2, w2_ref)


def head_rows(near, halo, w1, b1, w2):
    vmem = pl.BlockSpec(memory_space=pltpu.VMEM)
    half, channels, hid = LAG // 2, near.shape[1], w1.shape[1]
    return pl.pallas_call(
        head_kernel,
        in_specs=[vmem] * 5,
        out_specs=vmem,
        out_shape=jax.ShapeDtypeStruct((half, w2.shape[1]), BF16),
        scratch_shapes=[pltpu.VMEM((half + D1, channels), BF16), pltpu.VMEM((half, hid), BF16)],
        compiler_params=pltpu.CompilerParams(vmem_limit_bytes=8 * MIB),
    )(near, halo, w1, b1, w2)


def body_kernel(far_ref, head_ref, early_ref, middle_ref, hidden_ref, w1_ref, b1_ref, w2_ref, out_ref, hs):
    rows = out_ref.shape[0]
    steps = (rows - EARLY) // CHUNK
    half = LAG // 2
    hs[:D2, :] = hidden_ref[...]
    out_ref[:half, :] = head_ref[...]
    out_ref[half:LAG, :] = early_ref[...]
    out_ref[LAG:EARLY, :] = middle_ref[...]
    for step in range(steps + 1):
        at = step * CHUNK
        if step < steps:
            hs[D2 + at : D2 + at + CHUNK, :] = hidden_rows(far_ref, at, CHUNK, w1_ref, b1_ref)
        if step:
            out_ref[EARLY + at - CHUNK : EARLY + at, :] = feature_rows(hs, at - CHUNK, CHUNK, w2_ref)


def body(far, head, early, middle, hidden, w1, b1, w2):
    rows, hid, feat = far.shape[0] - D1 + EARLY, w1.shape[1], w2.shape[1]
    vmem = pl.BlockSpec(memory_space=pltpu.VMEM)
    return pl.pallas_call(
        body_kernel,
        in_specs=[vmem] * 8,
        out_specs=vmem,
        out_shape=jax.ShapeDtypeStruct((rows, feat), BF16),
        scratch_shapes=[pltpu.VMEM((rows - EARLY + D2, hid), BF16)],
        compiler_params=pltpu.CompilerParams(vmem_limit_bytes=16 * MIB),
    )(far, head, early, middle, hidden, w1, b1, w2)


def column_sum(rows):
    parts = rows.astype(F32).reshape(4, -1, 8, rows.shape[1])
    return jnp.sum(jnp.sum(parts, 1), 0)


def moment_kernel(feature_ref, inst, lag, total):
    rows, feat = feature_ref.shape
    tm_index, tm_last = lax.axis_index("tm"), lax.axis_size("tm") - 1
    for at in range(0, rows, LAG):
        weight = 2.0
        if at == 0:
            weight = jnp.where(tm_index == 0, 1.0, 2.0)
        elif at == rows - LAG:
            weight = jnp.where(tm_index == tm_last, 1.0, 2.0)
        now = feature_ref[at : at + LAG, :]
        if at == 0:
            inst[...] = weight * gram(now, now)
            total[...] = weight * column_sum(now)
            continue
        both = gram(now, jnp.concatenate([now, feature_ref[at - LAG : at, :]], 1))
        inst[...] += weight * both[:, :feat]
        lag[...] = both[:, feat:] if at == LAG else lag[...] + both[:, feat:]
        total[...] += weight * column_sum(now)


def moments(feature):
    feat = feature.shape[1]
    vmem = pl.BlockSpec(memory_space=pltpu.VMEM)
    square = jax.ShapeDtypeStruct((feat, feat), F32)
    return pl.pallas_call(
        moment_kernel,
        in_specs=[vmem],
        out_specs=(vmem,) * 3,
        out_shape=(square, square, jax.ShapeDtypeStruct((8, feat), F32)),
        compiler_params=pltpu.CompilerParams(vmem_limit_bytes=12 * MIB),
    )(feature)


def pack_kernel(feature_ref, ahead_head_ref, ahead_early_ref, inst, lag, total, kept_ref, sent_ref, packed):
    feat = inst.shape[0]
    half = LAG // 2
    edge = feature_ref.shape[0] - LAG
    cross = lag[...] + gram(ahead_head_ref[...], feature_ref[edge : edge + half, :])
    cross += gram(ahead_early_ref[...], feature_ref[edge + half :, :])
    both = cross + cross.T
    row = lax.broadcasted_iota(jnp.int32, (feat, feat), 0)
    column = lax.broadcasted_iota(jnp.int32, (feat, feat), 1)
    packed[...] = jnp.where(column >= row, inst[...], both)
    sums = jnp.sum(total[...], 0, keepdims=True)
    diagonal = jnp.sum(jnp.where(column == row, both, 0.0), 0, keepdims=True)
    core = lax.axis_index("core")
    for ref, owner in ((kept_ref, core), (sent_ref, 1 - core)):
        extra = jnp.where(owner == 0, sums, diagonal)
        for chunk, _, share_row, lanes in slots(ref.shape, feat):
            source = pl.ds(owner * (feat // 2) + share_row, 1)
            ref[chunk, 0:1, lanes] = packed[source, :]
        for chunk in range(ref.shape[0]):
            part = extra[:, chunk * 128 : chunk * 128 + 128] if chunk < feat // 128 else jnp.zeros((1, 128), F32)
            ref[chunk, 0:1, ref.shape[2] - 128 :] = part


def slots(shape, feat):
    rows = (shape[2] - 128) // feat
    for chunk in range(shape[0]):
        for row in range(rows):
            yield chunk, row, chunk * rows + row, slice(row * feat, (row + 1) * feat)


def pack(feature, ahead_head, ahead_early, inst, lag, total, chips):
    vmem = pl.BlockSpec(memory_space=pltpu.VMEM)
    feat = inst.shape[0]
    share = jax.ShapeDtypeStruct((chips, 1, feat // 2 // chips * feat + 128), F32)
    return pl.pallas_call(
        pack_kernel,
        in_specs=[vmem] * 6,
        out_specs=(vmem, vmem),
        out_shape=(share, share),
        scratch_shapes=[pltpu.VMEM((feat, feat), F32)],
        compiler_params=pltpu.CompilerParams(vmem_limit_bytes=8 * MIB),
    )(feature, ahead_head, ahead_early, inst, lag, total)


def three_parts(x):
    high = x.astype(BF16)
    rest = x - high.astype(F32)
    middle = rest.astype(BF16)
    low = (rest - middle.astype(F32)).astype(BF16)
    return high, middle, low


def product(a, b):
    high, middle, low = three_parts(a)
    left = jnp.concatenate([high, high, middle, high, low, middle], 1)
    high, middle, low = three_parts(b)
    right = jnp.concatenate([high, middle, high, low, high, middle], 0)
    return jnp.dot(left, right, preferred_element_type=F32)


def inverse_factor(work):
    size = work.shape[0]
    lane = lax.broadcasted_iota(jnp.int32, (PANEL, size), 1)
    sub = lax.broadcasted_iota(jnp.int32, (PANEL, size), 0)
    sub_narrow = lax.broadcasted_iota(jnp.int32, (PANEL, 128), 0)

    def wide(x):
        return jnp.concatenate([x] * (size // 128), 1)

    def spread(x, j):
        return jnp.broadcast_to(x[j : j + 1, :], x.shape)

    for start in range(0, size, PANEL):
        stop = start + PANEL
        panel = work[start:stop, :]
        columns = [
            jnp.broadcast_to(panel[:, start + k : start + k + 1], (PANEL, 128)) for k in range(PANEL)
        ]
        panel = jnp.where(
            (lane >= start) & (lane < stop), jnp.where(lane - start == sub, 1.0, 0.0), panel
        )
        pivots = jnp.ones((PANEL, 128), F32)
        pivot = spread(columns[0], 0)
        for j in range(PANEL):
            inverse = pl.reciprocal(pivot, approx=True)
            pivots = jnp.where(sub_narrow == j, pivot, pivots)
            if j + 1 == PANEL:
                break
            factor = jnp.where(sub_narrow > j, columns[j], 0.0) * inverse
            beside = [spread(columns[k], j) for k in range(j + 1, PANEL)]
            pivot = spread(columns[j + 1], j + 1) - beside[0] * beside[0] * inverse
            for k in range(j + 1, PANEL):
                columns[k] = columns[k] - factor * beside[k - j - 1]
            panel = panel - wide(factor) * spread(panel, j)
        panel = panel * wide(lax.rsqrt(pivots))
        work[start:stop, :] = panel
        if stop < size:
            high, middle, low = three_parts(panel)
            left = jnp.concatenate([high, high, middle, high, low, middle], 0)
            right = jnp.concatenate([high, middle, high, low, high, middle], 0)
            first = stop // 128 * 128
            update = gram(left[:, first:], right)
            kept = lax.broadcasted_iota(jnp.int32, (size - stop, size), 1)
            kept = (kept < start) | (kept >= stop)
            work[stop:, :] = jnp.where(kept, work[stop:, :], 0.0) - update[stop - first :]
    row = lax.broadcasted_iota(jnp.int32, (size, size), 0)
    column = lax.broadcasted_iota(jnp.int32, (size, size), 1)
    return jnp.where(column <= row, work[...], 0.0)


def koopman_kernel(scale_ref, mine_ref, other_ref, split_ref, shift_ref, work, packed_ref):
    feat = packed_ref.shape[1]
    scale = scale_ref[0]
    core = lax.axis_index("core")
    extras = []
    for ref, owner in ((mine_ref, core), (other_ref, 1 - core)):
        for chunk, _, share_row, lanes in slots(ref.shape, feat):
            packed_ref[pl.ds(owner * (feat // 2) + share_row, 1), :] = ref[chunk, 0:1, lanes]
        parts = [ref[chunk, 0:1, ref.shape[2] - 128 :] for chunk in range(feat // 128)]
        extras.append(jnp.concatenate(parts, 1))
    packed = packed_ref[...]
    mean = jnp.where(core == 0, extras[0], extras[1]) * scale
    diagonal = jnp.where(core == 0, extras[1], extras[0])
    row = lax.broadcasted_iota(jnp.int32, (feat, feat), 0)
    column = lax.broadcasted_iota(jnp.int32, (feat, feat), 1)
    turned = packed.T
    mean_column = jnp.broadcast_to(mean, (feat, feat)).T
    centre = mean_column * mean
    inst = jnp.where(column >= row, packed, turned)
    lag = jnp.where(column < row, packed, turned)
    lag = jnp.where(column == row, jnp.broadcast_to(diagonal, (feat, feat)), lag)
    work[...] = inst * scale - centre + jnp.where(column == row, RIDGE, 0.0)
    lag = lag * scale - centre
    inverse = inverse_factor(work)
    inverse_turned = inverse.T
    koopman = product(product(inverse, lag), inverse_turned)
    moved_turned = product(inverse_turned, koopman)
    for index, matrix in enumerate((inverse_turned, moved_turned)):
        high = matrix.astype(BF16)
        split_ref[index, :feat, :] = high
        split_ref[index, feat:, :] = (matrix - high.astype(F32)).astype(BF16)
        shift = jnp.sum(mean_column * matrix, 0, keepdims=True)
        shift_ref[index] = jnp.broadcast_to(shift, (8, feat))


def koopman_parts(scale, mine, other, feat):
    vmem = pl.BlockSpec(memory_space=pltpu.VMEM)
    return pl.pallas_call(
        koopman_kernel,
        in_specs=[pl.BlockSpec(memory_space=pltpu.SMEM), vmem, vmem],
        out_specs=(vmem, vmem),
        out_shape=(
            jax.ShapeDtypeStruct((2, 2 * feat, feat), BF16),
            jax.ShapeDtypeStruct((2, 8, feat), F32),
        ),
        scratch_shapes=[pltpu.VMEM((feat, feat), F32), pltpu.VMEM((feat, feat), F32)],
        compiler_params=pltpu.CompilerParams(vmem_limit_bytes=12 * MIB),
    )(scale, mine, other)


def project_kernel(
    feature_ref, ahead_head_ref, ahead_early_ref, split_ref, shift_ref, moved_out, residual_out, moved, residual, sems
):
    rows = feature_ref.shape[0]
    half = LAG // 2
    at_end = lax.axis_index("tm") == lax.axis_size("tm") - 1

    def product(block, index):
        twice = jnp.concatenate([block, block], 1)
        return jnp.dot(twice, split_ref[index], preferred_element_type=F32) - shift_ref[index][0:1]

    copies = []
    for step in range(rows // CHUNK):
        here = slice(step * CHUNK, (step + 1) * CHUNK)
        start = step * CHUNK + LAG
        if start < rows:
            later = feature_ref[start : start + CHUNK, :]
        else:
            later = (ahead_head_ref if start == rows else ahead_early_ref)[...]
        now = product(feature_ref[here, :], 1)
        moved[here, :] = now
        gap = product(later, 0) - now
        residual[here, :] = gap if start < rows else jnp.where(at_end, 0.0, gap)
        for index, (source, target) in enumerate(((moved, moved_out), (residual, residual_out))):
            copy = pltpu.make_async_copy(source.at[here], target.at[here], sems.at[index, step])
            copy.start()
            copies.append(copy)
    for copy in copies:
        copy.wait()


def project(feature, ahead_head, ahead_early, split, shift):
    rows, feat = feature.shape
    vmem = pl.BlockSpec(memory_space=pltpu.VMEM)
    hbm = pl.BlockSpec(memory_space=pltpu.HBM)
    out = jax.ShapeDtypeStruct((rows, feat), F32)
    return pl.pallas_call(
        project_kernel,
        in_specs=[vmem] * 5,
        out_specs=(hbm, hbm),
        out_shape=(out, out),
        scratch_shapes=[
            pltpu.VMEM((rows, feat), F32),
            pltpu.VMEM((rows, feat), F32),
            pltpu.SemaphoreType.DMA((2, rows // CHUNK)),
        ],
        compiler_params=pltpu.CompilerParams(vmem_limit_bytes=24 * MIB),
    )(feature, ahead_head, ahead_early, split, shift)


def summed(kept, sent):
    swap = [(0, 1), (1, 0)]
    chips = ("x", "tm")
    parts = kept + lax.ppermute(sent, "core", swap)
    mine = jnp.sum(lax.all_to_all(parts, chips, 0, 0, tiled=True), 0, keepdims=True)
    mine = lax.all_to_all(jnp.broadcast_to(mine, parts.shape), chips, 0, 0, tiled=True)
    return mine, lax.ppermute(mine, "core", swap)


def on_device(frames, first_weight, first_bias, second_weight):
    frame_block = frames[0]
    row_count, channels = frame_block.shape
    hid, feat = second_weight.shape[1:]
    weights = (
        first_weight.reshape(2 * channels, hid),
        first_bias.reshape(1, hid),
        second_weight.reshape(2 * hid, feat),
    )
    sent, near, *weights = tail_rows(frame_block, *weights)
    halo = passed_along(sent, "tm", 1)
    early, middle, hidden, far = early_rows(frame_block, near, *weights)
    ahead_early = passed_along(early, "tm", -1)
    head = head_rows(near, halo, *weights)
    ahead_head = passed_along(head, "tm", -1)
    feature = body(far, head, early, middle, hidden, *weights)
    inst, lag, total = moments(feature)
    chips = lax.axis_size("x") * lax.axis_size("tm")
    mine, other = summed(*pack(feature, ahead_head, ahead_early, inst, lag, total, chips))
    replicas = lax.axis_size("x") * lax.axis_size("core")
    pair_count = replicas * (row_count * lax.axis_size("tm") - LAG)
    scale = jnp.full((1,), 1.0 / (2.0 * pair_count), F32)
    split, shift = koopman_parts(scale, mine, other, feat)
    propagated, residual = project(feature, ahead_head, ahead_early, split, shift)
    return (propagated[None], residual[None])


def solution(mesh):
    replicas, blocks = mesh.devices.shape
    chips = Mesh(mesh.devices.reshape(replicas // 2, 2, blocks), ("x", "core", "tm"))
    split = P(("x", "core"), "tm", None)
    return jax.shard_map(
        on_device,
        mesh=chips,
        in_specs=(split, P(), P(), P()),
        out_specs=(split, split),
        check_vma=False,
    )
```

```python
import jax
import jax.numpy as jnp
from jax import lax
from jax.experimental import pallas as pl
from jax.experimental.pallas import tpu as pltpu
from jax.sharding import Mesh, PartitionSpec as P

D1 = 32
D2 = 256
LAG = 1024
RIDGE = 0.001
CHUNK = 512
EARLY = 1536
PANEL = 16
MIB = 1024 * 1024

F32 = jnp.float32
BF16 = jnp.bfloat16


def passed_along(value, axis, steps):
    count = lax.axis_size(axis)
    first, last = (max(0, -steps), min(count, count - steps))
    return lax.ppermute(value, axis, [(source, source + steps) for source in range(first, last)])


def gram(a, b):
    return lax.dot_general(a, b, (((0,), (0,)), ((), ())), preferred_element_type=F32)


def in_hbm(value):
    return pltpu.with_memory_space_constraint(value, pltpu.HBM)


def silu(x):
    half = 0.5 * x
    return half + half * jnp.tanh(half)


def hidden_rows(xs, at, rows, w1_ref, b1_ref):
    both = jnp.concatenate([xs[pl.ds(at + D1, rows), :], xs[pl.ds(at, rows), :]], 1)
    hid = w1_ref.shape[1]
    parts = []
    for lanes in (slice(0, hid // 2), slice(hid // 2, hid)):
        z = jnp.dot(both, w1_ref[:, lanes], preferred_element_type=F32)
        parts.append(silu(z + b1_ref[:, lanes]).astype(BF16))
    return jnp.concatenate(parts, 1)


def feature_rows(hs, at, rows, w2_ref):
    both = jnp.concatenate([hs[pl.ds(at + D2, rows), :], hs[pl.ds(at, rows), :]], 1)
    return jnp.dot(both, w2_ref[...], preferred_element_type=F32).astype(BF16)


def tail_kernel(frames_ref, w1_in, b1_in, w2_in, sent_ref, near_ref, w1_ref, b1_ref, w2_ref, xs, sems):
    rows = frames_ref.shape[0]
    pairs = (
        (frames_ref.at[pl.ds(rows - D1 - D2, D1 + D2)], xs),
        (w1_in, w1_ref),
        (b1_in, b1_ref),
        (w2_in, w2_ref),
        (frames_ref.at[pl.ds(0, LAG)], near_ref),
    )
    copies = [pltpu.make_async_copy(*pair, sems.at[index]) for index, pair in enumerate(pairs)]
    for copy in copies:
        copy.start()
    for copy in copies[:3]:
        copy.wait()
    hidden = hidden_rows(xs, 0, D2, w1_ref, b1_ref)
    copies[3].wait()
    hid, feat = hidden.shape[1], w2_ref.shape[1]
    sent_ref[:D2, :] = jnp.dot(hidden, w2_ref[hid:, :], preferred_element_type=F32).astype(BF16)
    for index in range(xs.shape[1] // feat):
        part = slice(D2 + index * D1, D2 + (index + 1) * D1)
        sent_ref[part, :] = xs[D2:, index * feat : (index + 1) * feat]
    copies[4].wait()


def tail_rows(frames, w1, b1, w2):
    vmem = pl.BlockSpec(memory_space=pltpu.VMEM)
    hbm = pl.BlockSpec(memory_space=pltpu.HBM)
    channels, feat = frames.shape[1], w2.shape[1]
    sent = (D2 + D1 * channels // feat, feat)
    shapes = ((sent, BF16), ((LAG, channels), BF16), (w1.shape, BF16), (b1.shape, F32), (w2.shape, BF16))
    return pl.pallas_call(
        tail_kernel,
        in_specs=[hbm] * 4,
        out_specs=(vmem,) * 5,
        out_shape=tuple(jax.ShapeDtypeStruct(*shape) for shape in shapes),
        scratch_shapes=[pltpu.VMEM((D1 + D2, channels), BF16), pltpu.SemaphoreType.DMA((5,))],
        compiler_params=pltpu.CompilerParams(vmem_limit_bytes=12 * MIB),
    )(*(in_hbm(value) for value in (frames, w1, b1, w2)))


def early_kernel(near_ref, w1_ref, b1_ref, w2_ref, out_ref, hidden_ref, hs):
    half = LAG // 2
    for at in range(0, hs.shape[0], D2):
        hs[at : at + D2, :] = hidden_rows(near_ref, half - D1 - D2 + at, D2, w1_ref, b1_ref)
    out_ref[...] = feature_rows(hs, 0, half, w2_ref)
    hidden_ref[...] = hs[half:, :]


def early_rows(near, w1, b1, w2):
    vmem = pl.BlockSpec(memory_space=pltpu.VMEM)
    half, hid = LAG // 2, w1.shape[1]
    return pl.pallas_call(
        early_kernel,
        in_specs=[vmem] * 4,
        out_specs=(vmem, vmem),
        out_shape=(
            jax.ShapeDtypeStruct((half, w2.shape[1]), BF16),
            jax.ShapeDtypeStruct((D2, hid), BF16),
        ),
        scratch_shapes=[pltpu.VMEM((half + D2, hid), BF16)],
        compiler_params=pltpu.CompilerParams(vmem_limit_bytes=8 * MIB),
    )(near, w1, b1, w2)


def middle_kernel(
    frames_ref, near_ref, before_ref, w1_ref, b1_ref, w2_ref, middle_ref, hidden_ref, far_ref, xs, hs, sems
):
    rows = EARLY - LAG
    now = pltpu.make_async_copy(frames_ref.at[pl.ds(LAG, rows)], xs.at[pl.ds(D1, rows)], sems.at[0])
    later = pltpu.make_async_copy(
        frames_ref.at[pl.ds(EARLY - D1, far_ref.shape[0])], far_ref, sems.at[1]
    )
    now.start()
    later.start()
    xs[:D1, :] = near_ref[LAG - D1 :, :]
    hs[:D2, :] = before_ref[...]
    now.wait()
    for at in range(0, rows, D2):
        hs[D2 + at : 2 * D2 + at, :] = hidden_rows(xs, at, D2, w1_ref, b1_ref)
    middle_ref[...] = feature_rows(hs, 0, rows, w2_ref)
    hidden_ref[...] = hs[rows:, :]
    later.wait()


def middle_rows(frames, near, before, w1, b1, w2):
    vmem = pl.BlockSpec(memory_space=pltpu.VMEM)
    hbm = pl.BlockSpec(memory_space=pltpu.HBM)
    rows, channels = frames.shape
    hid, feat = w1.shape[1], w2.shape[1]
    shapes = ((EARLY - LAG, feat), (D2, hid), (rows - EARLY + D1, channels))
    return pl.pallas_call(
        middle_kernel,
        in_specs=[hbm] + [vmem] * 5,
        out_specs=(vmem,) * 3,
        out_shape=tuple(jax.ShapeDtypeStruct(shape, BF16) for shape in shapes),
        scratch_shapes=[
            pltpu.VMEM((EARLY - LAG + D1, channels), BF16),
            pltpu.VMEM((EARLY - LAG + D2, hid), BF16),
            pltpu.SemaphoreType.DMA((2,)),
        ],
        compiler_params=pltpu.CompilerParams(vmem_limit_bytes=12 * MIB),
    )(in_hbm(frames), near, before, w1, b1, w2)


def head_kernel(near_ref, halo_ref, w1_ref, b1_ref, w2_ref, out_ref, xs, hs):
    half = LAG // 2
    hid, feat = w1_ref.shape[1], w2_ref.shape[1]
    for index in range(xs.shape[1] // feat):
        part = slice(D2 + index * D1, D2 + (index + 1) * D1)
        xs[:D1, index * feat : (index + 1) * feat] = halo_ref[part, :]
    xs[D1:, :] = near_ref[:half, :]
    for at in range(0, half, D2):
        hs[at : at + D2, :] = hidden_rows(xs, at, D2, w1_ref, b1_ref)
    value = jnp.dot(hs[:D2, :], w2_ref[:hid, :], preferred_element_type=F32)
    out_ref[:D2, :] = (value + halo_ref[:D2, :].astype(F32)).astype(BF16)
    out_ref[D2:, :] = feature_rows(hs, 0, half - D2, w2_ref)


def head_rows(near, halo, w1, b1, w2):
    vmem = pl.BlockSpec(memory_space=pltpu.VMEM)
    half, channels, hid = LAG // 2, near.shape[1], w1.shape[1]
    return pl.pallas_call(
        head_kernel,
        in_specs=[vmem] * 5,
        out_specs=vmem,
        out_shape=jax.ShapeDtypeStruct((half, w2.shape[1]), BF16),
        scratch_shapes=[pltpu.VMEM((half + D1, channels), BF16), pltpu.VMEM((half, hid), BF16)],
        compiler_params=pltpu.CompilerParams(vmem_limit_bytes=8 * MIB),
    )(near, halo, w1, b1, w2)


def body_kernel(far_ref, head_ref, early_ref, middle_ref, hidden_ref, w1_ref, b1_ref, w2_ref, out_ref, hs):
    rows = out_ref.shape[0]
    steps = (rows - EARLY) // CHUNK
    half = LAG // 2
    hs[:D2, :] = hidden_ref[...]
    out_ref[:half, :] = head_ref[...]
    out_ref[half:LAG, :] = early_ref[...]
    out_ref[LAG:EARLY, :] = middle_ref[...]
    for step in range(steps + 1):
        at = step * CHUNK
        if step < steps:
            hs[D2 + at : D2 + at + CHUNK, :] = hidden_rows(far_ref, at, CHUNK, w1_ref, b1_ref)
        if step:
            out_ref[EARLY + at - CHUNK : EARLY + at, :] = feature_rows(hs, at - CHUNK, CHUNK, w2_ref)


def body(far, head, early, middle, hidden, w1, b1, w2):
    rows, hid, feat = far.shape[0] - D1 + EARLY, w1.shape[1], w2.shape[1]
    vmem = pl.BlockSpec(memory_space=pltpu.VMEM)
    return pl.pallas_call(
        body_kernel,
        in_specs=[vmem] * 8,
        out_specs=vmem,
        out_shape=jax.ShapeDtypeStruct((rows, feat), BF16),
        scratch_shapes=[pltpu.VMEM((rows - EARLY + D2, hid), BF16)],
        compiler_params=pltpu.CompilerParams(vmem_limit_bytes=16 * MIB),
    )(far, head, early, middle, hidden, w1, b1, w2)


def column_sum(rows):
    parts = rows.astype(F32).reshape(4, -1, 8, rows.shape[1])
    return jnp.sum(jnp.sum(parts, 1), 0)


def moment_kernel(feature_ref, inst, lag, total):
    rows, feat = feature_ref.shape
    tm_index, tm_last = lax.axis_index("tm"), lax.axis_size("tm") - 1
    for at in range(0, rows, LAG):
        weight = 2.0
        if at == 0:
            weight = jnp.where(tm_index == 0, 1.0, 2.0)
        elif at == rows - LAG:
            weight = jnp.where(tm_index == tm_last, 1.0, 2.0)
        now = feature_ref[at : at + LAG, :]
        if at == 0:
            inst[...] = weight * gram(now, now)
            total[...] = weight * column_sum(now)
            continue
        both = gram(now, jnp.concatenate([now, feature_ref[at - LAG : at, :]], 1))
        inst[...] += weight * both[:, :feat]
        lag[...] = both[:, feat:] if at == LAG else lag[...] + both[:, feat:]
        total[...] += weight * column_sum(now)


def moments(feature):
    feat = feature.shape[1]
    vmem = pl.BlockSpec(memory_space=pltpu.VMEM)
    square = jax.ShapeDtypeStruct((feat, feat), F32)
    return pl.pallas_call(
        moment_kernel,
        in_specs=[vmem],
        out_specs=(vmem,) * 3,
        out_shape=(square, square, jax.ShapeDtypeStruct((8, feat), F32)),
        compiler_params=pltpu.CompilerParams(vmem_limit_bytes=12 * MIB),
    )(feature)


def pack_kernel(feature_ref, ahead_head_ref, ahead_early_ref, inst, lag, total, kept_ref, sent_ref, packed):
    feat = inst.shape[0]
    half = LAG // 2
    edge = feature_ref.shape[0] - LAG
    cross = lag[...] + gram(ahead_head_ref[...], feature_ref[edge : edge + half, :])
    cross += gram(ahead_early_ref[...], feature_ref[edge + half :, :])
    both = cross + cross.T
    row = lax.broadcasted_iota(jnp.int32, (feat, feat), 0)
    column = lax.broadcasted_iota(jnp.int32, (feat, feat), 1)
    packed[...] = jnp.where(column >= row, inst[...], both)
    sums = jnp.sum(total[...], 0, keepdims=True)
    diagonal = jnp.sum(jnp.where(column == row, both, 0.0), 0, keepdims=True)
    core = lax.axis_index("core")
    for ref, owner in ((kept_ref, core), (sent_ref, 1 - core)):
        extra = jnp.where(owner == 0, sums, diagonal)
        chunks = ref.shape[0]
        for index, lanes in slots(ref.shape, feat):
            at = pl.multiple_of(owner * (feat // 2) + index * chunks, 8)
            ref[:, 0, lanes] = packed[pl.ds(at, chunks), :]
        for chunk in range(chunks):
            part = extra[:, chunk * 128 : chunk * 128 + 128] if chunk < feat // 128 else jnp.zeros((1, 128), F32)
            ref[chunk, 0:1, ref.shape[2] - 128 :] = part


def slots(shape, feat):
    for index in range((shape[2] - 128) // feat):
        yield index, slice(index * feat, (index + 1) * feat)


def pack(feature, ahead_head, ahead_early, inst, lag, total, chips):
    vmem = pl.BlockSpec(memory_space=pltpu.VMEM)
    feat = inst.shape[0]
    share = jax.ShapeDtypeStruct((chips, 1, feat // 2 // chips * feat + 128), F32)
    return pl.pallas_call(
        pack_kernel,
        in_specs=[vmem] * 6,
        out_specs=(vmem, vmem),
        out_shape=(share, share),
        scratch_shapes=[pltpu.VMEM((feat, feat), F32)],
        compiler_params=pltpu.CompilerParams(vmem_limit_bytes=8 * MIB),
    )(feature, ahead_head, ahead_early, inst, lag, total)


def three_parts(x):
    high = x.astype(BF16)
    rest = x - high.astype(F32)
    middle = rest.astype(BF16)
    low = (rest - middle.astype(F32)).astype(BF16)
    return high, middle, low


def product(a, b):
    high, middle, low = three_parts(a)
    left = jnp.concatenate([high, high, middle, high, low, middle], 1)
    high, middle, low = three_parts(b)
    right = jnp.concatenate([high, middle, high, low, high, middle], 0)
    return jnp.dot(left, right, preferred_element_type=F32)


def inverse_factor(work):
    size = work.shape[0]
    parts = range(PANEL // 8)
    lane = lax.broadcasted_iota(jnp.int32, (PANEL, size), 1)
    sub = lax.broadcasted_iota(jnp.int32, (PANEL, size), 0)
    sub_narrow = lax.broadcasted_iota(jnp.int32, (8, 128), 0)

    def wide(x):
        return jnp.concatenate([x] * (size // 128), 1)

    def spread(x, j):
        return jnp.broadcast_to(x[j : j + 1, :], x.shape)

    for start in range(0, size, PANEL):
        stop = start + PANEL
        panel = work[start:stop, :]
        columns = [
            [
                jnp.broadcast_to(panel[8 * h : 8 * h + 8, start + k : start + k + 1], (8, 128))
                for h in parts
            ]
            for k in range(PANEL)
        ]
        panel = jnp.where(
            (lane >= start) & (lane < stop), jnp.where(lane - start == sub, 1.0, 0.0), panel
        )
        rows = [panel[8 * h : 8 * h + 8, :] for h in parts]
        pivots = [jnp.ones((8, 128), F32) for _ in parts]
        pivot_row = {k: spread(columns[k][0], 0) for k in range(PANEL)}
        panel_row = spread(rows[0], 0)
        for j in range(PANEL):
            inverse = pl.reciprocal(pivot_row[j], approx=True)
            here, at = divmod(j, 8)
            pivots[here] = jnp.where(sub_narrow == at, pivot_row[j], pivots[here])
            if j + 1 == PANEL:
                break
            there, after = divmod(j + 1, 8)
            share = pivot_row[j + 1] * inverse
            next_row = {
                k: spread(columns[k][there], after) - share * pivot_row[k] for k in range(j + 1, PANEL)
            }
            next_panel_row = spread(rows[there], after) - wide(share) * panel_row
            for h in parts:
                if 8 * h + 7 <= j:
                    continue
                factor = columns[j][h] * inverse
                if h == here:
                    factor = jnp.where(sub_narrow > at, factor, 0.0)
                for k in range(j + 1, PANEL):
                    columns[k][h] = columns[k][h] - factor * pivot_row[k]
                rows[h] = rows[h] - wide(factor) * panel_row
            pivot_row, panel_row = next_row, next_panel_row
        panel = jnp.concatenate([rows[h] * wide(lax.rsqrt(pivots[h])) for h in parts], 0)
        work[start:stop, :] = panel
        if stop < size:
            high, middle, low = three_parts(panel)
            left = jnp.concatenate([high, high, middle, high, low, middle], 0)
            right = jnp.concatenate([high, middle, high, low, high, middle], 0)
            first = stop // 128 * 128
            update = gram(left[:, first:], right)
            kept = lax.broadcasted_iota(jnp.int32, (size - stop, size), 1)
            kept = (kept < start) | (kept >= stop)
            work[stop:, :] = jnp.where(kept, work[stop:, :], 0.0) - update[stop - first :]
    row = lax.broadcasted_iota(jnp.int32, (size, size), 0)
    column = lax.broadcasted_iota(jnp.int32, (size, size), 1)
    return jnp.where(column <= row, work[...], 0.0)


def koopman_kernel(scale_ref, mine_ref, other_ref, split_ref, shift_ref, work, packed_ref):
    feat = packed_ref.shape[1]
    scale = scale_ref[0]
    core = lax.axis_index("core")
    extras = []
    for ref, owner in ((mine_ref, core), (other_ref, 1 - core)):
        chunks = ref.shape[0]
        for index, lanes in slots(ref.shape, feat):
            at = pl.multiple_of(owner * (feat // 2) + index * chunks, 8)
            packed_ref[pl.ds(at, chunks), :] = ref[:, 0, lanes]
        parts = [ref[chunk, 0:1, ref.shape[2] - 128 :] for chunk in range(feat // 128)]
        extras.append(jnp.concatenate(parts, 1))
    packed = packed_ref[...]
    mean = jnp.where(core == 0, extras[0], extras[1]) * scale
    diagonal = jnp.where(core == 0, extras[1], extras[0])
    row = lax.broadcasted_iota(jnp.int32, (feat, feat), 0)
    column = lax.broadcasted_iota(jnp.int32, (feat, feat), 1)
    turned = packed.T
    mean_column = jnp.broadcast_to(mean, (feat, feat)).T
    centre = mean_column * mean
    inst = jnp.where(column >= row, packed, turned)
    lag = jnp.where(column < row, packed, turned)
    lag = jnp.where(column == row, jnp.broadcast_to(diagonal, (feat, feat)), lag)
    work[...] = inst * scale - centre + jnp.where(column == row, RIDGE, 0.0)
    lag = lag * scale - centre
    inverse = inverse_factor(work)
    inverse_turned = inverse.T
    koopman = product(product(inverse, lag), inverse_turned)
    moved_turned = product(inverse_turned, koopman)
    for index, matrix in enumerate((inverse_turned, moved_turned)):
        high = matrix.astype(BF16)
        split_ref[index, :feat, :] = high
        split_ref[index, feat:, :] = (matrix - high.astype(F32)).astype(BF16)
        shift = jnp.sum(mean_column * matrix, 0, keepdims=True)
        shift_ref[index] = jnp.broadcast_to(shift, (8, feat))


def koopman_parts(scale, mine, other, feat):
    vmem = pl.BlockSpec(memory_space=pltpu.VMEM)
    return pl.pallas_call(
        koopman_kernel,
        in_specs=[pl.BlockSpec(memory_space=pltpu.SMEM), vmem, vmem],
        out_specs=(vmem, vmem),
        out_shape=(
            jax.ShapeDtypeStruct((2, 2 * feat, feat), BF16),
            jax.ShapeDtypeStruct((2, 8, feat), F32),
        ),
        scratch_shapes=[pltpu.VMEM((feat, feat), F32), pltpu.VMEM((feat, feat), F32)],
        compiler_params=pltpu.CompilerParams(vmem_limit_bytes=12 * MIB),
    )(scale, mine, other)


def project_kernel(
    feature_ref, ahead_head_ref, ahead_early_ref, split_ref, shift_ref, moved_out, residual_out, moved, residual, sems
):
    rows = feature_ref.shape[0]
    half = LAG // 2
    at_end = lax.axis_index("tm") == lax.axis_size("tm") - 1

    def product(block, index):
        twice = jnp.concatenate([block, block], 1)
        return jnp.dot(twice, split_ref[index], preferred_element_type=F32) - shift_ref[index][0:1]

    copies = []
    for step in range(rows // CHUNK):
        here = slice(step * CHUNK, (step + 1) * CHUNK)
        start = step * CHUNK + LAG
        if start < rows:
            later = feature_ref[start : start + CHUNK, :]
        else:
            later = (ahead_head_ref if start == rows else ahead_early_ref)[...]
        now = product(feature_ref[here, :], 1)
        moved[here, :] = now
        gap = product(later, 0) - now
        residual[here, :] = gap if start < rows else jnp.where(at_end, 0.0, gap)
        for index, (source, target) in enumerate(((moved, moved_out), (residual, residual_out))):
            copy = pltpu.make_async_copy(source.at[here], target.at[here], sems.at[index, step])
            copy.start()
            copies.append(copy)
    for copy in copies:
        copy.wait()


def project(feature, ahead_head, ahead_early, split, shift):
    rows, feat = feature.shape
    vmem = pl.BlockSpec(memory_space=pltpu.VMEM)
    hbm = pl.BlockSpec(memory_space=pltpu.HBM)
    out = jax.ShapeDtypeStruct((rows, feat), F32)
    return pl.pallas_call(
        project_kernel,
        in_specs=[vmem] * 5,
        out_specs=(hbm, hbm),
        out_shape=(out, out),
        scratch_shapes=[
            pltpu.VMEM((rows, feat), F32),
            pltpu.VMEM((rows, feat), F32),
            pltpu.SemaphoreType.DMA((2, rows // CHUNK)),
        ],
        compiler_params=pltpu.CompilerParams(vmem_limit_bytes=24 * MIB),
    )(feature, ahead_head, ahead_early, split, shift)


def summed(kept, sent):
    swap = [(0, 1), (1, 0)]
    chips = ("x", "tm")
    parts = kept + lax.ppermute(sent, "core", swap)
    mine = jnp.sum(lax.all_to_all(parts, chips, 0, 0, tiled=True), 0, keepdims=True)
    mine = lax.all_to_all(jnp.broadcast_to(mine, parts.shape), chips, 0, 0, tiled=True)
    return mine, lax.ppermute(mine, "core", swap)


def on_device(frames, first_weight, first_bias, second_weight):
    frame_block = frames[0]
    row_count, channels = frame_block.shape
    hid, feat = second_weight.shape[1:]
    weights = (
        first_weight.reshape(2 * channels, hid),
        first_bias.reshape(1, hid),
        second_weight.reshape(2 * hid, feat),
    )
    sent, near, *weights = tail_rows(frame_block, *weights)
    halo = passed_along(sent, "tm", 1)
    early, before = early_rows(near, *weights)
    ahead_early = passed_along(early, "tm", -1)
    middle, hidden, far = middle_rows(frame_block, near, before, *weights)
    head = head_rows(near, halo, *weights)
    ahead_head = passed_along(head, "tm", -1)
    feature = body(far, head, early, middle, hidden, *weights)
    inst, lag, total = moments(feature)
    chips = lax.axis_size("x") * lax.axis_size("tm")
    mine, other = summed(*pack(feature, ahead_head, ahead_early, inst, lag, total, chips))
    replicas = lax.axis_size("x") * lax.axis_size("core")
    pair_count = replicas * (row_count * lax.axis_size("tm") - LAG)
    scale = jnp.full((1,), 1.0 / (2.0 * pair_count), F32)
    split, shift = koopman_parts(scale, mine, other, feat)
    propagated, residual = project(feature, ahead_head, ahead_early, split, shift)
    return (propagated[None], residual[None])


def solution(mesh):
    replicas, blocks = mesh.devices.shape
    chips = Mesh(mesh.devices.reshape(replicas // 2, 2, blocks), ("x", "core", "tm"))
    split = P(("x", "core"), "tm", None)
    return jax.shard_map(
        on_device,
        mesh=chips,
        in_specs=(split, P(), P(), P()),
        out_specs=(split, split),
        check_vma=False,
    )
```

```python
import jax
import jax.numpy as jnp
from jax import lax
from jax.experimental import pallas as pl
from jax.experimental.pallas import tpu as pltpu
from jax.sharding import Mesh, PartitionSpec as P

D1 = 32
D2 = 256
LAG = 1024
RIDGE = 0.001
CHUNK = 512
EARLY = 1536
PANEL = 16
SUPER = 32
MIB = 1024 * 1024

F32 = jnp.float32
BF16 = jnp.bfloat16


def passed_along(value, axis, steps):
    count = lax.axis_size(axis)
    first, last = (max(0, -steps), min(count, count - steps))
    return lax.ppermute(value, axis, [(source, source + steps) for source in range(first, last)])


def gram(a, b):
    return lax.dot_general(a, b, (((0,), (0,)), ((), ())), preferred_element_type=F32)


def in_hbm(value):
    return pltpu.with_memory_space_constraint(value, pltpu.HBM)


def silu(x):
    half = 0.5 * x
    return half + half * jnp.tanh(half)


def hidden_rows(xs, at, rows, w1_ref, b1_ref):
    both = jnp.concatenate([xs[pl.ds(at + D1, rows), :], xs[pl.ds(at, rows), :]], 1)
    hid = w1_ref.shape[1]
    parts = []
    for lanes in (slice(0, hid // 2), slice(hid // 2, hid)):
        z = jnp.dot(both, w1_ref[:, lanes], preferred_element_type=F32)
        parts.append(silu(z + b1_ref[:, lanes]).astype(BF16))
    return jnp.concatenate(parts, 1)


def feature_rows(hs, at, rows, w2_ref):
    both = jnp.concatenate([hs[pl.ds(at + D2, rows), :], hs[pl.ds(at, rows), :]], 1)
    return jnp.dot(both, w2_ref[...], preferred_element_type=F32).astype(BF16)


def tail_kernel(frames_ref, w1_in, b1_in, w2_in, sent_ref, near_ref, w1_ref, b1_ref, w2_ref, xs, sems):
    rows = frames_ref.shape[0]
    pairs = (
        (frames_ref.at[pl.ds(rows - D1 - D2, D1 + D2)], xs),
        (w1_in, w1_ref),
        (b1_in, b1_ref),
        (w2_in, w2_ref),
        (frames_ref.at[pl.ds(0, LAG)], near_ref),
    )
    copies = [pltpu.make_async_copy(*pair, sems.at[index]) for index, pair in enumerate(pairs)]
    for copy in copies:
        copy.start()
    for copy in copies[:3]:
        copy.wait()
    hidden = hidden_rows(xs, 0, D2, w1_ref, b1_ref)
    copies[3].wait()
    hid, feat = hidden.shape[1], w2_ref.shape[1]
    sent_ref[:D2, :] = jnp.dot(hidden, w2_ref[hid:, :], preferred_element_type=F32).astype(BF16)
    for index in range(xs.shape[1] // feat):
        part = slice(D2 + index * D1, D2 + (index + 1) * D1)
        sent_ref[part, :] = xs[D2:, index * feat : (index + 1) * feat]
    copies[4].wait()


def tail_rows(frames, w1, b1, w2):
    vmem = pl.BlockSpec(memory_space=pltpu.VMEM)
    hbm = pl.BlockSpec(memory_space=pltpu.HBM)
    channels, feat = frames.shape[1], w2.shape[1]
    sent = (D2 + D1 * channels // feat, feat)
    shapes = ((sent, BF16), ((LAG, channels), BF16), (w1.shape, BF16), (b1.shape, F32), (w2.shape, BF16))
    return pl.pallas_call(
        tail_kernel,
        in_specs=[hbm] * 4,
        out_specs=(vmem,) * 5,
        out_shape=tuple(jax.ShapeDtypeStruct(*shape) for shape in shapes),
        scratch_shapes=[pltpu.VMEM((D1 + D2, channels), BF16), pltpu.SemaphoreType.DMA((5,))],
        compiler_params=pltpu.CompilerParams(vmem_limit_bytes=12 * MIB),
    )(*(in_hbm(value) for value in (frames, w1, b1, w2)))


def early_kernel(near_ref, w1_ref, b1_ref, w2_ref, out_ref, hidden_ref, hs):
    half = LAG // 2
    for at in range(0, hs.shape[0], D2):
        hs[at : at + D2, :] = hidden_rows(near_ref, half - D1 - D2 + at, D2, w1_ref, b1_ref)
    out_ref[...] = feature_rows(hs, 0, half, w2_ref)
    hidden_ref[...] = hs[half:, :]


def early_rows(near, w1, b1, w2):
    vmem = pl.BlockSpec(memory_space=pltpu.VMEM)
    half, hid = LAG // 2, w1.shape[1]
    return pl.pallas_call(
        early_kernel,
        in_specs=[vmem] * 4,
        out_specs=(vmem, vmem),
        out_shape=(
            jax.ShapeDtypeStruct((half, w2.shape[1]), BF16),
            jax.ShapeDtypeStruct((D2, hid), BF16),
        ),
        scratch_shapes=[pltpu.VMEM((half + D2, hid), BF16)],
        compiler_params=pltpu.CompilerParams(vmem_limit_bytes=8 * MIB),
    )(near, w1, b1, w2)


def middle_kernel(
    frames_ref, near_ref, before_ref, w1_ref, b1_ref, w2_ref, middle_ref, hidden_ref, far_ref, xs, hs, sems
):
    rows = EARLY - LAG
    now = pltpu.make_async_copy(frames_ref.at[pl.ds(LAG, rows)], xs.at[pl.ds(D1, rows)], sems.at[0])
    later = pltpu.make_async_copy(
        frames_ref.at[pl.ds(EARLY - D1, far_ref.shape[0])], far_ref, sems.at[1]
    )
    now.start()
    later.start()
    xs[:D1, :] = near_ref[LAG - D1 :, :]
    hs[:D2, :] = before_ref[...]
    now.wait()
    for at in range(0, rows, D2):
        hs[D2 + at : 2 * D2 + at, :] = hidden_rows(xs, at, D2, w1_ref, b1_ref)
    middle_ref[...] = feature_rows(hs, 0, rows, w2_ref)
    hidden_ref[...] = hs[rows:, :]
    later.wait()


def middle_rows(frames, near, before, w1, b1, w2):
    vmem = pl.BlockSpec(memory_space=pltpu.VMEM)
    hbm = pl.BlockSpec(memory_space=pltpu.HBM)
    rows, channels = frames.shape
    hid, feat = w1.shape[1], w2.shape[1]
    shapes = ((EARLY - LAG, feat), (D2, hid), (rows - EARLY + D1, channels))
    return pl.pallas_call(
        middle_kernel,
        in_specs=[hbm] + [vmem] * 5,
        out_specs=(vmem,) * 3,
        out_shape=tuple(jax.ShapeDtypeStruct(shape, BF16) for shape in shapes),
        scratch_shapes=[
            pltpu.VMEM((EARLY - LAG + D1, channels), BF16),
            pltpu.VMEM((EARLY - LAG + D2, hid), BF16),
            pltpu.SemaphoreType.DMA((2,)),
        ],
        compiler_params=pltpu.CompilerParams(vmem_limit_bytes=12 * MIB),
    )(in_hbm(frames), near, before, w1, b1, w2)


def head_kernel(near_ref, halo_ref, w1_ref, b1_ref, w2_ref, out_ref, xs, hs):
    half = LAG // 2
    hid, feat = w1_ref.shape[1], w2_ref.shape[1]
    for index in range(xs.shape[1] // feat):
        part = slice(D2 + index * D1, D2 + (index + 1) * D1)
        xs[:D1, index * feat : (index + 1) * feat] = halo_ref[part, :]
    xs[D1:, :] = near_ref[:half, :]
    for at in range(0, half, D2):
        hs[at : at + D2, :] = hidden_rows(xs, at, D2, w1_ref, b1_ref)
    value = jnp.dot(hs[:D2, :], w2_ref[:hid, :], preferred_element_type=F32)
    out_ref[:D2, :] = (value + halo_ref[:D2, :].astype(F32)).astype(BF16)
    out_ref[D2:, :] = feature_rows(hs, 0, half - D2, w2_ref)


def head_rows(near, halo, w1, b1, w2):
    vmem = pl.BlockSpec(memory_space=pltpu.VMEM)
    half, channels, hid = LAG // 2, near.shape[1], w1.shape[1]
    return pl.pallas_call(
        head_kernel,
        in_specs=[vmem] * 5,
        out_specs=vmem,
        out_shape=jax.ShapeDtypeStruct((half, w2.shape[1]), BF16),
        scratch_shapes=[pltpu.VMEM((half + D1, channels), BF16), pltpu.VMEM((half, hid), BF16)],
        compiler_params=pltpu.CompilerParams(vmem_limit_bytes=8 * MIB),
    )(near, halo, w1, b1, w2)


def body_kernel(far_ref, head_ref, early_ref, middle_ref, hidden_ref, w1_ref, b1_ref, w2_ref, out_ref, hs):
    rows = out_ref.shape[0]
    steps = (rows - EARLY) // CHUNK
    half = LAG // 2
    hs[:D2, :] = hidden_ref[...]
    out_ref[:half, :] = head_ref[...]
    out_ref[half:LAG, :] = early_ref[...]
    out_ref[LAG:EARLY, :] = middle_ref[...]
    for step in range(steps + 1):
        at = step * CHUNK
        if step < steps:
            hs[D2 + at : D2 + at + CHUNK, :] = hidden_rows(far_ref, at, CHUNK, w1_ref, b1_ref)
        if step:
            out_ref[EARLY + at - CHUNK : EARLY + at, :] = feature_rows(hs, at - CHUNK, CHUNK, w2_ref)


def body(far, head, early, middle, hidden, w1, b1, w2):
    rows, hid, feat = far.shape[0] - D1 + EARLY, w1.shape[1], w2.shape[1]
    vmem = pl.BlockSpec(memory_space=pltpu.VMEM)
    return pl.pallas_call(
        body_kernel,
        in_specs=[vmem] * 8,
        out_specs=vmem,
        out_shape=jax.ShapeDtypeStruct((rows, feat), BF16),
        scratch_shapes=[pltpu.VMEM((rows - EARLY + D2, hid), BF16)],
        compiler_params=pltpu.CompilerParams(vmem_limit_bytes=16 * MIB),
    )(far, head, early, middle, hidden, w1, b1, w2)


def column_sum(rows):
    parts = rows.astype(F32).reshape(4, -1, 8, rows.shape[1])
    return jnp.sum(jnp.sum(parts, 1), 0)


def moment_kernel(feature_ref, inst, lag, total):
    rows, feat = feature_ref.shape
    tm_index, tm_last = lax.axis_index("tm"), lax.axis_size("tm") - 1
    for at in range(0, rows, LAG):
        weight = 2.0
        if at == 0:
            weight = jnp.where(tm_index == 0, 1.0, 2.0)
        elif at == rows - LAG:
            weight = jnp.where(tm_index == tm_last, 1.0, 2.0)
        now = feature_ref[at : at + LAG, :]
        if at == 0:
            inst[...] = weight * gram(now, now)
            total[...] = weight * column_sum(now)
            continue
        both = gram(now, jnp.concatenate([now, feature_ref[at - LAG : at, :]], 1))
        inst[...] += weight * both[:, :feat]
        lag[...] = both[:, feat:] if at == LAG else lag[...] + both[:, feat:]
        total[...] += weight * column_sum(now)


def moments(feature):
    feat = feature.shape[1]
    vmem = pl.BlockSpec(memory_space=pltpu.VMEM)
    square = jax.ShapeDtypeStruct((feat, feat), F32)
    return pl.pallas_call(
        moment_kernel,
        in_specs=[vmem],
        out_specs=(vmem,) * 3,
        out_shape=(square, square, jax.ShapeDtypeStruct((8, feat), F32)),
        compiler_params=pltpu.CompilerParams(vmem_limit_bytes=12 * MIB),
    )(feature)


def pack_kernel(feature_ref, ahead_head_ref, ahead_early_ref, inst, lag, total, kept_ref, sent_ref, packed):
    feat = inst.shape[0]
    half = LAG // 2
    edge = feature_ref.shape[0] - LAG
    cross = lag[...] + gram(ahead_head_ref[...], feature_ref[edge : edge + half, :])
    cross += gram(ahead_early_ref[...], feature_ref[edge + half :, :])
    both = cross + cross.T
    row = lax.broadcasted_iota(jnp.int32, (feat, feat), 0)
    column = lax.broadcasted_iota(jnp.int32, (feat, feat), 1)
    packed[...] = jnp.where(column >= row, inst[...], both)
    sums = jnp.sum(total[...], 0, keepdims=True)
    diagonal = jnp.sum(jnp.where(column == row, both, 0.0), 0, keepdims=True)
    core = lax.axis_index("core")
    for ref, owner in ((kept_ref, core), (sent_ref, 1 - core)):
        extra = jnp.where(owner == 0, sums, diagonal)
        chunks = ref.shape[0]
        for index, lanes in slots(ref.shape, feat):
            at = pl.multiple_of(owner * (feat // 2) + index * chunks, 8)
            ref[:, 0, lanes] = packed[pl.ds(at, chunks), :]
        for chunk in range(chunks):
            part = extra[:, chunk * 128 : chunk * 128 + 128] if chunk < feat // 128 else jnp.zeros((1, 128), F32)
            ref[chunk, 0:1, ref.shape[2] - 128 :] = part


def slots(shape, feat):
    for index in range((shape[2] - 128) // feat):
        yield index, slice(index * feat, (index + 1) * feat)


def pack(feature, ahead_head, ahead_early, inst, lag, total, chips):
    vmem = pl.BlockSpec(memory_space=pltpu.VMEM)
    feat = inst.shape[0]
    share = jax.ShapeDtypeStruct((chips, 1, feat // 2 // chips * feat + 128), F32)
    return pl.pallas_call(
        pack_kernel,
        in_specs=[vmem] * 6,
        out_specs=(vmem, vmem),
        out_shape=(share, share),
        scratch_shapes=[pltpu.VMEM((feat, feat), F32)],
        compiler_params=pltpu.CompilerParams(vmem_limit_bytes=8 * MIB),
    )(feature, ahead_head, ahead_early, inst, lag, total)


def three_parts(x):
    high = x.astype(BF16)
    rest = x - high.astype(F32)
    middle = rest.astype(BF16)
    low = (rest - middle.astype(F32)).astype(BF16)
    return high, middle, low


def product(a, b):
    high, middle, low = three_parts(a)
    left = jnp.concatenate([high, high, middle, high, low, middle], 1)
    high, middle, low = three_parts(b)
    right = jnp.concatenate([high, middle, high, low, high, middle], 0)
    return jnp.dot(left, right, preferred_element_type=F32)


def eliminate(rows, start, size):
    lane = lax.broadcasted_iota(jnp.int32, (8, size), 1) - start
    sub = lax.broadcasted_iota(jnp.int32, (8, size), 0)
    sub_narrow = lax.broadcasted_iota(jnp.int32, (8, 128), 0)
    tiles = range(len(rows))

    def wide(x):
        return jnp.concatenate([x] * (size // 128), 1)

    def spread(x, j):
        return jnp.broadcast_to(x[j : j + 1, :], x.shape)

    columns = [
        [jnp.broadcast_to(rows[h][:, start + k : start + k + 1], (8, 128)) for h in tiles]
        for k in range(PANEL)
    ]
    inside = (lane >= 0) & (lane < PANEL)
    rows = [jnp.where(inside, jnp.where(lane == sub + 8 * h, 1.0, 0.0), rows[h]) for h in tiles]
    pivots = [jnp.ones((8, 128), F32) for _ in range(PANEL // 8)]
    pivot_row = {k: spread(columns[k][0], 0) for k in range(PANEL)}
    panel_row = spread(rows[0], 0)
    for j in range(PANEL):
        inverse = pl.reciprocal(pivot_row[j], approx=True)
        here, at = divmod(j, 8)
        pivots[here] = jnp.where(sub_narrow == at, pivot_row[j], pivots[here])
        last = j + 1 == PANEL
        if not last:
            there, after = divmod(j + 1, 8)
            share = pivot_row[j + 1] * inverse
            next_row = {
                k: spread(columns[k][there], after) - share * pivot_row[k] for k in range(j + 1, PANEL)
            }
            next_panel_row = spread(rows[there], after) - wide(share) * panel_row
        for h in tiles:
            if 8 * h + 7 <= j:
                continue
            factor = columns[j][h] * inverse
            if h == here:
                factor = jnp.where(sub_narrow > at, factor, 0.0)
            for k in range(j + 1, PANEL):
                columns[k][h] = columns[k][h] - factor * pivot_row[k]
            rows[h] = rows[h] - wide(factor) * panel_row
        if not last:
            pivot_row, panel_row = next_row, next_panel_row
    return [rows[h] * wide(lax.rsqrt(pivots[h])) if h < len(pivots) else rows[h] for h in tiles]


def inverse_factor(work):
    size = work.shape[0]
    for start in range(0, size, SUPER):
        stop = start + SUPER
        rows = [work[at : at + 8, :] for at in range(start, stop, 8)]
        for at in range(0, SUPER, PANEL):
            rows[at // 8 :] = eliminate(rows[at // 8 :], start + at, size)
        row = lax.broadcasted_iota(jnp.int32, (SUPER, size), 0)
        column = lax.broadcasted_iota(jnp.int32, (SUPER, size), 1) - start
        panel = jnp.where((column > row) & (column < SUPER), 0.0, jnp.concatenate(rows, 0))
        work[start:stop, :] = panel
        if stop < size:
            high, middle, low = three_parts(panel)
            left = jnp.concatenate([high, high, middle, high, low, middle], 0)
            right = jnp.concatenate([high, middle, high, low, high, middle], 0)
            first = stop // 128 * 128
            update = gram(left[:, first:], right)
            kept = lax.broadcasted_iota(jnp.int32, (size - stop, size), 1)
            kept = (kept < start) | (kept >= stop)
            work[stop:, :] = jnp.where(kept, work[stop:, :], 0.0) - update[stop - first :]
    row = lax.broadcasted_iota(jnp.int32, (size, size), 0)
    column = lax.broadcasted_iota(jnp.int32, (size, size), 1)
    return jnp.where(column <= row, work[...], 0.0)


def koopman_kernel(
    scale_ref, mine_ref, other_ref, feature_ref, ahead_head_ref, ahead_early_ref, moved_out, residual_out,
    work, packed_ref, split_ref, shift_ref, moved, residual, sems,
):
    feat = packed_ref.shape[1]
    scale = scale_ref[0]
    core = lax.axis_index("core")
    extras = []
    for ref, owner in ((mine_ref, core), (other_ref, 1 - core)):
        chunks = ref.shape[0]
        for index, lanes in slots(ref.shape, feat):
            at = pl.multiple_of(owner * (feat // 2) + index * chunks, 8)
            packed_ref[pl.ds(at, chunks), :] = ref[:, 0, lanes]
        parts = [ref[chunk, 0:1, ref.shape[2] - 128 :] for chunk in range(feat // 128)]
        extras.append(jnp.concatenate(parts, 1))
    packed = packed_ref[...]
    mean = jnp.where(core == 0, extras[0], extras[1]) * scale
    diagonal = jnp.where(core == 0, extras[1], extras[0])
    row = lax.broadcasted_iota(jnp.int32, (feat, feat), 0)
    column = lax.broadcasted_iota(jnp.int32, (feat, feat), 1)
    turned = packed.T
    mean_column = jnp.broadcast_to(mean, (feat, feat)).T
    centre = mean_column * mean
    inst = jnp.where(column >= row, packed, turned)
    lag = jnp.where(column < row, packed, turned)
    lag = jnp.where(column == row, jnp.broadcast_to(diagonal, (feat, feat)), lag)
    work[...] = inst * scale - centre + jnp.where(column == row, RIDGE, 0.0)
    lag = lag * scale - centre
    inverse = inverse_factor(work)
    inverse_turned = inverse.T
    koopman = product(product(inverse, lag), inverse_turned)
    moved_turned = product(inverse_turned, koopman)
    for index, matrix in enumerate((inverse_turned, moved_turned)):
        high = matrix.astype(BF16)
        split_ref[index, :feat, :] = high
        split_ref[index, feat:, :] = (matrix - high.astype(F32)).astype(BF16)
        shift = jnp.sum(mean_column * matrix, 0, keepdims=True)
        shift_ref[index] = jnp.broadcast_to(shift, (8, feat))
    project_rows(
        feature_ref, ahead_head_ref, ahead_early_ref, split_ref, shift_ref, moved_out, residual_out, moved, residual, sems
    )


def project_rows(
    feature_ref, ahead_head_ref, ahead_early_ref, split_ref, shift_ref, moved_out, residual_out, moved, residual, sems
):
    rows = feature_ref.shape[0]
    at_end = lax.axis_index("tm") == lax.axis_size("tm") - 1

    def image(block, index):
        twice = jnp.concatenate([block, block], 1)
        return jnp.dot(twice, split_ref[index], preferred_element_type=F32) - shift_ref[index][0:1]

    copies = []
    for step in range(rows // CHUNK):
        here = slice(step * CHUNK, (step + 1) * CHUNK)
        start = step * CHUNK + LAG
        if start < rows:
            later = feature_ref[start : start + CHUNK, :]
        else:
            later = (ahead_head_ref if start == rows else ahead_early_ref)[...]
        now = image(feature_ref[here, :], 1)
        moved[here, :] = now
        gap = image(later, 0) - now
        residual[here, :] = gap if start < rows else jnp.where(at_end, 0.0, gap)
        for index, (source, target) in enumerate(((moved, moved_out), (residual, residual_out))):
            copy = pltpu.make_async_copy(source.at[here], target.at[here], sems.at[index, step])
            copy.start()
            copies.append(copy)
    for copy in copies:
        copy.wait()


def project(scale, mine, other, feature, ahead_head, ahead_early):
    rows, feat = feature.shape
    vmem = pl.BlockSpec(memory_space=pltpu.VMEM)
    hbm = pl.BlockSpec(memory_space=pltpu.HBM)
    out = jax.ShapeDtypeStruct((rows, feat), F32)
    return pl.pallas_call(
        koopman_kernel,
        in_specs=[pl.BlockSpec(memory_space=pltpu.SMEM)] + [vmem] * 5,
        out_specs=(hbm, hbm),
        out_shape=(out, out),
        scratch_shapes=[
            pltpu.VMEM((feat, feat), F32),
            pltpu.VMEM((feat, feat), F32),
            pltpu.VMEM((2, 2 * feat, feat), BF16),
            pltpu.VMEM((2, 8, feat), F32),
            pltpu.VMEM((rows, feat), F32),
            pltpu.VMEM((rows, feat), F32),
            pltpu.SemaphoreType.DMA((2, rows // CHUNK)),
        ],
        compiler_params=pltpu.CompilerParams(vmem_limit_bytes=32 * MIB),
    )(scale, mine, other, feature, ahead_head, ahead_early)


def summed(kept, sent):
    swap = [(0, 1), (1, 0)]
    chips = ("x", "tm")
    parts = kept + lax.ppermute(sent, "core", swap)
    mine = jnp.sum(lax.all_to_all(parts, chips, 0, 0, tiled=True), 0, keepdims=True)
    mine = lax.all_to_all(jnp.broadcast_to(mine, parts.shape), chips, 0, 0, tiled=True)
    return mine, lax.ppermute(mine, "core", swap)


def on_device(frames, first_weight, first_bias, second_weight):
    frame_block = frames[0]
    row_count, channels = frame_block.shape
    hid, feat = second_weight.shape[1:]
    weights = (
        first_weight.reshape(2 * channels, hid),
        first_bias.reshape(1, hid),
        second_weight.reshape(2 * hid, feat),
    )
    sent, near, *weights = tail_rows(frame_block, *weights)
    halo = passed_along(sent, "tm", 1)
    early, before = early_rows(near, *weights)
    ahead_early = passed_along(early, "tm", -1)
    middle, hidden, far = middle_rows(frame_block, near, before, *weights)
    head = head_rows(near, halo, *weights)
    ahead_head = passed_along(head, "tm", -1)
    feature = body(far, head, early, middle, hidden, *weights)
    inst, lag, total = moments(feature)
    chips = lax.axis_size("x") * lax.axis_size("tm")
    mine, other = summed(*pack(feature, ahead_head, ahead_early, inst, lag, total, chips))
    replicas = lax.axis_size("x") * lax.axis_size("core")
    pair_count = replicas * (row_count * lax.axis_size("tm") - LAG)
    scale = jnp.full((1,), 1.0 / (2.0 * pair_count), F32)
    propagated, residual = project(scale, mine, other, feature, ahead_head, ahead_early)
    return (propagated[None], residual[None])


def solution(mesh):
    replicas, blocks = mesh.devices.shape
    chips = Mesh(mesh.devices.reshape(replicas // 2, 2, blocks), ("x", "core", "tm"))
    split = P(("x", "core"), "tm", None)
    return jax.shard_map(
        on_device,
        mesh=chips,
        in_specs=(split, P(), P(), P()),
        out_specs=(split, split),
        check_vma=False,
    )
```

```python
import jax
import jax.numpy as jnp
from jax import lax
from jax.experimental import pallas as pl
from jax.experimental.pallas import tpu as pltpu
from jax.sharding import Mesh, PartitionSpec as P

D1 = 32
D2 = 256
LAG = 1024
RIDGE = 0.001
CHUNK = 512
EARLY = 1536
PANEL = 16
SUPER = 32
MIB = 1024 * 1024

F32 = jnp.float32
BF16 = jnp.bfloat16


def passed_along(value, axis, steps):
    count = lax.axis_size(axis)
    first, last = (max(0, -steps), min(count, count - steps))
    return lax.ppermute(value, axis, [(source, source + steps) for source in range(first, last)])


def gram(a, b):
    return lax.dot_general(a, b, (((0,), (0,)), ((), ())), preferred_element_type=F32)


def in_hbm(value):
    return pltpu.with_memory_space_constraint(value, pltpu.HBM)


def silu(x):
    half = 0.5 * x
    return half + half * jnp.tanh(half)


def hidden_rows(xs, at, rows, w1_ref, b1_ref):
    both = jnp.concatenate([xs[pl.ds(at + D1, rows), :], xs[pl.ds(at, rows), :]], 1)
    hid = w1_ref.shape[1]
    parts = []
    for lanes in (slice(0, hid // 2), slice(hid // 2, hid)):
        z = jnp.dot(both, w1_ref[:, lanes], preferred_element_type=F32)
        parts.append(silu(z + b1_ref[:, lanes]).astype(BF16))
    return jnp.concatenate(parts, 1)


def feature_rows(hs, at, rows, w2_ref):
    both = jnp.concatenate([hs[pl.ds(at + D2, rows), :], hs[pl.ds(at, rows), :]], 1)
    return jnp.dot(both, w2_ref[...], preferred_element_type=F32).astype(BF16)


def tail_kernel(frames_ref, w1_in, b1_in, w2_in, sent_ref, near_ref, w1_ref, b1_ref, w2_ref, xs, sems):
    rows = frames_ref.shape[0]
    pairs = (
        (frames_ref.at[pl.ds(rows - D1 - D2, D1 + D2)], xs),
        (w1_in, w1_ref),
        (b1_in, b1_ref),
        (w2_in, w2_ref),
        (frames_ref.at[pl.ds(0, LAG)], near_ref),
    )
    copies = [pltpu.make_async_copy(*pair, sems.at[index]) for index, pair in enumerate(pairs)]
    for copy in copies:
        copy.start()
    for copy in copies[:3]:
        copy.wait()
    hidden = hidden_rows(xs, 0, D2, w1_ref, b1_ref)
    copies[3].wait()
    hid, feat = hidden.shape[1], w2_ref.shape[1]
    sent_ref[:D2, :] = jnp.dot(hidden, w2_ref[hid:, :], preferred_element_type=F32).astype(BF16)
    for index in range(xs.shape[1] // feat):
        part = slice(D2 + index * D1, D2 + (index + 1) * D1)
        sent_ref[part, :] = xs[D2:, index * feat : (index + 1) * feat]
    copies[4].wait()


def tail_rows(frames, w1, b1, w2):
    vmem = pl.BlockSpec(memory_space=pltpu.VMEM)
    hbm = pl.BlockSpec(memory_space=pltpu.HBM)
    channels, feat = frames.shape[1], w2.shape[1]
    sent = (D2 + D1 * channels // feat, feat)
    shapes = ((sent, BF16), ((LAG, channels), BF16), (w1.shape, BF16), (b1.shape, F32), (w2.shape, BF16))
    return pl.pallas_call(
        tail_kernel,
        in_specs=[hbm] * 4,
        out_specs=(vmem,) * 5,
        out_shape=tuple(jax.ShapeDtypeStruct(*shape) for shape in shapes),
        scratch_shapes=[pltpu.VMEM((D1 + D2, channels), BF16), pltpu.SemaphoreType.DMA((5,))],
        compiler_params=pltpu.CompilerParams(vmem_limit_bytes=12 * MIB),
    )(*(in_hbm(value) for value in (frames, w1, b1, w2)))


def early_kernel(near_ref, w1_ref, b1_ref, w2_ref, out_ref, hidden_ref, hs):
    half = LAG // 2
    for at in range(0, hs.shape[0], D2):
        hs[at : at + D2, :] = hidden_rows(near_ref, half - D1 - D2 + at, D2, w1_ref, b1_ref)
    out_ref[...] = feature_rows(hs, 0, half, w2_ref)
    hidden_ref[...] = hs[half:, :]


def early_rows(near, w1, b1, w2):
    vmem = pl.BlockSpec(memory_space=pltpu.VMEM)
    half, hid = LAG // 2, w1.shape[1]
    return pl.pallas_call(
        early_kernel,
        in_specs=[vmem] * 4,
        out_specs=(vmem, vmem),
        out_shape=(
            jax.ShapeDtypeStruct((half, w2.shape[1]), BF16),
            jax.ShapeDtypeStruct((D2, hid), BF16),
        ),
        scratch_shapes=[pltpu.VMEM((half + D2, hid), BF16)],
        compiler_params=pltpu.CompilerParams(vmem_limit_bytes=8 * MIB),
    )(near, w1, b1, w2)


def middle_kernel(
    frames_ref, near_ref, before_ref, w1_ref, b1_ref, w2_ref, middle_ref, hidden_ref, far_ref, xs, hs, sems
):
    rows = EARLY - LAG
    now = pltpu.make_async_copy(frames_ref.at[pl.ds(LAG, rows)], xs.at[pl.ds(D1, rows)], sems.at[0])
    later = pltpu.make_async_copy(
        frames_ref.at[pl.ds(EARLY - D1, far_ref.shape[0])], far_ref, sems.at[1]
    )
    now.start()
    later.start()
    xs[:D1, :] = near_ref[LAG - D1 :, :]
    hs[:D2, :] = before_ref[...]
    now.wait()
    for at in range(0, rows, D2):
        hs[D2 + at : 2 * D2 + at, :] = hidden_rows(xs, at, D2, w1_ref, b1_ref)
    middle_ref[...] = feature_rows(hs, 0, rows, w2_ref)
    hidden_ref[...] = hs[rows:, :]
    later.wait()


def middle_rows(frames, near, before, w1, b1, w2):
    vmem = pl.BlockSpec(memory_space=pltpu.VMEM)
    hbm = pl.BlockSpec(memory_space=pltpu.HBM)
    rows, channels = frames.shape
    hid, feat = w1.shape[1], w2.shape[1]
    shapes = ((EARLY - LAG, feat), (D2, hid), (rows - EARLY + D1, channels))
    return pl.pallas_call(
        middle_kernel,
        in_specs=[hbm] + [vmem] * 5,
        out_specs=(vmem,) * 3,
        out_shape=tuple(jax.ShapeDtypeStruct(shape, BF16) for shape in shapes),
        scratch_shapes=[
            pltpu.VMEM((EARLY - LAG + D1, channels), BF16),
            pltpu.VMEM((EARLY - LAG + D2, hid), BF16),
            pltpu.SemaphoreType.DMA((2,)),
        ],
        compiler_params=pltpu.CompilerParams(vmem_limit_bytes=12 * MIB),
    )(in_hbm(frames), near, before, w1, b1, w2)


def head_kernel(near_ref, halo_ref, w1_ref, b1_ref, w2_ref, out_ref, xs, hs):
    half = LAG // 2
    hid, feat = w1_ref.shape[1], w2_ref.shape[1]
    for index in range(xs.shape[1] // feat):
        part = slice(D2 + index * D1, D2 + (index + 1) * D1)
        xs[:D1, index * feat : (index + 1) * feat] = halo_ref[part, :]
    xs[D1:, :] = near_ref[:half, :]
    for at in range(0, half, D2):
        hs[at : at + D2, :] = hidden_rows(xs, at, D2, w1_ref, b1_ref)
    value = jnp.dot(hs[:D2, :], w2_ref[:hid, :], preferred_element_type=F32)
    out_ref[:D2, :] = (value + halo_ref[:D2, :].astype(F32)).astype(BF16)
    out_ref[D2:, :] = feature_rows(hs, 0, half - D2, w2_ref)


def head_rows(near, halo, w1, b1, w2):
    vmem = pl.BlockSpec(memory_space=pltpu.VMEM)
    half, channels, hid = LAG // 2, near.shape[1], w1.shape[1]
    return pl.pallas_call(
        head_kernel,
        in_specs=[vmem] * 5,
        out_specs=vmem,
        out_shape=jax.ShapeDtypeStruct((half, w2.shape[1]), BF16),
        scratch_shapes=[pltpu.VMEM((half + D1, channels), BF16), pltpu.VMEM((half, hid), BF16)],
        compiler_params=pltpu.CompilerParams(vmem_limit_bytes=8 * MIB),
    )(near, halo, w1, b1, w2)


def body_kernel(far_ref, head_ref, early_ref, middle_ref, hidden_ref, w1_ref, b1_ref, w2_ref, out_ref, hs):
    rows = out_ref.shape[0]
    steps = (rows - EARLY) // CHUNK
    half = LAG // 2
    hs[:D2, :] = hidden_ref[...]
    out_ref[:half, :] = head_ref[...]
    out_ref[half:LAG, :] = early_ref[...]
    out_ref[LAG:EARLY, :] = middle_ref[...]
    for step in range(steps + 1):
        at = step * CHUNK
        if step < steps:
            hs[D2 + at : D2 + at + CHUNK, :] = hidden_rows(far_ref, at, CHUNK, w1_ref, b1_ref)
        if step:
            out_ref[EARLY + at - CHUNK : EARLY + at, :] = feature_rows(hs, at - CHUNK, CHUNK, w2_ref)


def body(far, head, early, middle, hidden, w1, b1, w2):
    rows, hid, feat = far.shape[0] - D1 + EARLY, w1.shape[1], w2.shape[1]
    vmem = pl.BlockSpec(memory_space=pltpu.VMEM)
    return pl.pallas_call(
        body_kernel,
        in_specs=[vmem] * 8,
        out_specs=vmem,
        out_shape=jax.ShapeDtypeStruct((rows, feat), BF16),
        scratch_shapes=[pltpu.VMEM((rows - EARLY + D2, hid), BF16)],
        compiler_params=pltpu.CompilerParams(vmem_limit_bytes=16 * MIB),
    )(far, head, early, middle, hidden, w1, b1, w2)


def column_sum(rows):
    parts = rows.astype(F32).reshape(4, -1, 8, rows.shape[1])
    return jnp.sum(jnp.sum(parts, 1), 0)


def moment_kernel(feature_ref, inst, lag, total):
    rows, feat = feature_ref.shape
    tm_index, tm_last = lax.axis_index("tm"), lax.axis_size("tm") - 1
    for at in range(0, rows, LAG):
        weight = 2.0
        if at == 0:
            weight = jnp.where(tm_index == 0, 1.0, 2.0)
        elif at == rows - LAG:
            weight = jnp.where(tm_index == tm_last, 1.0, 2.0)
        now = feature_ref[at : at + LAG, :]
        if at == 0:
            inst[...] = weight * gram(now, now)
            total[...] = weight * column_sum(now)
            continue
        both = gram(now, jnp.concatenate([now, feature_ref[at - LAG : at, :]], 1))
        inst[...] += weight * both[:, :feat]
        lag[...] = both[:, feat:] if at == LAG else lag[...] + both[:, feat:]
        total[...] += weight * column_sum(now)


def moments(feature):
    feat = feature.shape[1]
    vmem = pl.BlockSpec(memory_space=pltpu.VMEM)
    square = jax.ShapeDtypeStruct((feat, feat), F32)
    return pl.pallas_call(
        moment_kernel,
        in_specs=[vmem],
        out_specs=(vmem,) * 3,
        out_shape=(square, square, jax.ShapeDtypeStruct((8, feat), F32)),
        compiler_params=pltpu.CompilerParams(vmem_limit_bytes=12 * MIB),
    )(feature)


def pack_kernel(feature_ref, ahead_head_ref, ahead_early_ref, inst, lag, total, kept_ref, sent_ref, packed):
    feat = inst.shape[0]
    half = LAG // 2
    edge = feature_ref.shape[0] - LAG
    cross = lag[...] + gram(ahead_head_ref[...], feature_ref[edge : edge + half, :])
    cross += gram(ahead_early_ref[...], feature_ref[edge + half :, :])
    both = cross + cross.T
    row = lax.broadcasted_iota(jnp.int32, (feat, feat), 0)
    column = lax.broadcasted_iota(jnp.int32, (feat, feat), 1)
    packed[...] = jnp.where(column >= row, inst[...], both)
    sums = jnp.sum(total[...], 0, keepdims=True)
    diagonal = jnp.sum(jnp.where(column == row, both, 0.0), 0, keepdims=True)
    core = lax.axis_index("core")
    for ref, owner in ((kept_ref, core), (sent_ref, 1 - core)):
        extra = jnp.where(owner == 0, sums, diagonal)
        chunks = ref.shape[0]
        for index, lanes in slots(ref.shape, feat):
            at = pl.multiple_of(owner * (feat // 2) + index * chunks, 8)
            ref[:, 0, lanes] = packed[pl.ds(at, chunks), :]
        for chunk in range(chunks):
            part = extra[:, chunk * 128 : chunk * 128 + 128] if chunk < feat // 128 else jnp.zeros((1, 128), F32)
            ref[chunk, 0:1, ref.shape[2] - 128 :] = part


def slots(shape, feat):
    for index in range((shape[2] - 128) // feat):
        yield index, slice(index * feat, (index + 1) * feat)


def pack(feature, ahead_head, ahead_early, inst, lag, total, chips):
    vmem = pl.BlockSpec(memory_space=pltpu.VMEM)
    feat = inst.shape[0]
    share = jax.ShapeDtypeStruct((chips, 1, feat // 2 // chips * feat + 128), F32)
    return pl.pallas_call(
        pack_kernel,
        in_specs=[vmem] * 6,
        out_specs=(vmem, vmem),
        out_shape=(share, share),
        scratch_shapes=[pltpu.VMEM((feat, feat), F32)],
        compiler_params=pltpu.CompilerParams(vmem_limit_bytes=8 * MIB),
    )(feature, ahead_head, ahead_early, inst, lag, total)


def three_parts(x):
    high = x.astype(BF16)
    rest = x - high.astype(F32)
    middle = rest.astype(BF16)
    low = (rest - middle.astype(F32)).astype(BF16)
    return high, middle, low


def product(a, b):
    high, middle, low = three_parts(a)
    left = jnp.concatenate([high, high, middle, high, low, middle], 1)
    high, middle, low = three_parts(b)
    right = jnp.concatenate([high, middle, high, low, high, middle], 0)
    return jnp.dot(left, right, preferred_element_type=F32)


def eliminate(rows, start, size):
    lane = lax.broadcasted_iota(jnp.int32, (8, size), 1) - start
    sub = lax.broadcasted_iota(jnp.int32, (8, size), 0)
    sub_narrow = lax.broadcasted_iota(jnp.int32, (8, 128), 0)
    tiles = range(len(rows))

    def wide(x):
        return jnp.concatenate([x] * (size // 128), 1)

    def spread(x, j):
        return jnp.broadcast_to(x[j : j + 1, :], x.shape)

    columns = [
        [jnp.broadcast_to(rows[h][:, start + k : start + k + 1], (8, 128)) for h in tiles]
        for k in range(PANEL)
    ]
    inside = (lane >= 0) & (lane < PANEL)
    rows = [jnp.where(inside, jnp.where(lane == sub + 8 * h, 1.0, 0.0), rows[h]) for h in tiles]
    inverses = [jnp.ones((8, 128), F32) for _ in range(PANEL // 8)]
    first, second = ({k: spread(columns[k][0], r) for k in range(PANEL)} for r in (0, 1))
    first_row, second_row = (spread(rows[0], r) for r in (0, 1))
    for j in range(0, PANEL, 2):
        here, at = divmod(j, 8)
        inverse = pl.reciprocal(first[j], approx=True)
        determinant = first[j] * second[j + 1] - first[j + 1] * first[j + 1]
        inverse_second = first[j] * pl.reciprocal(determinant, approx=True)
        inverses[here] = jnp.where(sub_narrow == at, inverse, inverses[here])
        inverses[here] = jnp.where(sub_narrow == at + 1, inverse_second, inverses[here])
        share = first[j + 1] * inverse
        second = {k: second[k] - share * first[k] for k in range(j + 1, PANEL)}
        second_row = second_row - wide(share) * first_row
        following = []
        if j + 2 < PANEL:
            there, after = divmod(j + 2, 8)
            for r in (0, 1):
                one = first[j + 2 + r] * inverse
                two = second[j + 2 + r] * inverse_second
                following.append(
                    {
                        k: spread(columns[k][there], after + r) - one * first[k] - two * second[k]
                        for k in range(j + 2, PANEL)
                    }
                )
                following.append(
                    spread(rows[there], after + r) - wide(one) * first_row - wide(two) * second_row
                )
        for h in tiles:
            if 8 * h + 7 <= j:
                continue
            one = columns[j][h] * inverse
            if h == here:
                one = jnp.where(sub_narrow > at, one, 0.0)
            two = (columns[j + 1][h] - one * first[j + 1]) * inverse_second
            if h == here:
                two = jnp.where(sub_narrow > at + 1, two, 0.0)
            for k in range(j + 2, PANEL):
                columns[k][h] = columns[k][h] - one * first[k] - two * second[k]
            rows[h] = rows[h] - wide(one) * first_row - wide(two) * second_row
        if following:
            first, first_row, second, second_row = following
    scales = [x * lax.rsqrt(x) for x in inverses]
    return [rows[h] * wide(scales[h]) if h < len(scales) else rows[h] for h in tiles]


def inverse_factor(work):
    size = work.shape[0]
    for start in range(0, size, SUPER):
        stop = start + SUPER
        rows = [work[at : at + 8, :] for at in range(start, stop, 8)]
        for at in range(0, SUPER, PANEL):
            rows[at // 8 :] = eliminate(rows[at // 8 :], start + at, size)
        row = lax.broadcasted_iota(jnp.int32, (SUPER, size), 0)
        column = lax.broadcasted_iota(jnp.int32, (SUPER, size), 1) - start
        panel = jnp.where((column > row) & (column < SUPER), 0.0, jnp.concatenate(rows, 0))
        work[start:stop, :] = panel
        if stop < size:
            high, middle, low = three_parts(panel)
            left = jnp.concatenate([high, high, middle, high, low, middle], 0)
            right = jnp.concatenate([high, middle, high, low, high, middle], 0)
            first = stop // 128 * 128
            update = gram(left[:, first:], right)
            kept = lax.broadcasted_iota(jnp.int32, (size - stop, size), 1)
            kept = (kept < start) | (kept >= stop)
            work[stop:, :] = jnp.where(kept, work[stop:, :], 0.0) - update[stop - first :]
    row = lax.broadcasted_iota(jnp.int32, (size, size), 0)
    column = lax.broadcasted_iota(jnp.int32, (size, size), 1)
    return jnp.where(column <= row, work[...], 0.0)


def koopman_kernel(
    scale_ref, mine_ref, other_ref, feature_ref, ahead_head_ref, ahead_early_ref, moved_out, residual_out,
    work, packed_ref, split_ref, shift_ref, moved, residual, sems,
):
    feat = packed_ref.shape[1]
    scale = scale_ref[0]
    core = lax.axis_index("core")
    extras = []
    for ref, owner in ((mine_ref, core), (other_ref, 1 - core)):
        chunks = ref.shape[0]
        for index, lanes in slots(ref.shape, feat):
            at = pl.multiple_of(owner * (feat // 2) + index * chunks, 8)
            packed_ref[pl.ds(at, chunks), :] = ref[:, 0, lanes]
        parts = [ref[chunk, 0:1, ref.shape[2] - 128 :] for chunk in range(feat // 128)]
        extras.append(jnp.concatenate(parts, 1))
    packed = packed_ref[...]
    mean = jnp.where(core == 0, extras[0], extras[1]) * scale
    diagonal = jnp.where(core == 0, extras[1], extras[0])
    row = lax.broadcasted_iota(jnp.int32, (feat, feat), 0)
    column = lax.broadcasted_iota(jnp.int32, (feat, feat), 1)
    turned = packed.T
    mean_column = jnp.broadcast_to(mean, (feat, feat)).T
    centre = mean_column * mean
    inst = jnp.where(column >= row, packed, turned)
    lag = jnp.where(column < row, packed, turned)
    lag = jnp.where(column == row, jnp.broadcast_to(diagonal, (feat, feat)), lag)
    work[...] = inst * scale - centre + jnp.where(column == row, RIDGE, 0.0)
    lag = lag * scale - centre
    inverse = inverse_factor(work)
    inverse_turned = inverse.T
    koopman = product(product(inverse, lag), inverse_turned)
    moved_turned = product(inverse_turned, koopman)
    for index, matrix in enumerate((inverse_turned, moved_turned)):
        high = matrix.astype(BF16)
        split_ref[index, :feat, :] = high
        split_ref[index, feat:, :] = (matrix - high.astype(F32)).astype(BF16)
        shift = jnp.sum(mean_column * matrix, 0, keepdims=True)
        shift_ref[index] = jnp.broadcast_to(shift, (8, feat))
    project_rows(
        feature_ref, ahead_head_ref, ahead_early_ref, split_ref, shift_ref, moved_out, residual_out, moved, residual, sems
    )


def project_rows(
    feature_ref, ahead_head_ref, ahead_early_ref, split_ref, shift_ref, moved_out, residual_out, moved, residual, sems
):
    rows = feature_ref.shape[0]
    at_end = lax.axis_index("tm") == lax.axis_size("tm") - 1

    def image(block, index):
        twice = jnp.concatenate([block, block], 1)
        return jnp.dot(twice, split_ref[index], preferred_element_type=F32) - shift_ref[index][0:1]

    copies = []
    for step in range(rows // CHUNK):
        here = slice(step * CHUNK, (step + 1) * CHUNK)
        start = step * CHUNK + LAG
        if start < rows:
            later = feature_ref[start : start + CHUNK, :]
        else:
            later = (ahead_head_ref if start == rows else ahead_early_ref)[...]
        now = image(feature_ref[here, :], 1)
        moved[here, :] = now
        gap = image(later, 0) - now
        residual[here, :] = gap if start < rows else jnp.where(at_end, 0.0, gap)
        for index, (source, target) in enumerate(((moved, moved_out), (residual, residual_out))):
            copy = pltpu.make_async_copy(source.at[here], target.at[here], sems.at[index, step])
            copy.start()
            copies.append(copy)
    for copy in copies:
        copy.wait()


def project(scale, mine, other, feature, ahead_head, ahead_early):
    rows, feat = feature.shape
    vmem = pl.BlockSpec(memory_space=pltpu.VMEM)
    hbm = pl.BlockSpec(memory_space=pltpu.HBM)
    out = jax.ShapeDtypeStruct((rows, feat), F32)
    return pl.pallas_call(
        koopman_kernel,
        in_specs=[pl.BlockSpec(memory_space=pltpu.SMEM)] + [vmem] * 5,
        out_specs=(hbm, hbm),
        out_shape=(out, out),
        scratch_shapes=[
            pltpu.VMEM((feat, feat), F32),
            pltpu.VMEM((feat, feat), F32),
            pltpu.VMEM((2, 2 * feat, feat), BF16),
            pltpu.VMEM((2, 8, feat), F32),
            pltpu.VMEM((rows, feat), F32),
            pltpu.VMEM((rows, feat), F32),
            pltpu.SemaphoreType.DMA((2, rows // CHUNK)),
        ],
        compiler_params=pltpu.CompilerParams(vmem_limit_bytes=32 * MIB),
    )(scale, mine, other, feature, ahead_head, ahead_early)


def summed(kept, sent):
    swap = [(0, 1), (1, 0)]
    chips = ("x", "tm")
    parts = kept + lax.ppermute(sent, "core", swap)
    mine = jnp.sum(lax.all_to_all(parts, chips, 0, 0, tiled=True), 0, keepdims=True)
    mine = lax.all_to_all(jnp.broadcast_to(mine, parts.shape), chips, 0, 0, tiled=True)
    return mine, lax.ppermute(mine, "core", swap)


def on_device(frames, first_weight, first_bias, second_weight):
    frame_block = frames[0]
    row_count, channels = frame_block.shape
    hid, feat = second_weight.shape[1:]
    weights = (
        first_weight.reshape(2 * channels, hid),
        first_bias.reshape(1, hid),
        second_weight.reshape(2 * hid, feat),
    )
    sent, near, *weights = tail_rows(frame_block, *weights)
    halo = passed_along(sent, "tm", 1)
    early, before = early_rows(near, *weights)
    ahead_early = passed_along(early, "tm", -1)
    middle, hidden, far = middle_rows(frame_block, near, before, *weights)
    head = head_rows(near, halo, *weights)
    ahead_head = passed_along(head, "tm", -1)
    feature = body(far, head, early, middle, hidden, *weights)
    inst, lag, total = moments(feature)
    chips = lax.axis_size("x") * lax.axis_size("tm")
    mine, other = summed(*pack(feature, ahead_head, ahead_early, inst, lag, total, chips))
    replicas = lax.axis_size("x") * lax.axis_size("core")
    pair_count = replicas * (row_count * lax.axis_size("tm") - LAG)
    scale = jnp.full((1,), 1.0 / (2.0 * pair_count), F32)
    propagated, residual = project(scale, mine, other, feature, ahead_head, ahead_early)
    return (propagated[None], residual[None])


def solution(mesh):
    replicas, blocks = mesh.devices.shape
    chips = Mesh(mesh.devices.reshape(replicas // 2, 2, blocks), ("x", "core", "tm"))
    split = P(("x", "core"), "tm", None)
    return jax.shard_map(
        on_device,
        mesh=chips,
        in_specs=(split, P(), P(), P()),
        out_specs=(split, split),
        check_vma=False,
    )
```

```python
import jax
import jax.numpy as jnp
from jax import lax
from jax.experimental import pallas as pl
from jax.experimental.pallas import tpu as pltpu
from jax.sharding import Mesh, PartitionSpec as P

D1 = 32
D2 = 256
LAG = 1024
RIDGE = 0.001
CHUNK = 512
EARLY = 1536
PANEL = 16
MIB = 1024 * 1024

F32 = jnp.float32
BF16 = jnp.bfloat16


def passed_along(value, axis, steps):
    count = lax.axis_size(axis)
    first, last = (max(0, -steps), min(count, count - steps))
    return lax.ppermute(value, axis, [(source, source + steps) for source in range(first, last)])


def gram(a, b):
    return lax.dot_general(a, b, (((0,), (0,)), ((), ())), preferred_element_type=F32)


def in_hbm(value):
    return pltpu.with_memory_space_constraint(value, pltpu.HBM)


def silu(x):
    half = 0.5 * x
    return half + half * jnp.tanh(half)


def hidden_rows(xs, at, rows, w1_ref, b1_ref):
    both = jnp.concatenate([xs[pl.ds(at + D1, rows), :], xs[pl.ds(at, rows), :]], 1)
    hid = w1_ref.shape[1]
    parts = []
    for lanes in (slice(0, hid // 2), slice(hid // 2, hid)):
        z = jnp.dot(both, w1_ref[:, lanes], preferred_element_type=F32)
        parts.append(silu(z + b1_ref[:, lanes]).astype(BF16))
    return jnp.concatenate(parts, 1)


def feature_rows(hs, at, rows, w2_ref):
    both = jnp.concatenate([hs[pl.ds(at + D2, rows), :], hs[pl.ds(at, rows), :]], 1)
    return jnp.dot(both, w2_ref[...], preferred_element_type=F32).astype(BF16)


def tail_kernel(frames_ref, w1_in, b1_in, w2_in, sent_ref, near_ref, w1_ref, b1_ref, w2_ref, xs, sems):
    rows = frames_ref.shape[0]
    pairs = (
        (frames_ref.at[pl.ds(rows - D1 - D2, D1 + D2)], xs),
        (w1_in, w1_ref),
        (b1_in, b1_ref),
        (w2_in, w2_ref),
        (frames_ref.at[pl.ds(0, LAG)], near_ref),
    )
    copies = [pltpu.make_async_copy(*pair, sems.at[index]) for index, pair in enumerate(pairs)]
    for copy in copies:
        copy.start()
    for copy in copies[:3]:
        copy.wait()
    hidden = hidden_rows(xs, 0, D2, w1_ref, b1_ref)
    copies[3].wait()
    hid, feat = hidden.shape[1], w2_ref.shape[1]
    sent_ref[:D2, :] = jnp.dot(hidden, w2_ref[hid:, :], preferred_element_type=F32).astype(BF16)
    for index in range(xs.shape[1] // feat):
        part = slice(D2 + index * D1, D2 + (index + 1) * D1)
        sent_ref[part, :] = xs[D2:, index * feat : (index + 1) * feat]
    copies[4].wait()


def tail_rows(frames, w1, b1, w2):
    vmem = pl.BlockSpec(memory_space=pltpu.VMEM)
    hbm = pl.BlockSpec(memory_space=pltpu.HBM)
    channels, feat = frames.shape[1], w2.shape[1]
    sent = (D2 + D1 * channels // feat, feat)
    shapes = ((sent, BF16), ((LAG, channels), BF16), (w1.shape, BF16), (b1.shape, F32), (w2.shape, BF16))
    return pl.pallas_call(
        tail_kernel,
        in_specs=[hbm] * 4,
        out_specs=(vmem,) * 5,
        out_shape=tuple(jax.ShapeDtypeStruct(*shape) for shape in shapes),
        scratch_shapes=[pltpu.VMEM((D1 + D2, channels), BF16), pltpu.SemaphoreType.DMA((5,))],
        compiler_params=pltpu.CompilerParams(vmem_limit_bytes=12 * MIB),
    )(*(in_hbm(value) for value in (frames, w1, b1, w2)))


def early_kernel(near_ref, w1_ref, b1_ref, w2_ref, out_ref, hidden_ref, hs):
    half = LAG // 2
    for at in range(0, hs.shape[0], D2):
        hs[at : at + D2, :] = hidden_rows(near_ref, half - D1 - D2 + at, D2, w1_ref, b1_ref)
    out_ref[...] = feature_rows(hs, 0, half, w2_ref)
    hidden_ref[...] = hs[half:, :]


def early_rows(near, w1, b1, w2):
    vmem = pl.BlockSpec(memory_space=pltpu.VMEM)
    half, hid = LAG // 2, w1.shape[1]
    return pl.pallas_call(
        early_kernel,
        in_specs=[vmem] * 4,
        out_specs=(vmem, vmem),
        out_shape=(
            jax.ShapeDtypeStruct((half, w2.shape[1]), BF16),
            jax.ShapeDtypeStruct((D2, hid), BF16),
        ),
        scratch_shapes=[pltpu.VMEM((half + D2, hid), BF16)],
        compiler_params=pltpu.CompilerParams(vmem_limit_bytes=8 * MIB),
    )(near, w1, b1, w2)


def middle_kernel(
    frames_ref, near_ref, before_ref, w1_ref, b1_ref, w2_ref, middle_ref, hidden_ref, far_ref, xs, hs, sems
):
    rows = EARLY - LAG
    now = pltpu.make_async_copy(frames_ref.at[pl.ds(LAG, rows)], xs.at[pl.ds(D1, rows)], sems.at[0])
    later = pltpu.make_async_copy(
        frames_ref.at[pl.ds(EARLY - D1, far_ref.shape[0])], far_ref, sems.at[1]
    )
    now.start()
    later.start()
    xs[:D1, :] = near_ref[LAG - D1 :, :]
    hs[:D2, :] = before_ref[...]
    now.wait()
    for at in range(0, rows, D2):
        hs[D2 + at : 2 * D2 + at, :] = hidden_rows(xs, at, D2, w1_ref, b1_ref)
    middle_ref[...] = feature_rows(hs, 0, rows, w2_ref)
    hidden_ref[...] = hs[rows:, :]
    later.wait()


def middle_rows(frames, near, before, w1, b1, w2):
    vmem = pl.BlockSpec(memory_space=pltpu.VMEM)
    hbm = pl.BlockSpec(memory_space=pltpu.HBM)
    rows, channels = frames.shape
    hid, feat = w1.shape[1], w2.shape[1]
    shapes = ((EARLY - LAG, feat), (D2, hid), (rows - EARLY + D1, channels))
    return pl.pallas_call(
        middle_kernel,
        in_specs=[hbm] + [vmem] * 5,
        out_specs=(vmem,) * 3,
        out_shape=tuple(jax.ShapeDtypeStruct(shape, BF16) for shape in shapes),
        scratch_shapes=[
            pltpu.VMEM((EARLY - LAG + D1, channels), BF16),
            pltpu.VMEM((EARLY - LAG + D2, hid), BF16),
            pltpu.SemaphoreType.DMA((2,)),
        ],
        compiler_params=pltpu.CompilerParams(vmem_limit_bytes=12 * MIB),
    )(in_hbm(frames), near, before, w1, b1, w2)


def head_kernel(near_ref, halo_ref, w1_ref, b1_ref, w2_ref, out_ref, xs, hs):
    half = LAG // 2
    hid, feat = w1_ref.shape[1], w2_ref.shape[1]
    for index in range(xs.shape[1] // feat):
        part = slice(D2 + index * D1, D2 + (index + 1) * D1)
        xs[:D1, index * feat : (index + 1) * feat] = halo_ref[part, :]
    xs[D1:, :] = near_ref[:half, :]
    for at in range(0, half, D2):
        hs[at : at + D2, :] = hidden_rows(xs, at, D2, w1_ref, b1_ref)
    value = jnp.dot(hs[:D2, :], w2_ref[:hid, :], preferred_element_type=F32)
    out_ref[:D2, :] = (value + halo_ref[:D2, :].astype(F32)).astype(BF16)
    out_ref[D2:, :] = feature_rows(hs, 0, half - D2, w2_ref)


def head_rows(near, halo, w1, b1, w2):
    vmem = pl.BlockSpec(memory_space=pltpu.VMEM)
    half, channels, hid = LAG // 2, near.shape[1], w1.shape[1]
    return pl.pallas_call(
        head_kernel,
        in_specs=[vmem] * 5,
        out_specs=vmem,
        out_shape=jax.ShapeDtypeStruct((half, w2.shape[1]), BF16),
        scratch_shapes=[pltpu.VMEM((half + D1, channels), BF16), pltpu.VMEM((half, hid), BF16)],
        compiler_params=pltpu.CompilerParams(vmem_limit_bytes=8 * MIB),
    )(near, halo, w1, b1, w2)


def body_kernel(far_ref, head_ref, early_ref, middle_ref, hidden_ref, w1_ref, b1_ref, w2_ref, out_ref, hs):
    rows = out_ref.shape[0]
    steps = (rows - EARLY) // CHUNK
    half = LAG // 2
    hs[:D2, :] = hidden_ref[...]
    out_ref[:half, :] = head_ref[...]
    out_ref[half:LAG, :] = early_ref[...]
    out_ref[LAG:EARLY, :] = middle_ref[...]
    for step in range(steps + 1):
        at = step * CHUNK
        if step < steps:
            hs[D2 + at : D2 + at + CHUNK, :] = hidden_rows(far_ref, at, CHUNK, w1_ref, b1_ref)
        if step:
            out_ref[EARLY + at - CHUNK : EARLY + at, :] = feature_rows(hs, at - CHUNK, CHUNK, w2_ref)


def body(far, head, early, middle, hidden, w1, b1, w2):
    rows, hid, feat = far.shape[0] - D1 + EARLY, w1.shape[1], w2.shape[1]
    vmem = pl.BlockSpec(memory_space=pltpu.VMEM)
    return pl.pallas_call(
        body_kernel,
        in_specs=[vmem] * 8,
        out_specs=vmem,
        out_shape=jax.ShapeDtypeStruct((rows, feat), BF16),
        scratch_shapes=[pltpu.VMEM((rows - EARLY + D2, hid), BF16)],
        compiler_params=pltpu.CompilerParams(vmem_limit_bytes=16 * MIB),
    )(far, head, early, middle, hidden, w1, b1, w2)


def column_sum(rows):
    parts = rows.astype(F32).reshape(4, -1, 8, rows.shape[1])
    return jnp.sum(jnp.sum(parts, 1), 0)


def moment_kernel(feature_ref, inst, lag, total):
    rows, feat = feature_ref.shape
    tm_index, tm_last = lax.axis_index("tm"), lax.axis_size("tm") - 1
    for at in range(0, rows, LAG):
        weight = 2.0
        if at == 0:
            weight = jnp.where(tm_index == 0, 1.0, 2.0)
        elif at == rows - LAG:
            weight = jnp.where(tm_index == tm_last, 1.0, 2.0)
        now = feature_ref[at : at + LAG, :]
        if at == 0:
            inst[...] = weight * gram(now, now)
            total[...] = weight * column_sum(now)
            continue
        both = gram(now, jnp.concatenate([now, feature_ref[at - LAG : at, :]], 1))
        inst[...] += weight * both[:, :feat]
        lag[...] = both[:, feat:] if at == LAG else lag[...] + both[:, feat:]
        total[...] += weight * column_sum(now)


def moments(feature):
    feat = feature.shape[1]
    vmem = pl.BlockSpec(memory_space=pltpu.VMEM)
    square = jax.ShapeDtypeStruct((feat, feat), F32)
    return pl.pallas_call(
        moment_kernel,
        in_specs=[vmem],
        out_specs=(vmem,) * 3,
        out_shape=(square, square, jax.ShapeDtypeStruct((8, feat), F32)),
        compiler_params=pltpu.CompilerParams(vmem_limit_bytes=12 * MIB),
    )(feature)


def pack_kernel(feature_ref, ahead_head_ref, ahead_early_ref, inst, lag, total, kept_ref, sent_ref, packed):
    feat = inst.shape[0]
    half = LAG // 2
    edge = feature_ref.shape[0] - LAG
    cross = lag[...] + gram(ahead_head_ref[...], feature_ref[edge : edge + half, :])
    cross += gram(ahead_early_ref[...], feature_ref[edge + half :, :])
    both = cross + cross.T
    row = lax.broadcasted_iota(jnp.int32, (feat, feat), 0)
    column = lax.broadcasted_iota(jnp.int32, (feat, feat), 1)
    packed[...] = jnp.where(column >= row, inst[...], both)
    sums = jnp.sum(total[...], 0, keepdims=True)
    diagonal = jnp.sum(jnp.where(column == row, both, 0.0), 0, keepdims=True)
    core = lax.axis_index("core")
    for ref, owner in ((kept_ref, core), (sent_ref, 1 - core)):
        extra = jnp.where(owner == 0, sums, diagonal)
        chunks = ref.shape[0]
        for index, lanes in slots(ref.shape, feat):
            at = pl.multiple_of(owner * (feat // 2) + index * chunks, 8)
            ref[:, 0, lanes] = packed[pl.ds(at, chunks), :]
        for chunk in range(chunks):
            part = extra[:, chunk * 128 : chunk * 128 + 128] if chunk < feat // 128 else jnp.zeros((1, 128), F32)
            ref[chunk, 0:1, ref.shape[2] - 128 :] = part


def slots(shape, feat):
    for index in range((shape[2] - 128) // feat):
        yield index, slice(index * feat, (index + 1) * feat)


def pack(feature, ahead_head, ahead_early, inst, lag, total, chips):
    vmem = pl.BlockSpec(memory_space=pltpu.VMEM)
    feat = inst.shape[0]
    share = jax.ShapeDtypeStruct((chips, 1, feat // 2 // chips * feat + 128), F32)
    return pl.pallas_call(
        pack_kernel,
        in_specs=[vmem] * 6,
        out_specs=(vmem, vmem),
        out_shape=(share, share),
        scratch_shapes=[pltpu.VMEM((feat, feat), F32)],
        compiler_params=pltpu.CompilerParams(vmem_limit_bytes=8 * MIB),
    )(feature, ahead_head, ahead_early, inst, lag, total)


def three_parts(x):
    high = x.astype(BF16)
    rest = x - high.astype(F32)
    middle = rest.astype(BF16)
    low = (rest - middle.astype(F32)).astype(BF16)
    return high, middle, low


def product(a, b):
    high, middle, low = three_parts(a)
    left = jnp.concatenate([high, high, middle, high, low, middle], 1)
    high, middle, low = three_parts(b)
    right = jnp.concatenate([high, middle, high, low, high, middle], 0)
    return jnp.dot(left, right, preferred_element_type=F32)


def eliminate(rows, columns, start):
    size = rows[0].shape[1]
    lane = lax.broadcasted_iota(jnp.int32, (8, size), 1) - start
    sub = lax.broadcasted_iota(jnp.int32, (8, size), 0)
    sub_narrow = lax.broadcasted_iota(jnp.int32, (8, 128), 0)
    tiles = range(len(rows))

    def wide(x):
        return jnp.concatenate([x] * (size // 128), 1)

    def spread(x, j):
        return jnp.broadcast_to(x[j : j + 1, :], x.shape)

    inside = (lane >= 0) & (lane < PANEL)
    rows = [jnp.where(inside, jnp.where(lane == sub + 8 * h, 1.0, 0.0), rows[h]) for h in tiles]
    pivots = [jnp.ones((8, 128), F32) for _ in tiles]
    pivot = spread(columns[0][0], 0)
    for j in range(PANEL):
        inverse = pl.reciprocal(pivot, approx=True)
        here, at = divmod(j, 8)
        pivots[here] = jnp.where(sub_narrow == at, pivot, pivots[here])
        if j + 1 == PANEL:
            break
        beside = {k: spread(columns[k][here], at) for k in range(j + 1, PANEL)}
        there, after = divmod(j + 1, 8)
        pivot = spread(columns[j + 1][there], after) - beside[j + 1] * beside[j + 1] * inverse
        panel_row = spread(rows[here], at)
        for h in tiles:
            if 8 * h + 7 <= j:
                continue
            factor = columns[j][h] * inverse
            if h == here:
                factor = jnp.where(sub_narrow > at, factor, 0.0)
            for k in range(j + 1, PANEL):
                columns[k][h] = columns[k][h] - factor * beside[k]
            rows[h] = rows[h] - wide(factor) * panel_row
    return [rows[h] * wide(lax.rsqrt(pivots[h])) for h in tiles]


def inverse_factor(work):
    size = work.shape[0]
    tiles = range(PANEL // 8)

    def step(index, carry):
        start = pl.multiple_of(index * PANEL, PANEL)
        panel = work[pl.ds(start, PANEL), :]
        near = pltpu.roll(panel, lax.rem(size - start, size), 1)
        columns = [
            [jnp.broadcast_to(near[8 * h : 8 * h + 8, k : k + 1], (8, 128)) for h in tiles]
            for k in range(PANEL)
        ]
        rows = eliminate([panel[8 * h : 8 * h + 8, :] for h in tiles], columns, start)
        panel = jnp.concatenate(rows, 0)
        high, middle, low = three_parts(panel)
        left = jnp.concatenate([high, high, middle, high, low, middle], 0)
        right = jnp.concatenate([high, middle, high, low, high, middle], 0)
        update = gram(left, right)
        row = lax.broadcasted_iota(jnp.int32, (size, size), 0)
        column = lax.broadcasted_iota(jnp.int32, (size, size), 1) - start
        old = work[...]
        rest = jnp.where((column >= 0) & (column < PANEL), 0.0, old) - update
        work[...] = jnp.where(row >= start + PANEL, rest, old)
        work[pl.ds(start, PANEL), :] = panel
        return carry

    lax.fori_loop(0, size // PANEL, step, 0)
    row = lax.broadcasted_iota(jnp.int32, (size, size), 0)
    column = lax.broadcasted_iota(jnp.int32, (size, size), 1)
    return jnp.where(column <= row, work[...], 0.0)


def koopman_kernel(
    scale_ref, mine_ref, other_ref, feature_ref, ahead_head_ref, ahead_early_ref, moved_out, residual_out,
    work, packed_ref, split_ref, shift_ref, moved, residual, sems,
):
    feat = packed_ref.shape[1]
    scale = scale_ref[0]
    core = lax.axis_index("core")
    extras = []
    for ref, owner in ((mine_ref, core), (other_ref, 1 - core)):
        chunks = ref.shape[0]
        for index, lanes in slots(ref.shape, feat):
            at = pl.multiple_of(owner * (feat // 2) + index * chunks, 8)
            packed_ref[pl.ds(at, chunks), :] = ref[:, 0, lanes]
        parts = [ref[chunk, 0:1, ref.shape[2] - 128 :] for chunk in range(feat // 128)]
        extras.append(jnp.concatenate(parts, 1))
    packed = packed_ref[...]
    mean = jnp.where(core == 0, extras[0], extras[1]) * scale
    diagonal = jnp.where(core == 0, extras[1], extras[0])
    row = lax.broadcasted_iota(jnp.int32, (feat, feat), 0)
    column = lax.broadcasted_iota(jnp.int32, (feat, feat), 1)
    turned = packed.T
    mean_column = jnp.broadcast_to(mean, (feat, feat)).T
    centre = mean_column * mean
    inst = jnp.where(column >= row, packed, turned)
    lag = jnp.where(column < row, packed, turned)
    lag = jnp.where(column == row, jnp.broadcast_to(diagonal, (feat, feat)), lag)
    work[...] = inst * scale - centre + jnp.where(column == row, RIDGE, 0.0)
    lag = lag * scale - centre
    inverse = inverse_factor(work)
    inverse_turned = inverse.T
    koopman = product(product(inverse, lag), inverse_turned)
    moved_turned = product(inverse_turned, koopman)
    for index, matrix in enumerate((inverse_turned, moved_turned)):
        high = matrix.astype(BF16)
        split_ref[index, :feat, :] = high
        split_ref[index, feat:, :] = (matrix - high.astype(F32)).astype(BF16)
        shift = jnp.sum(mean_column * matrix, 0, keepdims=True)
        shift_ref[index] = jnp.broadcast_to(shift, (8, feat))
    project_rows(
        feature_ref, ahead_head_ref, ahead_early_ref, split_ref, shift_ref, moved_out, residual_out, moved, residual, sems
    )


def project_rows(
    feature_ref, ahead_head_ref, ahead_early_ref, split_ref, shift_ref, moved_out, residual_out, moved, residual, sems
):
    rows = feature_ref.shape[0]
    at_end = lax.axis_index("tm") == lax.axis_size("tm") - 1

    def image(block, index):
        twice = jnp.concatenate([block, block], 1)
        return jnp.dot(twice, split_ref[index], preferred_element_type=F32) - shift_ref[index][0:1]

    copies = []
    for step in range(rows // CHUNK):
        here = slice(step * CHUNK, (step + 1) * CHUNK)
        start = step * CHUNK + LAG
        if start < rows:
            later = feature_ref[start : start + CHUNK, :]
        else:
            later = (ahead_head_ref if start == rows else ahead_early_ref)[...]
        now = image(feature_ref[here, :], 1)
        moved[here, :] = now
        gap = image(later, 0) - now
        residual[here, :] = gap if start < rows else jnp.where(at_end, 0.0, gap)
        for index, (source, target) in enumerate(((moved, moved_out), (residual, residual_out))):
            copy = pltpu.make_async_copy(source.at[here], target.at[here], sems.at[index, step])
            copy.start()
            copies.append(copy)
    for copy in copies:
        copy.wait()


def project(scale, mine, other, feature, ahead_head, ahead_early):
    rows, feat = feature.shape
    vmem = pl.BlockSpec(memory_space=pltpu.VMEM)
    hbm = pl.BlockSpec(memory_space=pltpu.HBM)
    out = jax.ShapeDtypeStruct((rows, feat), F32)
    return pl.pallas_call(
        koopman_kernel,
        in_specs=[pl.BlockSpec(memory_space=pltpu.SMEM)] + [vmem] * 5,
        out_specs=(hbm, hbm),
        out_shape=(out, out),
        scratch_shapes=[
            pltpu.VMEM((feat, feat), F32),
            pltpu.VMEM((feat, feat), F32),
            pltpu.VMEM((2, 2 * feat, feat), BF16),
            pltpu.VMEM((2, 8, feat), F32),
            pltpu.VMEM((rows, feat), F32),
            pltpu.VMEM((rows, feat), F32),
            pltpu.SemaphoreType.DMA((2, rows // CHUNK)),
        ],
        compiler_params=pltpu.CompilerParams(vmem_limit_bytes=32 * MIB),
    )(scale, mine, other, feature, ahead_head, ahead_early)


def summed(kept, sent):
    swap = [(0, 1), (1, 0)]
    chips = ("x", "tm")
    parts = kept + lax.ppermute(sent, "core", swap)
    mine = jnp.sum(lax.all_to_all(parts, chips, 0, 0, tiled=True), 0, keepdims=True)
    mine = lax.all_to_all(jnp.broadcast_to(mine, parts.shape), chips, 0, 0, tiled=True)
    return mine, lax.ppermute(mine, "core", swap)


def on_device(frames, first_weight, first_bias, second_weight):
    frame_block = frames[0]
    row_count, channels = frame_block.shape
    hid, feat = second_weight.shape[1:]
    weights = (
        first_weight.reshape(2 * channels, hid),
        first_bias.reshape(1, hid),
        second_weight.reshape(2 * hid, feat),
    )
    sent, near, *weights = tail_rows(frame_block, *weights)
    halo = passed_along(sent, "tm", 1)
    early, before = early_rows(near, *weights)
    ahead_early = passed_along(early, "tm", -1)
    middle, hidden, far = middle_rows(frame_block, near, before, *weights)
    head = head_rows(near, halo, *weights)
    ahead_head = passed_along(head, "tm", -1)
    feature = body(far, head, early, middle, hidden, *weights)
    inst, lag, total = moments(feature)
    chips = lax.axis_size("x") * lax.axis_size("tm")
    mine, other = summed(*pack(feature, ahead_head, ahead_early, inst, lag, total, chips))
    replicas = lax.axis_size("x") * lax.axis_size("core")
    pair_count = replicas * (row_count * lax.axis_size("tm") - LAG)
    scale = jnp.full((1,), 1.0 / (2.0 * pair_count), F32)
    propagated, residual = project(scale, mine, other, feature, ahead_head, ahead_early)
    return (propagated[None], residual[None])


def solution(mesh):
    replicas, blocks = mesh.devices.shape
    chips = Mesh(mesh.devices.reshape(replicas // 2, 2, blocks), ("x", "core", "tm"))
    split = P(("x", "core"), "tm", None)
    return jax.shard_map(
        on_device,
        mesh=chips,
        in_specs=(split, P(), P(), P()),
        out_specs=(split, split),
        check_vma=False,
    )
```

```python
import jax
import jax.numpy as jnp
from jax import lax
from jax.experimental import pallas as pl
from jax.experimental.pallas import tpu as pltpu
from jax.sharding import Mesh, PartitionSpec as P

D1 = 32
D2 = 256
LAG = 1024
RIDGE = 0.001
CHUNK = 512
EARLY = 1536
PANEL = 16
SUPER = 32
MIB = 1024 * 1024

F32 = jnp.float32
BF16 = jnp.bfloat16


def passed_along(value, axis, steps):
    count = lax.axis_size(axis)
    first, last = (max(0, -steps), min(count, count - steps))
    return lax.ppermute(value, axis, [(source, source + steps) for source in range(first, last)])


def gram(a, b):
    return lax.dot_general(a, b, (((0,), (0,)), ((), ())), preferred_element_type=F32)


def in_hbm(value):
    return pltpu.with_memory_space_constraint(value, pltpu.HBM)


def silu(x):
    half = 0.5 * x
    return half + half * jnp.tanh(half)


def hidden_rows(xs, at, rows, w1_ref, b1_ref):
    both = jnp.concatenate([xs[pl.ds(at + D1, rows), :], xs[pl.ds(at, rows), :]], 1)
    hid = w1_ref.shape[1]
    parts = []
    for lanes in (slice(0, hid // 2), slice(hid // 2, hid)):
        z = jnp.dot(both, w1_ref[:, lanes], preferred_element_type=F32)
        parts.append(silu(z + b1_ref[:, lanes]).astype(BF16))
    return jnp.concatenate(parts, 1)


def feature_rows(hs, at, rows, w2_ref):
    both = jnp.concatenate([hs[pl.ds(at + D2, rows), :], hs[pl.ds(at, rows), :]], 1)
    return jnp.dot(both, w2_ref[...], preferred_element_type=F32).astype(BF16)


def tail_kernel(frames_ref, w1_in, b1_in, w2_in, sent_ref, near_ref, w1_ref, b1_ref, w2_ref, xs, sems):
    rows = frames_ref.shape[0]
    pairs = (
        (frames_ref.at[pl.ds(rows - D1 - D2, D1 + D2)], xs),
        (w1_in, w1_ref),
        (b1_in, b1_ref),
        (w2_in, w2_ref),
        (frames_ref.at[pl.ds(0, LAG)], near_ref),
    )
    copies = [pltpu.make_async_copy(*pair, sems.at[index]) for index, pair in enumerate(pairs)]
    for copy in copies[:4]:
        copy.start()
    for copy in copies[:3]:
        copy.wait()
    copies[4].start()
    hidden = hidden_rows(xs, 0, D2, w1_ref, b1_ref)
    copies[3].wait()
    hid, feat = hidden.shape[1], w2_ref.shape[1]
    sent_ref[:D2, :] = jnp.dot(hidden, w2_ref[hid:, :], preferred_element_type=F32).astype(BF16)
    for index in range(xs.shape[1] // feat):
        part = slice(D2 + index * D1, D2 + (index + 1) * D1)
        sent_ref[part, :] = xs[D2:, index * feat : (index + 1) * feat]
    copies[4].wait()


def tail_rows(frames, w1, b1, w2):
    vmem = pl.BlockSpec(memory_space=pltpu.VMEM)
    hbm = pl.BlockSpec(memory_space=pltpu.HBM)
    channels, feat = frames.shape[1], w2.shape[1]
    sent = (D2 + D1 * channels // feat, feat)
    shapes = ((sent, BF16), ((LAG, channels), BF16), (w1.shape, BF16), (b1.shape, F32), (w2.shape, BF16))
    return pl.pallas_call(
        tail_kernel,
        in_specs=[hbm] * 4,
        out_specs=(vmem,) * 5,
        out_shape=tuple(jax.ShapeDtypeStruct(*shape) for shape in shapes),
        scratch_shapes=[pltpu.VMEM((D1 + D2, channels), BF16), pltpu.SemaphoreType.DMA((5,))],
        compiler_params=pltpu.CompilerParams(vmem_limit_bytes=12 * MIB),
    )(*(in_hbm(value) for value in (frames, w1, b1, w2)))


def early_kernel(near_ref, w1_ref, b1_ref, w2_ref, out_ref, hidden_ref, hs):
    half = LAG // 2
    for at in range(0, hs.shape[0], D2):
        hs[at : at + D2, :] = hidden_rows(near_ref, half - D1 - D2 + at, D2, w1_ref, b1_ref)
    out_ref[...] = feature_rows(hs, 0, half, w2_ref)
    hidden_ref[...] = hs[half:, :]


def early_rows(near, w1, b1, w2):
    vmem = pl.BlockSpec(memory_space=pltpu.VMEM)
    half, hid = LAG // 2, w1.shape[1]
    return pl.pallas_call(
        early_kernel,
        in_specs=[vmem] * 4,
        out_specs=(vmem, vmem),
        out_shape=(
            jax.ShapeDtypeStruct((half, w2.shape[1]), BF16),
            jax.ShapeDtypeStruct((D2, hid), BF16),
        ),
        scratch_shapes=[pltpu.VMEM((half + D2, hid), BF16)],
        compiler_params=pltpu.CompilerParams(vmem_limit_bytes=8 * MIB),
    )(near, w1, b1, w2)


def middle_kernel(
    frames_ref, near_ref, before_ref, w1_ref, b1_ref, w2_ref, middle_ref, hidden_ref, far_ref, xs, hs, sems
):
    rows = EARLY - LAG
    now = pltpu.make_async_copy(frames_ref.at[pl.ds(LAG, rows)], xs.at[pl.ds(D1, rows)], sems.at[0])
    later = pltpu.make_async_copy(
        frames_ref.at[pl.ds(EARLY - D1, far_ref.shape[0])], far_ref, sems.at[1]
    )
    now.start()
    later.start()
    xs[:D1, :] = near_ref[LAG - D1 :, :]
    hs[:D2, :] = before_ref[...]
    now.wait()
    for at in range(0, rows, D2):
        hs[D2 + at : 2 * D2 + at, :] = hidden_rows(xs, at, D2, w1_ref, b1_ref)
    middle_ref[...] = feature_rows(hs, 0, rows, w2_ref)
    hidden_ref[...] = hs[rows:, :]
    later.wait()


def middle_rows(frames, near, before, w1, b1, w2):
    vmem = pl.BlockSpec(memory_space=pltpu.VMEM)
    hbm = pl.BlockSpec(memory_space=pltpu.HBM)
    rows, channels = frames.shape
    hid, feat = w1.shape[1], w2.shape[1]
    shapes = ((EARLY - LAG, feat), (D2, hid), (rows - EARLY + D1, channels))
    return pl.pallas_call(
        middle_kernel,
        in_specs=[hbm] + [vmem] * 5,
        out_specs=(vmem,) * 3,
        out_shape=tuple(jax.ShapeDtypeStruct(shape, BF16) for shape in shapes),
        scratch_shapes=[
            pltpu.VMEM((EARLY - LAG + D1, channels), BF16),
            pltpu.VMEM((EARLY - LAG + D2, hid), BF16),
            pltpu.SemaphoreType.DMA((2,)),
        ],
        compiler_params=pltpu.CompilerParams(vmem_limit_bytes=12 * MIB),
    )(in_hbm(frames), near, before, w1, b1, w2)


def head_kernel(near_ref, halo_ref, w1_ref, b1_ref, w2_ref, out_ref, xs, hs):
    half = LAG // 2
    hid, feat = w1_ref.shape[1], w2_ref.shape[1]
    for index in range(xs.shape[1] // feat):
        part = slice(D2 + index * D1, D2 + (index + 1) * D1)
        xs[:D1, index * feat : (index + 1) * feat] = halo_ref[part, :]
    xs[D1:, :] = near_ref[:half, :]
    for at in range(0, half, D2):
        hs[at : at + D2, :] = hidden_rows(xs, at, D2, w1_ref, b1_ref)
    value = jnp.dot(hs[:D2, :], w2_ref[:hid, :], preferred_element_type=F32)
    out_ref[:D2, :] = (value + halo_ref[:D2, :].astype(F32)).astype(BF16)
    out_ref[D2:, :] = feature_rows(hs, 0, half - D2, w2_ref)


def head_rows(near, halo, w1, b1, w2):
    vmem = pl.BlockSpec(memory_space=pltpu.VMEM)
    half, channels, hid = LAG // 2, near.shape[1], w1.shape[1]
    return pl.pallas_call(
        head_kernel,
        in_specs=[vmem] * 5,
        out_specs=vmem,
        out_shape=jax.ShapeDtypeStruct((half, w2.shape[1]), BF16),
        scratch_shapes=[pltpu.VMEM((half + D1, channels), BF16), pltpu.VMEM((half, hid), BF16)],
        compiler_params=pltpu.CompilerParams(vmem_limit_bytes=8 * MIB),
    )(near, halo, w1, b1, w2)


def body_kernel(far_ref, head_ref, early_ref, middle_ref, hidden_ref, w1_ref, b1_ref, w2_ref, out_ref, hs):
    rows = out_ref.shape[0]
    steps = (rows - EARLY) // CHUNK
    half = LAG // 2
    hs[:D2, :] = hidden_ref[...]
    out_ref[:half, :] = head_ref[...]
    out_ref[half:LAG, :] = early_ref[...]
    out_ref[LAG:EARLY, :] = middle_ref[...]
    for step in range(steps + 1):
        at = step * CHUNK
        if step < steps:
            hs[D2 + at : D2 + at + CHUNK, :] = hidden_rows(far_ref, at, CHUNK, w1_ref, b1_ref)
        if step:
            out_ref[EARLY + at - CHUNK : EARLY + at, :] = feature_rows(hs, at - CHUNK, CHUNK, w2_ref)


def body(far, head, early, middle, hidden, w1, b1, w2):
    rows, hid, feat = far.shape[0] - D1 + EARLY, w1.shape[1], w2.shape[1]
    vmem = pl.BlockSpec(memory_space=pltpu.VMEM)
    return pl.pallas_call(
        body_kernel,
        in_specs=[vmem] * 8,
        out_specs=vmem,
        out_shape=jax.ShapeDtypeStruct((rows, feat), BF16),
        scratch_shapes=[pltpu.VMEM((rows - EARLY + D2, hid), BF16)],
        compiler_params=pltpu.CompilerParams(vmem_limit_bytes=16 * MIB),
    )(far, head, early, middle, hidden, w1, b1, w2)


def column_sum(rows):
    parts = rows.astype(F32).reshape(4, -1, 8, rows.shape[1])
    return jnp.sum(jnp.sum(parts, 1), 0)


def moment_kernel(feature_ref, inst, lag, total):
    rows, feat = feature_ref.shape
    tm_index, tm_last = lax.axis_index("tm"), lax.axis_size("tm") - 1
    for at in range(0, rows, LAG):
        weight = 2.0
        if at == 0:
            weight = jnp.where(tm_index == 0, 1.0, 2.0)
        elif at == rows - LAG:
            weight = jnp.where(tm_index == tm_last, 1.0, 2.0)
        now = feature_ref[at : at + LAG, :]
        if at == 0:
            inst[...] = weight * gram(now, now)
            total[...] = weight * column_sum(now)
            continue
        both = gram(now, jnp.concatenate([now, feature_ref[at - LAG : at, :]], 1))
        inst[...] += weight * both[:, :feat]
        lag[...] = both[:, feat:] if at == LAG else lag[...] + both[:, feat:]
        total[...] += weight * column_sum(now)


def moments(feature):
    feat = feature.shape[1]
    vmem = pl.BlockSpec(memory_space=pltpu.VMEM)
    square = jax.ShapeDtypeStruct((feat, feat), F32)
    return pl.pallas_call(
        moment_kernel,
        in_specs=[vmem],
        out_specs=(vmem,) * 3,
        out_shape=(square, square, jax.ShapeDtypeStruct((8, feat), F32)),
        compiler_params=pltpu.CompilerParams(vmem_limit_bytes=12 * MIB),
    )(feature)


def pack_kernel(feature_ref, ahead_head_ref, ahead_early_ref, inst, lag, total, kept_ref, sent_ref, packed):
    feat = inst.shape[0]
    half = LAG // 2
    edge = feature_ref.shape[0] - LAG
    cross = lag[...] + gram(ahead_head_ref[...], feature_ref[edge : edge + half, :])
    cross += gram(ahead_early_ref[...], feature_ref[edge + half :, :])
    both = cross + cross.T
    row = lax.broadcasted_iota(jnp.int32, (feat, feat), 0)
    column = lax.broadcasted_iota(jnp.int32, (feat, feat), 1)
    packed[...] = jnp.where(column >= row, inst[...], both)
    sums = jnp.sum(total[...], 0, keepdims=True)
    diagonal = jnp.sum(jnp.where(column == row, both, 0.0), 0, keepdims=True)
    core = lax.axis_index("core")
    for ref, owner in ((kept_ref, core), (sent_ref, 1 - core)):
        extra = jnp.where(owner == 0, sums, diagonal)
        chunks = ref.shape[0]
        for index, lanes in slots(ref.shape, feat):
            at = pl.multiple_of(owner * (feat // 2) + index * chunks, 8)
            ref[:, 0, lanes] = packed[pl.ds(at, chunks), :]
        for chunk in range(chunks):
            part = extra[:, chunk * 128 : chunk * 128 + 128] if chunk < feat // 128 else jnp.zeros((1, 128), F32)
            ref[chunk, 0:1, ref.shape[2] - 128 :] = part


def slots(shape, feat):
    for index in range((shape[2] - 128) // feat):
        yield index, slice(index * feat, (index + 1) * feat)


def pack(feature, ahead_head, ahead_early, inst, lag, total, chips):
    vmem = pl.BlockSpec(memory_space=pltpu.VMEM)
    feat = inst.shape[0]
    share = jax.ShapeDtypeStruct((chips, 1, feat // 2 // chips * feat + 128), F32)
    return pl.pallas_call(
        pack_kernel,
        in_specs=[vmem] * 6,
        out_specs=(vmem, vmem),
        out_shape=(share, share),
        scratch_shapes=[pltpu.VMEM((feat, feat), F32)],
        compiler_params=pltpu.CompilerParams(vmem_limit_bytes=8 * MIB),
    )(feature, ahead_head, ahead_early, inst, lag, total)


def three_parts(x):
    high = x.astype(BF16)
    rest = x - high.astype(F32)
    middle = rest.astype(BF16)
    low = (rest - middle.astype(F32)).astype(BF16)
    return high, middle, low


def product(a, b):
    high, middle, low = three_parts(a)
    left = jnp.concatenate([high, high, middle, high, low, middle], 1)
    high, middle, low = three_parts(b)
    right = jnp.concatenate([high, middle, high, low, high, middle], 0)
    return jnp.dot(left, right, preferred_element_type=F32)


def eliminate(rows, start, size):
    lane = lax.broadcasted_iota(jnp.int32, (8, size), 1) - start
    sub = lax.broadcasted_iota(jnp.int32, (8, size), 0)
    sub_narrow = lax.broadcasted_iota(jnp.int32, (8, 128), 0)
    tiles = range(len(rows))

    def wide(x):
        return jnp.concatenate([x] * (size // 128), 1)

    def spread(x, j):
        return jnp.broadcast_to(x[j : j + 1, :], x.shape)

    columns = [
        [jnp.broadcast_to(rows[h][:, start + k : start + k + 1], (8, 128)) for h in tiles]
        for k in range(PANEL)
    ]
    inside = (lane >= 0) & (lane < PANEL)
    rows = [jnp.where(inside, jnp.where(lane == sub + 8 * h, 1.0, 0.0), rows[h]) for h in tiles]
    pivots = [jnp.ones((8, 128), F32) for _ in range(PANEL // 8)]
    pivot = spread(columns[0][0], 0)
    for j in range(PANEL):
        inverse = pl.reciprocal(pivot, approx=True)
        here, at = divmod(j, 8)
        pivots[here] = jnp.where(sub_narrow == at, pivot, pivots[here])
        beside = {k: spread(columns[k][here], at) for k in range(j + 1, PANEL)}
        if beside:
            there, after = divmod(j + 1, 8)
            pivot = spread(columns[j + 1][there], after) - beside[j + 1] * beside[j + 1] * inverse
        panel_row = spread(rows[here], at)
        for h in tiles:
            if 8 * h + 7 <= j:
                continue
            factor = columns[j][h] * inverse
            if h == here:
                factor = jnp.where(sub_narrow > at, factor, 0.0)
            for k in beside:
                columns[k][h] = columns[k][h] - factor * beside[k]
            rows[h] = rows[h] - wide(factor) * panel_row
    return [rows[h] * wide(lax.rsqrt(pivots[h])) if h < len(pivots) else rows[h] for h in tiles]


def inverse_factor(work):
    size = work.shape[0]
    for start in range(0, size, SUPER):
        stop = start + SUPER
        rows = [work[at : at + 8, :] for at in range(start, stop, 8)]
        for at in range(0, SUPER, PANEL):
            rows[at // 8 :] = eliminate(rows[at // 8 :], start + at, size)
        row = lax.broadcasted_iota(jnp.int32, (SUPER, size), 0)
        column = lax.broadcasted_iota(jnp.int32, (SUPER, size), 1) - start
        panel = jnp.where((column > row) & (column < SUPER), 0.0, jnp.concatenate(rows, 0))
        work[start:stop, :] = panel
        if stop < size:
            high, middle, low = three_parts(panel)
            left = jnp.concatenate([high, high, middle, high, low, middle], 0)
            right = jnp.concatenate([high, middle, high, low, high, middle], 0)
            first = stop // 128 * 128
            update = gram(left[:, first:], right)
            kept = lax.broadcasted_iota(jnp.int32, (size - stop, size), 1)
            kept = (kept < start) | (kept >= stop)
            work[stop:, :] = jnp.where(kept, work[stop:, :], 0.0) - update[stop - first :]
    row = lax.broadcasted_iota(jnp.int32, (size, size), 0)
    column = lax.broadcasted_iota(jnp.int32, (size, size), 1)
    return jnp.where(column <= row, work[...], 0.0)


def koopman_kernel(
    scale_ref, mine_ref, other_ref, feature_ref, ahead_head_ref, ahead_early_ref, moved_out, residual_out,
    work, packed_ref, split_ref, shift_ref, moved, residual, sems,
):
    feat = packed_ref.shape[1]
    scale = scale_ref[0]
    core = lax.axis_index("core")
    extras = []
    for ref, owner in ((mine_ref, core), (other_ref, 1 - core)):
        chunks = ref.shape[0]
        for index, lanes in slots(ref.shape, feat):
            at = pl.multiple_of(owner * (feat // 2) + index * chunks, 8)
            packed_ref[pl.ds(at, chunks), :] = ref[:, 0, lanes]
        parts = [ref[chunk, 0:1, ref.shape[2] - 128 :] for chunk in range(feat // 128)]
        extras.append(jnp.concatenate(parts, 1))
    packed = packed_ref[...]
    mean = jnp.where(core == 0, extras[0], extras[1]) * scale
    diagonal = jnp.where(core == 0, extras[1], extras[0])
    row = lax.broadcasted_iota(jnp.int32, (feat, feat), 0)
    column = lax.broadcasted_iota(jnp.int32, (feat, feat), 1)
    turned = packed.T
    mean_column = jnp.broadcast_to(jnp.broadcast_to(mean, (8, feat)).T[:, 0:1], (feat, feat))
    centre = mean_column * mean
    inst = jnp.where(column >= row, packed, turned)
    lag = jnp.where(column < row, packed, turned)
    lag = jnp.where(column == row, jnp.broadcast_to(diagonal, (feat, feat)), lag)
    work[...] = inst * scale - centre + jnp.where(column == row, RIDGE, 0.0)
    lag = lag * scale - centre
    inverse = inverse_factor(work)
    inverse_turned = inverse.T
    koopman = product(product(inverse, lag), inverse_turned)
    moved_turned = product(inverse_turned, koopman)
    for index, matrix in enumerate((inverse_turned, moved_turned)):
        high = matrix.astype(BF16)
        split_ref[index, :feat, :] = high
        split_ref[index, feat:, :] = (matrix - high.astype(F32)).astype(BF16)
        shift = jnp.sum(mean_column * matrix, 0, keepdims=True)
        shift_ref[index] = jnp.broadcast_to(shift, (8, feat))
    project_rows(
        feature_ref, ahead_head_ref, ahead_early_ref, split_ref, shift_ref, moved_out, residual_out, moved, residual, sems
    )


def project_rows(
    feature_ref, ahead_head_ref, ahead_early_ref, split_ref, shift_ref, moved_out, residual_out, moved, residual, sems
):
    rows = feature_ref.shape[0]
    at_end = lax.axis_index("tm") == lax.axis_size("tm") - 1

    def image(block, index):
        twice = jnp.concatenate([block, block], 1)
        return jnp.dot(twice, split_ref[index], preferred_element_type=F32) - shift_ref[index][0:1]

    copies = []
    for step in range(rows // CHUNK):
        here = slice(step * CHUNK, (step + 1) * CHUNK)
        start = step * CHUNK + LAG
        if start < rows:
            later = feature_ref[start : start + CHUNK, :]
        else:
            later = (ahead_head_ref if start == rows else ahead_early_ref)[...]
        now = image(feature_ref[here, :], 1)
        moved[here, :] = now
        gap = image(later, 0) - now
        residual[here, :] = gap if start < rows else jnp.where(at_end, 0.0, gap)
        for index, (source, target) in enumerate(((moved, moved_out), (residual, residual_out))):
            copy = pltpu.make_async_copy(source.at[here], target.at[here], sems.at[index, step])
            copy.start()
            copies.append(copy)
    for copy in copies:
        copy.wait()


def project(scale, mine, other, feature, ahead_head, ahead_early):
    rows, feat = feature.shape
    vmem = pl.BlockSpec(memory_space=pltpu.VMEM)
    hbm = pl.BlockSpec(memory_space=pltpu.HBM)
    out = jax.ShapeDtypeStruct((rows, feat), F32)
    return pl.pallas_call(
        koopman_kernel,
        in_specs=[pl.BlockSpec(memory_space=pltpu.SMEM)] + [vmem] * 5,
        out_specs=(hbm, hbm),
        out_shape=(out, out),
        scratch_shapes=[
            pltpu.VMEM((feat, feat), F32),
            pltpu.VMEM((feat, feat), F32),
            pltpu.VMEM((2, 2 * feat, feat), BF16),
            pltpu.VMEM((2, 8, feat), F32),
            pltpu.VMEM((rows, feat), F32),
            pltpu.VMEM((rows, feat), F32),
            pltpu.SemaphoreType.DMA((2, rows // CHUNK)),
        ],
        compiler_params=pltpu.CompilerParams(vmem_limit_bytes=32 * MIB),
    )(scale, mine, other, feature, ahead_head, ahead_early)


def summed(kept, sent):
    swap = [(0, 1), (1, 0)]
    chips = ("x", "tm")
    parts = kept + lax.ppermute(sent, "core", swap)
    mine = jnp.sum(lax.all_to_all(parts, chips, 0, 0, tiled=True), 0, keepdims=True)
    mine = lax.all_to_all(jnp.broadcast_to(mine, parts.shape), chips, 0, 0, tiled=True)
    return mine, lax.ppermute(mine, "core", swap)


def on_device(frames, first_weight, first_bias, second_weight):
    frame_block = frames[0]
    row_count, channels = frame_block.shape
    hid, feat = second_weight.shape[1:]
    weights = (
        first_weight.reshape(2 * channels, hid),
        first_bias.reshape(1, hid),
        second_weight.reshape(2 * hid, feat),
    )
    sent, near, *weights = tail_rows(frame_block, *weights)
    halo = passed_along(sent, "tm", 1)
    early, before = early_rows(near, *weights)
    ahead_early = passed_along(early, "tm", -1)
    middle, hidden, far = middle_rows(frame_block, near, before, *weights)
    head = head_rows(near, halo, *weights)
    ahead_head = passed_along(head, "tm", -1)
    feature = body(far, head, early, middle, hidden, *weights)
    inst, lag, total = moments(feature)
    chips = lax.axis_size("x") * lax.axis_size("tm")
    mine, other = summed(*pack(feature, ahead_head, ahead_early, inst, lag, total, chips))
    replicas = lax.axis_size("x") * lax.axis_size("core")
    pair_count = replicas * (row_count * lax.axis_size("tm") - LAG)
    scale = jnp.full((1,), 1.0 / (2.0 * pair_count), F32)
    propagated, residual = project(scale, mine, other, feature, ahead_head, ahead_early)
    return (propagated[None], residual[None])


def solution(mesh):
    replicas, blocks = mesh.devices.shape
    chips = Mesh(mesh.devices.reshape(replicas // 2, 2, blocks), ("x", "core", "tm"))
    split = P(("x", "core"), "tm", None)
    return jax.shard_map(
        on_device,
        mesh=chips,
        in_specs=(split, P(), P(), P()),
        out_specs=(split, split),
        check_vma=False,
    )
```

```python
import jax
import jax.numpy as jnp
from jax import lax
from jax.experimental import pallas as pl
from jax.experimental.pallas import tpu as pltpu
from jax.sharding import Mesh, PartitionSpec as P

D1 = 32
D2 = 256
LAG = 1024
RIDGE = 0.001
CHUNK = 512
EARLY = 1536
PANEL = 8
SUPER = 32
MIB = 1024 * 1024

F32 = jnp.float32
BF16 = jnp.bfloat16


def passed_along(value, axis, steps):
    count = lax.axis_size(axis)
    first, last = (max(0, -steps), min(count, count - steps))
    return lax.ppermute(value, axis, [(source, source + steps) for source in range(first, last)])


def gram(a, b):
    return lax.dot_general(a, b, (((0,), (0,)), ((), ())), preferred_element_type=F32)


def in_hbm(value):
    return pltpu.with_memory_space_constraint(value, pltpu.HBM)


def silu(x):
    half = 0.5 * x
    return half + half * jnp.tanh(half)


def hidden_rows(xs, at, rows, w1_ref, b1_ref):
    both = jnp.concatenate([xs[pl.ds(at + D1, rows), :], xs[pl.ds(at, rows), :]], 1)
    hid = w1_ref.shape[1]
    parts = []
    for lanes in (slice(0, hid // 2), slice(hid // 2, hid)):
        z = jnp.dot(both, w1_ref[:, lanes], preferred_element_type=F32)
        parts.append(silu(z + b1_ref[:, lanes]).astype(BF16))
    return jnp.concatenate(parts, 1)


def feature_rows(hs, at, rows, w2_ref):
    both = jnp.concatenate([hs[pl.ds(at + D2, rows), :], hs[pl.ds(at, rows), :]], 1)
    return jnp.dot(both, w2_ref[...], preferred_element_type=F32).astype(BF16)


def tail_kernel(frames_ref, w1_in, b1_in, w2_in, sent_ref, near_ref, w1_ref, b1_ref, w2_ref, xs, sems):
    rows = frames_ref.shape[0]
    taps = w1_in.shape[0] // 2
    pairs = (
        (frames_ref.at[pl.ds(rows - D1 - D2, D1 + D2)], xs),
        (w1_in.at[pl.ds(0, taps)], w1_ref.at[pl.ds(0, taps)]),
        (w1_in.at[pl.ds(taps, taps)], w1_ref.at[pl.ds(taps, taps)]),
        (b1_in, b1_ref),
        (w2_in, w2_ref),
        (frames_ref.at[pl.ds(0, LAG)], near_ref),
    )
    copies = [pltpu.make_async_copy(*pair, sems.at[index]) for index, pair in enumerate(pairs)]
    for copy in copies:
        copy.start()
    for copy in copies[:4]:
        copy.wait()
    hidden = hidden_rows(xs, 0, D2, w1_ref, b1_ref)
    copies[4].wait()
    hid, feat = hidden.shape[1], w2_ref.shape[1]
    sent_ref[:D2, :] = jnp.dot(hidden, w2_ref[hid:, :], preferred_element_type=F32).astype(BF16)
    for index in range(xs.shape[1] // feat):
        part = slice(D2 + index * D1, D2 + (index + 1) * D1)
        sent_ref[part, :] = xs[D2:, index * feat : (index + 1) * feat]
    copies[5].wait()


def tail_rows(frames, w1, b1, w2):
    vmem = pl.BlockSpec(memory_space=pltpu.VMEM)
    hbm = pl.BlockSpec(memory_space=pltpu.HBM)
    channels, feat = frames.shape[1], w2.shape[1]
    sent = (D2 + D1 * channels // feat, feat)
    shapes = ((sent, BF16), ((LAG, channels), BF16), (w1.shape, BF16), (b1.shape, F32), (w2.shape, BF16))
    return pl.pallas_call(
        tail_kernel,
        in_specs=[hbm] * 4,
        out_specs=(vmem,) * 5,
        out_shape=tuple(jax.ShapeDtypeStruct(*shape) for shape in shapes),
        scratch_shapes=[pltpu.VMEM((D1 + D2, channels), BF16), pltpu.SemaphoreType.DMA((6,))],
        compiler_params=pltpu.CompilerParams(vmem_limit_bytes=12 * MIB),
    )(*(in_hbm(value) for value in (frames, w1, b1, w2)))


def early_kernel(near_ref, w1_ref, b1_ref, w2_ref, out_ref, hidden_ref, hs):
    half = LAG // 2
    for at in range(0, hs.shape[0], D2):
        hs[at : at + D2, :] = hidden_rows(near_ref, half - D1 - D2 + at, D2, w1_ref, b1_ref)
    out_ref[...] = feature_rows(hs, 0, half, w2_ref)
    hidden_ref[...] = hs[half:, :]


def early_rows(near, w1, b1, w2):
    vmem = pl.BlockSpec(memory_space=pltpu.VMEM)
    half, hid = LAG // 2, w1.shape[1]
    return pl.pallas_call(
        early_kernel,
        in_specs=[vmem] * 4,
        out_specs=(vmem, vmem),
        out_shape=(
            jax.ShapeDtypeStruct((half, w2.shape[1]), BF16),
            jax.ShapeDtypeStruct((D2, hid), BF16),
        ),
        scratch_shapes=[pltpu.VMEM((half + D2, hid), BF16)],
        compiler_params=pltpu.CompilerParams(vmem_limit_bytes=8 * MIB),
    )(near, w1, b1, w2)


def middle_kernel(
    frames_ref, near_ref, before_ref, w1_ref, b1_ref, w2_ref, middle_ref, hidden_ref, far_ref, xs, hs, sems
):
    rows = EARLY - LAG
    now = pltpu.make_async_copy(frames_ref.at[pl.ds(LAG, rows)], xs.at[pl.ds(D1, rows)], sems.at[0])
    later = pltpu.make_async_copy(
        frames_ref.at[pl.ds(EARLY - D1, far_ref.shape[0])], far_ref, sems.at[1]
    )
    now.start()
    later.start()
    xs[:D1, :] = near_ref[LAG - D1 :, :]
    hs[:D2, :] = before_ref[...]
    now.wait()
    for at in range(0, rows, D2):
        hs[D2 + at : 2 * D2 + at, :] = hidden_rows(xs, at, D2, w1_ref, b1_ref)
    middle_ref[...] = feature_rows(hs, 0, rows, w2_ref)
    hidden_ref[...] = hs[rows:, :]
    later.wait()


def middle_rows(frames, near, before, w1, b1, w2):
    vmem = pl.BlockSpec(memory_space=pltpu.VMEM)
    hbm = pl.BlockSpec(memory_space=pltpu.HBM)
    rows, channels = frames.shape
    hid, feat = w1.shape[1], w2.shape[1]
    shapes = ((EARLY - LAG, feat), (D2, hid), (rows - EARLY + D1, channels))
    return pl.pallas_call(
        middle_kernel,
        in_specs=[hbm] + [vmem] * 5,
        out_specs=(vmem,) * 3,
        out_shape=tuple(jax.ShapeDtypeStruct(shape, BF16) for shape in shapes),
        scratch_shapes=[
            pltpu.VMEM((EARLY - LAG + D1, channels), BF16),
            pltpu.VMEM((EARLY - LAG + D2, hid), BF16),
            pltpu.SemaphoreType.DMA((2,)),
        ],
        compiler_params=pltpu.CompilerParams(vmem_limit_bytes=12 * MIB),
    )(in_hbm(frames), near, before, w1, b1, w2)


def head_kernel(near_ref, halo_ref, w1_ref, b1_ref, w2_ref, out_ref, xs, hs):
    half = LAG // 2
    hid, feat = w1_ref.shape[1], w2_ref.shape[1]
    for index in range(xs.shape[1] // feat):
        part = slice(D2 + index * D1, D2 + (index + 1) * D1)
        xs[:D1, index * feat : (index + 1) * feat] = halo_ref[part, :]
    xs[D1:, :] = near_ref[:half, :]
    for at in range(0, half, D2):
        hs[at : at + D2, :] = hidden_rows(xs, at, D2, w1_ref, b1_ref)
    value = jnp.dot(hs[:D2, :], w2_ref[:hid, :], preferred_element_type=F32)
    out_ref[:D2, :] = (value + halo_ref[:D2, :].astype(F32)).astype(BF16)
    out_ref[D2:, :] = feature_rows(hs, 0, half - D2, w2_ref)


def head_rows(near, halo, w1, b1, w2):
    vmem = pl.BlockSpec(memory_space=pltpu.VMEM)
    half, channels, hid = LAG // 2, near.shape[1], w1.shape[1]
    return pl.pallas_call(
        head_kernel,
        in_specs=[vmem] * 5,
        out_specs=vmem,
        out_shape=jax.ShapeDtypeStruct((half, w2.shape[1]), BF16),
        scratch_shapes=[pltpu.VMEM((half + D1, channels), BF16), pltpu.VMEM((half, hid), BF16)],
        compiler_params=pltpu.CompilerParams(vmem_limit_bytes=8 * MIB),
    )(near, halo, w1, b1, w2)


def body_kernel(far_ref, head_ref, early_ref, middle_ref, hidden_ref, w1_ref, b1_ref, w2_ref, out_ref, hs):
    rows = out_ref.shape[0]
    steps = (rows - EARLY) // CHUNK
    half = LAG // 2
    hs[:D2, :] = hidden_ref[...]
    out_ref[:half, :] = head_ref[...]
    out_ref[half:LAG, :] = early_ref[...]
    out_ref[LAG:EARLY, :] = middle_ref[...]
    for step in range(steps + 1):
        at = step * CHUNK
        if step < steps:
            hs[D2 + at : D2 + at + CHUNK, :] = hidden_rows(far_ref, at, CHUNK, w1_ref, b1_ref)
        if step:
            out_ref[EARLY + at - CHUNK : EARLY + at, :] = feature_rows(hs, at - CHUNK, CHUNK, w2_ref)


def body(far, head, early, middle, hidden, w1, b1, w2):
    rows, hid, feat = far.shape[0] - D1 + EARLY, w1.shape[1], w2.shape[1]
    vmem = pl.BlockSpec(memory_space=pltpu.VMEM)
    return pl.pallas_call(
        body_kernel,
        in_specs=[vmem] * 8,
        out_specs=vmem,
        out_shape=jax.ShapeDtypeStruct((rows, feat), BF16),
        scratch_shapes=[pltpu.VMEM((rows - EARLY + D2, hid), BF16)],
        compiler_params=pltpu.CompilerParams(vmem_limit_bytes=16 * MIB),
    )(far, head, early, middle, hidden, w1, b1, w2)


def column_sum(rows):
    parts = rows.astype(F32).reshape(4, -1, 8, rows.shape[1])
    return jnp.sum(jnp.sum(parts, 1), 0)


def moment_kernel(feature_ref, inst, lag, total):
    rows, feat = feature_ref.shape
    tm_index, tm_last = lax.axis_index("tm"), lax.axis_size("tm") - 1
    for at in range(0, rows, LAG):
        weight = 2.0
        if at == 0:
            weight = jnp.where(tm_index == 0, 1.0, 2.0)
        elif at == rows - LAG:
            weight = jnp.where(tm_index == tm_last, 1.0, 2.0)
        now = feature_ref[at : at + LAG, :]
        if at == 0:
            inst[...] = weight * gram(now, now)
            total[...] = weight * column_sum(now)
            continue
        both = gram(now, jnp.concatenate([now, feature_ref[at - LAG : at, :]], 1))
        inst[...] += weight * both[:, :feat]
        lag[...] = both[:, feat:] if at == LAG else lag[...] + both[:, feat:]
        total[...] += weight * column_sum(now)


def moments(feature):
    feat = feature.shape[1]
    vmem = pl.BlockSpec(memory_space=pltpu.VMEM)
    square = jax.ShapeDtypeStruct((feat, feat), F32)
    return pl.pallas_call(
        moment_kernel,
        in_specs=[vmem],
        out_specs=(vmem,) * 3,
        out_shape=(square, square, jax.ShapeDtypeStruct((8, feat), F32)),
        compiler_params=pltpu.CompilerParams(vmem_limit_bytes=12 * MIB),
    )(feature)


def pack_kernel(feature_ref, ahead_head_ref, ahead_early_ref, inst, lag, total, kept_ref, sent_ref, packed):
    feat = inst.shape[0]
    half = LAG // 2
    edge = feature_ref.shape[0] - LAG
    cross = lag[...] + gram(ahead_head_ref[...], feature_ref[edge : edge + half, :])
    cross += gram(ahead_early_ref[...], feature_ref[edge + half :, :])
    both = cross + cross.T
    row = lax.broadcasted_iota(jnp.int32, (feat, feat), 0)
    column = lax.broadcasted_iota(jnp.int32, (feat, feat), 1)
    packed[...] = jnp.where(column >= row, inst[...], both)
    sums = jnp.sum(total[...], 0, keepdims=True)
    diagonal = jnp.sum(jnp.where(column == row, both, 0.0), 0, keepdims=True)
    core = lax.axis_index("core")
    for ref, owner in ((kept_ref, core), (sent_ref, 1 - core)):
        extra = jnp.where(owner == 0, sums, diagonal)
        chunks = ref.shape[0]
        for index, lanes in slots(ref.shape, feat):
            at = pl.multiple_of(owner * (feat // 2) + index * chunks, 8)
            ref[:, 0, lanes] = packed[pl.ds(at, chunks), :]
        for chunk in range(chunks):
            part = extra[:, chunk * 128 : chunk * 128 + 128] if chunk < feat // 128 else jnp.zeros((1, 128), F32)
            ref[chunk, 0:1, ref.shape[2] - 128 :] = part


def slots(shape, feat):
    for index in range((shape[2] - 128) // feat):
        yield index, slice(index * feat, (index + 1) * feat)


def pack(feature, ahead_head, ahead_early, inst, lag, total, chips):
    vmem = pl.BlockSpec(memory_space=pltpu.VMEM)
    feat = inst.shape[0]
    share = jax.ShapeDtypeStruct((chips, 1, feat // 2 // chips * feat + 128), F32)
    return pl.pallas_call(
        pack_kernel,
        in_specs=[vmem] * 6,
        out_specs=(vmem, vmem),
        out_shape=(share, share),
        scratch_shapes=[pltpu.VMEM((feat, feat), F32)],
        compiler_params=pltpu.CompilerParams(vmem_limit_bytes=8 * MIB),
    )(feature, ahead_head, ahead_early, inst, lag, total)


def three_parts(x):
    high = x.astype(BF16)
    rest = x - high.astype(F32)
    middle = rest.astype(BF16)
    low = (rest - middle.astype(F32)).astype(BF16)
    return high, middle, low


def product(a, b):
    high, middle, low = three_parts(a)
    left = jnp.concatenate([high, high, middle, high, low, middle], 1)
    high, middle, low = three_parts(b)
    right = jnp.concatenate([high, middle, high, low, high, middle], 0)
    return jnp.dot(left, right, preferred_element_type=F32)


def eliminate(rows, start, size):
    lane = lax.broadcasted_iota(jnp.int32, (8, size), 1) - start
    sub = lax.broadcasted_iota(jnp.int32, (8, size), 0)
    sub_narrow = lax.broadcasted_iota(jnp.int32, (8, 128), 0)
    tiles = range(len(rows))

    def wide(x):
        return jnp.concatenate([x] * (size // 128), 1)

    def spread(x, j):
        return jnp.broadcast_to(x[j : j + 1, :], x.shape)

    columns = [
        [jnp.broadcast_to(rows[h][:, start + k : start + k + 1], (8, 128)) for h in tiles]
        for k in range(PANEL)
    ]
    inside = (lane >= 0) & (lane < PANEL)
    rows = [jnp.where(inside, jnp.where(lane == sub + 8 * h, 1.0, 0.0), rows[h]) for h in tiles]
    pivots = [jnp.ones((8, 128), F32) for _ in range(PANEL // 8)]
    pivot = spread(columns[0][0], 0)
    for j in range(PANEL):
        inverse = pl.reciprocal(pivot, approx=True)
        here, at = divmod(j, 8)
        pivots[here] = jnp.where(sub_narrow == at, pivot, pivots[here])
        beside = {k: spread(columns[k][here], at) for k in range(j + 1, PANEL)}
        if beside:
            there, after = divmod(j + 1, 8)
            pivot = spread(columns[j + 1][there], after) - beside[j + 1] * beside[j + 1] * inverse
        panel_row = spread(rows[here], at)
        for h in tiles:
            if 8 * h + 7 <= j:
                continue
            factor = columns[j][h] * inverse
            if h == here:
                factor = jnp.where(sub_narrow > at, factor, 0.0)
            for k in beside:
                columns[k][h] = columns[k][h] - factor * beside[k]
            rows[h] = rows[h] - wide(factor) * panel_row
    return [rows[h] * wide(lax.rsqrt(pivots[h])) if h < len(pivots) else rows[h] for h in tiles]


def inverse_factor(work):
    size = work.shape[0]
    for start in range(0, size, SUPER):
        stop = start + SUPER
        rows = [work[at : at + 8, :] for at in range(start, stop, 8)]
        for at in range(0, SUPER, PANEL):
            rows[at // 8 :] = eliminate(rows[at // 8 :], start + at, size)
        row = lax.broadcasted_iota(jnp.int32, (SUPER, size), 0)
        column = lax.broadcasted_iota(jnp.int32, (SUPER, size), 1) - start
        panel = jnp.where((column > row) & (column < SUPER), 0.0, jnp.concatenate(rows, 0))
        work[start:stop, :] = panel
        if stop < size:
            high, middle, low = three_parts(panel)
            left = jnp.concatenate([high, high, middle, high, low, middle], 0)
            right = jnp.concatenate([high, middle, high, low, high, middle], 0)
            first = stop // 128 * 128
            update = gram(left[:, first:], right)
            for at in range(0, size, 128):
                lanes = slice(at, at + 128)
                old = work[stop:, lanes]
                if at <= start < at + 128:
                    place = lax.broadcasted_iota(jnp.int32, old.shape, 1) + at
                    old = jnp.where((place < start) | (place >= stop), old, 0.0)
                work[stop:, lanes] = old - update[stop - first :, lanes]
    row = lax.broadcasted_iota(jnp.int32, (size, size), 0)
    column = lax.broadcasted_iota(jnp.int32, (size, size), 1)
    return jnp.where(column <= row, work[...], 0.0)


def koopman_kernel(
    scale_ref, mine_ref, other_ref, feature_ref, ahead_head_ref, ahead_early_ref, moved_out, residual_out,
    work, packed_ref, split_ref, shift_ref, moved, residual, sems,
):
    feat = packed_ref.shape[1]
    scale = scale_ref[0]
    core = lax.axis_index("core")
    extras = []
    for ref, owner in ((mine_ref, core), (other_ref, 1 - core)):
        chunks = ref.shape[0]
        for index, lanes in slots(ref.shape, feat):
            at = pl.multiple_of(owner * (feat // 2) + index * chunks, 8)
            packed_ref[pl.ds(at, chunks), :] = ref[:, 0, lanes]
        parts = [ref[chunk, 0:1, ref.shape[2] - 128 :] for chunk in range(feat // 128)]
        extras.append(jnp.concatenate(parts, 1))
    packed = packed_ref[...]
    mean = jnp.where(core == 0, extras[0], extras[1]) * scale
    diagonal = jnp.where(core == 0, extras[1], extras[0])
    row = lax.broadcasted_iota(jnp.int32, (feat, feat), 0)
    column = lax.broadcasted_iota(jnp.int32, (feat, feat), 1)
    turned = packed.T
    mean_column = jnp.broadcast_to(jnp.broadcast_to(mean, (8, feat)).T[:, 0:1], (feat, feat))
    centre = mean_column * mean
    inst = jnp.where(column >= row, packed, turned)
    lag = jnp.where(column < row, packed, turned)
    lag = jnp.where(column == row, jnp.broadcast_to(diagonal, (feat, feat)), lag)
    work[...] = inst * scale - centre + jnp.where(column == row, RIDGE, 0.0)
    lag = lag * scale - centre
    inverse = inverse_factor(work)
    inverse_turned = inverse.T
    koopman = product(product(inverse, lag), inverse_turned)
    moved_turned = product(inverse_turned, koopman)
    for index, matrix in enumerate((inverse_turned, moved_turned)):
        high = matrix.astype(BF16)
        split_ref[index, :feat, :] = high
        split_ref[index, feat:, :] = (matrix - high.astype(F32)).astype(BF16)
        shift = jnp.sum(mean_column * matrix, 0, keepdims=True)
        shift_ref[index] = jnp.broadcast_to(shift, (8, feat))
    project_rows(
        feature_ref, ahead_head_ref, ahead_early_ref, split_ref, shift_ref, moved_out, residual_out, moved, residual, sems
    )


def project_rows(
    feature_ref, ahead_head_ref, ahead_early_ref, split_ref, shift_ref, moved_out, residual_out, moved, residual, sems
):
    rows = feature_ref.shape[0]
    at_end = lax.axis_index("tm") == lax.axis_size("tm") - 1

    def image(block, index):
        twice = jnp.concatenate([block, block], 1)
        return jnp.dot(twice, split_ref[index], preferred_element_type=F32) - shift_ref[index][0:1]

    copies = []
    for step in range(rows // CHUNK):
        here = slice(step * CHUNK, (step + 1) * CHUNK)
        start = step * CHUNK + LAG
        if start < rows:
            later = feature_ref[start : start + CHUNK, :]
        else:
            later = (ahead_head_ref if start == rows else ahead_early_ref)[...]
        now = image(feature_ref[here, :], 1)
        moved[here, :] = now
        gap = image(later, 0) - now
        residual[here, :] = gap if start < rows else jnp.where(at_end, 0.0, gap)
        for index, (source, target) in enumerate(((moved, moved_out), (residual, residual_out))):
            copy = pltpu.make_async_copy(source.at[here], target.at[here], sems.at[index, step])
            copy.start()
            copies.append(copy)
    for copy in copies:
        copy.wait()


def project(scale, mine, other, feature, ahead_head, ahead_early):
    rows, feat = feature.shape
    vmem = pl.BlockSpec(memory_space=pltpu.VMEM)
    hbm = pl.BlockSpec(memory_space=pltpu.HBM)
    out = jax.ShapeDtypeStruct((rows, feat), F32)
    return pl.pallas_call(
        koopman_kernel,
        in_specs=[pl.BlockSpec(memory_space=pltpu.SMEM)] + [vmem] * 5,
        out_specs=(hbm, hbm),
        out_shape=(out, out),
        scratch_shapes=[
            pltpu.VMEM((feat, feat), F32),
            pltpu.VMEM((feat, feat), F32),
            pltpu.VMEM((2, 2 * feat, feat), BF16),
            pltpu.VMEM((2, 8, feat), F32),
            pltpu.VMEM((rows, feat), F32),
            pltpu.VMEM((rows, feat), F32),
            pltpu.SemaphoreType.DMA((2, rows // CHUNK)),
        ],
        compiler_params=pltpu.CompilerParams(vmem_limit_bytes=32 * MIB),
    )(scale, mine, other, feature, ahead_head, ahead_early)


def summed(kept, sent):
    swap = [(0, 1), (1, 0)]
    chips = ("x", "tm")
    parts = kept + lax.ppermute(sent, "core", swap)
    mine = jnp.sum(lax.all_to_all(parts, chips, 0, 0, tiled=True), 0, keepdims=True)
    mine = lax.all_to_all(jnp.broadcast_to(mine, parts.shape), chips, 0, 0, tiled=True)
    return mine, lax.ppermute(mine, "core", swap)


def on_device(frames, first_weight, first_bias, second_weight):
    frame_block = frames[0]
    row_count, channels = frame_block.shape
    hid, feat = second_weight.shape[1:]
    weights = (
        first_weight.reshape(2 * channels, hid),
        first_bias.reshape(1, hid),
        second_weight.reshape(2 * hid, feat),
    )
    sent, near, *weights = tail_rows(frame_block, *weights)
    halo = passed_along(sent, "tm", 1)
    early, before = early_rows(near, *weights)
    ahead_early = passed_along(early, "tm", -1)
    middle, hidden, far = middle_rows(frame_block, near, before, *weights)
    head = head_rows(near, halo, *weights)
    ahead_head = passed_along(head, "tm", -1)
    feature = body(far, head, early, middle, hidden, *weights)
    inst, lag, total = moments(feature)
    chips = lax.axis_size("x") * lax.axis_size("tm")
    mine, other = summed(*pack(feature, ahead_head, ahead_early, inst, lag, total, chips))
    replicas = lax.axis_size("x") * lax.axis_size("core")
    pair_count = replicas * (row_count * lax.axis_size("tm") - LAG)
    scale = jnp.full((1,), 1.0 / (2.0 * pair_count), F32)
    propagated, residual = project(scale, mine, other, feature, ahead_head, ahead_early)
    return (propagated[None], residual[None])


def solution(mesh):
    replicas, blocks = mesh.devices.shape
    chips = Mesh(mesh.devices.reshape(replicas // 2, 2, blocks), ("x", "core", "tm"))
    split = P(("x", "core"), "tm", None)
    return jax.shard_map(
        on_device,
        mesh=chips,
        in_specs=(split, P(), P(), P()),
        out_specs=(split, split),
        check_vma=False,
    )
```

```python
import jax
import jax.numpy as jnp
from jax import lax
from jax.experimental import pallas as pl
from jax.experimental.pallas import tpu as pltpu
from jax.sharding import Mesh, PartitionSpec as P

D1 = 32
D2 = 256
LAG = 1024
RIDGE = 0.001
CHUNK = 512
EARLY = 1536
PANEL = 16
SUPER = 32
MIB = 1024 * 1024

F32 = jnp.float32
BF16 = jnp.bfloat16


def passed_along(value, axis, steps):
    count = lax.axis_size(axis)
    first, last = (max(0, -steps), min(count, count - steps))
    return lax.ppermute(value, axis, [(source, source + steps) for source in range(first, last)])


def gram(a, b):
    return lax.dot_general(a, b, (((0,), (0,)), ((), ())), preferred_element_type=F32)


def in_hbm(value):
    return pltpu.with_memory_space_constraint(value, pltpu.HBM)


def silu(x):
    half = 0.5 * x
    return half + half * jnp.tanh(half)


def hidden_rows(xs, at, rows, w1_ref, b1_ref):
    both = jnp.concatenate([xs[pl.ds(at + D1, rows), :], xs[pl.ds(at, rows), :]], 1)
    hid = w1_ref.shape[1]
    parts = []
    for lanes in (slice(0, hid // 2), slice(hid // 2, hid)):
        z = jnp.dot(both, w1_ref[:, lanes], preferred_element_type=F32)
        parts.append(silu(z + b1_ref[:, lanes]).astype(BF16))
    return jnp.concatenate(parts, 1)


def feature_rows(hs, at, rows, w2_ref):
    both = jnp.concatenate([hs[pl.ds(at + D2, rows), :], hs[pl.ds(at, rows), :]], 1)
    return jnp.dot(both, w2_ref[...], preferred_element_type=F32).astype(BF16)


def tail_kernel(frames_ref, w1_in, b1_in, w2_in, sent_ref, near_ref, w1_ref, b1_ref, w2_ref, xs, sems):
    rows = frames_ref.shape[0]
    taps = w1_in.shape[0] // 2
    pairs = (
        (frames_ref.at[pl.ds(rows - D1 - D2, D1 + D2)], xs),
        (w1_in.at[pl.ds(0, taps)], w1_ref.at[pl.ds(0, taps)]),
        (w1_in.at[pl.ds(taps, taps)], w1_ref.at[pl.ds(taps, taps)]),
        (b1_in, b1_ref),
        (w2_in, w2_ref),
        (frames_ref.at[pl.ds(0, LAG)], near_ref),
    )
    copies = [pltpu.make_async_copy(*pair, sems.at[index]) for index, pair in enumerate(pairs)]
    for copy in copies:
        copy.start()
    for copy in copies[:4]:
        copy.wait()
    hidden = hidden_rows(xs, 0, D2, w1_ref, b1_ref)
    copies[4].wait()
    hid, feat = hidden.shape[1], w2_ref.shape[1]
    sent_ref[:D2, :] = jnp.dot(hidden, w2_ref[hid:, :], preferred_element_type=F32).astype(BF16)
    for index in range(xs.shape[1] // feat):
        part = slice(D2 + index * D1, D2 + (index + 1) * D1)
        sent_ref[part, :] = xs[D2:, index * feat : (index + 1) * feat]
    copies[5].wait()


def tail_rows(frames, w1, b1, w2):
    vmem = pl.BlockSpec(memory_space=pltpu.VMEM)
    hbm = pl.BlockSpec(memory_space=pltpu.HBM)
    channels, feat = frames.shape[1], w2.shape[1]
    sent = (D2 + D1 * channels // feat, feat)
    shapes = ((sent, BF16), ((LAG, channels), BF16), (w1.shape, BF16), (b1.shape, F32), (w2.shape, BF16))
    return pl.pallas_call(
        tail_kernel,
        in_specs=[hbm] * 4,
        out_specs=(vmem,) * 5,
        out_shape=tuple(jax.ShapeDtypeStruct(*shape) for shape in shapes),
        scratch_shapes=[pltpu.VMEM((D1 + D2, channels), BF16), pltpu.SemaphoreType.DMA((6,))],
        compiler_params=pltpu.CompilerParams(vmem_limit_bytes=12 * MIB),
    )(*(in_hbm(value) for value in (frames, w1, b1, w2)))


def early_kernel(near_ref, w1_ref, b1_ref, w2_ref, out_ref, hidden_ref, hs):
    half = LAG // 2
    for at in range(0, hs.shape[0], D2):
        hs[at : at + D2, :] = hidden_rows(near_ref, half - D1 - D2 + at, D2, w1_ref, b1_ref)
    out_ref[...] = feature_rows(hs, 0, half, w2_ref)
    hidden_ref[...] = hs[half:, :]


def early_rows(near, w1, b1, w2):
    vmem = pl.BlockSpec(memory_space=pltpu.VMEM)
    half, hid = LAG // 2, w1.shape[1]
    return pl.pallas_call(
        early_kernel,
        in_specs=[vmem] * 4,
        out_specs=(vmem, vmem),
        out_shape=(
            jax.ShapeDtypeStruct((half, w2.shape[1]), BF16),
            jax.ShapeDtypeStruct((D2, hid), BF16),
        ),
        scratch_shapes=[pltpu.VMEM((half + D2, hid), BF16)],
        compiler_params=pltpu.CompilerParams(vmem_limit_bytes=8 * MIB),
    )(near, w1, b1, w2)


def middle_kernel(
    frames_ref, near_ref, before_ref, w1_ref, b1_ref, w2_ref, middle_ref, hidden_ref, far_ref, xs, hs, sems
):
    rows = EARLY - LAG
    now = pltpu.make_async_copy(frames_ref.at[pl.ds(LAG, rows)], xs.at[pl.ds(D1, rows)], sems.at[0])
    later = pltpu.make_async_copy(
        frames_ref.at[pl.ds(EARLY - D1, far_ref.shape[0])], far_ref, sems.at[1]
    )
    now.start()
    later.start()
    xs[:D1, :] = near_ref[LAG - D1 :, :]
    hs[:D2, :] = before_ref[...]
    now.wait()
    for at in range(0, rows, D2):
        hs[D2 + at : 2 * D2 + at, :] = hidden_rows(xs, at, D2, w1_ref, b1_ref)
    middle_ref[...] = feature_rows(hs, 0, rows, w2_ref)
    hidden_ref[...] = hs[rows:, :]
    later.wait()


def middle_rows(frames, near, before, w1, b1, w2):
    vmem = pl.BlockSpec(memory_space=pltpu.VMEM)
    hbm = pl.BlockSpec(memory_space=pltpu.HBM)
    rows, channels = frames.shape
    hid, feat = w1.shape[1], w2.shape[1]
    shapes = ((EARLY - LAG, feat), (D2, hid), (rows - EARLY + D1, channels))
    return pl.pallas_call(
        middle_kernel,
        in_specs=[hbm] + [vmem] * 5,
        out_specs=(vmem,) * 3,
        out_shape=tuple(jax.ShapeDtypeStruct(shape, BF16) for shape in shapes),
        scratch_shapes=[
            pltpu.VMEM((EARLY - LAG + D1, channels), BF16),
            pltpu.VMEM((EARLY - LAG + D2, hid), BF16),
            pltpu.SemaphoreType.DMA((2,)),
        ],
        compiler_params=pltpu.CompilerParams(vmem_limit_bytes=12 * MIB),
    )(in_hbm(frames), near, before, w1, b1, w2)


def head_kernel(near_ref, halo_ref, w1_ref, b1_ref, w2_ref, out_ref, xs, hs):
    half = LAG // 2
    hid, feat = w1_ref.shape[1], w2_ref.shape[1]
    for index in range(xs.shape[1] // feat):
        part = slice(D2 + index * D1, D2 + (index + 1) * D1)
        xs[:D1, index * feat : (index + 1) * feat] = halo_ref[part, :]
    xs[D1:, :] = near_ref[:half, :]
    for at in range(0, half, D2):
        hs[at : at + D2, :] = hidden_rows(xs, at, D2, w1_ref, b1_ref)
    value = jnp.dot(hs[:D2, :], w2_ref[:hid, :], preferred_element_type=F32)
    out_ref[:D2, :] = (value + halo_ref[:D2, :].astype(F32)).astype(BF16)
    out_ref[D2:, :] = feature_rows(hs, 0, half - D2, w2_ref)


def head_rows(near, halo, w1, b1, w2):
    vmem = pl.BlockSpec(memory_space=pltpu.VMEM)
    half, channels, hid = LAG // 2, near.shape[1], w1.shape[1]
    return pl.pallas_call(
        head_kernel,
        in_specs=[vmem] * 5,
        out_specs=vmem,
        out_shape=jax.ShapeDtypeStruct((half, w2.shape[1]), BF16),
        scratch_shapes=[pltpu.VMEM((half + D1, channels), BF16), pltpu.VMEM((half, hid), BF16)],
        compiler_params=pltpu.CompilerParams(vmem_limit_bytes=8 * MIB),
    )(near, halo, w1, b1, w2)


def body_kernel(far_ref, head_ref, early_ref, middle_ref, hidden_ref, w1_ref, b1_ref, w2_ref, out_ref, hs):
    rows = out_ref.shape[0]
    steps = (rows - EARLY) // CHUNK
    half = LAG // 2
    hs[:D2, :] = hidden_ref[...]
    out_ref[:half, :] = head_ref[...]
    out_ref[half:LAG, :] = early_ref[...]
    out_ref[LAG:EARLY, :] = middle_ref[...]
    for step in range(steps + 1):
        at = step * CHUNK
        if step < steps:
            hs[D2 + at : D2 + at + CHUNK, :] = hidden_rows(far_ref, at, CHUNK, w1_ref, b1_ref)
        if step:
            out_ref[EARLY + at - CHUNK : EARLY + at, :] = feature_rows(hs, at - CHUNK, CHUNK, w2_ref)


def body(far, head, early, middle, hidden, w1, b1, w2):
    rows, hid, feat = far.shape[0] - D1 + EARLY, w1.shape[1], w2.shape[1]
    vmem = pl.BlockSpec(memory_space=pltpu.VMEM)
    return pl.pallas_call(
        body_kernel,
        in_specs=[vmem] * 8,
        out_specs=vmem,
        out_shape=jax.ShapeDtypeStruct((rows, feat), BF16),
        scratch_shapes=[pltpu.VMEM((rows - EARLY + D2, hid), BF16)],
        compiler_params=pltpu.CompilerParams(vmem_limit_bytes=16 * MIB),
    )(far, head, early, middle, hidden, w1, b1, w2)


def column_sum(rows):
    parts = rows.astype(F32).reshape(4, -1, 8, rows.shape[1])
    return jnp.sum(jnp.sum(parts, 1), 0)


def moment_kernel(feature_ref, inst, lag, total):
    rows, feat = feature_ref.shape
    tm_index, tm_last = lax.axis_index("tm"), lax.axis_size("tm") - 1
    for at in range(0, rows, LAG):
        weight = 2.0
        if at == 0:
            weight = jnp.where(tm_index == 0, 1.0, 2.0)
        elif at == rows - LAG:
            weight = jnp.where(tm_index == tm_last, 1.0, 2.0)
        now = feature_ref[at : at + LAG, :]
        if at == 0:
            inst[...] = weight * gram(now, now)
            total[...] = weight * column_sum(now)
            continue
        both = gram(now, jnp.concatenate([now, feature_ref[at - LAG : at, :]], 1))
        inst[...] += weight * both[:, :feat]
        lag[...] = both[:, feat:] if at == LAG else lag[...] + both[:, feat:]
        total[...] += weight * column_sum(now)


def moments(feature):
    feat = feature.shape[1]
    vmem = pl.BlockSpec(memory_space=pltpu.VMEM)
    square = jax.ShapeDtypeStruct((feat, feat), F32)
    return pl.pallas_call(
        moment_kernel,
        in_specs=[vmem],
        out_specs=(vmem,) * 3,
        out_shape=(square, square, jax.ShapeDtypeStruct((8, feat), F32)),
        compiler_params=pltpu.CompilerParams(vmem_limit_bytes=12 * MIB),
    )(feature)


def pack_kernel(feature_ref, ahead_head_ref, ahead_early_ref, inst, lag, total, kept_ref, sent_ref, packed):
    feat = inst.shape[0]
    half = LAG // 2
    edge = feature_ref.shape[0] - LAG
    cross = lag[...] + gram(ahead_head_ref[...], feature_ref[edge : edge + half, :])
    cross += gram(ahead_early_ref[...], feature_ref[edge + half :, :])
    both = cross + cross.T
    row = lax.broadcasted_iota(jnp.int32, (feat, feat), 0)
    column = lax.broadcasted_iota(jnp.int32, (feat, feat), 1)
    packed[...] = jnp.where(column >= row, inst[...], both)
    sums = jnp.sum(total[...], 0, keepdims=True)
    diagonal = jnp.sum(jnp.where(column == row, both, 0.0), 0, keepdims=True)
    core = lax.axis_index("core")
    for ref, owner in ((kept_ref, core), (sent_ref, 1 - core)):
        extra = jnp.where(owner == 0, sums, diagonal)
        chunks = ref.shape[0]
        for index, lanes in slots(ref.shape, feat):
            at = pl.multiple_of(owner * (feat // 2) + index * chunks, 8)
            ref[:, 0, lanes] = packed[pl.ds(at, chunks), :]
        for chunk in range(chunks):
            part = extra[:, chunk * 128 : chunk * 128 + 128] if chunk < feat // 128 else jnp.zeros((1, 128), F32)
            ref[chunk, 0:1, ref.shape[2] - 128 :] = part


def slots(shape, feat):
    for index in range((shape[2] - 128) // feat):
        yield index, slice(index * feat, (index + 1) * feat)


def pack(feature, ahead_head, ahead_early, inst, lag, total, chips):
    vmem = pl.BlockSpec(memory_space=pltpu.VMEM)
    feat = inst.shape[0]
    share = jax.ShapeDtypeStruct((chips, 1, feat // 2 // chips * feat + 128), F32)
    return pl.pallas_call(
        pack_kernel,
        in_specs=[vmem] * 6,
        out_specs=(vmem, vmem),
        out_shape=(share, share),
        scratch_shapes=[pltpu.VMEM((feat, feat), F32)],
        compiler_params=pltpu.CompilerParams(vmem_limit_bytes=8 * MIB),
    )(feature, ahead_head, ahead_early, inst, lag, total)


def three_parts(x):
    high = x.astype(BF16)
    rest = x - high.astype(F32)
    middle = rest.astype(BF16)
    low = (rest - middle.astype(F32)).astype(BF16)
    return high, middle, low


def product(a, b):
    high, middle, low = three_parts(a)
    left = jnp.concatenate([high, high, middle, high, low, middle], 1)
    high, middle, low = three_parts(b)
    right = jnp.concatenate([high, middle, high, low, high, middle], 0)
    return jnp.dot(left, right, preferred_element_type=F32)


def eliminate(rows, start, size):
    lane = lax.broadcasted_iota(jnp.int32, (8, size), 1) - start
    sub = lax.broadcasted_iota(jnp.int32, (8, size), 0)
    sub_narrow = lax.broadcasted_iota(jnp.int32, (8, 128), 0)
    tiles = range(len(rows))

    def wide(x):
        return jnp.concatenate([x] * (size // 128), 1)

    def spread(x, j):
        return jnp.broadcast_to(x[j : j + 1, :], x.shape)

    columns = [
        [jnp.broadcast_to(rows[h][:, start + k : start + k + 1], (8, 128)) for h in tiles]
        for k in range(PANEL)
    ]
    inside = (lane >= 0) & (lane < PANEL)
    rows = [jnp.where(inside, jnp.where(lane == sub + 8 * h, 1.0, 0.0), rows[h]) for h in tiles]
    pivots = [jnp.ones((8, 128), F32) for _ in range(PANEL // 8)]
    pivot = spread(columns[0][0], 0)
    for j in range(PANEL):
        inverse = pl.reciprocal(pivot, approx=True)
        here, at = divmod(j, 8)
        pivots[here] = jnp.where(sub_narrow == at, pivot, pivots[here])
        beside = {k: spread(columns[j][k // 8], k % 8) for k in range(j + 1, PANEL)}
        if beside:
            there, after = divmod(j + 1, 8)
            pivot = spread(columns[j + 1][there], after) - beside[j + 1] * beside[j + 1] * inverse
        panel_row = spread(rows[here], at)
        for h in tiles:
            if 8 * h + 7 <= j:
                continue
            factor = columns[j][h] * inverse
            if h == here:
                factor = jnp.where(sub_narrow > at, factor, 0.0)
            for k in beside:
                if 8 * h + 7 >= k:
                    columns[k][h] = columns[k][h] - factor * beside[k]
            rows[h] = rows[h] - wide(factor) * panel_row
    return [rows[h] * wide(lax.rsqrt(pivots[h])) if h < len(pivots) else rows[h] for h in tiles]


def inverse_factor(work):
    size = work.shape[0]
    for start in range(0, size, SUPER):
        stop = start + SUPER
        rows = [work[at : at + 8, :] for at in range(start, stop, 8)]
        for at in range(0, SUPER, PANEL):
            rows[at // 8 :] = eliminate(rows[at // 8 :], start + at, size)
        row = lax.broadcasted_iota(jnp.int32, (SUPER, size), 0)
        column = lax.broadcasted_iota(jnp.int32, (SUPER, size), 1) - start
        panel = jnp.where((column > row) & (column < SUPER), 0.0, jnp.concatenate(rows, 0))
        work[start:stop, :] = panel
        if stop < size:
            high, middle, low = three_parts(panel)
            left = jnp.concatenate([high, high, middle, high, low, middle], 0)
            right = jnp.concatenate([high, middle, high, low, high, middle], 0)
            first = stop // 128 * 128
            update = gram(left[:, first:], right)
            for at in range(0, size, 128):
                lanes = slice(at, at + 128)
                old = work[stop:, lanes]
                if at <= start < at + 128:
                    place = lax.broadcasted_iota(jnp.int32, old.shape, 1) + at
                    old = jnp.where((place < start) | (place >= stop), old, 0.0)
                work[stop:, lanes] = old - update[stop - first :, lanes]
    row = lax.broadcasted_iota(jnp.int32, (size, size), 0)
    column = lax.broadcasted_iota(jnp.int32, (size, size), 1)
    return jnp.where(column <= row, work[...], 0.0)


def koopman_kernel(
    scale_ref, mine_ref, other_ref, feature_ref, ahead_head_ref, ahead_early_ref, moved_out, residual_out,
    work, packed_ref, split_ref, shift_ref, moved, residual, sems,
):
    feat = packed_ref.shape[1]
    scale = scale_ref[0]
    core = lax.axis_index("core")
    extras = []
    for ref, owner in ((mine_ref, core), (other_ref, 1 - core)):
        chunks = ref.shape[0]
        for index, lanes in slots(ref.shape, feat):
            at = pl.multiple_of(owner * (feat // 2) + index * chunks, 8)
            packed_ref[pl.ds(at, chunks), :] = ref[:, 0, lanes]
        parts = [ref[chunk, 0:1, ref.shape[2] - 128 :] for chunk in range(feat // 128)]
        extras.append(jnp.concatenate(parts, 1))
    packed = packed_ref[...]
    mean = jnp.where(core == 0, extras[0], extras[1]) * scale
    diagonal = jnp.where(core == 0, extras[1], extras[0])
    row = lax.broadcasted_iota(jnp.int32, (feat, feat), 0)
    column = lax.broadcasted_iota(jnp.int32, (feat, feat), 1)
    turned = packed.T
    mean_column = jnp.broadcast_to(jnp.broadcast_to(mean, (8, feat)).T[:, 0:1], (feat, feat))
    centre = mean_column * mean
    inst = jnp.where(column >= row, packed, turned)
    lag = jnp.where(column < row, packed, turned)
    lag = jnp.where(column == row, jnp.broadcast_to(diagonal, (feat, feat)), lag)
    work[...] = inst * scale - centre + jnp.where(column == row, RIDGE, 0.0)
    lag = lag * scale - centre
    inverse = inverse_factor(work)
    inverse_turned = inverse.T
    koopman = product(product(inverse, lag), inverse_turned)
    moved_turned = product(inverse_turned, koopman)
    for index, matrix in enumerate((inverse_turned, moved_turned)):
        high = matrix.astype(BF16)
        split_ref[index, :feat, :] = high
        split_ref[index, feat:, :] = (matrix - high.astype(F32)).astype(BF16)
        shift = jnp.sum(mean_column * matrix, 0, keepdims=True)
        shift_ref[index] = jnp.broadcast_to(shift, (8, feat))
    project_rows(
        feature_ref, ahead_head_ref, ahead_early_ref, split_ref, shift_ref, moved_out, residual_out, moved, residual, sems
    )


def project_rows(
    feature_ref, ahead_head_ref, ahead_early_ref, split_ref, shift_ref, moved_out, residual_out, moved, residual, sems
):
    rows = feature_ref.shape[0]
    at_end = lax.axis_index("tm") == lax.axis_size("tm") - 1

    def image(block, index):
        twice = jnp.concatenate([block, block], 1)
        return jnp.dot(twice, split_ref[index], preferred_element_type=F32) - shift_ref[index][0:1]

    copies = []
    for step in range(rows // CHUNK):
        here = slice(step * CHUNK, (step + 1) * CHUNK)
        start = step * CHUNK + LAG
        if start < rows:
            later = feature_ref[start : start + CHUNK, :]
        else:
            later = (ahead_head_ref if start == rows else ahead_early_ref)[...]
        now = image(feature_ref[here, :], 1)
        moved[here, :] = now
        gap = image(later, 0) - now
        residual[here, :] = gap if start < rows else jnp.where(at_end, 0.0, gap)
        for index, (source, target) in enumerate(((moved, moved_out), (residual, residual_out))):
            copy = pltpu.make_async_copy(source.at[here], target.at[here], sems.at[index, step])
            copy.start()
            copies.append(copy)
    for copy in copies:
        copy.wait()


def project(scale, mine, other, feature, ahead_head, ahead_early):
    rows, feat = feature.shape
    vmem = pl.BlockSpec(memory_space=pltpu.VMEM)
    hbm = pl.BlockSpec(memory_space=pltpu.HBM)
    out = jax.ShapeDtypeStruct((rows, feat), F32)
    return pl.pallas_call(
        koopman_kernel,
        in_specs=[pl.BlockSpec(memory_space=pltpu.SMEM)] + [vmem] * 5,
        out_specs=(hbm, hbm),
        out_shape=(out, out),
        scratch_shapes=[
            pltpu.VMEM((feat, feat), F32),
            pltpu.VMEM((feat, feat), F32),
            pltpu.VMEM((2, 2 * feat, feat), BF16),
            pltpu.VMEM((2, 8, feat), F32),
            pltpu.VMEM((rows, feat), F32),
            pltpu.VMEM((rows, feat), F32),
            pltpu.SemaphoreType.DMA((2, rows // CHUNK)),
        ],
        compiler_params=pltpu.CompilerParams(vmem_limit_bytes=32 * MIB),
    )(scale, mine, other, feature, ahead_head, ahead_early)


def summed(kept, sent):
    swap = [(0, 1), (1, 0)]
    chips = ("x", "tm")
    parts = kept + lax.ppermute(sent, "core", swap)
    mine = jnp.sum(lax.all_to_all(parts, chips, 0, 0, tiled=True), 0, keepdims=True)
    mine = lax.all_to_all(jnp.broadcast_to(mine, parts.shape), chips, 0, 0, tiled=True)
    return mine, lax.ppermute(mine, "core", swap)


def on_device(frames, first_weight, first_bias, second_weight):
    frame_block = frames[0]
    row_count, channels = frame_block.shape
    hid, feat = second_weight.shape[1:]
    weights = (
        first_weight.reshape(2 * channels, hid),
        first_bias.reshape(1, hid),
        second_weight.reshape(2 * hid, feat),
    )
    sent, near, *weights = tail_rows(frame_block, *weights)
    halo = passed_along(sent, "tm", 1)
    early, before = early_rows(near, *weights)
    ahead_early = passed_along(early, "tm", -1)
    middle, hidden, far = middle_rows(frame_block, near, before, *weights)
    head = head_rows(near, halo, *weights)
    ahead_head = passed_along(head, "tm", -1)
    feature = body(far, head, early, middle, hidden, *weights)
    inst, lag, total = moments(feature)
    chips = lax.axis_size("x") * lax.axis_size("tm")
    mine, other = summed(*pack(feature, ahead_head, ahead_early, inst, lag, total, chips))
    replicas = lax.axis_size("x") * lax.axis_size("core")
    pair_count = replicas * (row_count * lax.axis_size("tm") - LAG)
    scale = jnp.full((1,), 1.0 / (2.0 * pair_count), F32)
    propagated, residual = project(scale, mine, other, feature, ahead_head, ahead_early)
    return (propagated[None], residual[None])


def solution(mesh):
    replicas, blocks = mesh.devices.shape
    chips = Mesh(mesh.devices.reshape(replicas // 2, 2, blocks), ("x", "core", "tm"))
    split = P(("x", "core"), "tm", None)
    return jax.shard_map(
        on_device,
        mesh=chips,
        in_specs=(split, P(), P(), P()),
        out_specs=(split, split),
        check_vma=False,
    )
```

```python
import jax
import jax.numpy as jnp
from jax import lax
from jax.experimental import pallas as pl
from jax.experimental.pallas import tpu as pltpu
from jax.sharding import Mesh, PartitionSpec as P

D1 = 32
D2 = 256
LAG = 1024
RIDGE = 0.001
CHUNK = 512
EARLY = 1536
PANEL = 16
SUPER = 32
MIB = 1024 * 1024

F32 = jnp.float32
BF16 = jnp.bfloat16


def passed_along(value, axis, steps):
    count = lax.axis_size(axis)
    first, last = (max(0, -steps), min(count, count - steps))
    return lax.ppermute(value, axis, [(source, source + steps) for source in range(first, last)])


def gram(a, b):
    return lax.dot_general(a, b, (((0,), (0,)), ((), ())), preferred_element_type=F32)


def in_hbm(value):
    return pltpu.with_memory_space_constraint(value, pltpu.HBM)


def silu(x):
    half = 0.5 * x
    return half + half * jnp.tanh(half)


def hidden_rows(xs, at, rows, w1_ref, b1_ref):
    both = jnp.concatenate([xs[pl.ds(at + D1, rows), :], xs[pl.ds(at, rows), :]], 1)
    hid = w1_ref.shape[1]
    parts = []
    for lanes in (slice(0, hid // 2), slice(hid // 2, hid)):
        z = jnp.dot(both, w1_ref[:, lanes], preferred_element_type=F32)
        parts.append(silu(z + b1_ref[:, lanes]).astype(BF16))
    return jnp.concatenate(parts, 1)


def feature_rows(hs, at, rows, w2_ref):
    both = jnp.concatenate([hs[pl.ds(at + D2, rows), :], hs[pl.ds(at, rows), :]], 1)
    return jnp.dot(both, w2_ref[...], preferred_element_type=F32).astype(BF16)


def tail_kernel(frames_ref, w1_in, b1_in, w2_in, sent_ref, near_ref, w1_ref, b1_ref, w2_ref, xs, sems):
    rows = frames_ref.shape[0]
    taps = w1_in.shape[0] // 2
    pairs = (
        (frames_ref.at[pl.ds(rows - D1 - D2, D1 + D2)], xs),
        (w1_in.at[pl.ds(0, taps)], w1_ref.at[pl.ds(0, taps)]),
        (w1_in.at[pl.ds(taps, taps)], w1_ref.at[pl.ds(taps, taps)]),
        (b1_in, b1_ref),
        (w2_in, w2_ref),
        (frames_ref.at[pl.ds(0, LAG)], near_ref),
    )
    copies = [pltpu.make_async_copy(*pair, sems.at[index]) for index, pair in enumerate(pairs)]
    for copy in copies:
        copy.start()
    for copy in copies[:4]:
        copy.wait()
    hidden = hidden_rows(xs, 0, D2, w1_ref, b1_ref)
    copies[4].wait()
    hid, feat = hidden.shape[1], w2_ref.shape[1]
    sent_ref[:D2, :] = jnp.dot(hidden, w2_ref[hid:, :], preferred_element_type=F32).astype(BF16)
    for index in range(xs.shape[1] // feat):
        part = slice(D2 + index * D1, D2 + (index + 1) * D1)
        sent_ref[part, :] = xs[D2:, index * feat : (index + 1) * feat]
    copies[5].wait()


def tail_rows(frames, w1, b1, w2):
    vmem = pl.BlockSpec(memory_space=pltpu.VMEM)
    hbm = pl.BlockSpec(memory_space=pltpu.HBM)
    channels, feat = frames.shape[1], w2.shape[1]
    sent = (D2 + D1 * channels // feat, feat)
    shapes = ((sent, BF16), ((LAG, channels), BF16), (w1.shape, BF16), (b1.shape, F32), (w2.shape, BF16))
    return pl.pallas_call(
        tail_kernel,
        in_specs=[hbm] * 4,
        out_specs=(vmem,) * 5,
        out_shape=tuple(jax.ShapeDtypeStruct(*shape) for shape in shapes),
        scratch_shapes=[pltpu.VMEM((D1 + D2, channels), BF16), pltpu.SemaphoreType.DMA((6,))],
        compiler_params=pltpu.CompilerParams(vmem_limit_bytes=12 * MIB),
    )(*(in_hbm(value) for value in (frames, w1, b1, w2)))


def early_kernel(near_ref, w1_ref, b1_ref, w2_ref, out_ref, hidden_ref, hs):
    half = LAG // 2
    for at in range(0, hs.shape[0], D2):
        hs[at : at + D2, :] = hidden_rows(near_ref, half - D1 - D2 + at, D2, w1_ref, b1_ref)
    out_ref[...] = feature_rows(hs, 0, half, w2_ref)
    hidden_ref[...] = hs[half:, :]


def early_rows(near, w1, b1, w2):
    vmem = pl.BlockSpec(memory_space=pltpu.VMEM)
    half, hid = LAG // 2, w1.shape[1]
    return pl.pallas_call(
        early_kernel,
        in_specs=[vmem] * 4,
        out_specs=(vmem, vmem),
        out_shape=(
            jax.ShapeDtypeStruct((half, w2.shape[1]), BF16),
            jax.ShapeDtypeStruct((D2, hid), BF16),
        ),
        scratch_shapes=[pltpu.VMEM((half + D2, hid), BF16)],
        compiler_params=pltpu.CompilerParams(vmem_limit_bytes=8 * MIB),
    )(near, w1, b1, w2)


def middle_kernel(
    frames_ref, near_ref, before_ref, w1_ref, b1_ref, w2_ref, middle_ref, hidden_ref, far_ref, xs, hs, sems
):
    rows = EARLY - LAG
    now = pltpu.make_async_copy(frames_ref.at[pl.ds(LAG, rows)], xs.at[pl.ds(D1, rows)], sems.at[0])
    later = pltpu.make_async_copy(
        frames_ref.at[pl.ds(EARLY - D1, far_ref.shape[0])], far_ref, sems.at[1]
    )
    now.start()
    later.start()
    xs[:D1, :] = near_ref[LAG - D1 :, :]
    hs[:D2, :] = before_ref[...]
    now.wait()
    for at in range(0, rows, D2):
        hs[D2 + at : 2 * D2 + at, :] = hidden_rows(xs, at, D2, w1_ref, b1_ref)
    middle_ref[...] = feature_rows(hs, 0, rows, w2_ref)
    hidden_ref[...] = hs[rows:, :]
    later.wait()


def middle_rows(frames, near, before, w1, b1, w2):
    vmem = pl.BlockSpec(memory_space=pltpu.VMEM)
    hbm = pl.BlockSpec(memory_space=pltpu.HBM)
    rows, channels = frames.shape
    hid, feat = w1.shape[1], w2.shape[1]
    shapes = ((EARLY - LAG, feat), (D2, hid), (rows - EARLY + D1, channels))
    return pl.pallas_call(
        middle_kernel,
        in_specs=[hbm] + [vmem] * 5,
        out_specs=(vmem,) * 3,
        out_shape=tuple(jax.ShapeDtypeStruct(shape, BF16) for shape in shapes),
        scratch_shapes=[
            pltpu.VMEM((EARLY - LAG + D1, channels), BF16),
            pltpu.VMEM((EARLY - LAG + D2, hid), BF16),
            pltpu.SemaphoreType.DMA((2,)),
        ],
        compiler_params=pltpu.CompilerParams(vmem_limit_bytes=12 * MIB),
    )(in_hbm(frames), near, before, w1, b1, w2)


def head_kernel(near_ref, halo_ref, w1_ref, b1_ref, w2_ref, out_ref, xs, hs):
    half = LAG // 2
    hid, feat = w1_ref.shape[1], w2_ref.shape[1]
    for index in range(xs.shape[1] // feat):
        part = slice(D2 + index * D1, D2 + (index + 1) * D1)
        xs[:D1, index * feat : (index + 1) * feat] = halo_ref[part, :]
    xs[D1:, :] = near_ref[:half, :]
    for at in range(0, half, D2):
        hs[at : at + D2, :] = hidden_rows(xs, at, D2, w1_ref, b1_ref)
    value = jnp.dot(hs[:D2, :], w2_ref[:hid, :], preferred_element_type=F32)
    out_ref[:D2, :] = (value + halo_ref[:D2, :].astype(F32)).astype(BF16)
    out_ref[D2:, :] = feature_rows(hs, 0, half - D2, w2_ref)


def head_rows(near, halo, w1, b1, w2):
    vmem = pl.BlockSpec(memory_space=pltpu.VMEM)
    half, channels, hid = LAG // 2, near.shape[1], w1.shape[1]
    return pl.pallas_call(
        head_kernel,
        in_specs=[vmem] * 5,
        out_specs=vmem,
        out_shape=jax.ShapeDtypeStruct((half, w2.shape[1]), BF16),
        scratch_shapes=[pltpu.VMEM((half + D1, channels), BF16), pltpu.VMEM((half, hid), BF16)],
        compiler_params=pltpu.CompilerParams(vmem_limit_bytes=8 * MIB),
    )(near, halo, w1, b1, w2)


def body_kernel(far_ref, head_ref, early_ref, middle_ref, hidden_ref, w1_ref, b1_ref, w2_ref, out_ref, hs):
    rows = out_ref.shape[0]
    steps = (rows - EARLY) // CHUNK
    half = LAG // 2
    hs[:D2, :] = hidden_ref[...]
    out_ref[:half, :] = head_ref[...]
    out_ref[half:LAG, :] = early_ref[...]
    out_ref[LAG:EARLY, :] = middle_ref[...]
    for step in range(steps + 1):
        at = step * CHUNK
        if step < steps:
            hs[D2 + at : D2 + at + CHUNK, :] = hidden_rows(far_ref, at, CHUNK, w1_ref, b1_ref)
        if step:
            out_ref[EARLY + at - CHUNK : EARLY + at, :] = feature_rows(hs, at - CHUNK, CHUNK, w2_ref)


def body(far, head, early, middle, hidden, w1, b1, w2):
    rows, hid, feat = far.shape[0] - D1 + EARLY, w1.shape[1], w2.shape[1]
    vmem = pl.BlockSpec(memory_space=pltpu.VMEM)
    return pl.pallas_call(
        body_kernel,
        in_specs=[vmem] * 8,
        out_specs=vmem,
        out_shape=jax.ShapeDtypeStruct((rows, feat), BF16),
        scratch_shapes=[pltpu.VMEM((rows - EARLY + D2, hid), BF16)],
        compiler_params=pltpu.CompilerParams(vmem_limit_bytes=16 * MIB),
    )(far, head, early, middle, hidden, w1, b1, w2)


def column_sum(rows):
    parts = rows.astype(F32).reshape(4, -1, 8, rows.shape[1])
    return jnp.sum(jnp.sum(parts, 1), 0)


def moment_kernel(feature_ref, inst, lag, total, turned_ref):
    rows, feat = feature_ref.shape
    turned_ref[...] = feature_ref[rows - LAG :, :].T
    tm_index, tm_last = lax.axis_index("tm"), lax.axis_size("tm") - 1
    for at in range(0, rows, LAG):
        weight = 2.0
        if at == 0:
            weight = jnp.where(tm_index == 0, 1.0, 2.0)
        elif at == rows - LAG:
            weight = jnp.where(tm_index == tm_last, 1.0, 2.0)
        now = feature_ref[at : at + LAG, :]
        if at == 0:
            inst[...] = weight * gram(now, now)
            total[...] = weight * column_sum(now)
            continue
        both = gram(now, jnp.concatenate([now, feature_ref[at - LAG : at, :]], 1))
        inst[...] += weight * both[:, :feat]
        lag[...] = both[:, feat:] if at == LAG else lag[...] + both[:, feat:]
        total[...] += weight * column_sum(now)


def moments(feature):
    feat = feature.shape[1]
    vmem = pl.BlockSpec(memory_space=pltpu.VMEM)
    square = jax.ShapeDtypeStruct((feat, feat), F32)
    return pl.pallas_call(
        moment_kernel,
        in_specs=[vmem],
        out_specs=(vmem,) * 4,
        out_shape=(
            square,
            square,
            jax.ShapeDtypeStruct((8, feat), F32),
            jax.ShapeDtypeStruct((feat, LAG), BF16),
        ),
        compiler_params=pltpu.CompilerParams(vmem_limit_bytes=12 * MIB),
    )(feature)


def pack_kernel(turned_ref, ahead_head_ref, ahead_early_ref, inst, lag, total, kept_ref, sent_ref, packed):
    feat = inst.shape[0]
    half = LAG // 2
    cross = lag[...] + jnp.dot(turned_ref[:, :half], ahead_head_ref[...], preferred_element_type=F32)
    cross += jnp.dot(turned_ref[:, half:], ahead_early_ref[...], preferred_element_type=F32)
    both = cross + cross.T
    row = lax.broadcasted_iota(jnp.int32, (feat, feat), 0)
    column = lax.broadcasted_iota(jnp.int32, (feat, feat), 1)
    packed[...] = jnp.where(column >= row, inst[...], both)
    sums = jnp.sum(total[...], 0, keepdims=True)
    diagonal = jnp.sum(jnp.where(column == row, both, 0.0), 0, keepdims=True)
    core = lax.axis_index("core")
    for ref, owner in ((kept_ref, core), (sent_ref, 1 - core)):
        extra = jnp.where(owner == 0, sums, diagonal)
        chunks = ref.shape[0]
        for index, lanes in slots(ref.shape, feat):
            at = pl.multiple_of(owner * (feat // 2) + index * chunks, 8)
            ref[:, 0, lanes] = packed[pl.ds(at, chunks), :]
        for chunk in range(chunks):
            part = extra[:, chunk * 128 : chunk * 128 + 128] if chunk < feat // 128 else jnp.zeros((1, 128), F32)
            ref[chunk, 0:1, ref.shape[2] - 128 :] = part


def slots(shape, feat):
    for index in range((shape[2] - 128) // feat):
        yield index, slice(index * feat, (index + 1) * feat)


def pack(turned, ahead_head, ahead_early, inst, lag, total, chips):
    vmem = pl.BlockSpec(memory_space=pltpu.VMEM)
    feat = inst.shape[0]
    share = jax.ShapeDtypeStruct((chips, 1, feat // 2 // chips * feat + 128), F32)
    return pl.pallas_call(
        pack_kernel,
        in_specs=[vmem] * 6,
        out_specs=(vmem, vmem),
        out_shape=(share, share),
        scratch_shapes=[pltpu.VMEM((feat, feat), F32)],
        compiler_params=pltpu.CompilerParams(vmem_limit_bytes=8 * MIB),
    )(turned, ahead_head, ahead_early, inst, lag, total)


def three_parts(x):
    high = x.astype(BF16)
    rest = x - high.astype(F32)
    middle = rest.astype(BF16)
    low = (rest - middle.astype(F32)).astype(BF16)
    return high, middle, low


def product(a, b):
    high, middle, low = a
    left = jnp.concatenate([high, high, middle, high, low, middle], 1)
    high, middle, low = b
    right = jnp.concatenate([high, middle, high, low, high, middle], 0)
    return jnp.dot(left, right, preferred_element_type=F32)


def eliminate(rows, start, size):
    lane = lax.broadcasted_iota(jnp.int32, (8, size), 1) - start
    sub = lax.broadcasted_iota(jnp.int32, (8, size), 0)
    sub_narrow = lax.broadcasted_iota(jnp.int32, (8, 128), 0)
    tiles = range(len(rows))

    def wide(x):
        return jnp.concatenate([x] * (size // 128), 1)

    def spread(x, j):
        return jnp.broadcast_to(x[j : j + 1, :], x.shape)

    columns = [
        [jnp.broadcast_to(rows[h][:, start + k : start + k + 1], (8, 128)) for h in tiles]
        for k in range(PANEL)
    ]
    inside = (lane >= 0) & (lane < PANEL)
    rows = [jnp.where(inside, jnp.where(lane == sub + 8 * h, 1.0, 0.0), rows[h]) for h in tiles]
    pivots = [jnp.ones((8, 128), F32) for _ in range(PANEL // 8)]
    pivot = spread(columns[0][0], 0)
    for j in range(PANEL):
        inverse = pl.reciprocal(pivot, approx=True)
        here, at = divmod(j, 8)
        pivots[here] = jnp.where(sub_narrow == at, pivot, pivots[here])
        beside = {k: spread(columns[j][k // 8], k % 8) for k in range(j + 1, PANEL)}
        if beside:
            there, after = divmod(j + 1, 8)
            pivot = spread(columns[j + 1][there], after) - beside[j + 1] * beside[j + 1] * inverse
        panel_row = spread(rows[here], at)
        for h in tiles:
            if 8 * h + 7 <= j:
                continue
            factor = columns[j][h] * inverse
            if h == here:
                factor = jnp.where(sub_narrow > at, factor, 0.0)
            for k in beside:
                if 8 * h + 7 >= k:
                    columns[k][h] = columns[k][h] - factor * beside[k]
            rows[h] = rows[h] - wide(factor) * panel_row
    return [rows[h] * wide(lax.rsqrt(pivots[h])) if h < len(pivots) else rows[h] for h in tiles]


def inverse_factor(work):
    size = work.shape[0]
    for start in range(0, size, SUPER):
        stop = start + SUPER
        rows = [work[at : at + 8, :] for at in range(start, stop, 8)]
        for at in range(0, SUPER, PANEL):
            rows[at // 8 :] = eliminate(rows[at // 8 :], start + at, size)
        row = lax.broadcasted_iota(jnp.int32, (SUPER, size), 0)
        column = lax.broadcasted_iota(jnp.int32, (SUPER, size), 1) - start
        panel = jnp.where((column > row) & (column < SUPER), 0.0, jnp.concatenate(rows, 0))
        work[start:stop, :] = panel
        if stop < size:
            high, middle, low = three_parts(panel)
            left = jnp.concatenate([high, high, middle, high, low, middle], 0)
            right = jnp.concatenate([high, middle, high, low, high, middle], 0)
            first = stop // 128 * 128
            update = gram(left[:, first:], right)
            for at in range(0, size, 128):
                lanes = slice(at, at + 128)
                old = work[stop:, lanes]
                if at <= start < at + 128:
                    place = lax.broadcasted_iota(jnp.int32, old.shape, 1) + at
                    old = jnp.where((place < start) | (place >= stop), old, 0.0)
                work[stop:, lanes] = old - update[stop - first :, lanes]
    row = lax.broadcasted_iota(jnp.int32, (size, size), 0)
    column = lax.broadcasted_iota(jnp.int32, (size, size), 1)
    return jnp.where(column <= row, work[...], 0.0)


def koopman_kernel(
    scale_ref, mine_ref, other_ref, feature_ref, ahead_head_ref, ahead_early_ref, moved_out, residual_out,
    work, packed_ref, split_ref, shift_ref, moved, residual, sems,
):
    feat = packed_ref.shape[1]
    scale = scale_ref[0]
    core = lax.axis_index("core")
    extras = []
    for ref, owner in ((mine_ref, core), (other_ref, 1 - core)):
        chunks = ref.shape[0]
        for index, lanes in slots(ref.shape, feat):
            at = pl.multiple_of(owner * (feat // 2) + index * chunks, 8)
            packed_ref[pl.ds(at, chunks), :] = ref[:, 0, lanes]
        parts = [ref[chunk, 0:1, ref.shape[2] - 128 :] for chunk in range(feat // 128)]
        extras.append(jnp.concatenate(parts, 1))
    packed = packed_ref[...]
    mean = jnp.where(core == 0, extras[0], extras[1]) * scale
    diagonal = jnp.where(core == 0, extras[1], extras[0])
    row = lax.broadcasted_iota(jnp.int32, (feat, feat), 0)
    column = lax.broadcasted_iota(jnp.int32, (feat, feat), 1)
    turned = packed.T
    mean_column = jnp.broadcast_to(jnp.broadcast_to(mean, (8, feat)).T[:, 0:1], (feat, feat))
    centre = mean_column * mean
    inst = jnp.where(column >= row, packed, turned)
    lag = jnp.where(column < row, packed, turned)
    lag = jnp.where(column == row, jnp.broadcast_to(diagonal, (feat, feat)), lag)
    work[...] = inst * scale - centre + jnp.where(column == row, RIDGE, 0.0)
    lag = lag * scale - centre
    inverse = inverse_factor(work)
    turned_parts = three_parts(inverse.T)
    half_step = product(three_parts(inverse), three_parts(lag))
    koopman_part = three_parts(product(three_parts(half_step), turned_parts))
    moved_parts = three_parts(product(turned_parts, koopman_part))
    for index, (high, middle, _) in enumerate((turned_parts, moved_parts)):
        split_ref[index, :feat, :] = high
        split_ref[index, feat:, :] = middle
        matrix = high.astype(F32) + middle.astype(F32)
        shift = jnp.sum(mean_column * matrix, 0, keepdims=True)
        shift_ref[index] = jnp.broadcast_to(shift, (8, feat))
    project_rows(
        feature_ref, ahead_head_ref, ahead_early_ref, split_ref, shift_ref, moved_out, residual_out, moved, residual, sems
    )


def project_rows(
    feature_ref, ahead_head_ref, ahead_early_ref, split_ref, shift_ref, moved_out, residual_out, moved, residual, sems
):
    rows = feature_ref.shape[0]
    at_end = lax.axis_index("tm") == lax.axis_size("tm") - 1

    def image(block, index):
        twice = jnp.concatenate([block, block], 1)
        return jnp.dot(twice, split_ref[index], preferred_element_type=F32) - shift_ref[index][0:1]

    copies = []
    for step in range(rows // CHUNK):
        here = slice(step * CHUNK, (step + 1) * CHUNK)
        start = step * CHUNK + LAG
        if start < rows:
            later = feature_ref[start : start + CHUNK, :]
        else:
            later = (ahead_head_ref if start == rows else ahead_early_ref)[...]
        now = image(feature_ref[here, :], 1)
        moved[here, :] = now
        gap = image(later, 0) - now
        residual[here, :] = gap if start < rows else jnp.where(at_end, 0.0, gap)
        for index, (source, target) in enumerate(((moved, moved_out), (residual, residual_out))):
            copy = pltpu.make_async_copy(source.at[here], target.at[here], sems.at[index, step])
            copy.start()
            copies.append(copy)
    for copy in copies:
        copy.wait()


def project(scale, mine, other, feature, ahead_head, ahead_early):
    rows, feat = feature.shape
    vmem = pl.BlockSpec(memory_space=pltpu.VMEM)
    hbm = pl.BlockSpec(memory_space=pltpu.HBM)
    out = jax.ShapeDtypeStruct((rows, feat), F32)
    return pl.pallas_call(
        koopman_kernel,
        in_specs=[pl.BlockSpec(memory_space=pltpu.SMEM)] + [vmem] * 5,
        out_specs=(hbm, hbm),
        out_shape=(out, out),
        scratch_shapes=[
            pltpu.VMEM((feat, feat), F32),
            pltpu.VMEM((feat, feat), F32),
            pltpu.VMEM((2, 2 * feat, feat), BF16),
            pltpu.VMEM((2, 8, feat), F32),
            pltpu.VMEM((rows, feat), F32),
            pltpu.VMEM((rows, feat), F32),
            pltpu.SemaphoreType.DMA((2, rows // CHUNK)),
        ],
        compiler_params=pltpu.CompilerParams(vmem_limit_bytes=32 * MIB),
    )(scale, mine, other, feature, ahead_head, ahead_early)


def summed(kept, sent):
    swap = [(0, 1), (1, 0)]
    chips = ("x", "tm")
    parts = kept + lax.ppermute(sent, "core", swap)
    mine = jnp.sum(lax.all_to_all(parts, chips, 0, 0, tiled=True), 0, keepdims=True)
    mine = lax.all_to_all(jnp.broadcast_to(mine, parts.shape), chips, 0, 0, tiled=True)
    return mine, lax.ppermute(mine, "core", swap)


def on_device(frames, first_weight, first_bias, second_weight):
    frame_block = frames[0]
    row_count, channels = frame_block.shape
    hid, feat = second_weight.shape[1:]
    weights = (
        first_weight.reshape(2 * channels, hid),
        first_bias.reshape(1, hid),
        second_weight.reshape(2 * hid, feat),
    )
    sent, near, *weights = tail_rows(frame_block, *weights)
    halo = passed_along(sent, "tm", 1)
    early, before = early_rows(near, *weights)
    ahead_early = passed_along(early, "tm", -1)
    middle, hidden, far = middle_rows(frame_block, near, before, *weights)
    head = head_rows(near, halo, *weights)
    ahead_head = passed_along(head, "tm", -1)
    feature = body(far, head, early, middle, hidden, *weights)
    inst, lag, total, turned = moments(feature)
    chips = lax.axis_size("x") * lax.axis_size("tm")
    mine, other = summed(*pack(turned, ahead_head, ahead_early, inst, lag, total, chips))
    replicas = lax.axis_size("x") * lax.axis_size("core")
    pair_count = replicas * (row_count * lax.axis_size("tm") - LAG)
    scale = jnp.full((1,), 1.0 / (2.0 * pair_count), F32)
    propagated, residual = project(scale, mine, other, feature, ahead_head, ahead_early)
    return (propagated[None], residual[None])


def solution(mesh):
    replicas, blocks = mesh.devices.shape
    chips = Mesh(mesh.devices.reshape(replicas // 2, 2, blocks), ("x", "core", "tm"))
    split = P(("x", "core"), "tm", None)
    return jax.shard_map(
        on_device,
        mesh=chips,
        in_specs=(split, P(), P(), P()),
        out_specs=(split, split),
        check_vma=False,
    )
```

```python
import jax
import jax.numpy as jnp
from jax import lax
from jax.experimental import pallas as pl
from jax.experimental.pallas import tpu as pltpu
from jax.sharding import Mesh, PartitionSpec as P

D1 = 32
D2 = 256
LAG = 1024
RIDGE = 0.001
CHUNK = 512
PIECE = 256
EARLY = 1536
PANEL = 16
SUPER = 32
MIB = 1024 * 1024

F32 = jnp.float32
BF16 = jnp.bfloat16


def passed_along(value, axis, steps):
    count = lax.axis_size(axis)
    first, last = (max(0, -steps), min(count, count - steps))
    return lax.ppermute(value, axis, [(source, source + steps) for source in range(first, last)])


def gram(a, b):
    return lax.dot_general(a, b, (((0,), (0,)), ((), ())), preferred_element_type=F32)


def in_hbm(value):
    return pltpu.with_memory_space_constraint(value, pltpu.HBM)


def silu(x):
    half = 0.5 * x
    return half + half * jnp.tanh(half)


def hidden_rows(xs, at, rows, w1_ref, b1_ref):
    both = jnp.concatenate([xs[pl.ds(at + D1, rows), :], xs[pl.ds(at, rows), :]], 1)
    hid = w1_ref.shape[1]
    parts = []
    for lanes in (slice(0, hid // 2), slice(hid // 2, hid)):
        z = jnp.dot(both, w1_ref[:, lanes], preferred_element_type=F32)
        parts.append(silu(z + b1_ref[:, lanes]).astype(BF16))
    return jnp.concatenate(parts, 1)


def feature_rows(hs, at, rows, w2_ref):
    both = jnp.concatenate([hs[pl.ds(at + D2, rows), :], hs[pl.ds(at, rows), :]], 1)
    return jnp.dot(both, w2_ref[...], preferred_element_type=F32).astype(BF16)


def tail_kernel(frames_ref, w1_in, b1_in, w2_in, sent_ref, near_ref, w1_ref, b1_ref, w2_ref, xs, sems):
    rows = frames_ref.shape[0]
    taps = w1_in.shape[0] // 2
    pairs = (
        (frames_ref.at[pl.ds(rows - D1 - D2, D1 + D2)], xs),
        (w1_in.at[pl.ds(0, taps)], w1_ref.at[pl.ds(0, taps)]),
        (w1_in.at[pl.ds(taps, taps)], w1_ref.at[pl.ds(taps, taps)]),
        (b1_in, b1_ref),
        (w2_in, w2_ref),
        (frames_ref.at[pl.ds(0, LAG)], near_ref),
    )
    copies = [pltpu.make_async_copy(*pair, sems.at[index]) for index, pair in enumerate(pairs)]
    for copy in copies:
        copy.start()
    for copy in copies[:4]:
        copy.wait()
    hidden = hidden_rows(xs, 0, D2, w1_ref, b1_ref)
    copies[4].wait()
    hid, feat = hidden.shape[1], w2_ref.shape[1]
    sent_ref[:D2, :] = jnp.dot(hidden, w2_ref[hid:, :], preferred_element_type=F32).astype(BF16)
    for index in range(xs.shape[1] // feat):
        part = slice(D2 + index * D1, D2 + (index + 1) * D1)
        sent_ref[part, :] = xs[D2:, index * feat : (index + 1) * feat]
    copies[5].wait()


def tail_rows(frames, w1, b1, w2):
    vmem = pl.BlockSpec(memory_space=pltpu.VMEM)
    hbm = pl.BlockSpec(memory_space=pltpu.HBM)
    channels, feat = frames.shape[1], w2.shape[1]
    sent = (D2 + D1 * channels // feat, feat)
    shapes = ((sent, BF16), ((LAG, channels), BF16), (w1.shape, BF16), (b1.shape, F32), (w2.shape, BF16))
    return pl.pallas_call(
        tail_kernel,
        in_specs=[hbm] * 4,
        out_specs=(vmem,) * 5,
        out_shape=tuple(jax.ShapeDtypeStruct(*shape) for shape in shapes),
        scratch_shapes=[pltpu.VMEM((D1 + D2, channels), BF16), pltpu.SemaphoreType.DMA((6,))],
        compiler_params=pltpu.CompilerParams(vmem_limit_bytes=12 * MIB),
    )(*(in_hbm(value) for value in (frames, w1, b1, w2)))


def early_kernel(near_ref, w1_ref, b1_ref, w2_ref, out_ref, hidden_ref, hs):
    half = LAG // 2
    for at in range(0, hs.shape[0], D2):
        hs[at : at + D2, :] = hidden_rows(near_ref, half - D1 - D2 + at, D2, w1_ref, b1_ref)
    out_ref[...] = feature_rows(hs, 0, half, w2_ref)
    hidden_ref[...] = hs[half:, :]


def early_rows(near, w1, b1, w2):
    vmem = pl.BlockSpec(memory_space=pltpu.VMEM)
    half, hid = LAG // 2, w1.shape[1]
    return pl.pallas_call(
        early_kernel,
        in_specs=[vmem] * 4,
        out_specs=(vmem, vmem),
        out_shape=(
            jax.ShapeDtypeStruct((half, w2.shape[1]), BF16),
            jax.ShapeDtypeStruct((D2, hid), BF16),
        ),
        scratch_shapes=[pltpu.VMEM((half + D2, hid), BF16)],
        compiler_params=pltpu.CompilerParams(vmem_limit_bytes=8 * MIB),
    )(near, w1, b1, w2)


def middle_kernel(
    frames_ref, near_ref, before_ref, w1_ref, b1_ref, w2_ref, middle_ref, hidden_ref, far_ref, xs, hs, sems
):
    rows = EARLY - LAG
    now = pltpu.make_async_copy(frames_ref.at[pl.ds(LAG, rows)], xs.at[pl.ds(D1, rows)], sems.at[0])
    later = pltpu.make_async_copy(
        frames_ref.at[pl.ds(EARLY - D1, far_ref.shape[0])], far_ref, sems.at[1]
    )
    now.start()
    later.start()
    xs[:D1, :] = near_ref[LAG - D1 :, :]
    hs[:D2, :] = before_ref[...]
    now.wait()
    for at in range(0, rows, D2):
        hs[D2 + at : 2 * D2 + at, :] = hidden_rows(xs, at, D2, w1_ref, b1_ref)
    middle_ref[...] = feature_rows(hs, 0, rows, w2_ref)
    hidden_ref[...] = hs[rows:, :]
    later.wait()


def middle_rows(frames, near, before, w1, b1, w2):
    vmem = pl.BlockSpec(memory_space=pltpu.VMEM)
    hbm = pl.BlockSpec(memory_space=pltpu.HBM)
    rows, channels = frames.shape
    hid, feat = w1.shape[1], w2.shape[1]
    shapes = ((EARLY - LAG, feat), (D2, hid), (rows - EARLY + D1, channels))
    return pl.pallas_call(
        middle_kernel,
        in_specs=[hbm] + [vmem] * 5,
        out_specs=(vmem,) * 3,
        out_shape=tuple(jax.ShapeDtypeStruct(shape, BF16) for shape in shapes),
        scratch_shapes=[
            pltpu.VMEM((EARLY - LAG + D1, channels), BF16),
            pltpu.VMEM((EARLY - LAG + D2, hid), BF16),
            pltpu.SemaphoreType.DMA((2,)),
        ],
        compiler_params=pltpu.CompilerParams(vmem_limit_bytes=12 * MIB),
    )(in_hbm(frames), near, before, w1, b1, w2)


def head_kernel(near_ref, halo_ref, w1_ref, b1_ref, w2_ref, out_ref, xs, hs):
    half = LAG // 2
    hid, feat = w1_ref.shape[1], w2_ref.shape[1]
    for index in range(xs.shape[1] // feat):
        part = slice(D2 + index * D1, D2 + (index + 1) * D1)
        xs[:D1, index * feat : (index + 1) * feat] = halo_ref[part, :]
    xs[D1:, :] = near_ref[:half, :]
    for at in range(0, half, D2):
        hs[at : at + D2, :] = hidden_rows(xs, at, D2, w1_ref, b1_ref)
    value = jnp.dot(hs[:D2, :], w2_ref[:hid, :], preferred_element_type=F32)
    out_ref[:D2, :] = (value + halo_ref[:D2, :].astype(F32)).astype(BF16)
    out_ref[D2:, :] = feature_rows(hs, 0, half - D2, w2_ref)


def head_rows(near, halo, w1, b1, w2):
    vmem = pl.BlockSpec(memory_space=pltpu.VMEM)
    half, channels, hid = LAG // 2, near.shape[1], w1.shape[1]
    return pl.pallas_call(
        head_kernel,
        in_specs=[vmem] * 5,
        out_specs=vmem,
        out_shape=jax.ShapeDtypeStruct((half, w2.shape[1]), BF16),
        scratch_shapes=[pltpu.VMEM((half + D1, channels), BF16), pltpu.VMEM((half, hid), BF16)],
        compiler_params=pltpu.CompilerParams(vmem_limit_bytes=8 * MIB),
    )(near, halo, w1, b1, w2)


def body_kernel(far_ref, head_ref, early_ref, middle_ref, hidden_ref, w1_ref, b1_ref, w2_ref, out_ref, hs):
    rows = out_ref.shape[0]
    steps = (rows - EARLY) // CHUNK
    half = LAG // 2
    hs[:D2, :] = hidden_ref[...]
    out_ref[:half, :] = head_ref[...]
    out_ref[half:LAG, :] = early_ref[...]
    out_ref[LAG:EARLY, :] = middle_ref[...]
    for step in range(steps + 1):
        at = step * CHUNK
        if step < steps:
            hs[D2 + at : D2 + at + CHUNK, :] = hidden_rows(far_ref, at, CHUNK, w1_ref, b1_ref)
        if step:
            out_ref[EARLY + at - CHUNK : EARLY + at, :] = feature_rows(hs, at - CHUNK, CHUNK, w2_ref)


def body(far, head, early, middle, hidden, w1, b1, w2):
    rows, hid, feat = far.shape[0] - D1 + EARLY, w1.shape[1], w2.shape[1]
    vmem = pl.BlockSpec(memory_space=pltpu.VMEM)
    return pl.pallas_call(
        body_kernel,
        in_specs=[vmem] * 8,
        out_specs=vmem,
        out_shape=jax.ShapeDtypeStruct((rows, feat), BF16),
        scratch_shapes=[pltpu.VMEM((rows - EARLY + D2, hid), BF16)],
        compiler_params=pltpu.CompilerParams(vmem_limit_bytes=16 * MIB),
    )(far, head, early, middle, hidden, w1, b1, w2)


def column_sum(rows):
    parts = rows.astype(F32).reshape(4, -1, 8, rows.shape[1])
    return jnp.sum(jnp.sum(parts, 1), 0)


def moment_kernel(feature_ref, inst, lag, total, turned_ref):
    rows, feat = feature_ref.shape
    turned_ref[...] = feature_ref[rows - LAG :, :].T
    tm_index, tm_last = lax.axis_index("tm"), lax.axis_size("tm") - 1
    for at in range(0, rows, LAG):
        weight = 2.0
        if at == 0:
            weight = jnp.where(tm_index == 0, 1.0, 2.0)
        elif at == rows - LAG:
            weight = jnp.where(tm_index == tm_last, 1.0, 2.0)
        now = feature_ref[at : at + LAG, :]
        if at == 0:
            inst[...] = weight * gram(now, now)
            total[...] = weight * column_sum(now)
            continue
        both = gram(now, jnp.concatenate([now, feature_ref[at - LAG : at, :]], 1))
        inst[...] += weight * both[:, :feat]
        lag[...] = both[:, feat:] if at == LAG else lag[...] + both[:, feat:]
        total[...] += weight * column_sum(now)


def moments(feature):
    feat = feature.shape[1]
    vmem = pl.BlockSpec(memory_space=pltpu.VMEM)
    square = jax.ShapeDtypeStruct((feat, feat), F32)
    return pl.pallas_call(
        moment_kernel,
        in_specs=[vmem],
        out_specs=(vmem,) * 4,
        out_shape=(
            square,
            square,
            jax.ShapeDtypeStruct((8, feat), F32),
            jax.ShapeDtypeStruct((feat, LAG), BF16),
        ),
        compiler_params=pltpu.CompilerParams(vmem_limit_bytes=12 * MIB),
    )(feature)


def pack_kernel(turned_ref, ahead_head_ref, ahead_early_ref, inst, lag, total, kept_ref, sent_ref, packed):
    feat = inst.shape[0]
    half = LAG // 2
    cross = lag[...] + jnp.dot(turned_ref[:, :half], ahead_head_ref[...], preferred_element_type=F32)
    cross += jnp.dot(turned_ref[:, half:], ahead_early_ref[...], preferred_element_type=F32)
    both = cross + cross.T
    row = lax.broadcasted_iota(jnp.int32, (feat, feat), 0)
    column = lax.broadcasted_iota(jnp.int32, (feat, feat), 1)
    packed[...] = jnp.where(column >= row, inst[...], both)
    sums = jnp.sum(total[...], 0, keepdims=True)
    diagonal = jnp.sum(jnp.where(column == row, both, 0.0), 0, keepdims=True)
    core = lax.axis_index("core")
    for ref, owner in ((kept_ref, core), (sent_ref, 1 - core)):
        extra = jnp.where(owner == 0, sums, diagonal)
        chunks = ref.shape[0]
        for index, lanes in slots(ref.shape, feat):
            at = pl.multiple_of(owner * (feat // 2) + index * chunks, 8)
            ref[:, 0, lanes] = packed[pl.ds(at, chunks), :]
        for chunk in range(chunks):
            part = extra[:, chunk * 128 : chunk * 128 + 128] if chunk < feat // 128 else jnp.zeros((1, 128), F32)
            ref[chunk, 0:1, ref.shape[2] - 128 :] = part


def slots(shape, feat):
    for index in range((shape[2] - 128) // feat):
        yield index, slice(index * feat, (index + 1) * feat)


def pack(turned, ahead_head, ahead_early, inst, lag, total, chips):
    vmem = pl.BlockSpec(memory_space=pltpu.VMEM)
    feat = inst.shape[0]
    share = jax.ShapeDtypeStruct((chips, 1, feat // 2 // chips * feat + 128), F32)
    return pl.pallas_call(
        pack_kernel,
        in_specs=[vmem] * 6,
        out_specs=(vmem, vmem),
        out_shape=(share, share),
        scratch_shapes=[pltpu.VMEM((feat, feat), F32)],
        compiler_params=pltpu.CompilerParams(vmem_limit_bytes=8 * MIB),
    )(turned, ahead_head, ahead_early, inst, lag, total)


def three_parts(x):
    high = x.astype(BF16)
    rest = x - high.astype(F32)
    middle = rest.astype(BF16)
    low = (rest - middle.astype(F32)).astype(BF16)
    return high, middle, low


def product(a, b):
    high, middle, low = a
    left = jnp.concatenate([high, high, middle, high, low, middle], 1)
    high, middle, low = b
    right = jnp.concatenate([high, middle, high, low, high, middle], 0)
    return jnp.dot(left, right, preferred_element_type=F32)


def eliminate(rows, start, size):
    lane = lax.broadcasted_iota(jnp.int32, (8, size), 1) - start
    sub = lax.broadcasted_iota(jnp.int32, (8, size), 0)
    sub_narrow = lax.broadcasted_iota(jnp.int32, (8, 128), 0)
    tiles = range(len(rows))

    def wide(x):
        return jnp.concatenate([x] * (size // 128), 1)

    def spread(x, j):
        return jnp.broadcast_to(x[j : j + 1, :], x.shape)

    columns = [
        [jnp.broadcast_to(rows[h][:, start + k : start + k + 1], (8, 128)) for h in tiles]
        for k in range(PANEL)
    ]
    inside = (lane >= 0) & (lane < PANEL)
    rows = [jnp.where(inside, jnp.where(lane == sub + 8 * h, 1.0, 0.0), rows[h]) for h in tiles]
    pivots = [jnp.ones((8, 128), F32) for _ in range(PANEL // 8)]
    pivot = spread(columns[0][0], 0)
    for j in range(PANEL):
        inverse = pl.reciprocal(pivot, approx=True)
        here, at = divmod(j, 8)
        pivots[here] = jnp.where(sub_narrow == at, pivot, pivots[here])
        beside = {k: spread(columns[j][k // 8], k % 8) for k in range(j + 1, PANEL)}
        if beside:
            there, after = divmod(j + 1, 8)
            pivot = spread(columns[j + 1][there], after) - beside[j + 1] * beside[j + 1] * inverse
        panel_row = spread(rows[here], at)
        for h in tiles:
            if 8 * h + 7 <= j:
                continue
            factor = columns[j][h] * inverse
            if h == here:
                factor = jnp.where(sub_narrow > at, factor, 0.0)
            for k in beside:
                if 8 * h + 7 >= k:
                    columns[k][h] = columns[k][h] - factor * beside[k]
            rows[h] = rows[h] - wide(factor) * panel_row
    return [rows[h] * wide(lax.rsqrt(pivots[h])) if h < len(pivots) else rows[h] for h in tiles]


def inverse_factor(work):
    size = work.shape[0]
    for start in range(0, size, SUPER):
        stop = start + SUPER
        rows = [work[at : at + 8, :] for at in range(start, stop, 8)]
        for at in range(0, SUPER, PANEL):
            rows[at // 8 :] = eliminate(rows[at // 8 :], start + at, size)
        row = lax.broadcasted_iota(jnp.int32, (SUPER, size), 0)
        column = lax.broadcasted_iota(jnp.int32, (SUPER, size), 1) - start
        panel = jnp.where((column > row) & (column < SUPER), 0.0, jnp.concatenate(rows, 0))
        work[start:stop, :] = panel
        if stop < size:
            high, middle, low = three_parts(panel)
            left = jnp.concatenate([high, high, middle, high, low, middle], 0)
            right = jnp.concatenate([high, middle, high, low, high, middle], 0)
            first = stop // 128 * 128
            update = gram(left[:, first:], right)
            for at in range(0, size, 128):
                lanes = slice(at, at + 128)
                old = work[stop:, lanes]
                if at <= start < at + 128:
                    place = lax.broadcasted_iota(jnp.int32, old.shape, 1) + at
                    old = jnp.where((place < start) | (place >= stop), old, 0.0)
                work[stop:, lanes] = old - update[stop - first :, lanes]
    row = lax.broadcasted_iota(jnp.int32, (size, size), 0)
    column = lax.broadcasted_iota(jnp.int32, (size, size), 1)
    return jnp.where(column <= row, work[...], 0.0)


def koopman_kernel(
    scale_ref, mine_ref, other_ref, feature_ref, ahead_head_ref, ahead_early_ref, moved_out, residual_out,
    work, packed_ref, split_ref, shift_ref, moved, residual, sems,
):
    feat = packed_ref.shape[1]
    scale = scale_ref[0]
    core = lax.axis_index("core")
    extras = []
    for ref, owner in ((mine_ref, core), (other_ref, 1 - core)):
        chunks = ref.shape[0]
        for index, lanes in slots(ref.shape, feat):
            at = pl.multiple_of(owner * (feat // 2) + index * chunks, 8)
            packed_ref[pl.ds(at, chunks), :] = ref[:, 0, lanes]
        parts = [ref[chunk, 0:1, ref.shape[2] - 128 :] for chunk in range(feat // 128)]
        extras.append(jnp.concatenate(parts, 1))
    packed = packed_ref[...]
    mean = jnp.where(core == 0, extras[0], extras[1]) * scale
    diagonal = jnp.where(core == 0, extras[1], extras[0])
    row = lax.broadcasted_iota(jnp.int32, (feat, feat), 0)
    column = lax.broadcasted_iota(jnp.int32, (feat, feat), 1)
    turned = packed.T
    mean_column = jnp.broadcast_to(jnp.broadcast_to(mean, (8, feat)).T[:, 0:1], (feat, feat))
    centre = mean_column * mean
    inst = jnp.where(column >= row, packed, turned)
    lag = jnp.where(column < row, packed, turned)
    lag = jnp.where(column == row, jnp.broadcast_to(diagonal, (feat, feat)), lag)
    work[...] = inst * scale - centre + jnp.where(column == row, RIDGE, 0.0)
    lag = lag * scale - centre
    inverse = inverse_factor(work)
    turned_parts = three_parts(inverse.T)
    half_step = product(three_parts(inverse), three_parts(lag))
    koopman_part = three_parts(product(three_parts(half_step), turned_parts))
    moved_parts = three_parts(product(turned_parts, koopman_part))
    for index, (high, middle, _) in enumerate((turned_parts, moved_parts)):
        split_ref[index, :feat, :] = high
        split_ref[index, feat:, :] = middle
        matrix = high.astype(F32) + middle.astype(F32)
        shift = jnp.sum(mean_column * matrix, 0, keepdims=True)
        shift_ref[index] = jnp.broadcast_to(shift, (8, feat))
    project_rows(
        feature_ref, ahead_head_ref, ahead_early_ref, split_ref, shift_ref, moved_out, residual_out, moved, residual, sems
    )


def project_rows(
    feature_ref, ahead_head_ref, ahead_early_ref, split_ref, shift_ref, moved_out, residual_out, moved, residual, sems
):
    rows = feature_ref.shape[0]
    at_end = lax.axis_index("tm") == lax.axis_size("tm") - 1

    def image(block, index):
        twice = jnp.concatenate([block, block], 1)
        return jnp.dot(twice, split_ref[index], preferred_element_type=F32) - shift_ref[index][0:1]

    copies = []
    for step in range(rows // PIECE):
        here = slice(step * PIECE, (step + 1) * PIECE)
        start = step * PIECE + LAG
        if start < rows:
            later = feature_ref[start : start + PIECE, :]
        else:
            ahead_ref = ahead_head_ref if start - rows < LAG // 2 else ahead_early_ref
            at = (start - rows) % (LAG // 2)
            later = ahead_ref[at : at + PIECE, :]
        now = image(feature_ref[here, :], 1)
        moved[here, :] = now
        gap = image(later, 0) - now
        residual[here, :] = gap if start < rows else jnp.where(at_end, 0.0, gap)
        for index, (source, target) in enumerate(((moved, moved_out), (residual, residual_out))):
            copy = pltpu.make_async_copy(source.at[here], target.at[here], sems.at[index, step])
            copy.start()
            copies.append(copy)
    for copy in copies:
        copy.wait()


def project(scale, mine, other, feature, ahead_head, ahead_early):
    rows, feat = feature.shape
    vmem = pl.BlockSpec(memory_space=pltpu.VMEM)
    hbm = pl.BlockSpec(memory_space=pltpu.HBM)
    out = jax.ShapeDtypeStruct((rows, feat), F32)
    return pl.pallas_call(
        koopman_kernel,
        in_specs=[pl.BlockSpec(memory_space=pltpu.SMEM)] + [vmem] * 5,
        out_specs=(hbm, hbm),
        out_shape=(out, out),
        scratch_shapes=[
            pltpu.VMEM((feat, feat), F32),
            pltpu.VMEM((feat, feat), F32),
            pltpu.VMEM((2, 2 * feat, feat), BF16),
            pltpu.VMEM((2, 8, feat), F32),
            pltpu.VMEM((rows, feat), F32),
            pltpu.VMEM((rows, feat), F32),
            pltpu.SemaphoreType.DMA((2, rows // PIECE)),
        ],
        compiler_params=pltpu.CompilerParams(vmem_limit_bytes=32 * MIB),
    )(scale, mine, other, feature, ahead_head, ahead_early)


def summed(kept, sent):
    swap = [(0, 1), (1, 0)]
    chips = ("x", "tm")
    parts = kept + lax.ppermute(sent, "core", swap)
    mine = jnp.sum(lax.all_to_all(parts, chips, 0, 0, tiled=True), 0, keepdims=True)
    mine = lax.all_to_all(jnp.broadcast_to(mine, parts.shape), chips, 0, 0, tiled=True)
    return mine, lax.ppermute(mine, "core", swap)


def on_device(frames, first_weight, first_bias, second_weight):
    frame_block = frames[0]
    row_count, channels = frame_block.shape
    hid, feat = second_weight.shape[1:]
    weights = (
        first_weight.reshape(2 * channels, hid),
        first_bias.reshape(1, hid),
        second_weight.reshape(2 * hid, feat),
    )
    sent, near, *weights = tail_rows(frame_block, *weights)
    halo = passed_along(sent, "tm", 1)
    early, before = early_rows(near, *weights)
    ahead_early = passed_along(early, "tm", -1)
    middle, hidden, far = middle_rows(frame_block, near, before, *weights)
    head = head_rows(near, halo, *weights)
    ahead_head = passed_along(head, "tm", -1)
    feature = body(far, head, early, middle, hidden, *weights)
    inst, lag, total, turned = moments(feature)
    chips = lax.axis_size("x") * lax.axis_size("tm")
    mine, other = summed(*pack(turned, ahead_head, ahead_early, inst, lag, total, chips))
    replicas = lax.axis_size("x") * lax.axis_size("core")
    pair_count = replicas * (row_count * lax.axis_size("tm") - LAG)
    scale = jnp.full((1,), 1.0 / (2.0 * pair_count), F32)
    propagated, residual = project(scale, mine, other, feature, ahead_head, ahead_early)
    return (propagated[None], residual[None])


def solution(mesh):
    replicas, blocks = mesh.devices.shape
    chips = Mesh(mesh.devices.reshape(replicas // 2, 2, blocks), ("x", "core", "tm"))
    split = P(("x", "core"), "tm", None)
    return jax.shard_map(
        on_device,
        mesh=chips,
        in_specs=(split, P(), P(), P()),
        out_specs=(split, split),
        check_vma=False,
    )
```

```python
import jax
import jax.numpy as jnp
from jax import lax
from jax.experimental import pallas as pl
from jax.experimental.pallas import tpu as pltpu
from jax.sharding import Mesh, PartitionSpec as P

D1 = 32
D2 = 256
LAG = 1024
RIDGE = 0.001
CHUNK = 512
PIECE = 256
EARLY = 1536
PANEL = 16
SUPER = 32
MIB = 1024 * 1024

F32 = jnp.float32
BF16 = jnp.bfloat16


def passed_along(value, axis, steps):
    count = lax.axis_size(axis)
    first, last = (max(0, -steps), min(count, count - steps))
    return lax.ppermute(value, axis, [(source, source + steps) for source in range(first, last)])


def gram(a, b):
    return lax.dot_general(a, b, (((0,), (0,)), ((), ())), preferred_element_type=F32)


def in_hbm(value):
    return pltpu.with_memory_space_constraint(value, pltpu.HBM)


def silu(x):
    half = 0.5 * x
    return half + half * jnp.tanh(half)


def hidden_rows(xs, at, rows, w1_ref, b1_ref):
    both = jnp.concatenate([xs[pl.ds(at + D1, rows), :], xs[pl.ds(at, rows), :]], 1)
    hid = w1_ref.shape[1]
    parts = []
    for lanes in (slice(0, hid // 2), slice(hid // 2, hid)):
        z = jnp.dot(both, w1_ref[:, lanes], preferred_element_type=F32)
        parts.append(silu(z + b1_ref[:, lanes]).astype(BF16))
    return jnp.concatenate(parts, 1)


def feature_rows(hs, at, rows, w2_ref):
    both = jnp.concatenate([hs[pl.ds(at + D2, rows), :], hs[pl.ds(at, rows), :]], 1)
    return jnp.dot(both, w2_ref[...], preferred_element_type=F32).astype(BF16)


def tail_kernel(frames_ref, w1_in, b1_in, w2_in, sent_ref, near_ref, w1_ref, b1_ref, w2_ref, xs, sems):
    rows = frames_ref.shape[0]
    taps = w1_in.shape[0] // 2
    pairs = (
        (frames_ref.at[pl.ds(rows - D1 - D2, D1 + D2)], xs),
        (w1_in.at[pl.ds(0, taps)], w1_ref.at[pl.ds(0, taps)]),
        (w1_in.at[pl.ds(taps, taps)], w1_ref.at[pl.ds(taps, taps)]),
        (b1_in, b1_ref),
        (w2_in, w2_ref),
        (frames_ref.at[pl.ds(0, LAG)], near_ref),
    )
    copies = [pltpu.make_async_copy(*pair, sems.at[index]) for index, pair in enumerate(pairs)]
    for copy in copies:
        copy.start()
    for copy in copies[:4]:
        copy.wait()
    hidden = hidden_rows(xs, 0, D2, w1_ref, b1_ref)
    copies[4].wait()
    hid, feat = hidden.shape[1], w2_ref.shape[1]
    sent_ref[:D2, :] = jnp.dot(hidden, w2_ref[hid:, :], preferred_element_type=F32).astype(BF16)
    for index in range(xs.shape[1] // feat):
        part = slice(D2 + index * D1, D2 + (index + 1) * D1)
        sent_ref[part, :] = xs[D2:, index * feat : (index + 1) * feat]
    copies[5].wait()


def tail_rows(frames, w1, b1, w2):
    vmem = pl.BlockSpec(memory_space=pltpu.VMEM)
    hbm = pl.BlockSpec(memory_space=pltpu.HBM)
    channels, feat = frames.shape[1], w2.shape[1]
    sent = (D2 + D1 * channels // feat, feat)
    shapes = ((sent, BF16), ((LAG, channels), BF16), (w1.shape, BF16), (b1.shape, F32), (w2.shape, BF16))
    return pl.pallas_call(
        tail_kernel,
        in_specs=[hbm] * 4,
        out_specs=(vmem,) * 5,
        out_shape=tuple(jax.ShapeDtypeStruct(*shape) for shape in shapes),
        scratch_shapes=[pltpu.VMEM((D1 + D2, channels), BF16), pltpu.SemaphoreType.DMA((6,))],
        compiler_params=pltpu.CompilerParams(vmem_limit_bytes=12 * MIB),
    )(*(in_hbm(value) for value in (frames, w1, b1, w2)))


def early_kernel(near_ref, w1_ref, b1_ref, w2_ref, out_ref, hidden_ref, hs):
    half = LAG // 2
    for at in range(0, hs.shape[0], D2):
        hs[at : at + D2, :] = hidden_rows(near_ref, half - D1 - D2 + at, D2, w1_ref, b1_ref)
    out_ref[...] = feature_rows(hs, 0, half, w2_ref)
    hidden_ref[...] = hs[half:, :]


def early_rows(near, w1, b1, w2):
    vmem = pl.BlockSpec(memory_space=pltpu.VMEM)
    half, hid = LAG // 2, w1.shape[1]
    return pl.pallas_call(
        early_kernel,
        in_specs=[vmem] * 4,
        out_specs=(vmem, vmem),
        out_shape=(
            jax.ShapeDtypeStruct((half, w2.shape[1]), BF16),
            jax.ShapeDtypeStruct((D2, hid), BF16),
        ),
        scratch_shapes=[pltpu.VMEM((half + D2, hid), BF16)],
        compiler_params=pltpu.CompilerParams(vmem_limit_bytes=8 * MIB),
    )(near, w1, b1, w2)


def middle_kernel(
    frames_ref, near_ref, before_ref, w1_ref, b1_ref, w2_ref, middle_ref, hidden_ref, far_ref, xs, hs, sems
):
    rows = EARLY - LAG
    now = pltpu.make_async_copy(frames_ref.at[pl.ds(LAG, rows)], xs.at[pl.ds(D1, rows)], sems.at[0])
    later = pltpu.make_async_copy(
        frames_ref.at[pl.ds(EARLY - D1, far_ref.shape[0])], far_ref, sems.at[1]
    )
    now.start()
    later.start()
    xs[:D1, :] = near_ref[LAG - D1 :, :]
    hs[:D2, :] = before_ref[...]
    now.wait()
    for at in range(0, rows, D2):
        hs[D2 + at : 2 * D2 + at, :] = hidden_rows(xs, at, D2, w1_ref, b1_ref)
    middle_ref[...] = feature_rows(hs, 0, rows, w2_ref)
    hidden_ref[...] = hs[rows:, :]
    later.wait()


def middle_rows(frames, near, before, w1, b1, w2):
    vmem = pl.BlockSpec(memory_space=pltpu.VMEM)
    hbm = pl.BlockSpec(memory_space=pltpu.HBM)
    rows, channels = frames.shape
    hid, feat = w1.shape[1], w2.shape[1]
    shapes = ((EARLY - LAG, feat), (D2, hid), (rows - EARLY + D1, channels))
    return pl.pallas_call(
        middle_kernel,
        in_specs=[hbm] + [vmem] * 5,
        out_specs=(vmem,) * 3,
        out_shape=tuple(jax.ShapeDtypeStruct(shape, BF16) for shape in shapes),
        scratch_shapes=[
            pltpu.VMEM((EARLY - LAG + D1, channels), BF16),
            pltpu.VMEM((EARLY - LAG + D2, hid), BF16),
            pltpu.SemaphoreType.DMA((2,)),
        ],
        compiler_params=pltpu.CompilerParams(vmem_limit_bytes=12 * MIB),
    )(in_hbm(frames), near, before, w1, b1, w2)


def head_kernel(near_ref, halo_ref, w1_ref, b1_ref, w2_ref, out_ref, xs, hs):
    half = LAG // 2
    hid, feat = w1_ref.shape[1], w2_ref.shape[1]
    for index in range(xs.shape[1] // feat):
        part = slice(D2 + index * D1, D2 + (index + 1) * D1)
        xs[:D1, index * feat : (index + 1) * feat] = halo_ref[part, :]
    xs[D1:, :] = near_ref[:half, :]
    for at in range(0, half, D2):
        hs[at : at + D2, :] = hidden_rows(xs, at, D2, w1_ref, b1_ref)
    value = jnp.dot(hs[:D2, :], w2_ref[:hid, :], preferred_element_type=F32)
    out_ref[:D2, :] = (value + halo_ref[:D2, :].astype(F32)).astype(BF16)
    out_ref[D2:, :] = feature_rows(hs, 0, half - D2, w2_ref)


def head_rows(near, halo, w1, b1, w2):
    vmem = pl.BlockSpec(memory_space=pltpu.VMEM)
    half, channels, hid = LAG // 2, near.shape[1], w1.shape[1]
    return pl.pallas_call(
        head_kernel,
        in_specs=[vmem] * 5,
        out_specs=vmem,
        out_shape=jax.ShapeDtypeStruct((half, w2.shape[1]), BF16),
        scratch_shapes=[pltpu.VMEM((half + D1, channels), BF16), pltpu.VMEM((half, hid), BF16)],
        compiler_params=pltpu.CompilerParams(vmem_limit_bytes=8 * MIB),
    )(near, halo, w1, b1, w2)


def body_kernel(far_ref, head_ref, early_ref, middle_ref, hidden_ref, w1_ref, b1_ref, w2_ref, out_ref, hs):
    rows = out_ref.shape[0]
    steps = (rows - EARLY) // CHUNK
    half = LAG // 2
    hs[:D2, :] = hidden_ref[...]
    out_ref[:half, :] = head_ref[...]
    out_ref[half:LAG, :] = early_ref[...]
    out_ref[LAG:EARLY, :] = middle_ref[...]
    for step in range(steps + 1):
        at = step * CHUNK
        if step < steps:
            hs[D2 + at : D2 + at + CHUNK, :] = hidden_rows(far_ref, at, CHUNK, w1_ref, b1_ref)
        if step:
            out_ref[EARLY + at - CHUNK : EARLY + at, :] = feature_rows(hs, at - CHUNK, CHUNK, w2_ref)


def body(far, head, early, middle, hidden, w1, b1, w2):
    rows, hid, feat = far.shape[0] - D1 + EARLY, w1.shape[1], w2.shape[1]
    vmem = pl.BlockSpec(memory_space=pltpu.VMEM)
    return pl.pallas_call(
        body_kernel,
        in_specs=[vmem] * 8,
        out_specs=vmem,
        out_shape=jax.ShapeDtypeStruct((rows, feat), BF16),
        scratch_shapes=[pltpu.VMEM((rows - EARLY + D2, hid), BF16)],
        compiler_params=pltpu.CompilerParams(vmem_limit_bytes=16 * MIB),
    )(far, head, early, middle, hidden, w1, b1, w2)


def column_sum(rows):
    parts = rows.astype(F32).reshape(4, -1, 8, rows.shape[1])
    return jnp.sum(jnp.sum(parts, 1), 0)


def moment_kernel(feature_ref, inst, lag, total, turned_ref):
    rows, feat = feature_ref.shape
    turned_ref[...] = feature_ref[rows - LAG :, :].T
    tm_index, tm_last = lax.axis_index("tm"), lax.axis_size("tm") - 1
    for at in range(0, rows, LAG):
        weight = 2.0
        if at == 0:
            weight = jnp.where(tm_index == 0, 1.0, 2.0)
        elif at == rows - LAG:
            weight = jnp.where(tm_index == tm_last, 1.0, 2.0)
        now = feature_ref[at : at + LAG, :]
        if at == 0:
            inst[...] = weight * gram(now, now)
            total[...] = weight * column_sum(now)
            continue
        both = gram(now, jnp.concatenate([now, feature_ref[at - LAG : at, :]], 1))
        inst[...] += weight * both[:, :feat]
        lag[...] = both[:, feat:] if at == LAG else lag[...] + both[:, feat:]
        total[...] += weight * column_sum(now)


def moments(feature):
    feat = feature.shape[1]
    vmem = pl.BlockSpec(memory_space=pltpu.VMEM)
    square = jax.ShapeDtypeStruct((feat, feat), F32)
    return pl.pallas_call(
        moment_kernel,
        in_specs=[vmem],
        out_specs=(vmem,) * 4,
        out_shape=(
            square,
            square,
            jax.ShapeDtypeStruct((8, feat), F32),
            jax.ShapeDtypeStruct((feat, LAG), BF16),
        ),
        compiler_params=pltpu.CompilerParams(vmem_limit_bytes=12 * MIB),
    )(feature)


def pack_kernel(turned_ref, ahead_head_ref, ahead_early_ref, inst, lag, total, kept_ref, sent_ref, packed):
    feat = inst.shape[0]
    half = LAG // 2
    cross = lag[...] + jnp.dot(turned_ref[:, :half], ahead_head_ref[...], preferred_element_type=F32)
    cross += jnp.dot(turned_ref[:, half:], ahead_early_ref[...], preferred_element_type=F32)
    both = cross + cross.T
    row = lax.broadcasted_iota(jnp.int32, (feat, feat), 0)
    column = lax.broadcasted_iota(jnp.int32, (feat, feat), 1)
    packed[...] = jnp.where(column >= row, inst[...], both)
    sums = jnp.sum(total[...], 0, keepdims=True)
    diagonal = jnp.sum(jnp.where(column == row, both, 0.0), 0, keepdims=True)
    core = lax.axis_index("core")
    for ref, owner in ((kept_ref, core), (sent_ref, 1 - core)):
        extra = jnp.where(owner == 0, sums, diagonal)
        chunks = ref.shape[0]
        for index, lanes in slots(ref.shape, feat):
            at = pl.multiple_of(owner * (feat // 2) + index * chunks, 8)
            ref[:, 0, lanes] = packed[pl.ds(at, chunks), :]
        for chunk in range(chunks):
            part = extra[:, chunk * 128 : chunk * 128 + 128] if chunk < feat // 128 else jnp.zeros((1, 128), F32)
            ref[chunk, 0:1, ref.shape[2] - 128 :] = part


def slots(shape, feat):
    for index in range((shape[2] - 128) // feat):
        yield index, slice(index * feat, (index + 1) * feat)


def pack(turned, ahead_head, ahead_early, inst, lag, total, chips):
    vmem = pl.BlockSpec(memory_space=pltpu.VMEM)
    feat = inst.shape[0]
    share = jax.ShapeDtypeStruct((chips, 1, feat // 2 // chips * feat + 128), F32)
    return pl.pallas_call(
        pack_kernel,
        in_specs=[vmem] * 6,
        out_specs=(vmem, vmem),
        out_shape=(share, share),
        scratch_shapes=[pltpu.VMEM((feat, feat), F32)],
        compiler_params=pltpu.CompilerParams(vmem_limit_bytes=8 * MIB),
    )(turned, ahead_head, ahead_early, inst, lag, total)


def three_parts(x):
    high = x.astype(BF16)
    rest = x - high.astype(F32)
    middle = rest.astype(BF16)
    low = (rest - middle.astype(F32)).astype(BF16)
    return high, middle, low


def product(a, b):
    high, middle, low = a
    left = jnp.concatenate([high, high, middle, high, low, middle], 1)
    high, middle, low = b
    right = jnp.concatenate([high, middle, high, low, high, middle], 0)
    return jnp.dot(left, right, preferred_element_type=F32)


def eliminate(rows, start, size):
    lane = lax.broadcasted_iota(jnp.int32, (8, size), 1) - start
    sub = lax.broadcasted_iota(jnp.int32, (8, size), 0)
    sub_narrow = lax.broadcasted_iota(jnp.int32, (8, 128), 0)
    tiles = range(len(rows))

    def wide(x):
        return jnp.concatenate([x] * (size // 128), 1)

    def spread(x, j):
        return jnp.broadcast_to(x[j : j + 1, :], x.shape)

    columns = [
        [jnp.broadcast_to(rows[h][:, start + k : start + k + 1], (8, 128)) for h in tiles]
        for k in range(PANEL)
    ]
    inside = (lane >= 0) & (lane < PANEL)
    rows = [jnp.where(inside, jnp.where(lane == sub + 8 * h, 1.0, 0.0), rows[h]) for h in tiles]
    pivots = [jnp.ones((8, 128), F32) for _ in range(PANEL // 8)]
    pivot = spread(columns[0][0], 0)
    for j in range(PANEL):
        inverse = pl.reciprocal(pivot, approx=True)
        here, at = divmod(j, 8)
        pivots[here] = jnp.where(sub_narrow == at, pivot, pivots[here])
        beside = {k: spread(columns[j][k // 8], k % 8) for k in range(j + 1, PANEL)}
        if beside:
            there, after = divmod(j + 1, 8)
            pivot = spread(columns[j + 1][there], after) - beside[j + 1] * beside[j + 1] * inverse
        panel_row = spread(rows[here], at)
        for h in tiles:
            if 8 * h + 7 <= j:
                continue
            factor = columns[j][h] * inverse
            if h == here:
                factor = jnp.where(sub_narrow > at, factor, 0.0)
            for k in beside:
                if 8 * h + 7 >= k:
                    columns[k][h] = columns[k][h] - factor * beside[k]
            rows[h] = rows[h] - wide(factor) * panel_row
    return [rows[h] * wide(lax.rsqrt(pivots[h])) if h < len(pivots) else rows[h] for h in tiles]


def inverse_factor(work):
    size = work.shape[0]
    for start in range(0, size, SUPER):
        stop = start + SUPER
        rows = [work[at : at + 8, :] for at in range(start, stop, 8)]
        for at in range(0, SUPER, PANEL):
            rows[at // 8 :] = eliminate(rows[at // 8 :], start + at, size)
        row = lax.broadcasted_iota(jnp.int32, (SUPER, size), 0)
        column = lax.broadcasted_iota(jnp.int32, (SUPER, size), 1) - start
        panel = jnp.where((column > row) & (column < SUPER), 0.0, jnp.concatenate(rows, 0))
        work[start:stop, :] = panel
        if stop < size:
            high, middle, low = three_parts(panel)
            left = jnp.concatenate([high, high, middle, high, low, middle], 0)
            right = jnp.concatenate([high, middle, high, low, high, middle], 0)
            first = stop // 128 * 128
            update = gram(left[:, first:], right)
            for at in range(0, size, 128):
                lanes = slice(at, at + 128)
                old = work[stop:, lanes]
                if at <= start < at + 128:
                    place = lax.broadcasted_iota(jnp.int32, old.shape, 1) + at
                    old = jnp.where((place < start) | (place >= stop), old, 0.0)
                work[stop:, lanes] = old - update[stop - first :, lanes]
    row = lax.broadcasted_iota(jnp.int32, (size, size), 0)
    column = lax.broadcasted_iota(jnp.int32, (size, size), 1)
    return jnp.where(column <= row, work[...], 0.0)


def koopman_kernel(
    scale_ref, mine_ref, other_ref, feature_ref, ahead_head_ref, ahead_early_ref, moved_out, residual_out,
    work, packed_ref, split_ref, shift_ref, moved, residual, sems,
):
    feat = packed_ref.shape[1]
    scale = scale_ref[0]
    core = lax.axis_index("core")
    extras = []
    for ref, owner in ((mine_ref, core), (other_ref, 1 - core)):
        chunks = ref.shape[0]
        for index, lanes in slots(ref.shape, feat):
            at = pl.multiple_of(owner * (feat // 2) + index * chunks, 8)
            packed_ref[pl.ds(at, chunks), :] = ref[:, 0, lanes]
        parts = [ref[chunk, 0:1, ref.shape[2] - 128 :] for chunk in range(feat // 128)]
        extras.append(jnp.concatenate(parts, 1))
    packed = packed_ref[...]
    mean = jnp.where(core == 0, extras[0], extras[1]) * scale
    diagonal = jnp.where(core == 0, extras[1], extras[0])
    row = lax.broadcasted_iota(jnp.int32, (feat, feat), 0)
    column = lax.broadcasted_iota(jnp.int32, (feat, feat), 1)
    turned = packed.T
    mean_column = jnp.broadcast_to(jnp.broadcast_to(mean, (8, feat)).T[:, 0:1], (feat, feat))
    centre = mean_column * mean
    inst = jnp.where(column >= row, packed, turned)
    lag = jnp.where(column < row, packed, turned)
    lag = jnp.where(column == row, jnp.broadcast_to(diagonal, (feat, feat)), lag)
    work[...] = inst * scale - centre + jnp.where(column == row, RIDGE, 0.0)
    lag = lag * scale - centre
    inverse = inverse_factor(work)
    turned_parts = three_parts(inverse.T)
    half_step = product(three_parts(inverse), three_parts(lag))
    koopman_part = three_parts(product(three_parts(half_step), turned_parts))
    moved_parts = three_parts(product(turned_parts, koopman_part))
    for index, (high, middle, _) in enumerate((turned_parts, moved_parts)):
        split_ref[index, :feat, :] = high
        split_ref[index, feat:, :] = middle
        matrix = high.astype(F32) + middle.astype(F32)
        shift = jnp.sum(mean_column * matrix, 0, keepdims=True)
        shift_ref[index] = jnp.broadcast_to(shift, (8, feat))
    project_rows(
        feature_ref, ahead_head_ref, ahead_early_ref, split_ref, shift_ref, moved_out, residual_out, moved, residual, sems
    )


def project_rows(
    feature_ref, ahead_head_ref, ahead_early_ref, split_ref, shift_ref, moved_out, residual_out, moved, residual, sems
):
    rows = feature_ref.shape[0]
    at_end = lax.axis_index("tm") == lax.axis_size("tm") - 1

    def image(block, index):
        twice = jnp.concatenate([block, block], 1)
        return jnp.dot(twice, split_ref[index], preferred_element_type=F32) - shift_ref[index][0:1]

    copies = []
    for step in range(rows // PIECE):
        here = slice(step * PIECE, (step + 1) * PIECE)
        start = step * PIECE + LAG
        if start < rows:
            later = feature_ref[start : start + PIECE, :]
        else:
            ahead_ref = ahead_head_ref if start - rows < LAG // 2 else ahead_early_ref
            at = (start - rows) % (LAG // 2)
            later = ahead_ref[at : at + PIECE, :]
        now = image(feature_ref[here, :], 1)
        moved[here, :] = now
        gap = image(later, 0) - now
        residual[here, :] = gap if start < rows else jnp.where(at_end, 0.0, gap)
        for index, (source, target) in enumerate(((moved, moved_out), (residual, residual_out))):
            copy = pltpu.make_async_copy(source.at[here], target.at[here], sems.at[index, step])
            copy.start()
            copies.append(copy)
    for copy in copies:
        copy.wait()


def project(scale, mine, other, feature, ahead_head, ahead_early):
    rows, feat = feature.shape
    vmem = pl.BlockSpec(memory_space=pltpu.VMEM)
    hbm = pl.BlockSpec(memory_space=pltpu.HBM)
    out = jax.ShapeDtypeStruct((rows, feat), F32)
    return pl.pallas_call(
        koopman_kernel,
        in_specs=[pl.BlockSpec(memory_space=pltpu.SMEM)] + [vmem] * 5,
        out_specs=(hbm, hbm),
        out_shape=(out, out),
        scratch_shapes=[
            pltpu.VMEM((feat, feat), F32),
            pltpu.VMEM((feat, feat), F32),
            pltpu.VMEM((2, 2 * feat, feat), BF16),
            pltpu.VMEM((2, 8, feat), F32),
            pltpu.VMEM((rows, feat), F32),
            pltpu.VMEM((rows, feat), F32),
            pltpu.SemaphoreType.DMA((2, rows // PIECE)),
        ],
        compiler_params=pltpu.CompilerParams(vmem_limit_bytes=32 * MIB),
    )(scale, mine, other, feature, ahead_head, ahead_early)


def summed(kept, sent):
    swap = [(0, 1), (1, 0)]
    chips = ("x", "tm")
    parts = kept + lax.ppermute(sent, "core", swap)
    mine = jnp.sum(lax.all_to_all(parts, chips, 0, 0, tiled=True), 0, keepdims=True)
    mine = lax.all_to_all(jnp.broadcast_to(mine, parts.shape), chips, 0, 0, tiled=True)
    return mine, lax.ppermute(mine, "core", swap)


def on_device(frames, first_weight, first_bias, second_weight):
    frame_block = frames[0]
    row_count, channels = frame_block.shape
    hid, feat = second_weight.shape[1:]
    weights = (
        first_weight.reshape(2 * channels, hid),
        first_bias.reshape(1, hid),
        second_weight.reshape(2 * hid, feat),
    )
    sent, near, *weights = tail_rows(frame_block, *weights)
    halo = passed_along(sent, "tm", 1)
    early, before = early_rows(near, *weights)
    ahead_early = passed_along(early, "tm", -1)
    middle, hidden, far = middle_rows(frame_block, near, before, *weights)
    halo, hidden = lax.optimization_barrier((halo, hidden))
    head = head_rows(near, halo, *weights)
    ahead_head = passed_along(head, "tm", -1)
    feature = body(far, head, early, middle, hidden, *weights)
    inst, lag, total, turned = moments(feature)
    chips = lax.axis_size("x") * lax.axis_size("tm")
    mine, other = summed(*pack(turned, ahead_head, ahead_early, inst, lag, total, chips))
    replicas = lax.axis_size("x") * lax.axis_size("core")
    pair_count = replicas * (row_count * lax.axis_size("tm") - LAG)
    scale = jnp.full((1,), 1.0 / (2.0 * pair_count), F32)
    propagated, residual = project(scale, mine, other, feature, ahead_head, ahead_early)
    return (propagated[None], residual[None])


def solution(mesh):
    replicas, blocks = mesh.devices.shape
    chips = Mesh(mesh.devices.reshape(replicas // 2, 2, blocks), ("x", "core", "tm"))
    split = P(("x", "core"), "tm", None)
    return jax.shard_map(
        on_device,
        mesh=chips,
        in_specs=(split, P(), P(), P()),
        out_specs=(split, split),
        check_vma=False,
    )
```
